256 devices in a mesh: seq: 64 (over z, x, core), heads: 4 (over y).
Axes of the slice: x: 4, y: 4, z: 8, core: 2. Of those that a mesh axis runs over, the one named last changes fastest.
Arguments:
- q_delta: bfloat16 [8192, 4096], P('seq', 'heads'), may hold values from -6 to 6
- k_delta: bfloat16 [8192, 4096], P('seq', 'heads'), may hold values from -6 to 6
- v_delta: bfloat16 [8192, 4096], P('seq', 'heads'), may hold values from -6 to 6
- decay: float32 [32, 8192], P('heads', 'seq'), may hold values from 0 to 2
- beta: float32 [32, 8192], P('heads', 'seq'), may hold values from 0 to 1
- gain: float32 [128], replicated, may hold values from 0.1 to 1.9
- attn_weight: bfloat16 [32, 128, 384], P('heads'), may hold values from -5 to 5
- out_weight: bfloat16 [4096, 4096], P('heads'), may hold values from -0.09375 to 0.09375
Outputs:
- block_out: bfloat16 [8192, 4096], P(('seq', 'heads'))
The draws below stay inside these ranges and needn't reach their ends.
All inputs are finite; a program needn't handle non-finite values.
Results may differ from the reference program's by a relative error of at most 0.0142.
Values may be sent and summed in bfloat16 or wider, within the bound.
No kernel may reach another device: no remote copies, remote signals or barrier semaphores. Data moves between devices by JAX's collectives and lax.ppermute only.
A program may use at most 256 MiB of HBM per device.

```python
import math
import jax
import jax.numpy as jnp
from jax import lax

D = 4096
HEADS = 32
HDIM = 128
WINDOW = 1024
TOK_DEV = 128
TOKENS = 8192


def head_flags(key, share):
    picks = jax.random.uniform(jax.random.fold_in(key, 101), (HEADS,), jnp.float32)
    return (picks < share).astype(jnp.float32)[:, None]


def roughness(key, shape):
    return jnp.exp(jax.random.uniform(key, shape, jnp.float32, -0.6931, 0.6931))


def draw_decay(key, part):
    share = 0.5
    longest = 400.0
    slow = head_flags(key, share)
    key = jax.random.fold_in(key, 1)
    first, second, third, fourth, fifth = jax.random.split(key, 5)
    fast_rate = jnp.exp(jax.random.uniform(first, (HEADS, 1), jnp.float32, math.log(1.0 / longest), math.log(1.0 / 20.0)))
    slow_rate = jax.random.uniform(second, (HEADS, 1), jnp.float32, 0.2, 1.0) / TOKENS
    base_rate = slow * slow_rate + (1.0 - slow) * fast_rate
    update_strengths = base_rate * roughness(third, (HEADS, TOKENS))
    spots = jax.random.randint(fourth, (HEADS, 2), 0, TOKENS)
    objective_scores = jax.random.uniform(fifth, (HEADS, 2), jnp.float32, 0.2, 0.5)
    positions = jnp.arange(TOKENS, dtype=jnp.int32)
    span_matches = positions[None, None, :] == spots[:, :, None]
    spike_tally = jnp.sum(jnp.where(span_matches, -jnp.log(1.0 - objective_scores)[:, :, None], 0.0), axis=1)
    return update_strengths + spike_tally


def draw_beta(key, part):
    share = 0.5
    slow = head_flags(key, share)
    key = jax.random.fold_in(key, 2)
    first, second, third, fourth = jax.random.split(key, 4)
    slow_beta = jax.random.uniform(first, (HEADS, 1), jnp.float32, 0.1, 0.5) * HDIM / TOKENS
    slow_beta = slow_beta * roughness(third, (HEADS, TOKENS))
    fast_level = jnp.exp(jax.random.uniform(second, (HEADS, 1), jnp.float32, math.log(0.15), 0.0))
    fast_beta = fast_level * jax.random.uniform(fourth, (HEADS, TOKENS), jnp.float32, 0.5, 1.0)
    return slow * slow_beta + (1.0 - slow) * fast_beta


def draw_attn_weight(key, part):
    key = jax.random.fold_in(key, 3)
    first, second = jax.random.split(key, 2)
    factor = HDIM ** (-0.5)
    query_key = jnp.clip(jax.random.normal(first, (HEADS, HDIM, 2 * HDIM), jnp.float32), -4.0, 4.0) * factor
    values = jnp.clip(jax.random.normal(second, (HEADS, HDIM, HDIM), jnp.float32), -4.0, 4.0) * factor
    return jnp.concatenate([query_key, values], axis=-1).astype(jnp.bfloat16)


def level_of(key, extent, shards, low, top_value):
    loudness, own = 1.0, jax.random.fold_in(key, 6)
    for axis_at, parts in shards:
        draws = jnp.exp(jax.random.uniform(jax.random.fold_in(own, axis_at), (parts,), jnp.float32, low / len(shards), top_value / len(shards)))
        loudness = loudness * jnp.repeat(draws, extent[axis_at] // parts).reshape([-1 if axis == axis_at else 1 for axis in range(len(extent))])
    return loudness


def noise(own_key, extent, width, bound, cuts=(), kind=jnp.bfloat16):
    array = width * jax.random.normal(own_key, extent, jnp.float32)
    if cuts:
        array = array * level_of(own_key, extent, cuts, -0.22, 0.18)
    return jnp.clip(array, -bound, bound).astype(kind)


def setup_inputs(seed: int = 0) -> dict:
    splits = jax.random.split(jax.random.key(seed), 9)
    q_delta = noise(splits[0], (TOKENS, D), 1.0, 6.0, ((0, 64), (1, 4)))
    k_delta = noise(splits[1], (TOKENS, D), 1.0, 6.0, ((0, 64), (1, 4)))
    v_delta = noise(splits[2], (TOKENS, D), 1.0, 6.0, ((0, 64), (1, 4)))
    decay = draw_decay(jax.random.fold_in(splits[8], 71), 0)
    beta = draw_beta(jax.random.fold_in(splits[8], 71), 0)
    gain = jnp.clip(1.0 + 0.18 * jax.random.normal(splits[5], (HDIM,), jnp.float32), 0.1, 1.9)
    attn_weight = draw_attn_weight(jax.random.fold_in(splits[8], 71), 0)
    out_weight = noise(splits[7], (D, D), D ** -0.5, 0.09375, ((0, 4),))
    return {"q_delta": q_delta, "k_delta": k_delta, "v_delta": v_delta, "decay": decay, "beta": beta, "gain": gain, "attn_weight": attn_weight, "out_weight": out_weight}


def normalize(values, factor):
    return values * lax.rsqrt(lax.optimization_barrier(jnp.sum(values * values, axis=-1, keepdims=True)) + 1e-06) * factor

def reference(q_delta, k_delta, v_delta, decay, beta, gain, attn_weight, out_weight):
    length = q_delta.shape[0]

    def by_heads(values):
        return values.astype(jnp.float32).reshape(length, HEADS, HDIM)
    probe_vectors = normalize(by_heads(q_delta), HDIM ** (-0.5))
    key_rows = normalize(by_heads(k_delta), 1.0)
    values = by_heads(v_delta)
    alphas = jnp.exp(-decay).T
    betas = beta.T

    def step_forward(carried, inputs_now):
        key_now, value_now, query_now, alpha_now, beta_now = inputs_now
        against = jnp.einsum('hd,hdv->hv', key_now, carried, precision=lax.Precision.HIGHEST)
        erased_state = carried - beta_now[:, None, None] * key_now[:, :, None] * against[:, None, :]
        carried = alpha_now[:, None, None] * erased_state + beta_now[:, None, None] * key_now[:, :, None] * value_now[:, None, :]
        result = jnp.einsum('hd,hdv->hv', query_now, carried, precision=lax.Precision.HIGHEST)
        return (carried, result)
    initial = jnp.zeros((HEADS, HDIM, HDIM), jnp.float32)
    unused, delta_out = lax.scan(step_forward, initial, (key_rows, values, probe_vectors, alphas, betas))
    normed = (delta_out * lax.rsqrt(lax.optimization_barrier(jnp.mean(delta_out * delta_out, axis=-1, keepdims=True)) + 1e-06) * gain).astype(jnp.bfloat16)
    projected = jnp.einsum('thd,hde->hte', normed.astype(jnp.float32), attn_weight.astype(jnp.float32)).astype(jnp.bfloat16)
    query_two = projected[..., :HDIM]
    padding = jnp.zeros((HEADS, WINDOW, HDIM), jnp.bfloat16)
    key_all = jnp.concatenate([padding, projected[..., HDIM:2 * HDIM]], axis=1)
    value_all = jnp.concatenate([padding, projected[..., 2 * HDIM:]], axis=1)
    query_block = min(512, TOK_DEV)
    key_span = query_block + WINDOW

    def attend(block_index):
        begin_row = (block_index * query_block).astype(jnp.int32)
        query_now = lax.dynamic_slice_in_dim(query_two, begin_row, query_block, 1)
        key_slice = lax.dynamic_slice_in_dim(key_all, begin_row, key_span, 1)
        value_slice = lax.dynamic_slice_in_dim(value_all, begin_row, key_span, 1)
        scores = jnp.einsum('htd,hsd->hts', query_now.astype(jnp.float32), key_slice.astype(jnp.float32)) * HDIM ** (-0.5)
        line_position = lax.broadcasted_iota(jnp.int32, (query_block, key_span), 0)
        col_index = lax.broadcasted_iota(jnp.int32, (query_block, key_span), 1)
        allowed = (col_index > line_position) & (col_index <= line_position + WINDOW) & (col_index >= WINDOW - begin_row)
        masked = jnp.where(allowed[None], scores, -1e+30)
        row_maximum = lax.optimization_barrier(jnp.max(masked, axis=-1, keepdims=True))
        raised = jnp.exp(masked - row_maximum)
        weights = (raised / lax.optimization_barrier(jnp.sum(raised, axis=-1, keepdims=True))).astype(jnp.bfloat16)
        return jnp.einsum('hts,hsd->htd', weights.astype(jnp.float32), value_slice.astype(jnp.float32)).astype(jnp.bfloat16)
    pieces = lax.map(attend, jnp.arange(length // query_block, dtype=jnp.int32))
    attended = pieces.transpose(1, 0, 2, 3).reshape(HEADS, length, HDIM)
    flat_heads = attended.transpose(1, 0, 2).reshape(length, D)
    return jnp.dot(flat_heads, out_weight, preferred_element_type=jnp.float32).astype(jnp.bfloat16)
```

```python
import jax
import jax.numpy as jnp
from jax import lax
from jax.experimental import pallas as pl
from jax.experimental.pallas import tpu as pltpu
from jax.sharding import PartitionSpec as P

F32 = jnp.float32
BF16 = jnp.bfloat16
C = 128
PLANE = 8
PLANES = 8
BLK = 3 * C + 16
EPS = 1e-06
NEG = -1e30
VMEM_LIMIT = 48 * 1024 * 1024


def params():
    return pltpu.CompilerParams(vmem_limit_bytes=VMEM_LIMIT)


def cost(flops, nbytes, trans=0):
    return pl.CostEstimate(flops=int(flops), bytes_accessed=int(nbytes), transcendentals=int(trans))


def vmem():
    return pl.BlockSpec(memory_space=pltpu.VMEM)


def smem():
    return pl.BlockSpec(memory_space=pltpu.SMEM)


def split(a):
    hi = a.astype(BF16)
    lo = (a - hi.astype(F32)).astype(BF16)
    return hi, lo


def dot(a, b):
    return lax.dot_general(a, b, (((1,), (0,)), ((), ())), preferred_element_type=F32)


def dot_nt(a, b):
    return lax.dot_general(a, b, (((1,), (1,)), ((), ())), preferred_element_type=F32)


def dot_tn(a, b):
    return lax.dot_general(a, b, (((0,), (0,)), ((), ())), preferred_element_type=F32)


def mm(a, b):
    ah, al = split(a)
    bh, bl = split(b)
    return dot(ah, bh) + (dot(al, bh) + dot(ah, bl))


def mm_exact_right(a, b):
    ah, al = split(a)
    return dot(ah, b) + dot(al, b)


def iotas():
    row = lax.broadcasted_iota(jnp.int32, (C, C), 0)
    col = lax.broadcasted_iota(jnp.int32, (C, C), 1)
    return row, col


def pack_kernel(me_ref, q_ref, k_ref, v_ref, decay_ref, beta_ref, *rest):
    outs, scratch = rest[:PLANE], rest[PLANE]
    me = me_ref[0]

    def pieces(x):
        a = x.astype(BF16).astype(F32)
        b = (x - a).astype(BF16).astype(F32)
        c = ((x - a) - b).astype(BF16).astype(F32)
        return a, b, c

    for i, part in enumerate(pieces(decay_ref[...]) + pieces(beta_ref[...])):
        scratch[i] = part
    zeros = jnp.zeros((10, C), F32)
    for d in range(PLANE):
        head = jnp.bitwise_xor(me, d)
        cols = pl.ds(pl.multiple_of(head * C, C), C)
        out = outs[d]
        out[0:C, :] = k_ref[:, cols]
        out[C : 2 * C, :] = v_ref[:, cols]
        out[2 * C : 3 * C, :] = q_ref[:, cols]
        rows = [scratch[i, pl.ds(head, 1), :] for i in range(6)]
        out[3 * C :, :] = jnp.concatenate(rows + [zeros], axis=0).astype(BF16)


def pack(me, q, k, v, decay, beta):
    return pl.pallas_call(
        pack_kernel,
        out_shape=[jax.ShapeDtypeStruct((BLK, C), BF16)] * PLANE,
        in_specs=[smem()] + [vmem()] * 5,
        out_specs=[vmem()] * PLANE,
        scratch_shapes=[pltpu.VMEM((6, PLANE, C), F32)],
        compiler_params=params(),
        name="pack",
    )(me, q, k, v, decay, beta)


def gates(blocks):
    row, col = iotas()
    pieces = jnp.concatenate([b[3 * C :, :] for b in blocks], axis=0)
    upper = jnp.where(row <= col, 1.0, 0.0).astype(BF16)
    lower = jnp.where(row >= col, 1.0, 0.0).astype(BF16)
    eye = jnp.where(row == col, 1.0, 0.0).astype(BF16)
    along_row = dot(pieces, upper)
    along_col = dot_nt(jnp.concatenate([lower, eye], axis=0), pieces)
    plain = pieces.astype(F32)
    found = []
    for d in range(PLANE):
        o = 16 * d
        g_row = -(along_row[o : o + 1] + along_row[o + 1 : o + 2] + along_row[o + 2 : o + 3])
        b_row = plain[o + 3 : o + 4] + plain[o + 4 : o + 5] + plain[o + 5 : o + 6]
        g_col = -(
            along_col[:C, o : o + 1] + along_col[:C, o + 1 : o + 2] + along_col[:C, o + 2 : o + 3]
        )
        b_col = (
            along_col[C:, o + 3 : o + 4]
            + along_col[C:, o + 4 : o + 5]
            + along_col[C:, o + 5 : o + 6]
        )
        found.append((g_row, b_row, g_col, b_col))
    return found


def unit_lower_inverse(low, row, col):
    x = jnp.where(row == col, 1.0, 0.0) - jnp.where(
        (jnp.bitwise_xor(row, col) == 1) & (row > col), low, 0.0
    )
    size = 2
    while size < C:
        level = (row > col) & (jnp.bitwise_xor(row, col) >= size) & (
            jnp.bitwise_xor(row, col) < 2 * size
        )
        corner = jnp.where(level, low, 0.0)
        x = x - mm(mm(x, corner), x)
        size *= 2
    return x


def prep_kernel(me_ref, *refs):
    blocks = refs[:PLANE]
    mix_ref, wu_ref, ab_ref, level_ref = refs[PLANE : PLANE + 4]
    maps = refs[PLANE + 4]
    me = me_ref[0]
    row, col = iotas()
    eye = jnp.where(row == col, 1.0, 0.0)
    found = gates(blocks)
    for d in range(PLANE):
        g_row, b_row, g_col, b_col = found[d]
        keys = blocks[d][0:C, :]
        values = blocks[d][C : 2 * C, :]
        gram = dot_nt(keys, keys)
        diag = gram * eye
        r_col = lax.rsqrt(jnp.sum(diag, axis=1, keepdims=True) + EPS)
        r_row = lax.rsqrt(jnp.sum(diag, axis=0, keepdims=True) + EPS)
        ratio = jnp.where(row >= col, jnp.exp(jnp.minimum(g_col - g_row, 0.0)), 0.0)
        mix = ratio * (b_row * r_row)
        mix_ref[d] = mix
        low = jnp.where(row > col, mix * gram * r_col, 0.0)
        inverse = unit_lower_inverse(low, row, col)
        w = mm_exact_right(inverse * (jnp.exp(g_row) * r_row), keys)
        u = mm_exact_right(inverse, values)
        wu = jnp.concatenate([w, u], axis=1)
        wu_ref[d] = wu
        g_end = g_row[:, C - 1 : C]
        tail = jnp.exp(g_end - g_col) * b_col * r_col
        hi, lo = split(wu * tail)
        made = dot_tn(keys, hi) + dot_tn(keys, lo)
        chunk = jnp.bitwise_xor(me, d)
        maps[chunk] = jnp.concatenate([eye * jnp.exp(g_end) - made[:, :C], made[:, C:]], axis=1)

    def after(earlier, later):
        both = mm(later[:, :C], earlier)
        return jnp.concatenate([both[:, :C], both[:, C:] + later[:, C:]], axis=1)

    one = [maps[i] for i in range(PLANE)]
    two = [after(one[2 * i], one[2 * i + 1]) for i in range(4)]
    four = [after(two[2 * i], two[2 * i + 1]) for i in range(2)]
    ab_ref[...] = after(four[0], four[1])
    level_ref[0] = one[0]
    level_ref[1] = two[0]
    level_ref[2] = one[2]
    level_ref[3] = four[0]
    level_ref[4] = one[4]
    level_ref[5] = two[2]
    level_ref[6] = one[6]


def prep(me, blocks):
    return pl.pallas_call(
        prep_kernel,
        out_shape=[
            jax.ShapeDtypeStruct((PLANE, C, C), F32),
            jax.ShapeDtypeStruct((PLANE, C, 2 * C), F32),
            jax.ShapeDtypeStruct((C, 2 * C), F32),
            jax.ShapeDtypeStruct((7, C, 2 * C), F32),
        ],
        in_specs=[smem()] + [vmem()] * PLANE,
        out_specs=[vmem()] * 4,
        scratch_shapes=[pltpu.VMEM((PLANE, C, 2 * C), F32)],
        compiler_params=params(),
        cost_estimate=cost(2e9, 4e6),
        name="prep",
    )(me, *blocks)


def query_kernel(me_ref, *refs):
    blocks = refs[:PLANE]
    mix_ref, wu_ref, level_ref, no_ref, before = refs[PLANE:]
    me = me_ref[0]
    row, col = iotas()
    eye = jnp.where(row == col, 1.0, 0.0)

    def after(earlier, later):
        both = mm(later[:, :C], earlier)
        return jnp.concatenate([both[:, :C], both[:, C:] + later[:, C:]], axis=1)

    before[0] = jnp.concatenate([eye, jnp.zeros((C, C), F32)], axis=1)
    before[1] = level_ref[0]
    before[2] = level_ref[1]
    before[3] = after(level_ref[1], level_ref[2])
    before[4] = level_ref[3]
    before[5] = after(level_ref[3], level_ref[4])
    six = after(level_ref[3], level_ref[5])
    before[6] = six
    before[7] = after(six, level_ref[6])
    found = gates(blocks)
    for d in range(PLANE):
        g_row, b_row, g_col, b_col = found[d]
        keys = blocks[d][0:C, :]
        queries = blocks[d][2 * C : 3 * C, :]
        wide = queries.astype(F32)
        r_col = lax.rsqrt(jnp.sum(wide * wide, axis=1, keepdims=True) + EPS) * (C**-0.5)
        scored = dot_nt(queries, keys) * r_col * mix_ref[d]
        part = mm(scored, wu_ref[d])
        reach = wide * (r_col * jnp.exp(g_col)) - part[:, :C]
        chunk = jnp.bitwise_xor(me, d)
        both = mm(reach, before[chunk])
        rows = pl.ds(pl.multiple_of(chunk * C, C), C)
        no_ref[rows, :] = jnp.concatenate([both[:, :C], both[:, C:] + part[:, C:]], axis=1)


def query(me, blocks, mix, wu, level):
    return pl.pallas_call(
        query_kernel,
        out_shape=jax.ShapeDtypeStruct((PLANE * C, 2 * C), F32),
        in_specs=[smem()] + [vmem()] * (PLANE + 3),
        out_specs=vmem(),
        scratch_shapes=[pltpu.VMEM((PLANE, C, 2 * C), F32)],
        compiler_params=params(),
        cost_estimate=cost(1e9, 4e6),
        name="query",
    )(me, *blocks, mix, wu, level)


def norm_kernel(no_ref, gain_ref, *refs):
    maps, normed_ref = refs[:-1], refs[-1]
    state = maps[-1][:, C:]
    for ab in reversed(maps[:-1]):
        state = mm(ab[:, :C], state) + ab[:, C:]
    out = mm(no_ref[:, :C], state) + no_ref[:, C:]
    scale = lax.rsqrt(jnp.mean(out * out, axis=1, keepdims=True) + EPS)
    normed_ref[...] = (out * scale * gain_ref[...]).astype(BF16)


def norm(no, gain, maps):
    return pl.pallas_call(
        norm_kernel,
        out_shape=jax.ShapeDtypeStruct((PLANE * C, C), BF16),
        in_specs=[vmem()] * (2 + len(maps)),
        out_specs=vmem(),
        compiler_params=params(),
        cost_estimate=cost(2e8, 2e6),
        name="norm",
    )(no, gain, *maps)


QB = 256


def own_kernel(me_ref, normed_ref, weight_ref, acc_ref, stat_ref, q2_ref):
    proj = dot(normed_ref[...], weight_ref[0]).astype(BF16)
    q2_ref[...] = proj[:, :C]
    row = lax.broadcasted_iota(jnp.int32, (QB, QB), 0)
    col = lax.broadcasted_iota(jnp.int32, (QB, QB), 1)
    for i in range(PLANE * C // QB):
        at = i * QB
        q = proj[at : at + QB, :C]
        s = dot_nt(q, proj[: at + QB, C : 2 * C]) * (C**-0.5)
        last = jnp.where(col <= row, s[:, at:], NEG)
        s = last if i == 0 else jnp.concatenate([s[:, :at], last], axis=1)
        top = jnp.max(s, axis=1, keepdims=True)
        p = jnp.exp(s - top)
        total = jnp.sum(p, axis=1, keepdims=True)
        acc_ref[at : at + QB, :] = dot(p.astype(BF16), proj[: at + QB, 2 * C :])
        stat_ref[0, at : at + QB, :] = jnp.broadcast_to(top, (QB, C))
        stat_ref[1, at : at + QB, :] = jnp.broadcast_to(total, (QB, C))


def own(me, normed, weight):
    n = PLANE * C
    return pl.pallas_call(
        own_kernel,
        out_shape=[
            jax.ShapeDtypeStruct((n, C), F32),
            jax.ShapeDtypeStruct((2, n, C), F32),
            jax.ShapeDtypeStruct((n, C), BF16),
        ],
        grid_spec=pltpu.PrefetchScalarGridSpec(
            num_scalar_prefetch=1,
            grid=(1,),
            in_specs=[
                pl.BlockSpec((n, C), lambda i, me: (0, 0)),
                pl.BlockSpec((1, C, 3 * C), lambda i, me: (me[0], 0, 0)),
            ],
            out_specs=[
                pl.BlockSpec((n, C), lambda i, me: (0, 0)),
                pl.BlockSpec((2, n, C), lambda i, me: (0, 0, 0)),
                pl.BlockSpec((n, C), lambda i, me: (0, 0)),
            ],
        ),
        compiler_params=params(),
        cost_estimate=cost(1e9, 3e6, 6e5),
        name="own",
    )(me, normed, weight)


def halo_kernel(me_ref, halo_ref, weight_ref, acc_ref, stat_ref, q2_ref, *refs):
    outs, attended = refs[:PLANE], refs[PLANE]
    me, plane = me_ref[0], me_ref[1]
    proj = dot(halo_ref[...], weight_ref[0, :, C:]).astype(BF16)
    n = PLANE * C
    for i in range(n // QB):
        at = i * QB
        row = lax.broadcasted_iota(jnp.int32, (QB, n - at), 0)
        col = lax.broadcasted_iota(jnp.int32, (QB, n - at), 1)
        allowed = (col > row) & (plane > 0)
        s = dot_nt(q2_ref[at : at + QB, :], proj[at:, :C]) * (C**-0.5)
        s = jnp.where(allowed, s, NEG)
        before = stat_ref[0, at : at + QB, 0:1]
        top = jnp.maximum(jnp.max(s, axis=1, keepdims=True), before)
        p = jnp.where(allowed, jnp.exp(s - top), 0.0)
        keep = jnp.exp(before - top)
        total = jnp.sum(p, axis=1, keepdims=True) + keep * stat_ref[1, at : at + QB, 0:1]
        acc = acc_ref[at : at + QB, :] * keep + dot(p.astype(BF16), proj[at:, C:])
        attended[at : at + QB, :] = (acc / total).astype(BF16)
    for d in range(PLANE):
        chunk = jnp.bitwise_xor(me, d)
        outs[d][...] = attended[pl.ds(pl.multiple_of(chunk * C, C), C), :]


def halo_part(me, halo, weight, acc, stat, q2):
    n = PLANE * C
    return pl.pallas_call(
        halo_kernel,
        out_shape=[jax.ShapeDtypeStruct((C, C), BF16)] * PLANE,
        grid_spec=pltpu.PrefetchScalarGridSpec(
            num_scalar_prefetch=1,
            grid=(1,),
            in_specs=[
                pl.BlockSpec((n, C), lambda i, me: (0, 0)),
                pl.BlockSpec((1, C, 3 * C), lambda i, me: (me[0], 0, 0)),
                pl.BlockSpec((n, C), lambda i, me: (0, 0)),
                pl.BlockSpec((2, n, C), lambda i, me: (0, 0, 0)),
                pl.BlockSpec((n, C), lambda i, me: (0, 0)),
            ],
            out_specs=[pl.BlockSpec((C, C), lambda i, me: (0, 0))] * PLANE,
            scratch_shapes=[pltpu.VMEM((n, C), BF16)],
        ),
        compiler_params=params(),
        cost_estimate=cost(1e9, 3e6, 6e5),
        name="halo",
    )(me, halo, weight, acc, stat, q2)


COLS = 512


def project_kernel(me_ref, *refs):
    blocks = refs[:PLANE]
    weight_ref = refs[PLANE]
    outs = refs[PLANE + 1 : PLANE + 5]
    flat = refs[PLANE + 5]
    me, mine = me_ref[0], me_ref[2]

    @pl.when(pl.program_id(0) == 0)
    def _():
        for d in range(PLANE):
            head = jnp.bitwise_xor(me, d)
            cols = pl.ds(pl.multiple_of(head * C, C), C)
            for e in range(4):
                rows = pl.ds(pl.multiple_of(jnp.bitwise_xor(mine, e) * 32, 32), 32)
                flat[e * 32 : e * 32 + 32, cols] = blocks[d][rows, :]

    got = dot(flat[...], weight_ref[...])
    for e in range(4):
        outs[e][...] = got[e * 32 : e * 32 + 32].astype(outs[e].dtype)


def project(me, blocks, weight):
    depth, width = weight.shape
    return pl.pallas_call(
        project_kernel,
        out_shape=[jax.ShapeDtypeStruct((32, width), F32)]
        + [jax.ShapeDtypeStruct((32, width), BF16)] * 3,
        grid_spec=pltpu.PrefetchScalarGridSpec(
            num_scalar_prefetch=1,
            grid=(width // COLS,),
            in_specs=[pl.BlockSpec((C, C), lambda i, me: (0, 0))] * PLANE
            + [pl.BlockSpec((depth, COLS), lambda i, me: (0, i))],
            out_specs=[pl.BlockSpec((32, COLS), lambda i, me: (0, i))] * 4,
            scratch_shapes=[pltpu.VMEM((C, depth), BF16)],
        ),
        compiler_params=params(),
        cost_estimate=cost(1e9, 9e6),
        name="project",
    )(me, *blocks, weight)


def exchange(blocks):
    moved = [blocks[0]]
    for d in range(1, PLANE):
        route = [(s, s ^ d) for s in range(PLANE * PLANES)]
        moved.append(lax.ppermute(blocks[d], "seq", route))
    return moved


def later_plane(block, distance):
    n = PLANE * PLANES
    step = PLANE * distance
    return lax.ppermute(block, "seq", [(s, s + step) for s in range(n - step)])


def local(q_delta, k_delta, v_delta, decay, beta, gain, attn_weight, out_weight):
    place = lax.axis_index("seq")
    mine = lax.axis_index("heads")
    me = jnp.stack([place % PLANE, place // PLANE, mine]).astype(jnp.int32)
    blocks = exchange(pack(me, q_delta, k_delta, v_delta, decay, beta))
    mix, wu, ab, level = prep(me, blocks)
    maps = [later_plane(ab, distance) for distance in range(1, PLANES)]
    no = query(me, blocks, mix, wu, level)
    normed = norm(no, gain[None, :], maps)
    halo = later_plane(normed, 1)
    acc, stat, q2 = own(me, normed, attn_weight)
    attended = exchange(halo_part(me, halo, attn_weight, acc, stat, q2))
    sums = project(me, attended, out_weight)
    total = sums[0]
    for d in range(1, 4):
        got = lax.ppermute(sums[d], "heads", [(s, s ^ d) for s in range(4)])
        total = total + got.astype(F32)
    return total.astype(BF16)


def solution(mesh):
    placed = (
        P("seq", "heads"),
        P("seq", "heads"),
        P("seq", "heads"),
        P("heads", "seq"),
        P("heads", "seq"),
        P(),
        P("heads", None, None),
        P("heads", None),
    )
    return jax.shard_map(
        local, mesh=mesh, in_specs=placed, out_specs=P(("seq", "heads"), None), check_vma=False
    )
```

```python
import jax
import jax.numpy as jnp
from jax import lax
from jax.experimental import pallas as pl
from jax.experimental.pallas import tpu as pltpu
from jax.sharding import PartitionSpec as P

F32 = jnp.float32
BF16 = jnp.bfloat16
C = 128
PLANE = 8
PLANES = 8
BLK = 2 * C + 16
B = 16
GROUP = 4
EPS = 1e-06
NEG = -1e30
VMEM_LIMIT = 24 * 1024 * 1024


def params():
    return pltpu.CompilerParams(vmem_limit_bytes=VMEM_LIMIT)


def cost(flops, nbytes, trans=0):
    return pl.CostEstimate(flops=int(flops), bytes_accessed=int(nbytes), transcendentals=int(trans))


def vmem():
    return pl.BlockSpec(memory_space=pltpu.VMEM)


def smem():
    return pl.BlockSpec(memory_space=pltpu.SMEM)


def split(a):
    hi = a.astype(BF16)
    lo = (a - hi.astype(F32)).astype(BF16)
    return hi, lo


def dot(a, b):
    return lax.dot_general(a, b, (((1,), (0,)), ((), ())), preferred_element_type=F32)


def dot_nt(a, b):
    return lax.dot_general(a, b, (((1,), (1,)), ((), ())), preferred_element_type=F32)


def dot_tn(a, b):
    return lax.dot_general(a, b, (((0,), (0,)), ((), ())), preferred_element_type=F32)


def mm(a, b):
    ah, al = split(a)
    bh, bl = split(b)
    left = jnp.concatenate([ah, al], axis=1)
    n = b.shape[1]
    if n > C:
        return dot(left, jnp.concatenate([bh, bh], axis=0)) + dot(ah, bl)
    pair = jnp.concatenate([bh, bl], axis=1)
    out = dot(left, jnp.concatenate([pair, pair], axis=0))
    return out[:, :n] + out[:, n:]


def mm_exact_right(a, b):
    ah, al = split(a)
    return dot(jnp.concatenate([ah, al], axis=1), jnp.concatenate([b, b], axis=0))


def iotas():
    row = lax.broadcasted_iota(jnp.int32, (C, C), 0)
    col = lax.broadcasted_iota(jnp.int32, (C, C), 1)
    return row, col


def pack_kernel(me_ref, q_ref, k_ref, v_ref, decay_ref, beta_ref, *rest):
    keep, send, keep_q, send_q, gate, raw, sems = rest
    me = me_ref[0]
    copies = [
        pltpu.make_async_copy(decay_ref, raw.at[0], sems.at[24]),
        pltpu.make_async_copy(beta_ref, raw.at[1], sems.at[25]),
    ]
    for d in range(PLANE):
        cols = pl.ds(pl.multiple_of(jnp.bitwise_xor(me, d) * C, C), C)
        out, out_q = (send, send_q) if d % 2 else (keep, keep_q)
        at = d // 2
        copies += [
            pltpu.make_async_copy(k_ref.at[:, cols], out.at[at, pl.ds(0, C)], sems.at[3 * d]),
            pltpu.make_async_copy(v_ref.at[:, cols], out.at[at, pl.ds(C, C)], sems.at[3 * d + 1]),
            pltpu.make_async_copy(q_ref.at[:, cols], out_q.at[at], sems.at[3 * d + 2]),
        ]
    for copy in copies:
        copy.start()
    copies[0].wait()
    copies[1].wait()
    for i in range(2):
        x = raw[i]
        for j in range(3):
            part = x.astype(BF16).astype(F32)
            gate[3 * i + j] = part
            x = x - part
    zeros = jnp.zeros((10, C), F32)
    for d in range(PLANE):
        head = jnp.bitwise_xor(me, d)
        rows = [gate[i, pl.ds(head, 1), :] for i in range(6)]
        out = send if d % 2 else keep
        out[d // 2, 2 * C :, :] = jnp.concatenate(rows + [zeros], axis=0).astype(BF16)
    for copy in copies[2:]:
        copy.wait()


def pack(me, q, k, v, decay, beta):
    any_space = pl.BlockSpec(memory_space=pl.ANY)
    wide = jax.ShapeDtypeStruct((4, BLK, C), BF16)
    thin = jax.ShapeDtypeStruct((4, C, C), BF16)
    return pl.pallas_call(
        pack_kernel,
        out_shape=[wide, wide, thin, thin],
        in_specs=[smem()] + [any_space] * 5,
        out_specs=[vmem()] * 4,
        scratch_shapes=[
            pltpu.VMEM((6, PLANE, C), F32),
            pltpu.VMEM((2, PLANE, C), F32),
            pltpu.SemaphoreType.DMA((26,)),
        ],
        compiler_params=params(),
        name="pack",
    )(me, q, k, v, decay, beta)


def gather_slots(refs, out_ref):
    keep, came = refs[0], refs[1]
    out_ref[0] = keep[0]
    out_ref[1] = came[0]
    for dx in range(1, 4):
        out_ref[2 * dx] = refs[dx + 1][0]
        out_ref[2 * dx + 1] = refs[dx + 1][1]


def gates(pieces):
    row, col = iotas()
    upper = jnp.where(row <= col, 1.0, 0.0).astype(BF16)
    lower = jnp.where(row >= col, 1.0, 0.0).astype(BF16)
    eye = jnp.where(row == col, 1.0, 0.0).astype(BF16)
    along_row = dot(pieces, upper)
    along_col = dot_nt(jnp.concatenate([lower, eye], axis=0), pieces)
    plain = pieces.astype(F32)
    g_row = -(along_row[0:1] + along_row[1:2] + along_row[2:3])
    b_row = plain[3:4] + plain[4:5] + plain[5:6]
    g_col = -(along_col[:C, 0:1] + along_col[:C, 1:2] + along_col[:C, 2:3])
    b_col = along_col[C:, 3:4] + along_col[C:, 4:5] + along_col[C:, 5:6]
    return g_row, b_row, g_col, b_col


def base_inverses(packed):
    row, col = iotas()
    high = packed.astype(BF16)
    rest = packed - high.astype(F32)
    mid = rest.astype(BF16)
    low = (rest - mid.astype(F32)).astype(BF16)
    three = jnp.concatenate([high, mid, low], axis=1)
    x = jnp.where(row % B == col % B, 1.0, 0.0)
    for j in range(B - 1):
        pick = jnp.where(row == col - col % B + j, 1.0, 0.0).astype(BF16)
        factor = dot(three, jnp.concatenate([pick, pick, pick], axis=0))
        line = x.reshape(PLANE, B, C)[:, j : j + 1, :]
        x = x - factor * jnp.broadcast_to(line, (PLANE, B, C)).reshape(C, C)
    return x


def after(earlier, later):
    both = mm(later[:, :C], earlier)
    return jnp.concatenate([both[:, :C], both[:, C:] + later[:, C:]], axis=1)


def prep_kernel(me_ref, *refs):
    kv_ref, mix_ref, wu_ref, ab_ref, level_ref = refs[5:10]
    maps, lows, packs, r_cols, ends = refs[10:]
    me = me_ref[0]
    row, col = iotas()
    gather_slots(refs[:5], kv_ref)
    blocks = (row // B) == (col // B)

    def first(step, _):
        for i in range(GROUP):
            d = step * GROUP + i
            keys = kv_ref[d, 0:C, :]
            g_row, b_row, g_col, b_col = gates(kv_ref[d, 2 * C :, :])
            gram = dot_nt(keys, keys)
            diag = jnp.where(row == col, gram, 0.0)
            r_col = lax.rsqrt(jnp.sum(diag, axis=1, keepdims=True) + EPS)
            r_row = lax.rsqrt(jnp.sum(diag, axis=0, keepdims=True) + EPS)
            ratio = jnp.where(row >= col, jnp.exp(jnp.minimum(g_col - g_row, 0.0)), 0.0)
            mix = ratio * (b_row * r_row)
            mix_ref[d] = mix
            low = jnp.where(row > col, mix * gram * r_col, 0.0)
            lows[d] = low
            held = jnp.where(blocks, low, 0.0)
            packed = held[0:B]
            for b in range(1, C // B):
                packed = packed + held[B * b : B * b + B]
            packs[pl.ds(pl.multiple_of(d * B, B), B), :] = packed
            g_end = g_row[:, C - 1 : C]
            tail = jnp.exp(g_end - g_col) * b_col * r_col
            fold = jnp.exp(g_row) * r_row
            r_cols[d, 0] = jnp.broadcast_to(tail, (C, C))
            r_cols[d, 1] = jnp.broadcast_to(fold, (C, C))
            ends[d] = jnp.broadcast_to(jnp.exp(g_end), (C, C))
        return _

    lax.fori_loop(0, PLANE // GROUP, first, 0)
    packs[...] = base_inverses(packs[...])

    def second(step, _):
        for i in range(GROUP):
            d = step * GROUP + i
            keys = kv_ref[d, 0:C, :]
            values = kv_ref[d, C : 2 * C, :]
            low = lows[d]
            x = packs[pl.ds(pl.multiple_of(d * B, B), B), :]
            x = jnp.where(blocks, jnp.concatenate([x] * (C // B), axis=0), 0.0)
            size = B
            while size < C:
                apart = jnp.bitwise_xor(row, col)
                corner = jnp.where((row > col) & (apart >= size) & (apart < 2 * size), low, 0.0)
                x = x - mm(mm(x, corner), x)
                size *= 2
            tail, fold = r_cols[d, 0], r_cols[d, 1]
            w = mm_exact_right(x * fold, keys)
            u = mm_exact_right(x, values)
            wu = jnp.concatenate([w, u], axis=1)
            wu_ref[d] = wu
            hi, lo = split(jnp.concatenate([w * tail, u * tail], axis=1))
            made = dot_tn(
                jnp.concatenate([keys, keys], axis=0), jnp.concatenate([hi, lo], axis=0)
            )
            g_end = ends[d]
            chunk = jnp.bitwise_xor(me, d)
            maps[chunk] = jnp.concatenate(
                [jnp.where(row == col, g_end, 0.0) - made[:, :C], made[:, C:]], axis=1
            )
        return _

    lax.fori_loop(0, PLANE // GROUP, second, 0)
    one = [maps[i] for i in range(PLANE)]
    two = [after(one[2 * i], one[2 * i + 1]) for i in range(4)]
    four = [after(two[2 * i], two[2 * i + 1]) for i in range(2)]
    ab_ref[...] = after(four[0], four[1]).astype(BF16)
    for i, part in enumerate((one[0], two[0], one[2], four[0], one[4], two[2], one[6])):
        level_ref[i] = part


def prep(me, slots):
    return pl.pallas_call(
        prep_kernel,
        out_shape=[
            jax.ShapeDtypeStruct((PLANE, BLK, C), BF16),
            jax.ShapeDtypeStruct((PLANE, C, C), F32),
            jax.ShapeDtypeStruct((PLANE, C, 2 * C), F32),
            jax.ShapeDtypeStruct((C, 2 * C), BF16),
            jax.ShapeDtypeStruct((7, C, 2 * C), F32),
        ],
        in_specs=[smem()] + [vmem()] * 5,
        out_specs=[vmem()] * 5,
        scratch_shapes=[
            pltpu.VMEM((PLANE, C, 2 * C), F32),
            pltpu.VMEM((PLANE, C, C), F32),
            pltpu.VMEM((C, C), F32),
            pltpu.VMEM((PLANE, 2, C, C), F32),
            pltpu.VMEM((PLANE, C, C), F32),
        ],
        compiler_params=params(),
        cost_estimate=cost(2e9, 4e6),
        name="prep",
    )(me, *slots)


def query_kernel(me_ref, *refs):
    kv_ref, mix_ref, wu_ref, level_ref, no_ref, queries_ref, before = refs[5:]
    me = me_ref[0]
    row, col = iotas()
    gather_slots(refs[:5], queries_ref)
    before[0] = jnp.concatenate([jnp.where(row == col, 1.0, 0.0), jnp.zeros((C, C), F32)], axis=1)
    before[1] = level_ref[0]
    before[2] = level_ref[1]
    before[3] = after(level_ref[1], level_ref[2])
    before[4] = level_ref[3]
    before[5] = after(level_ref[3], level_ref[4])
    six = after(level_ref[3], level_ref[5])
    before[6] = six
    before[7] = after(six, level_ref[6])

    def one(step, _):
        for i in range(GROUP):
            d = step * GROUP + i
            keys = kv_ref[d, 0:C, :]
            g_row, b_row, g_col, b_col = gates(kv_ref[d, 2 * C :, :])
            queries = queries_ref[d]
            wide = queries.astype(F32)
            r_col = lax.rsqrt(jnp.sum(wide * wide, axis=1, keepdims=True) + EPS) * (C**-0.5)
            scored = dot_nt(queries, keys) * r_col * mix_ref[d]
            part = mm(scored, wu_ref[d])
            reach = wide * (r_col * jnp.exp(g_col)) - part[:, :C]
            chunk = jnp.bitwise_xor(me, d)
            both = mm(reach, before[chunk])
            rows = pl.ds(pl.multiple_of(chunk * C, C), C)
            no_ref[rows, :] = jnp.concatenate([both[:, :C], both[:, C:] + part[:, C:]], axis=1)
        return _

    lax.fori_loop(0, PLANE // GROUP, one, 0)


def query(me, slots, kv, mix, wu, level):
    return pl.pallas_call(
        query_kernel,
        out_shape=jax.ShapeDtypeStruct((PLANE * C, 2 * C), F32),
        in_specs=[smem()] + [vmem()] * 9,
        out_specs=vmem(),
        scratch_shapes=[
            pltpu.VMEM((PLANE, C, C), BF16),
            pltpu.VMEM((PLANE, C, 2 * C), F32),
        ],
        compiler_params=params(),
        cost_estimate=cost(1e9, 4e6),
        name="query",
    )(me, *slots, kv, mix, wu, level)


def combine_kernel(own_ref, one_ref, two_ref, three_ref, out_ref, b_ref):
    def times(a, x):
        hi, lo = split(x)
        return dot(a, hi) + dot(a, lo)

    state = two_ref[:, C:].astype(F32) + dot(two_ref[:, :C], three_ref[...])
    state = one_ref[:, C:].astype(F32) + times(one_ref[:, :C], state)
    state = own_ref[:, C:].astype(F32) + times(own_ref[:, :C], state)
    reach = times(own_ref[:, :C], dot(one_ref[:, :C], two_ref[:, :C]))
    out_ref[:, :C] = reach.astype(BF16)
    out_ref[:, C:] = state.astype(BF16)
    b_ref[...] = state.astype(BF16)


def combine(own_map, one, two, three):
    return pl.pallas_call(
        combine_kernel,
        out_shape=[
            jax.ShapeDtypeStruct((C, 2 * C), BF16),
            jax.ShapeDtypeStruct((C, C), BF16),
        ],
        in_specs=[vmem()] * 4,
        out_specs=[vmem()] * 2,
        compiler_params=params(),
        name="combine",
    )(own_map, one, two, three)


def norm_kernel(no_ref, gain_ref, near_ref, far_ref, normed_ref):
    state = dot(near_ref[:, :C], far_ref[...]) + near_ref[:, C:].astype(F32)
    out = mm(no_ref[:, :C], state) + no_ref[:, C:]
    scale = lax.rsqrt(jnp.mean(out * out, axis=1, keepdims=True) + EPS)
    normed_ref[...] = (out * scale * gain_ref[...]).astype(BF16)


def norm(no, gain, near, far):
    return pl.pallas_call(
        norm_kernel,
        out_shape=jax.ShapeDtypeStruct((PLANE * C, C), BF16),
        in_specs=[vmem()] * 4,
        out_specs=vmem(),
        compiler_params=params(),
        cost_estimate=cost(2e8, 2e6),
        name="norm",
    )(no, gain, near, far)


QB = 256


def own_kernel(me_ref, normed_ref, weight_ref, acc_ref, stat_ref, q2_ref):
    proj = dot(normed_ref[...], weight_ref[0]).astype(BF16)
    q2_ref[...] = proj[:, :C]
    row = lax.broadcasted_iota(jnp.int32, (QB, QB), 0)
    col = lax.broadcasted_iota(jnp.int32, (QB, QB), 1)
    for i in range(PLANE * C // QB):
        at = i * QB
        q = proj[at : at + QB, :C]
        s = dot_nt(q, proj[: at + QB, C : 2 * C]) * (C**-0.5)
        last = jnp.where(col <= row, s[:, at:], NEG)
        s = last if i == 0 else jnp.concatenate([s[:, :at], last], axis=1)
        top = jnp.max(s, axis=1, keepdims=True)
        p = jnp.exp(s - top)
        total = jnp.sum(p, axis=1, keepdims=True)
        acc_ref[at : at + QB, :] = dot(p.astype(BF16), proj[: at + QB, 2 * C :])
        stat_ref[0, at : at + QB, :] = jnp.broadcast_to(top, (QB, C))
        stat_ref[1, at : at + QB, :] = jnp.broadcast_to(total, (QB, C))


def own(me, normed, weight):
    n = PLANE * C
    return pl.pallas_call(
        own_kernel,
        out_shape=[
            jax.ShapeDtypeStruct((n, C), F32),
            jax.ShapeDtypeStruct((2, n, C), F32),
            jax.ShapeDtypeStruct((n, C), BF16),
        ],
        grid_spec=pltpu.PrefetchScalarGridSpec(
            num_scalar_prefetch=1,
            grid=(1,),
            in_specs=[
                pl.BlockSpec((n, C), lambda i, me: (0, 0)),
                pl.BlockSpec((1, C, 3 * C), lambda i, me: (me[0], 0, 0)),
            ],
            out_specs=[
                pl.BlockSpec((n, C), lambda i, me: (0, 0)),
                pl.BlockSpec((2, n, C), lambda i, me: (0, 0, 0)),
                pl.BlockSpec((n, C), lambda i, me: (0, 0)),
            ],
        ),
        compiler_params=params(),
        cost_estimate=cost(1e9, 3e6, 6e5),
        name="own",
    )(me, normed, weight)


def halo_kernel(me_ref, halo_ref, weight_ref, acc_ref, stat_ref, q2_ref, *refs):
    keep, send, attended = refs
    me, plane = me_ref[0], me_ref[1]
    proj = dot(halo_ref[...], weight_ref[0, :, C:]).astype(BF16)
    n = PLANE * C
    for i in range(n // QB):
        at = i * QB
        row = lax.broadcasted_iota(jnp.int32, (QB, n - at), 0)
        col = lax.broadcasted_iota(jnp.int32, (QB, n - at), 1)
        allowed = (col > row) & (plane > 0)
        s = dot_nt(q2_ref[at : at + QB, :], proj[at:, :C]) * (C**-0.5)
        s = jnp.where(allowed, s, NEG)
        before = stat_ref[0, at : at + QB, 0:1]
        top = jnp.maximum(jnp.max(s, axis=1, keepdims=True), before)
        p = jnp.where(allowed, jnp.exp(s - top), 0.0)
        fade = jnp.exp(before - top)
        total = jnp.sum(p, axis=1, keepdims=True) + fade * stat_ref[1, at : at + QB, 0:1]
        acc = acc_ref[at : at + QB, :] * fade + dot(p.astype(BF16), proj[at:, C:])
        attended[at : at + QB, :] = (acc / total).astype(BF16)
    for d in range(PLANE):
        chunk = jnp.bitwise_xor(me, d)
        out = send if d % 2 else keep
        out[d // 2] = attended[pl.ds(pl.multiple_of(chunk * C, C), C), :]


def halo_part(me, halo, weight, acc, stat, q2):
    n = PLANE * C
    return pl.pallas_call(
        halo_kernel,
        out_shape=[jax.ShapeDtypeStruct((4, C, C), BF16)] * 2,
        grid_spec=pltpu.PrefetchScalarGridSpec(
            num_scalar_prefetch=1,
            grid=(1,),
            in_specs=[
                pl.BlockSpec((n, C), lambda i, me: (0, 0)),
                pl.BlockSpec((1, C, 3 * C), lambda i, me: (me[0], 0, 0)),
                pl.BlockSpec((n, C), lambda i, me: (0, 0)),
                pl.BlockSpec((2, n, C), lambda i, me: (0, 0, 0)),
                pl.BlockSpec((n, C), lambda i, me: (0, 0)),
            ],
            out_specs=[pl.BlockSpec((4, C, C), lambda i, me: (0, 0, 0))] * 2,
            scratch_shapes=[pltpu.VMEM((n, C), BF16)],
        ),
        compiler_params=params(),
        cost_estimate=cost(1e9, 3e6, 6e5),
        name="halo",
    )(me, halo, weight, acc, stat, q2)


COLS = 1024


def project_kernel(me_ref, *refs):
    slots, weight_ref, outs, flat = refs[:5], refs[5], refs[6:10], refs[10]
    me, mine = me_ref[0], me_ref[2]
    found = [slots[0].at[0], slots[1].at[0]]
    for dx in range(1, 4):
        found += [slots[dx + 1].at[0], slots[dx + 1].at[1]]
    for d in range(PLANE):
        cols = pl.ds(pl.multiple_of(jnp.bitwise_xor(me, d) * C, C), C)
        for e in range(4):
            rows = pl.ds(pl.multiple_of(jnp.bitwise_xor(mine, e) * 32, 32), 32)
            flat[e * 32 : e * 32 + 32, cols] = found[d][rows, :]

    def one(step, _):
        cols = pl.ds(pl.multiple_of(step * COLS, COLS), COLS)
        got = dot(flat[...], weight_ref[:, cols])
        for e in range(4):
            outs[e][:, cols] = got[e * 32 : e * 32 + 32].astype(outs[e].dtype)
        return _

    lax.fori_loop(0, weight_ref.shape[1] // COLS, one, 0)


def project(me, slots, weight):
    depth, width = weight.shape
    return pl.pallas_call(
        project_kernel,
        out_shape=[jax.ShapeDtypeStruct((32, width), F32)]
        + [jax.ShapeDtypeStruct((32, width), BF16)] * 3,
        in_specs=[smem()] + [vmem()] * 6,
        out_specs=[vmem()] * 4,
        scratch_shapes=[pltpu.VMEM((C, depth), BF16)],
        compiler_params=params(),
        cost_estimate=cost(1e9, 9e6),
        name="project",
    )(me, *slots, weight)


def swap(block, d):
    return lax.ppermute(block, "seq", [(s, s ^ d) for s in range(PLANE * PLANES)])


def exchange(keep, send):
    came = swap(send, 1)
    slots = [keep, came]
    for dx in (2, 1, 3):
        slots.append((dx, swap(jnp.stack([keep[dx], came[dx]]), 2 * dx)))
    return slots[:2] + [pair for _, pair in sorted(slots[2:], key=lambda item: item[0])]


def later_plane(block, distance, first=0, last=PLANES - 1):
    step = PLANE * distance
    route = []
    for z in range(first, last + 1):
        if z + distance < PLANES:
            route += [(z * PLANE + i, z * PLANE + i + step) for i in range(PLANE)]
    return lax.ppermute(block, "seq", route)


def local(q_delta, k_delta, v_delta, decay, beta, gain, attn_weight, out_weight):
    place = lax.axis_index("seq")
    mine = lax.axis_index("heads")
    me = jnp.stack([place % PLANE, place // PLANE, mine]).astype(jnp.int32)
    keep, send, keep_q, send_q = pack(me, q_delta, k_delta, v_delta, decay, beta)
    slots = exchange(keep, send)
    slots_q = exchange(keep_q, send_q)
    kv, mix, wu, ab, level = prep(me, slots)
    one = later_plane(ab, 1)
    two = later_plane(ab, 2)
    three = later_plane(ab[:, C:], 3, 0, 0)
    no = query(me, slots_q, kv, mix, wu, level)
    reach, state = combine(ab, one, two, three)
    near = later_plane(reach, 1)
    far = later_plane(state, 4, 1, 3)
    normed = norm(no, gain[None, :], near, far)
    halo = later_plane(normed, 1)
    acc, stat, q2 = own(me, normed, attn_weight)
    attended = exchange(*halo_part(me, halo, attn_weight, acc, stat, q2))
    sums = project(me, attended, out_weight)
    moved = {}
    for d in (2, 1, 3):
        moved[d] = lax.ppermute(sums[d], "heads", [(s, s ^ d) for s in range(4)])
    total = sums[0]
    for d in (1, 3, 2):
        total = total + moved[d].astype(F32)
    return total.astype(BF16)


def solution(mesh):
    placed = (
        P("seq", "heads"),
        P("seq", "heads"),
        P("seq", "heads"),
        P("heads", "seq"),
        P("heads", "seq"),
        P(),
        P("heads", None, None),
        P("heads", None),
    )
    return jax.shard_map(
        local, mesh=mesh, in_specs=placed, out_specs=P(("seq", "heads"), None), check_vma=False
    )
```

```python
import jax
import jax.numpy as jnp
from jax import lax
from jax.experimental import pallas as pl
from jax.experimental.pallas import tpu as pltpu
from jax.sharding import PartitionSpec as P

F32 = jnp.float32
BF16 = jnp.bfloat16
C = 128
PLANE = 8
PLANES = 8
BLK = 2 * C + 16
B = 16
EPS = 1e-06
NEG = -1e30
VMEM_LIMIT = 24 * 1024 * 1024


def params(limit=VMEM_LIMIT):
    return pltpu.CompilerParams(vmem_limit_bytes=limit)


def cost(flops, nbytes, trans=0):
    return pl.CostEstimate(flops=int(flops), bytes_accessed=int(nbytes), transcendentals=int(trans))


def vmem():
    return pl.BlockSpec(memory_space=pltpu.VMEM)


def smem():
    return pl.BlockSpec(memory_space=pltpu.SMEM)


def split(a):
    hi = a.astype(BF16)
    lo = (a - hi.astype(F32)).astype(BF16)
    return hi, lo


def dot(a, b):
    return lax.dot_general(a, b, (((1,), (0,)), ((), ())), preferred_element_type=F32)


def dot_nt(a, b):
    return lax.dot_general(a, b, (((1,), (1,)), ((), ())), preferred_element_type=F32)


def dot_tn(a, b):
    return lax.dot_general(a, b, (((0,), (0,)), ((), ())), preferred_element_type=F32)


def mm(a, b):
    ah, al = split(a)
    bh, bl = split(b)
    left = jnp.concatenate([ah, al], axis=1)
    n = b.shape[1]
    if n > C:
        return dot(left, jnp.concatenate([bh, bh], axis=0)) + dot(ah, bl)
    pair = jnp.concatenate([bh, bl], axis=1)
    out = dot(left, jnp.concatenate([pair, pair], axis=0))
    return out[:, :n] + out[:, n:]


def mm_exact_right(a, b):
    ah, al = split(a)
    return dot(jnp.concatenate([ah, al], axis=1), jnp.concatenate([b, b], axis=0))


def iotas():
    row = lax.broadcasted_iota(jnp.int32, (C, C), 0)
    col = lax.broadcasted_iota(jnp.int32, (C, C), 1)
    return row, col


def pack_kernel(me_ref, q_ref, k_ref, v_ref, decay_ref, beta_ref, *rest):
    keep, send, keep_q, send_q, gate, raw, sems = rest
    me = me_ref[0]
    copies = [
        pltpu.make_async_copy(decay_ref, raw.at[0], sems.at[24]),
        pltpu.make_async_copy(beta_ref, raw.at[1], sems.at[25]),
    ]
    for d in range(PLANE):
        cols = pl.ds(pl.multiple_of(jnp.bitwise_xor(me, d) * C, C), C)
        out, out_q = (send, send_q) if d % 2 else (keep, keep_q)
        at = d // 2
        copies += [
            pltpu.make_async_copy(k_ref.at[:, cols], out.at[at, pl.ds(0, C)], sems.at[3 * d]),
            pltpu.make_async_copy(v_ref.at[:, cols], out.at[at, pl.ds(C, C)], sems.at[3 * d + 1]),
            pltpu.make_async_copy(q_ref.at[:, cols], out_q.at[at], sems.at[3 * d + 2]),
        ]
    for copy in copies:
        copy.start()
    copies[0].wait()
    copies[1].wait()
    for i in range(2):
        x = raw[i]
        for j in range(3):
            part = x.astype(BF16).astype(F32)
            gate[3 * i + j] = part
            x = x - part
    zeros = jnp.zeros((10, C), F32)
    for d in range(PLANE):
        head = jnp.bitwise_xor(me, d)
        rows = [gate[i, pl.ds(head, 1), :] for i in range(6)]
        out = send if d % 2 else keep
        out[d // 2, 2 * C :, :] = jnp.concatenate(rows + [zeros], axis=0).astype(BF16)
    for copy in copies[2:]:
        copy.wait()


def pack(me, q, k, v, decay, beta):
    any_space = pl.BlockSpec(memory_space=pltpu.HBM)
    wide = jax.ShapeDtypeStruct((4, BLK, C), BF16)
    thin = jax.ShapeDtypeStruct((4, C, C), BF16)
    return pl.pallas_call(
        pack_kernel,
        out_shape=[wide, wide, thin, thin],
        in_specs=[smem()] + [any_space] * 5,
        out_specs=[vmem()] * 4,
        scratch_shapes=[
            pltpu.VMEM((6, PLANE, C), F32),
            pltpu.VMEM((2, PLANE, C), F32),
            pltpu.SemaphoreType.DMA((26,)),
        ],
        compiler_params=params(60 * 1024 * 1024),
        name="pack",
    )(me, q, k, v, decay, beta)


def gather_slots(refs, out_ref):
    keep, came = refs[0], refs[1]
    out_ref[0] = keep[0]
    out_ref[1] = came[0]
    for dx in range(1, 4):
        out_ref[2 * dx] = refs[dx + 1][0]
        out_ref[2 * dx + 1] = refs[dx + 1][1]


def gates(kv_ref):
    row, col = iotas()
    pieces = jnp.concatenate([kv_ref[d, 2 * C :, :] for d in range(PLANE)], axis=0)
    upper = jnp.where(row <= col, 1.0, 0.0).astype(BF16)
    lower = jnp.where(row >= col, 1.0, 0.0).astype(BF16)
    eye = jnp.where(row == col, 1.0, 0.0).astype(BF16)
    along_row = dot(pieces, upper)
    along_col = dot_nt(jnp.concatenate([lower, eye], axis=0), pieces)
    plain = pieces.astype(F32)
    found = []
    for d in range(PLANE):
        o = 16 * d
        g_row = -(along_row[o : o + 1] + along_row[o + 1 : o + 2] + along_row[o + 2 : o + 3])
        b_row = plain[o + 3 : o + 4] + plain[o + 4 : o + 5] + plain[o + 5 : o + 6]
        g_col = -(
            along_col[:C, o : o + 1] + along_col[:C, o + 1 : o + 2] + along_col[:C, o + 2 : o + 3]
        )
        b_col = (
            along_col[C:, o + 3 : o + 4]
            + along_col[C:, o + 4 : o + 5]
            + along_col[C:, o + 5 : o + 6]
        )
        found.append((g_row, b_row, g_col, b_col))
    return found


def base_inverses(packed):
    row, col = iotas()
    high = packed.astype(BF16)
    rest = packed - high.astype(F32)
    mid = rest.astype(BF16)
    low = (rest - mid.astype(F32)).astype(BF16)
    three = jnp.concatenate([high, mid, low], axis=1)
    x = jnp.where(row % B == col % B, 1.0, 0.0)
    for j in range(B - 1):
        pick = jnp.where(row == col - col % B + j, 1.0, 0.0).astype(BF16)
        factor = dot(three, jnp.concatenate([pick, pick, pick], axis=0))
        line = x.reshape(PLANE, B, C)[:, j : j + 1, :]
        x = x - factor * jnp.broadcast_to(line, (PLANE, B, C)).reshape(C, C)
    return x


def after(earlier, later):
    both = mm(later[:, :C], earlier)
    return jnp.concatenate([both[:, :C], both[:, C:] + later[:, C:]], axis=1)


def prep_kernel(me_ref, *refs):
    kv_ref, mix_ref, wu_ref, ab_ref, level_ref = refs[5:10]
    maps = refs[10]
    me = me_ref[0]
    row, col = iotas()
    gather_slots(refs[:5], kv_ref)
    every = range(PLANE)
    blocks = (row // B) == (col // B)
    apart = jnp.bitwise_xor(row, col)
    found = gates(kv_ref)
    keys = [kv_ref[d, 0:C, :] for d in every]
    grams = [dot_nt(k, k) for k in keys]
    diags = [jnp.where(row == col, g, 0.0) for g in grams]
    r_cols = [lax.rsqrt(jnp.sum(g, axis=1, keepdims=True) + EPS) for g in diags]
    r_rows = [lax.rsqrt(jnp.sum(g, axis=0, keepdims=True) + EPS) for g in diags]
    lows, packs = [], []
    for d in every:
        g_row, b_row, g_col, _ = found[d]
        ratio = jnp.where(row >= col, jnp.exp(jnp.minimum(g_col - g_row, 0.0)), 0.0)
        mix = ratio * (b_row * r_rows[d])
        mix_ref[d] = mix
        low = jnp.where(row > col, mix * grams[d] * r_cols[d], 0.0)
        lows.append(low)
        held = jnp.where(blocks, low, 0.0)
        packed = held[0:B]
        for b in range(1, C // B):
            packed = packed + held[B * b : B * b + B]
        packs.append(packed)
    base = base_inverses(jnp.concatenate(packs, axis=0))
    inverse = [
        jnp.where(blocks, jnp.concatenate([base[B * d : B * d + B]] * (C // B), axis=0), 0.0)
        for d in every
    ]
    size = B
    while size < C:
        level = (row > col) & (apart >= size) & (apart < 2 * size)
        half = [mm(x, jnp.where(level, low, 0.0)) for x, low in zip(inverse, lows)]
        inverse = [x - mm(h, x) for x, h in zip(inverse, half)]
        size *= 2
    folded = [inverse[d] * (jnp.exp(found[d][0]) * r_rows[d]) for d in every]
    values = [kv_ref[d, C : 2 * C, :] for d in every]
    w = [mm_exact_right(folded[d], keys[d]) for d in every]
    u = [mm_exact_right(inverse[d], values[d]) for d in every]
    halves = []
    for d in every:
        wu = jnp.concatenate([w[d], u[d]], axis=1)
        wu_ref[d] = wu
        g_row, _, g_col, b_col = found[d]
        tail = jnp.exp(g_row[:, C - 1 : C] - g_col) * b_col * r_cols[d]
        halves.append(jnp.concatenate(split(wu * tail), axis=0))
    made = [dot_tn(jnp.concatenate([keys[d], keys[d]], axis=0), halves[d]) for d in every]
    for d in every:
        g_end = found[d][0][:, C - 1 : C]
        maps[jnp.bitwise_xor(me, d)] = jnp.concatenate(
            [jnp.where(row == col, jnp.exp(g_end), 0.0) - made[d][:, :C], made[d][:, C:]], axis=1
        )
    one = [maps[i] for i in every]
    two = [after(one[2 * i], one[2 * i + 1]) for i in range(4)]
    four = [after(two[2 * i], two[2 * i + 1]) for i in range(2)]
    ab_ref[...] = after(four[0], four[1]).astype(BF16)
    for i, part in enumerate((one[0], two[0], one[2], four[0], one[4], two[2], one[6])):
        level_ref[i] = part


def prep(me, slots):
    return pl.pallas_call(
        prep_kernel,
        out_shape=[
            jax.ShapeDtypeStruct((PLANE, BLK, C), BF16),
            jax.ShapeDtypeStruct((PLANE, C, C), F32),
            jax.ShapeDtypeStruct((PLANE, C, 2 * C), F32),
            jax.ShapeDtypeStruct((C, 2 * C), BF16),
            jax.ShapeDtypeStruct((7, C, 2 * C), F32),
        ],
        in_specs=[smem()] + [vmem()] * 5,
        out_specs=[vmem()] * 5,
        scratch_shapes=[
            pltpu.VMEM((PLANE, C, 2 * C), F32),
        ],
        compiler_params=params(),
        cost_estimate=cost(2e9, 4e6),
        name="prep",
    )(me, *slots)


def query_kernel(me_ref, *refs):
    kv_ref, mix_ref, wu_ref, level_ref, no_ref, queries_ref, before = refs[5:]
    me = me_ref[0]
    row, col = iotas()
    gather_slots(refs[:5], queries_ref)
    before[0] = jnp.concatenate([jnp.where(row == col, 1.0, 0.0), jnp.zeros((C, C), F32)], axis=1)
    before[1] = level_ref[0]
    before[2] = level_ref[1]
    before[3] = after(level_ref[1], level_ref[2])
    before[4] = level_ref[3]
    before[5] = after(level_ref[3], level_ref[4])
    six = after(level_ref[3], level_ref[5])
    before[6] = six
    before[7] = after(six, level_ref[6])

    every = range(PLANE)
    found = gates(kv_ref)
    queries = [queries_ref[d] for d in every]
    scored = [dot_nt(queries[d], kv_ref[d, 0:C, :]) for d in every]
    r_cols = []
    for q in queries:
        wide = q.astype(F32)
        r_cols.append(lax.rsqrt(jnp.sum(wide * wide, axis=1, keepdims=True) + EPS) * (C**-0.5))
    scored = [scored[d] * r_cols[d] * mix_ref[d] for d in every]
    parts = [mm(scored[d], wu_ref[d]) for d in every]
    reach = [
        queries[d].astype(F32) * (r_cols[d] * jnp.exp(found[d][2])) - parts[d][:, :C]
        for d in every
    ]
    chunks = [jnp.bitwise_xor(me, d) for d in every]
    both = [mm(reach[d], before[chunks[d]]) for d in every]
    for d in every:
        rows = pl.ds(pl.multiple_of(chunks[d] * C, C), C)
        no_ref[rows, :] = jnp.concatenate(
            [both[d][:, :C], both[d][:, C:] + parts[d][:, C:]], axis=1
        )


def query(me, slots, kv, mix, wu, level):
    return pl.pallas_call(
        query_kernel,
        out_shape=jax.ShapeDtypeStruct((PLANE * C, 2 * C), F32),
        in_specs=[smem()] + [vmem()] * 9,
        out_specs=vmem(),
        scratch_shapes=[
            pltpu.VMEM((PLANE, C, C), BF16),
            pltpu.VMEM((PLANE, C, 2 * C), F32),
        ],
        compiler_params=params(),
        cost_estimate=cost(1e9, 4e6),
        name="query",
    )(me, *slots, kv, mix, wu, level)


def times(a, x):
    hi, lo = split(x)
    return dot(jnp.concatenate([a, a], axis=1), jnp.concatenate([hi, lo], axis=0))


def combine_kernel(own_ref, one_ref, two_ref, before_ref, upto_ref):
    a_one, a_own = one_ref[:, :C], own_ref[:, :C]
    reach = dot(a_one, two_ref[:, :C])
    state = one_ref[:, C:].astype(F32) + dot(a_one, two_ref[:, C:])
    before_ref[:, :C] = reach
    before_ref[:, C:] = state
    upto_ref[:, :C] = times(a_own, reach).astype(BF16)
    upto_ref[:, C:] = (own_ref[:, C:].astype(F32) + times(a_own, state)).astype(BF16)


def combine(own_map, one, two):
    return pl.pallas_call(
        combine_kernel,
        out_shape=[
            jax.ShapeDtypeStruct((C, 2 * C), F32),
            jax.ShapeDtypeStruct((C, 2 * C), BF16),
        ],
        in_specs=[vmem()] * 3,
        out_specs=[vmem()] * 2,
        compiler_params=params(),
        name="combine",
    )(own_map, one, two)


def norm_kernel(no_ref, gain_ref, before_ref, three_ref, six_ref, normed_ref):
    state = three_ref[:, C:].astype(F32) + dot(three_ref[:, :C], six_ref[:, C:])
    state = before_ref[:, C:] + mm(before_ref[:, :C], state)
    out = mm(no_ref[:, :C], state) + no_ref[:, C:]
    scale = lax.rsqrt(jnp.mean(out * out, axis=1, keepdims=True) + EPS)
    normed_ref[...] = (out * scale * gain_ref[...]).astype(BF16)


def norm(no, gain, before, three, six):
    return pl.pallas_call(
        norm_kernel,
        out_shape=jax.ShapeDtypeStruct((PLANE * C, C), BF16),
        in_specs=[vmem()] * 5,
        out_specs=vmem(),
        compiler_params=params(),
        cost_estimate=cost(2e8, 2e6),
        name="norm",
    )(no, gain, before, three, six)


QB = 256
SCALE = C**-0.5 * 1.4426950408889634


def own_kernel(me_ref, normed_ref, weight_ref, acc_ref, stat_ref, q2_ref):
    proj = dot(normed_ref[...], weight_ref[0]).astype(BF16)
    q2_ref[...] = proj[:, :C]
    row = lax.broadcasted_iota(jnp.int32, (QB, QB), 0)
    col = lax.broadcasted_iota(jnp.int32, (QB, QB), 1)
    starts = range(0, PLANE * C, QB)
    scores = [dot_nt(proj[at : at + QB, :C], proj[: at + QB, C : 2 * C]) for at in starts]
    for i, at in enumerate(starts):
        last = jnp.where(col <= row, scores[i][:, at:], NEG)
        scores[i] = last if i == 0 else jnp.concatenate([scores[i][:, :at], last], axis=1)
    tops = [jnp.max(s, axis=1, keepdims=True) for s in scores]
    raised = [jnp.exp2((s - top) * SCALE) for s, top in zip(scores, tops)]
    totals = [jnp.sum(p, axis=1, keepdims=True) for p in raised]
    for i, at in enumerate(starts):
        acc_ref[at : at + QB, :] = dot(raised[i].astype(BF16), proj[: at + QB, 2 * C :])
        stat_ref[0, at : at + QB, :] = jnp.broadcast_to(tops[i], (QB, C))
        stat_ref[1, at : at + QB, :] = jnp.broadcast_to(totals[i], (QB, C))


def own(me, normed, weight):
    n = PLANE * C
    return pl.pallas_call(
        own_kernel,
        out_shape=[
            jax.ShapeDtypeStruct((n, C), F32),
            jax.ShapeDtypeStruct((2, n, C), F32),
            jax.ShapeDtypeStruct((n, C), BF16),
        ],
        grid_spec=pltpu.PrefetchScalarGridSpec(
            num_scalar_prefetch=1,
            grid=(1,),
            in_specs=[
                pl.BlockSpec((n, C), lambda i, me: (0, 0)),
                pl.BlockSpec((1, C, 3 * C), lambda i, me: (me[0], 0, 0)),
            ],
            out_specs=[
                pl.BlockSpec((n, C), lambda i, me: (0, 0)),
                pl.BlockSpec((2, n, C), lambda i, me: (0, 0, 0)),
                pl.BlockSpec((n, C), lambda i, me: (0, 0)),
            ],
        ),
        compiler_params=params(),
        cost_estimate=cost(1e9, 3e6, 6e5),
        name="own",
    )(me, normed, weight)


def halo_kernel(me_ref, halo_ref, weight_ref, acc_ref, stat_ref, q2_ref, *refs):
    keep, send, attended = refs
    me, plane = me_ref[0], me_ref[1]
    proj = dot(halo_ref[...], weight_ref[0, :, C:]).astype(BF16)
    n = PLANE * C
    row = lax.broadcasted_iota(jnp.int32, (QB, QB), 0)
    col = lax.broadcasted_iota(jnp.int32, (QB, QB), 1)
    starts = range(0, n, QB)
    floor = jnp.where(plane > 0, 0.0, NEG)
    scores = [dot_nt(q2_ref[at : at + QB, :], proj[at:, :C]) for at in starts]
    for i, at in enumerate(starts):
        first = jnp.where(col > row, scores[i][:, :QB], NEG)
        scores[i] = (
            first if at + QB == n else jnp.concatenate([first, scores[i][:, QB:]], axis=1)
        )
    before = [stat_ref[0, at : at + QB, 0:1] for at in starts]
    tops = [
        jnp.maximum(jnp.max(s, axis=1, keepdims=True) + floor, old)
        for s, old in zip(scores, before)
    ]
    raised = [jnp.exp2((s - (top - floor)) * SCALE) for s, top in zip(scores, tops)]
    fades = [jnp.exp2((old - top) * SCALE) for old, top in zip(before, tops)]
    totals = [
        jnp.sum(raised[i], axis=1, keepdims=True) + fades[i] * stat_ref[1, at : at + QB, 0:1]
        for i, at in enumerate(starts)
    ]
    for i, at in enumerate(starts):
        acc = acc_ref[at : at + QB, :] * fades[i] + dot(raised[i].astype(BF16), proj[at:, C:])
        attended[at : at + QB, :] = (acc / totals[i]).astype(BF16)
    for d in range(PLANE):
        chunk = jnp.bitwise_xor(me, d)
        out = send if d % 2 else keep
        out[d // 2] = attended[pl.ds(pl.multiple_of(chunk * C, C), C), :]


def halo_part(me, halo, weight, acc, stat, q2):
    n = PLANE * C
    return pl.pallas_call(
        halo_kernel,
        out_shape=[jax.ShapeDtypeStruct((4, C, C), BF16)] * 2,
        grid_spec=pltpu.PrefetchScalarGridSpec(
            num_scalar_prefetch=1,
            grid=(1,),
            in_specs=[
                pl.BlockSpec((n, C), lambda i, me: (0, 0)),
                pl.BlockSpec((1, C, 3 * C), lambda i, me: (me[0], 0, 0)),
                pl.BlockSpec((n, C), lambda i, me: (0, 0)),
                pl.BlockSpec((2, n, C), lambda i, me: (0, 0, 0)),
                pl.BlockSpec((n, C), lambda i, me: (0, 0)),
            ],
            out_specs=[pl.BlockSpec((4, C, C), lambda i, me: (0, 0, 0))] * 2,
            scratch_shapes=[pltpu.VMEM((n, C), BF16)],
        ),
        compiler_params=params(),
        cost_estimate=cost(1e9, 3e6, 6e5),
        name="halo",
    )(me, halo, weight, acc, stat, q2)


COLS = 1024


def project_kernel(me_ref, *refs):
    slots, weight_ref, outs, flat = refs[:5], refs[5], refs[6:10], refs[10]
    me, mine = me_ref[0], me_ref[2]
    found = [slots[0].at[0], slots[1].at[0]]
    for dx in range(1, 4):
        found += [slots[dx + 1].at[0], slots[dx + 1].at[1]]
    for d in range(PLANE):
        cols = pl.ds(pl.multiple_of(jnp.bitwise_xor(me, d) * C, C), C)
        for e in range(4):
            rows = pl.ds(pl.multiple_of(jnp.bitwise_xor(mine, e) * 32, 32), 32)
            flat[e * 32 : e * 32 + 32, cols] = found[d][rows, :]

    def one(step, _):
        cols = pl.ds(pl.multiple_of(step * COLS, COLS), COLS)
        got = dot(flat[...], weight_ref[:, cols])
        for e in range(4):
            outs[e][:, cols] = got[e * 32 : e * 32 + 32].astype(outs[e].dtype)
        return _

    lax.fori_loop(0, weight_ref.shape[1] // COLS, one, 0)


def project(me, slots, weight):
    depth, width = weight.shape
    return pl.pallas_call(
        project_kernel,
        out_shape=[jax.ShapeDtypeStruct((32, width), F32)]
        + [jax.ShapeDtypeStruct((32, width), BF16)] * 3,
        in_specs=[smem()] + [vmem()] * 6,
        out_specs=[vmem()] * 4,
        scratch_shapes=[pltpu.VMEM((C, depth), BF16)],
        compiler_params=params(),
        cost_estimate=cost(1e9, 9e6),
        name="project",
    )(me, *slots, weight)


def swap(block, d):
    return lax.ppermute(block, "seq", [(s, s ^ d) for s in range(PLANE * PLANES)])


def exchange(keep, send):
    came = swap(send, 1)
    slots = [keep, came]
    for dx in (2, 1, 3):
        slots.append((dx, swap(jnp.stack([keep[dx], came[dx]]), 2 * dx)))
    return slots[:2] + [pair for _, pair in sorted(slots[2:], key=lambda item: item[0])]


def later_plane(block, distance):
    step = PLANE * distance
    route = [(s, s + step) for s in range(PLANE * PLANES - step)]
    return lax.ppermute(block, "seq", route)


def local(q_delta, k_delta, v_delta, decay, beta, gain, attn_weight, out_weight):
    place = lax.axis_index("seq")
    mine = lax.axis_index("heads")
    me = jnp.stack([place % PLANE, place // PLANE, mine]).astype(jnp.int32)
    keep, send, keep_q, send_q = pack(me, q_delta, k_delta, v_delta, decay, beta)
    slots = exchange(keep, send)
    kv, mix, wu, ab, level = prep(me, slots)
    one = later_plane(ab, 1)
    two = later_plane(ab, 2)
    keep_q, send_q, _ = lax.optimization_barrier((keep_q, send_q, ab))
    slots_q = exchange(keep_q, send_q)
    no = query(me, slots_q, kv, mix, wu, level)
    before, upto = combine(ab, one, two)
    three = later_plane(upto, 3)
    six = later_plane(upto, 6)
    normed = norm(no, gain[None, :], before, three, six)
    halo = later_plane(normed, 1)
    acc, stat, q2 = own(me, normed, attn_weight)
    attended = exchange(*halo_part(me, halo, attn_weight, acc, stat, q2))
    sums = project(me, attended, out_weight)
    moved = {}
    for d in (2, 1, 3):
        moved[d] = lax.ppermute(sums[d], "heads", [(s, s ^ d) for s in range(4)])
    total = sums[0]
    for d in (1, 3, 2):
        total = total + moved[d].astype(F32)
    return total.astype(BF16)


def solution(mesh):
    placed = (
        P("seq", "heads"),
        P("seq", "heads"),
        P("seq", "heads"),
        P("heads", "seq"),
        P("heads", "seq"),
        P(),
        P("heads", None, None),
        P("heads", None),
    )
    return jax.shard_map(
        local, mesh=mesh, in_specs=placed, out_specs=P(("seq", "heads"), None), check_vma=False
    )
```

```python
import jax
import jax.numpy as jnp
from jax import lax
from jax.experimental import pallas as pl
from jax.experimental.pallas import tpu as pltpu
from jax.sharding import PartitionSpec as P

F32 = jnp.float32
BF16 = jnp.bfloat16
C = 128
PLANE = 8
PLANES = 8
BLK = 2 * C + 16
B = 16
EPS = 1e-06
NEG = -1e30
VMEM_LIMIT = 24 * 1024 * 1024


def params(limit=VMEM_LIMIT):
    return pltpu.CompilerParams(vmem_limit_bytes=limit)


def cost(flops, nbytes, trans=0):
    return pl.CostEstimate(flops=int(flops), bytes_accessed=int(nbytes), transcendentals=int(trans))


def vmem():
    return pl.BlockSpec(memory_space=pltpu.VMEM)


def split(a):
    hi = a.astype(BF16)
    lo = (a - hi.astype(F32)).astype(BF16)
    return hi, lo


def dot(a, b):
    return lax.dot_general(a, b, (((1,), (0,)), ((), ())), preferred_element_type=F32)


def dot_nt(a, b):
    return lax.dot_general(a, b, (((1,), (1,)), ((), ())), preferred_element_type=F32)


def dot_tn(a, b):
    return lax.dot_general(a, b, (((0,), (0,)), ((), ())), preferred_element_type=F32)


def mm(a, b):
    ah, al = split(a)
    bh, bl = split(b)
    left = jnp.concatenate([ah, al], axis=1)
    n = b.shape[1]
    if n > C:
        return dot(left, jnp.concatenate([bh, bh], axis=0)) + dot(ah, bl)
    pair = jnp.concatenate([bh, bl], axis=1)
    out = dot(left, jnp.concatenate([pair, pair], axis=0))
    return out[:, :n] + out[:, n:]


def mm_exact_right(a, b):
    ah, al = split(a)
    return dot(jnp.concatenate([ah, al], axis=1), jnp.concatenate([b, b], axis=0))


def iotas():
    row = lax.broadcasted_iota(jnp.int32, (C, C), 0)
    col = lax.broadcasted_iota(jnp.int32, (C, C), 1)
    return row, col


def pack_kernel(q_ref, k_ref, v_ref, decay_ref, beta_ref, *rest):
    keep, send, keep_q, send_q, gate, raw, sems = rest
    me = lax.axis_index("seq") % PLANE
    copies = [
        pltpu.make_async_copy(decay_ref, raw.at[0], sems.at[24]),
        pltpu.make_async_copy(beta_ref, raw.at[1], sems.at[25]),
    ]
    for d in range(PLANE):
        cols = pl.ds(pl.multiple_of(jnp.bitwise_xor(me, d) * C, C), C)
        out, out_q = (send, send_q) if d % 2 else (keep, keep_q)
        at = d // 2
        copies += [
            pltpu.make_async_copy(k_ref.at[:, cols], out.at[at, pl.ds(0, C)], sems.at[3 * d]),
            pltpu.make_async_copy(v_ref.at[:, cols], out.at[at, pl.ds(C, C)], sems.at[3 * d + 1]),
            pltpu.make_async_copy(q_ref.at[:, cols], out_q.at[at], sems.at[3 * d + 2]),
        ]
    for copy in copies:
        copy.start()
    copies[0].wait()
    copies[1].wait()
    for i in range(2):
        x = raw[i]
        for j in range(3):
            part = x.astype(BF16).astype(F32)
            gate[3 * i + j] = part
            x = x - part
    zeros = jnp.zeros((10, C), F32)
    for d in range(PLANE):
        head = jnp.bitwise_xor(me, d)
        rows = [gate[i, pl.ds(head, 1), :] for i in range(6)]
        out = send if d % 2 else keep
        out[d // 2, 2 * C :, :] = jnp.concatenate(rows + [zeros], axis=0).astype(BF16)
    for copy in copies[2:]:
        copy.wait()


def pack(q, k, v, decay, beta):
    any_space = pl.BlockSpec(memory_space=pltpu.HBM)
    wide = jax.ShapeDtypeStruct((4, BLK, C), BF16)
    thin = jax.ShapeDtypeStruct((4, C, C), BF16)
    return pl.pallas_call(
        pack_kernel,
        out_shape=[wide, wide, thin, thin],
        in_specs=[any_space] * 5,
        out_specs=[vmem()] * 4,
        scratch_shapes=[
            pltpu.VMEM((6, PLANE, C), F32),
            pltpu.VMEM((2, PLANE, C), F32),
            pltpu.SemaphoreType.DMA((26,)),
        ],
        compiler_params=params(),
        name="pack",
    )(*[pltpu.with_memory_space_constraint(x, pltpu.HBM) for x in (q, k, v, decay, beta)])


def gather_slots(refs, out_ref):
    keep, came = refs[0], refs[1]
    out_ref[0] = keep[0]
    out_ref[1] = came[0]
    for dx in range(1, 4):
        out_ref[2 * dx] = refs[dx + 1][0]
        out_ref[2 * dx + 1] = refs[dx + 1][1]


def gates(kv_ref):
    row, col = iotas()
    pieces = jnp.concatenate([kv_ref[d, 2 * C :, :] for d in range(PLANE)], axis=0)
    upper = jnp.where(row <= col, 1.0, 0.0).astype(BF16)
    lower = jnp.where(row >= col, 1.0, 0.0).astype(BF16)
    eye = jnp.where(row == col, 1.0, 0.0).astype(BF16)
    along_row = dot(pieces, upper)
    along_col = dot_nt(jnp.concatenate([lower, eye], axis=0), pieces)
    plain = pieces.astype(F32)
    found = []
    for d in range(PLANE):
        o = 16 * d
        g_row = -(along_row[o : o + 1] + along_row[o + 1 : o + 2] + along_row[o + 2 : o + 3])
        b_row = plain[o + 3 : o + 4] + plain[o + 4 : o + 5] + plain[o + 5 : o + 6]
        g_col = -(
            along_col[:C, o : o + 1] + along_col[:C, o + 1 : o + 2] + along_col[:C, o + 2 : o + 3]
        )
        b_col = (
            along_col[C:, o + 3 : o + 4]
            + along_col[C:, o + 4 : o + 5]
            + along_col[C:, o + 5 : o + 6]
        )
        found.append((g_row, b_row, g_col, b_col))
    return found


def base_inverses(packed):
    row, col = iotas()
    high = packed.astype(BF16)
    rest = packed - high.astype(F32)
    mid = rest.astype(BF16)
    low = (rest - mid.astype(F32)).astype(BF16)
    three = jnp.concatenate([high, mid, low], axis=1)
    x = jnp.where(row % B == col % B, 1.0, 0.0)
    for j in range(B - 1):
        pick = jnp.where(row == col - col % B + j, 1.0, 0.0).astype(BF16)
        factor = dot(three, jnp.concatenate([pick, pick, pick], axis=0))
        line = x.reshape(PLANE, B, C)[:, j : j + 1, :]
        x = x - factor * jnp.broadcast_to(line, (PLANE, B, C)).reshape(C, C)
    return x


def after(earlier, later):
    both = mm(later[:, :C], earlier)
    return jnp.concatenate([both[:, :C], both[:, C:] + later[:, C:]], axis=1)


def prep_kernel(*refs):
    kv_ref, mix_ref, wu_ref, ab_ref, level_ref = refs[5:10]
    maps = refs[10]
    me = lax.axis_index("seq") % PLANE
    row, col = iotas()
    gather_slots(refs[:5], kv_ref)
    every = range(PLANE)
    blocks = (row // B) == (col // B)
    apart = jnp.bitwise_xor(row, col)
    found = gates(kv_ref)
    keys = [kv_ref[d, 0:C, :] for d in every]
    grams = [dot_nt(k, k) for k in keys]
    diags = [jnp.where(row == col, g, 0.0) for g in grams]
    r_cols = [lax.rsqrt(jnp.sum(g, axis=1, keepdims=True) + EPS) for g in diags]
    r_rows = [lax.rsqrt(jnp.sum(g, axis=0, keepdims=True) + EPS) for g in diags]
    lows, packs = [], []
    for d in every:
        g_row, b_row, g_col, _ = found[d]
        ratio = jnp.where(row >= col, jnp.exp(jnp.minimum(g_col - g_row, 0.0)), 0.0)
        mix = ratio * (b_row * r_rows[d])
        mix_ref[d] = mix
        low = jnp.where(row > col, mix * grams[d] * r_cols[d], 0.0)
        lows.append(low)
        held = jnp.where(blocks, low, 0.0)
        packed = held[0:B]
        for b in range(1, C // B):
            packed = packed + held[B * b : B * b + B]
        packs.append(packed)
    base = base_inverses(jnp.concatenate(packs, axis=0))
    inverse = [
        jnp.where(blocks, jnp.concatenate([base[B * d : B * d + B]] * (C // B), axis=0), 0.0)
        for d in every
    ]
    size = B
    while size < C:
        level = (row > col) & (apart >= size) & (apart < 2 * size)
        half = [mm(x, jnp.where(level, low, 0.0)) for x, low in zip(inverse, lows)]
        inverse = [x - mm(h, x) for x, h in zip(inverse, half)]
        size *= 2
    folded = [inverse[d] * (jnp.exp(found[d][0]) * r_rows[d]) for d in every]
    values = [kv_ref[d, C : 2 * C, :] for d in every]
    w = [mm_exact_right(folded[d], keys[d]) for d in every]
    u = [mm_exact_right(inverse[d], values[d]) for d in every]
    halves = []
    for d in every:
        wu = jnp.concatenate([w[d], u[d]], axis=1)
        wu_ref[d] = wu
        g_row, _, g_col, b_col = found[d]
        tail = jnp.exp(g_row[:, C - 1 : C] - g_col) * b_col * r_cols[d]
        halves.append(jnp.concatenate(split(wu * tail), axis=0))
    made = [dot_tn(jnp.concatenate([keys[d], keys[d]], axis=0), halves[d]) for d in every]
    for d in every:
        g_end = found[d][0][:, C - 1 : C]
        maps[jnp.bitwise_xor(me, d)] = jnp.concatenate(
            [jnp.where(row == col, jnp.exp(g_end), 0.0) - made[d][:, :C], made[d][:, C:]], axis=1
        )
    one = [maps[i] for i in every]
    two = [after(one[2 * i], one[2 * i + 1]) for i in range(4)]
    four = [after(two[2 * i], two[2 * i + 1]) for i in range(2)]
    ab_ref[...] = after(four[0], four[1]).astype(BF16)
    for i, part in enumerate((one[0], two[0], one[2], four[0], one[4], two[2], one[6])):
        level_ref[i] = part


def prep(slots):
    return pl.pallas_call(
        prep_kernel,
        out_shape=[
            jax.ShapeDtypeStruct((PLANE, BLK, C), BF16),
            jax.ShapeDtypeStruct((PLANE, C, C), F32),
            jax.ShapeDtypeStruct((PLANE, C, 2 * C), F32),
            jax.ShapeDtypeStruct((C, 2 * C), BF16),
            jax.ShapeDtypeStruct((7, C, 2 * C), F32),
        ],
        in_specs=[vmem()] * 5,
        out_specs=[vmem()] * 5,
        scratch_shapes=[
            pltpu.VMEM((PLANE, C, 2 * C), F32),
        ],
        compiler_params=params(),
        cost_estimate=cost(2e9, 4e6),
        name="prep",
    )(*slots)


def query_kernel(*refs):
    kv_ref, mix_ref, wu_ref, level_ref, no_ref, queries_ref, before = refs[5:]
    me = lax.axis_index("seq") % PLANE
    row, col = iotas()
    gather_slots(refs[:5], queries_ref)
    before[0] = jnp.concatenate([jnp.where(row == col, 1.0, 0.0), jnp.zeros((C, C), F32)], axis=1)
    before[1] = level_ref[0]
    before[2] = level_ref[1]
    before[3] = after(level_ref[1], level_ref[2])
    before[4] = level_ref[3]
    before[5] = after(level_ref[3], level_ref[4])
    six = after(level_ref[3], level_ref[5])
    before[6] = six
    before[7] = after(six, level_ref[6])

    every = range(PLANE)
    found = gates(kv_ref)
    queries = [queries_ref[d] for d in every]
    scored = [dot_nt(queries[d], kv_ref[d, 0:C, :]) for d in every]
    r_cols = []
    for q in queries:
        wide = q.astype(F32)
        r_cols.append(lax.rsqrt(jnp.sum(wide * wide, axis=1, keepdims=True) + EPS) * (C**-0.5))
    scored = [scored[d] * r_cols[d] * mix_ref[d] for d in every]
    parts = [mm(scored[d], wu_ref[d]) for d in every]
    reach = [
        queries[d].astype(F32) * (r_cols[d] * jnp.exp(found[d][2])) - parts[d][:, :C]
        for d in every
    ]
    chunks = [jnp.bitwise_xor(me, d) for d in every]
    both = [mm(reach[d], before[chunks[d]]) for d in every]
    for d in every:
        rows = pl.ds(pl.multiple_of(chunks[d] * C, C), C)
        no_ref[rows, :] = jnp.concatenate(
            [both[d][:, :C], both[d][:, C:] + parts[d][:, C:]], axis=1
        )


def query(slots, kv, mix, wu, level):
    return pl.pallas_call(
        query_kernel,
        out_shape=jax.ShapeDtypeStruct((PLANE * C, 2 * C), F32),
        in_specs=[vmem()] * 9,
        out_specs=vmem(),
        scratch_shapes=[
            pltpu.VMEM((PLANE, C, C), BF16),
            pltpu.VMEM((PLANE, C, 2 * C), F32),
        ],
        compiler_params=params(),
        cost_estimate=cost(1e9, 4e6),
        name="query",
    )(*slots, kv, mix, wu, level)


def times(a, x):
    hi, lo = split(x)
    return dot(jnp.concatenate([a, a], axis=1), jnp.concatenate([hi, lo], axis=0))


def combine_kernel(own_ref, one_ref, two_ref, before_ref, upto_ref):
    a_one, a_own = one_ref[:, :C], own_ref[:, :C]
    reach = dot(a_one, two_ref[:, :C])
    state = one_ref[:, C:].astype(F32) + dot(a_one, two_ref[:, C:])
    before_ref[:, :C] = reach
    before_ref[:, C:] = state
    upto_ref[:, :C] = times(a_own, reach).astype(BF16)
    upto_ref[:, C:] = (own_ref[:, C:].astype(F32) + times(a_own, state)).astype(BF16)


def combine(own_map, one, two):
    return pl.pallas_call(
        combine_kernel,
        out_shape=[
            jax.ShapeDtypeStruct((C, 2 * C), F32),
            jax.ShapeDtypeStruct((C, 2 * C), BF16),
        ],
        in_specs=[vmem()] * 3,
        out_specs=[vmem()] * 2,
        compiler_params=params(),
        name="combine",
    )(own_map, one, two)


def norm_kernel(no_ref, gain_ref, before_ref, three_ref, six_ref, normed_ref):
    state = three_ref[:, C:].astype(F32) + dot(three_ref[:, :C], six_ref[:, C:])
    state = before_ref[:, C:] + mm(before_ref[:, :C], state)
    out = mm(no_ref[:, :C], state) + no_ref[:, C:]
    scale = lax.rsqrt(jnp.mean(out * out, axis=1, keepdims=True) + EPS)
    normed_ref[...] = (out * scale * gain_ref[...]).astype(BF16)


def norm(no, gain, before, three, six):
    return pl.pallas_call(
        norm_kernel,
        out_shape=jax.ShapeDtypeStruct((PLANE * C, C), BF16),
        in_specs=[vmem()] * 5,
        out_specs=vmem(),
        compiler_params=params(),
        cost_estimate=cost(2e8, 2e6),
        name="norm",
    )(no, gain, before, three, six)


QB = 256
SCALE = C**-0.5 * 1.4426950408889634


def squares():
    row = lax.broadcasted_iota(jnp.int32, (QB, QB), 0)
    col = lax.broadcasted_iota(jnp.int32, (QB, QB), 1)
    return row, col


def row_max(parts):
    top = jnp.max(parts[0], axis=1, keepdims=True)
    for part in parts[1:]:
        top = jnp.maximum(top, jnp.max(part, axis=1, keepdims=True))
    return top


def row_sum(parts):
    total = jnp.sum(parts[0], axis=1, keepdims=True)
    for part in parts[1:]:
        total = total + jnp.sum(part, axis=1, keepdims=True)
    return total


def weighted(parts, values):
    out = dot(parts[0].astype(BF16), values[0])
    for part, value in zip(parts[1:], values[1:]):
        out = out + dot(part.astype(BF16), value)
    return out


def own_kernel(normed_ref, weight_ref, acc_ref, stat_ref, q2_ref):
    me = lax.axis_index("seq") % PLANE
    proj = dot(normed_ref[...], weight_ref[me]).astype(BF16)
    q2_ref[...] = proj[:, :C]
    row, col = squares()
    starts = range(0, PLANE * C, QB)
    spans = [[(at, at + QB)] + ([(0, at)] if at else []) for at in starts]
    scores = [
        [dot_nt(proj[at : at + QB, :C], proj[a:b, C : 2 * C]) for a, b in span]
        for at, span in zip(starts, spans)
    ]
    scores = [[jnp.where(col <= row, parts[0], NEG)] + parts[1:] for parts in scores]
    tops = [row_max(parts) for parts in scores]
    raised = [[jnp.exp2((s - top) * SCALE) for s in parts] for parts, top in zip(scores, tops)]
    for i, at in enumerate(starts):
        rows = slice(at, at + QB)
        acc_ref[rows, :] = weighted(raised[i], [proj[a:b, 2 * C :] for a, b in spans[i]])
        stat_ref[0, rows, :] = jnp.broadcast_to(tops[i], (QB, C))
        stat_ref[1, rows, :] = jnp.broadcast_to(row_sum(raised[i]), (QB, C))


def own(normed, weight):
    n = PLANE * C
    return pl.pallas_call(
        own_kernel,
        out_shape=[
            jax.ShapeDtypeStruct((n, C), F32),
            jax.ShapeDtypeStruct((2, n, C), F32),
            jax.ShapeDtypeStruct((n, C), BF16),
        ],
        in_specs=[vmem()] * 2,
        out_specs=[vmem()] * 3,
        compiler_params=params(),
        cost_estimate=cost(1e9, 3e6, 6e5),
        name="own",
    )(normed, weight)


def halo_kernel(halo_ref, weight_ref, acc_ref, stat_ref, q2_ref, keep, send, attended):
    place = lax.axis_index("seq")
    me, plane = place % PLANE, place // PLANE
    proj = dot(halo_ref[...], weight_ref[me, :, C:]).astype(BF16)
    n = PLANE * C
    row, col = squares()
    starts = range(0, n, QB)
    spans = [[(at, at + QB)] + ([(at + QB, n)] if at + QB < n else []) for at in starts]
    floor = jnp.where(plane > 0, 0.0, NEG)
    scores = [
        [dot_nt(q2_ref[at : at + QB, :], proj[a:b, :C]) for a, b in span]
        for at, span in zip(starts, spans)
    ]
    scores = [[jnp.where(col > row, parts[0], NEG)] + parts[1:] for parts in scores]
    before = [stat_ref[0, at : at + QB, 0:1] for at in starts]
    tops = [jnp.maximum(row_max(parts) + floor, old) for parts, old in zip(scores, before)]
    raised = [
        [jnp.exp2((s - (top - floor)) * SCALE) for s in parts] for parts, top in zip(scores, tops)
    ]
    fades = [jnp.exp2((old - top) * SCALE) for old, top in zip(before, tops)]
    for i, at in enumerate(starts):
        rows = slice(at, at + QB)
        total = row_sum(raised[i]) + fades[i] * stat_ref[1, rows, 0:1]
        acc = acc_ref[rows, :] * fades[i] + weighted(
            raised[i], [proj[a:b, C:] for a, b in spans[i]]
        )
        attended[rows, :] = (acc / total).astype(BF16)
    for d in range(PLANE):
        chunk = jnp.bitwise_xor(me, d)
        out = send if d % 2 else keep
        out[d // 2] = attended[pl.ds(pl.multiple_of(chunk * C, C), C), :]


def halo_part(halo, weight, acc, stat, q2):
    n = PLANE * C
    return pl.pallas_call(
        halo_kernel,
        out_shape=[jax.ShapeDtypeStruct((4, C, C), BF16)] * 2,
        in_specs=[vmem()] * 5,
        out_specs=[vmem()] * 2,
        scratch_shapes=[pltpu.VMEM((n, C), BF16)],
        compiler_params=params(),
        cost_estimate=cost(1e9, 3e6, 6e5),
        name="halo",
    )(halo, weight, acc, stat, q2)


COLS = 1024


def project_kernel(*refs):
    slots, weight_ref, outs, flat = refs[:5], refs[5], refs[6:10], refs[10]
    me, mine = lax.axis_index("seq") % PLANE, lax.axis_index("heads")
    found = [slots[0].at[0], slots[1].at[0]]
    for dx in range(1, 4):
        found += [slots[dx + 1].at[0], slots[dx + 1].at[1]]
    for d in range(PLANE):
        cols = pl.ds(pl.multiple_of(jnp.bitwise_xor(me, d) * C, C), C)
        for e in range(4):
            rows = pl.ds(pl.multiple_of(jnp.bitwise_xor(mine, e) * 32, 32), 32)
            flat[e * 32 : e * 32 + 32, cols] = found[d][rows, :]

    def one(step, _):
        cols = pl.ds(pl.multiple_of(step * COLS, COLS), COLS)
        got = dot(flat[...], weight_ref[:, cols])
        for e in range(4):
            outs[e][:, cols] = got[e * 32 : e * 32 + 32].astype(outs[e].dtype)
        return _

    lax.fori_loop(0, weight_ref.shape[1] // COLS, one, 0)


def project(slots, weight):
    depth, width = weight.shape
    return pl.pallas_call(
        project_kernel,
        out_shape=[jax.ShapeDtypeStruct((32, width), F32)]
        + [jax.ShapeDtypeStruct((32, width), BF16)] * 3,
        in_specs=[vmem()] * 6,
        out_specs=[vmem()] * 4,
        scratch_shapes=[pltpu.VMEM((C, depth), BF16)],
        compiler_params=params(),
        cost_estimate=cost(1e9, 9e6),
        name="project",
    )(*slots, weight)


def swap(block, d):
    return lax.ppermute(block, "seq", [(s, s ^ d) for s in range(PLANE * PLANES)])


def exchange(keep, send):
    came = swap(send, 1)
    slots = [keep, came]
    for dx in (2, 1, 3):
        slots.append((dx, swap(jnp.stack([keep[dx], came[dx]]), 2 * dx)))
    return slots[:2] + [pair for _, pair in sorted(slots[2:], key=lambda item: item[0])]


def later_plane(block, distance):
    step = PLANE * distance
    route = [(s, s + step) for s in range(PLANE * PLANES - step)]
    return lax.ppermute(block, "seq", route)


def local(q_delta, k_delta, v_delta, decay, beta, gain, attn_weight, out_weight):
    keep, send, keep_q, send_q = pack(q_delta, k_delta, v_delta, decay, beta)
    slots = exchange(keep, send)
    slots_q = exchange(keep_q, send_q)
    kv, mix, wu, ab, level = prep(slots)
    one = later_plane(ab, 1)
    two = later_plane(ab, 2)
    no = query(slots_q, kv, mix, wu, level)
    before, upto = combine(ab, one, two)
    three = later_plane(upto, 3)
    six = later_plane(upto, 6)
    normed = norm(no, gain[None, :], before, three, six)
    halo = later_plane(normed, 1)
    acc, stat, q2 = own(normed, attn_weight)
    attended = exchange(*halo_part(halo, attn_weight, acc, stat, q2))
    sums = project(attended, out_weight)
    moved = {}
    for d in (2, 1, 3):
        moved[d] = lax.ppermute(sums[d], "heads", [(s, s ^ d) for s in range(4)])
    total = sums[0]
    for d in (1, 3, 2):
        total = total + moved[d].astype(F32)
    return total.astype(BF16)


def solution(mesh):
    placed = (
        P("seq", "heads"),
        P("seq", "heads"),
        P("seq", "heads"),
        P("heads", "seq"),
        P("heads", "seq"),
        P(),
        P("heads", None, None),
        P("heads", None),
    )
    return jax.shard_map(
        local, mesh=mesh, in_specs=placed, out_specs=P(("seq", "heads"), None), check_vma=False
    )
```

```python
import jax
import jax.numpy as jnp
from jax import lax
from jax.experimental import pallas as pl
from jax.experimental.pallas import tpu as pltpu
from jax.sharding import PartitionSpec as P

F32 = jnp.float32
BF16 = jnp.bfloat16
C = 128
PLANE = 8
PLANES = 8
BLK = 2 * C + 16
B = 16
EPS = 1e-06
NEG = -1e30
VMEM_LIMIT = 24 * 1024 * 1024


def params(limit=VMEM_LIMIT):
    return pltpu.CompilerParams(vmem_limit_bytes=limit)


def cost(flops, nbytes, trans=0):
    return pl.CostEstimate(flops=int(flops), bytes_accessed=int(nbytes), transcendentals=int(trans))


def vmem():
    return pl.BlockSpec(memory_space=pltpu.VMEM)


def split(a):
    hi = a.astype(BF16)
    lo = (a - hi.astype(F32)).astype(BF16)
    return hi, lo


def dot(a, b):
    return lax.dot_general(a, b, (((1,), (0,)), ((), ())), preferred_element_type=F32)


def dot_nt(a, b):
    return lax.dot_general(a, b, (((1,), (1,)), ((), ())), preferred_element_type=F32)


def dot_tn(a, b):
    return lax.dot_general(a, b, (((0,), (0,)), ((), ())), preferred_element_type=F32)


def mm(a, b):
    ah, al = split(a)
    bh, bl = split(b)
    left = jnp.concatenate([ah, al], axis=1)
    n = b.shape[1]
    if n > C:
        return dot(left, jnp.concatenate([bh, bh], axis=0)) + dot(ah, bl)
    pair = jnp.concatenate([bh, bl], axis=1)
    out = dot(left, jnp.concatenate([pair, pair], axis=0))
    return out[:, :n] + out[:, n:]


def mm_exact_right(a, b):
    ah, al = split(a)
    return dot(jnp.concatenate([ah, al], axis=1), jnp.concatenate([b, b], axis=0))


def iotas():
    row = lax.broadcasted_iota(jnp.int32, (C, C), 0)
    col = lax.broadcasted_iota(jnp.int32, (C, C), 1)
    return row, col


def pack_kernel(q_ref, k_ref, v_ref, decay_ref, beta_ref, *rest):
    keep, send, keep_q, send_q, gate, raw, sems = rest
    me = lax.axis_index("seq") % PLANE
    copies = [
        pltpu.make_async_copy(decay_ref, raw.at[0], sems.at[24]),
        pltpu.make_async_copy(beta_ref, raw.at[1], sems.at[25]),
    ]
    for d in range(PLANE):
        cols = pl.ds(pl.multiple_of(jnp.bitwise_xor(me, d) * C, C), C)
        out, out_q = (send, send_q) if d % 2 else (keep, keep_q)
        at = d // 2
        copies += [
            pltpu.make_async_copy(k_ref.at[:, cols], out.at[at, pl.ds(0, C)], sems.at[3 * d]),
            pltpu.make_async_copy(v_ref.at[:, cols], out.at[at, pl.ds(C, C)], sems.at[3 * d + 1]),
            pltpu.make_async_copy(q_ref.at[:, cols], out_q.at[at], sems.at[3 * d + 2]),
        ]
    for copy in copies:
        copy.start()
    copies[0].wait()
    copies[1].wait()
    for i in range(2):
        x = raw[i]
        for j in range(3):
            part = x.astype(BF16).astype(F32)
            gate[3 * i + j] = part
            x = x - part
    zeros = jnp.zeros((10, C), F32)
    for d in range(PLANE):
        head = jnp.bitwise_xor(me, d)
        rows = [gate[i, pl.ds(head, 1), :] for i in range(6)]
        out = send if d % 2 else keep
        out[d // 2, 2 * C :, :] = jnp.concatenate(rows + [zeros], axis=0).astype(BF16)
    for copy in copies[2:]:
        copy.wait()


def pack(q, k, v, decay, beta):
    any_space = pl.BlockSpec(memory_space=pltpu.HBM)
    wide = jax.ShapeDtypeStruct((4, BLK, C), BF16)
    thin = jax.ShapeDtypeStruct((4, C, C), BF16)
    return pl.pallas_call(
        pack_kernel,
        out_shape=[wide, wide, thin, thin],
        in_specs=[any_space] * 5,
        out_specs=[vmem()] * 4,
        scratch_shapes=[
            pltpu.VMEM((6, PLANE, C), F32),
            pltpu.VMEM((2, PLANE, C), F32),
            pltpu.SemaphoreType.DMA((26,)),
        ],
        compiler_params=params(),
        name="pack",
    )(*[pltpu.with_memory_space_constraint(x, pltpu.HBM) for x in (q, k, v, decay, beta)])


def gather_slots(refs, out_ref):
    keep, came = refs[0], refs[1]
    out_ref[0] = keep[0]
    out_ref[1] = came[0]
    for dx in range(1, 4):
        out_ref[2 * dx] = refs[dx + 1][0]
        out_ref[2 * dx + 1] = refs[dx + 1][1]


def gates(kv_ref):
    row, col = iotas()
    pieces = jnp.concatenate([kv_ref[d, 2 * C :, :] for d in range(PLANE)], axis=0)
    upper = jnp.where(row <= col, 1.0, 0.0).astype(BF16)
    lower = jnp.where(row >= col, 1.0, 0.0).astype(BF16)
    eye = jnp.where(row == col, 1.0, 0.0).astype(BF16)
    along_row = dot(pieces, upper)
    along_col = dot_nt(jnp.concatenate([lower, eye], axis=0), pieces)
    plain = pieces.astype(F32)
    found = []
    for d in range(PLANE):
        o = 16 * d
        g_row = -(along_row[o : o + 1] + along_row[o + 1 : o + 2] + along_row[o + 2 : o + 3])
        b_row = plain[o + 3 : o + 4] + plain[o + 4 : o + 5] + plain[o + 5 : o + 6]
        g_col = -(
            along_col[:C, o : o + 1] + along_col[:C, o + 1 : o + 2] + along_col[:C, o + 2 : o + 3]
        )
        b_col = (
            along_col[C:, o + 3 : o + 4]
            + along_col[C:, o + 4 : o + 5]
            + along_col[C:, o + 5 : o + 6]
        )
        found.append((g_row, b_row, g_col, b_col))
    return found


def base_inverses(packed):
    row, col = iotas()
    high = packed.astype(BF16)
    rest = packed - high.astype(F32)
    mid = rest.astype(BF16)
    low = (rest - mid.astype(F32)).astype(BF16)
    three = jnp.concatenate([high, mid, low], axis=1)
    x = jnp.where(row % B == col % B, 1.0, 0.0)
    for j in range(B - 1):
        pick = jnp.where(row == col - col % B + j, 1.0, 0.0).astype(BF16)
        factor = dot(three, jnp.concatenate([pick, pick, pick], axis=0))
        line = x.reshape(PLANE, B, C)[:, j : j + 1, :]
        x = x - factor * jnp.broadcast_to(line, (PLANE, B, C)).reshape(C, C)
    return x


def after(earlier, later):
    both = mm(later[:, :C], earlier)
    return jnp.concatenate([both[:, :C], both[:, C:] + later[:, C:]], axis=1)


def prep_kernel(*refs):
    kv_ref, mix_ref, wu_ref, ab_ref, level_ref = refs[5:10]
    maps = refs[10]
    me = lax.axis_index("seq") % PLANE
    row, col = iotas()
    gather_slots(refs[:5], kv_ref)
    every = range(PLANE)
    blocks = (row // B) == (col // B)
    apart = jnp.bitwise_xor(row, col)
    found = gates(kv_ref)
    keys = [kv_ref[d, 0:C, :] for d in every]
    grams = [dot_nt(k, k) for k in keys]
    diags = [jnp.where(row == col, g, 0.0) for g in grams]
    r_cols = [lax.rsqrt(jnp.sum(g, axis=1, keepdims=True) + EPS) for g in diags]
    r_rows = [lax.rsqrt(jnp.sum(g, axis=0, keepdims=True) + EPS) for g in diags]
    lows, packs = [], []
    for d in every:
        g_row, b_row, g_col, _ = found[d]
        ratio = jnp.where(row >= col, jnp.exp(jnp.minimum(g_col - g_row, 0.0)), 0.0)
        mix = ratio * (b_row * r_rows[d])
        mix_ref[d] = mix
        low = jnp.where(row > col, mix * grams[d] * r_cols[d], 0.0)
        lows.append(low)
        held = jnp.where(blocks, low, 0.0)
        packed = held[0:B]
        for b in range(1, C // B):
            packed = packed + held[B * b : B * b + B]
        packs.append(packed)
    base = base_inverses(jnp.concatenate(packs, axis=0))
    inverse = [
        jnp.where(blocks, jnp.concatenate([base[B * d : B * d + B]] * (C // B), axis=0), 0.0)
        for d in every
    ]
    size = B
    while size < C:
        level = (row > col) & (apart >= size) & (apart < 2 * size)
        half = [mm(x, jnp.where(level, low, 0.0)) for x, low in zip(inverse, lows)]
        inverse = [x - mm(h, x) for x, h in zip(inverse, half)]
        size *= 2
    folded = [inverse[d] * (jnp.exp(found[d][0]) * r_rows[d]) for d in every]
    values = [kv_ref[d, C : 2 * C, :] for d in every]
    w = [mm_exact_right(folded[d], keys[d]) for d in every]
    u = [mm_exact_right(inverse[d], values[d]) for d in every]
    halves = []
    for d in every:
        wu = jnp.concatenate([w[d], u[d]], axis=1)
        wu_ref[d] = wu
        g_row, _, g_col, b_col = found[d]
        tail = jnp.exp(g_row[:, C - 1 : C] - g_col) * b_col * r_cols[d]
        halves.append(jnp.concatenate(split(wu * tail), axis=0))
    made = [dot_tn(jnp.concatenate([keys[d], keys[d]], axis=0), halves[d]) for d in every]
    for d in every:
        g_end = found[d][0][:, C - 1 : C]
        maps[jnp.bitwise_xor(me, d)] = jnp.concatenate(
            [jnp.where(row == col, jnp.exp(g_end), 0.0) - made[d][:, :C], made[d][:, C:]], axis=1
        )
    one = [maps[i] for i in every]
    two = [after(one[2 * i], one[2 * i + 1]) for i in range(4)]
    four = [after(two[2 * i], two[2 * i + 1]) for i in range(2)]
    ab_ref[...] = after(four[0], four[1]).astype(BF16)
    for i, part in enumerate((one[0], two[0], one[2], four[0], one[4], two[2], one[6])):
        level_ref[i] = part


def prep(slots):
    return pl.pallas_call(
        prep_kernel,
        out_shape=[
            jax.ShapeDtypeStruct((PLANE, BLK, C), BF16),
            jax.ShapeDtypeStruct((PLANE, C, C), F32),
            jax.ShapeDtypeStruct((PLANE, C, 2 * C), F32),
            jax.ShapeDtypeStruct((C, 2 * C), BF16),
            jax.ShapeDtypeStruct((7, C, 2 * C), F32),
        ],
        in_specs=[vmem()] * 5,
        out_specs=[vmem()] * 5,
        scratch_shapes=[
            pltpu.VMEM((PLANE, C, 2 * C), F32),
        ],
        compiler_params=params(),
        cost_estimate=cost(2e9, 4e6),
        name="prep",
    )(*slots)


def query_kernel(*refs):
    kv_ref, mix_ref, wu_ref, level_ref, no_ref, queries_ref, before = refs[5:]
    me = lax.axis_index("seq") % PLANE
    row, col = iotas()
    gather_slots(refs[:5], queries_ref)
    before[0] = jnp.concatenate([jnp.where(row == col, 1.0, 0.0), jnp.zeros((C, C), F32)], axis=1)
    before[1] = level_ref[0]
    before[2] = level_ref[1]
    before[3] = after(level_ref[1], level_ref[2])
    before[4] = level_ref[3]
    before[5] = after(level_ref[3], level_ref[4])
    six = after(level_ref[3], level_ref[5])
    before[6] = six
    before[7] = after(six, level_ref[6])

    every = range(PLANE)
    found = gates(kv_ref)
    queries = [queries_ref[d] for d in every]
    scored = [dot_nt(queries[d], kv_ref[d, 0:C, :]) for d in every]
    r_cols = []
    for q in queries:
        wide = q.astype(F32)
        r_cols.append(lax.rsqrt(jnp.sum(wide * wide, axis=1, keepdims=True) + EPS) * (C**-0.5))
    scored = [scored[d] * r_cols[d] * mix_ref[d] for d in every]
    parts = [mm(scored[d], wu_ref[d]) for d in every]
    reach = [
        queries[d].astype(F32) * (r_cols[d] * jnp.exp(found[d][2])) - parts[d][:, :C]
        for d in every
    ]
    chunks = [jnp.bitwise_xor(me, d) for d in every]
    both = [mm(reach[d], before[chunks[d]]) for d in every]
    for d in every:
        rows = pl.ds(pl.multiple_of(chunks[d] * C, C), C)
        no_ref[rows, :] = jnp.concatenate(
            [both[d][:, :C], both[d][:, C:] + parts[d][:, C:]], axis=1
        )


def query(slots, kv, mix, wu, level):
    return pl.pallas_call(
        query_kernel,
        out_shape=jax.ShapeDtypeStruct((PLANE * C, 2 * C), F32),
        in_specs=[vmem()] * 9,
        out_specs=vmem(),
        scratch_shapes=[
            pltpu.VMEM((PLANE, C, C), BF16),
            pltpu.VMEM((PLANE, C, 2 * C), F32),
        ],
        compiler_params=params(),
        cost_estimate=cost(1e9, 4e6),
        name="query",
    )(*slots, kv, mix, wu, level)


def times(a, x):
    hi, lo = split(x)
    return dot(jnp.concatenate([a, a], axis=1), jnp.concatenate([hi, lo], axis=0))


def combine_kernel(own_ref, one_ref, two_ref, before_ref, upto_ref):
    a_one, a_own = one_ref[:, :C], own_ref[:, :C]
    reach = dot(a_one, two_ref[:, :C])
    state = one_ref[:, C:].astype(F32) + dot(a_one, two_ref[:, C:])
    before_ref[:, :C] = reach
    before_ref[:, C:] = state
    upto_ref[:, :C] = times(a_own, reach).astype(BF16)
    upto_ref[:, C:] = (own_ref[:, C:].astype(F32) + times(a_own, state)).astype(BF16)


def combine(own_map, one, two):
    return pl.pallas_call(
        combine_kernel,
        out_shape=[
            jax.ShapeDtypeStruct((C, 2 * C), F32),
            jax.ShapeDtypeStruct((C, 2 * C), BF16),
        ],
        in_specs=[vmem()] * 3,
        out_specs=[vmem()] * 2,
        compiler_params=params(),
        name="combine",
    )(own_map, one, two)


def norm_kernel(no_ref, gain_ref, before_ref, three_ref, six_ref, normed_ref):
    state = three_ref[:, C:].astype(F32) + dot(three_ref[:, :C], six_ref[:, C:])
    state = before_ref[:, C:] + mm(before_ref[:, :C], state)
    out = mm(no_ref[:, :C], state) + no_ref[:, C:]
    scale = lax.rsqrt(jnp.mean(out * out, axis=1, keepdims=True) + EPS)
    normed_ref[...] = (out * scale * gain_ref[...]).astype(BF16)


def norm(no, gain, before, three, six):
    return pl.pallas_call(
        norm_kernel,
        out_shape=jax.ShapeDtypeStruct((PLANE * C, C), BF16),
        in_specs=[vmem()] * 5,
        out_specs=vmem(),
        compiler_params=params(),
        cost_estimate=cost(2e8, 2e6),
        name="norm",
    )(no, gain, before, three, six)


QB = 256
SCALE = C**-0.5 * 1.4426950408889634


def squares():
    row = lax.broadcasted_iota(jnp.int32, (QB, QB), 0)
    col = lax.broadcasted_iota(jnp.int32, (QB, QB), 1)
    return row, col


def row_max(parts):
    top = jnp.max(parts[0], axis=1, keepdims=True)
    for part in parts[1:]:
        top = jnp.maximum(top, jnp.max(part, axis=1, keepdims=True))
    return top


def row_sum(parts):
    total = jnp.sum(parts[0], axis=1, keepdims=True)
    for part in parts[1:]:
        total = total + jnp.sum(part, axis=1, keepdims=True)
    return total


def weighted(parts, values):
    out = dot(parts[0].astype(BF16), values[0])
    for part, value in zip(parts[1:], values[1:]):
        out = out + dot(part.astype(BF16), value)
    return out


def tiled(column, like):
    return jnp.concatenate([column] * (like.shape[1] // C), axis=1)


def own_kernel(normed_ref, weight_ref, acc_ref, stat_ref, q2_ref):
    me = lax.axis_index("seq") % PLANE
    proj = dot(normed_ref[...], weight_ref[me]).astype(BF16)
    q2_ref[...] = proj[:, :C]
    row, col = squares()
    starts = range(0, PLANE * C, QB)
    spans = [[(at, at + QB)] + ([(0, at)] if at else []) for at in starts]
    scores = [
        [dot_nt(proj[at : at + QB, :C], proj[a:b, C : 2 * C]) for a, b in span]
        for at, span in zip(starts, spans)
    ]
    scores = [[jnp.where(col <= row, parts[0], NEG)] + parts[1:] for parts in scores]
    tops = [row_max(parts) for parts in scores]
    raised = [[jnp.exp2((s - top) * SCALE) for s in parts] for parts, top in zip(scores, tops)]
    for i, at in enumerate(starts):
        rows = slice(at, at + QB)
        acc_ref[rows, :] = weighted(raised[i], [proj[a:b, 2 * C :] for a, b in spans[i]])
        stat_ref[0, rows, :] = jnp.broadcast_to(tops[i], (QB, C))
        stat_ref[1, rows, :] = jnp.broadcast_to(row_sum(raised[i]), (QB, C))


def own(normed, weight):
    n = PLANE * C
    return pl.pallas_call(
        own_kernel,
        out_shape=[
            jax.ShapeDtypeStruct((n, C), F32),
            jax.ShapeDtypeStruct((2, n, C), F32),
            jax.ShapeDtypeStruct((n, C), BF16),
        ],
        in_specs=[vmem()] * 2,
        out_specs=[vmem()] * 3,
        compiler_params=params(),
        cost_estimate=cost(1e9, 3e6, 6e5),
        name="own",
    )(normed, weight)


def halo_kernel(halo_ref, weight_ref, acc_ref, stat_ref, q2_ref, keep, send, attended):
    place = lax.axis_index("seq")
    me, plane = place % PLANE, place // PLANE
    proj = dot(halo_ref[...], weight_ref[me, :, C:]).astype(BF16)
    n = PLANE * C
    row, col = squares()
    starts = range(0, n, QB)
    spans = [[(at, at + QB)] + ([(at + QB, n)] if at + QB < n else []) for at in starts]
    floor = jnp.where(plane > 0, 0.0, NEG)
    scores = [
        [dot_nt(q2_ref[at : at + QB, :], proj[a:b, :C]) for a, b in span]
        for at, span in zip(starts, spans)
    ]
    scores = [[jnp.where(col > row, parts[0], NEG)] + parts[1:] for parts in scores]
    before = [stat_ref[0, at : at + QB, :] for at in starts]
    tops = [jnp.maximum(row_max(parts) + floor, old) for parts, old in zip(scores, before)]
    raised = [
        [jnp.exp2((s - tiled(top - floor, s)) * SCALE) for s in parts]
        for parts, top in zip(scores, tops)
    ]
    fades = [jnp.exp2((old - top) * SCALE) for old, top in zip(before, tops)]
    for i, at in enumerate(starts):
        rows = slice(at, at + QB)
        total = row_sum(raised[i]) + fades[i] * stat_ref[1, rows, :]
        acc = acc_ref[rows, :] * fades[i] + weighted(
            raised[i], [proj[a:b, C:] for a, b in spans[i]]
        )
        attended[rows, :] = (acc / total).astype(BF16)
    for d in range(PLANE):
        chunk = jnp.bitwise_xor(me, d)
        out = send if d % 2 else keep
        out[d // 2] = attended[pl.ds(pl.multiple_of(chunk * C, C), C), :]


def halo_part(halo, weight, acc, stat, q2):
    n = PLANE * C
    return pl.pallas_call(
        halo_kernel,
        out_shape=[jax.ShapeDtypeStruct((4, C, C), BF16)] * 2,
        in_specs=[vmem()] * 5,
        out_specs=[vmem()] * 2,
        scratch_shapes=[pltpu.VMEM((n, C), BF16)],
        compiler_params=params(),
        cost_estimate=cost(1e9, 3e6, 6e5),
        name="halo",
    )(halo, weight, acc, stat, q2)


COLS = 1024


def project_kernel(*refs):
    slots, weight_ref, outs, flat = refs[:5], refs[5], refs[6:10], refs[10]
    me, mine = lax.axis_index("seq") % PLANE, lax.axis_index("heads")
    found = [slots[0].at[0], slots[1].at[0]]
    for dx in range(1, 4):
        found += [slots[dx + 1].at[0], slots[dx + 1].at[1]]
    for d in range(PLANE):
        cols = pl.ds(pl.multiple_of(jnp.bitwise_xor(me, d) * C, C), C)
        for e in range(4):
            rows = pl.ds(pl.multiple_of(jnp.bitwise_xor(mine, e) * 32, 32), 32)
            flat[e * 32 : e * 32 + 32, cols] = found[d][rows, :]

    def one(step, _):
        cols = pl.ds(pl.multiple_of(step * COLS, COLS), COLS)
        got = dot(flat[...], weight_ref[:, cols])
        for e in range(4):
            outs[e][:, cols] = got[e * 32 : e * 32 + 32].astype(outs[e].dtype)
        return _

    lax.fori_loop(0, weight_ref.shape[1] // COLS, one, 0)


def project(slots, weight):
    depth, width = weight.shape
    return pl.pallas_call(
        project_kernel,
        out_shape=[jax.ShapeDtypeStruct((32, width), F32)]
        + [jax.ShapeDtypeStruct((32, width), BF16)] * 3,
        in_specs=[vmem()] * 6,
        out_specs=[vmem()] * 4,
        scratch_shapes=[pltpu.VMEM((C, depth), BF16)],
        compiler_params=params(),
        cost_estimate=cost(1e9, 9e6),
        name="project",
    )(*slots, weight)


def swap(block, d):
    return lax.ppermute(block, "seq", [(s, s ^ d) for s in range(PLANE * PLANES)])


def exchange(keep, send):
    came = swap(send, 1)
    slots = [keep, came]
    for dx in (2, 1, 3):
        slots.append((dx, swap(jnp.stack([keep[dx], came[dx]]), 2 * dx)))
    return slots[:2] + [pair for _, pair in sorted(slots[2:], key=lambda item: item[0])]


def later_plane(block, distance):
    step = PLANE * distance
    route = [(s, s + step) for s in range(PLANE * PLANES - step)]
    return lax.ppermute(block, "seq", route)


def local(q_delta, k_delta, v_delta, decay, beta, gain, attn_weight, out_weight):
    keep, send, keep_q, send_q = pack(q_delta, k_delta, v_delta, decay, beta)
    slots = exchange(keep, send)
    slots_q = exchange(keep_q, send_q)
    kv, mix, wu, ab, level = prep(slots)
    one = later_plane(ab, 1)
    two = later_plane(ab, 2)
    no = query(slots_q, kv, mix, wu, level)
    before, upto = combine(ab, one, two)
    three = later_plane(upto, 3)
    six = later_plane(upto, 6)
    normed = norm(no, gain[None, :], before, three, six)
    halo = later_plane(normed, 1)
    acc, stat, q2 = own(normed, attn_weight)
    attended = exchange(*halo_part(halo, attn_weight, acc, stat, q2))
    sums = project(attended, out_weight)
    moved = {}
    for d in (2, 1, 3):
        moved[d] = lax.ppermute(sums[d], "heads", [(s, s ^ d) for s in range(4)])
    total = sums[0]
    for d in (1, 3, 2):
        total = total + moved[d].astype(F32)
    return total.astype(BF16)


def solution(mesh):
    placed = (
        P("seq", "heads"),
        P("seq", "heads"),
        P("seq", "heads"),
        P("heads", "seq"),
        P("heads", "seq"),
        P(),
        P("heads", None, None),
        P("heads", None),
    )
    return jax.shard_map(
        local, mesh=mesh, in_specs=placed, out_specs=P(("seq", "heads"), None), check_vma=False
    )
```

```python
import jax
import jax.numpy as jnp
from jax import lax
from jax.experimental import pallas as pl
from jax.experimental.pallas import tpu as pltpu
from jax.sharding import PartitionSpec as P

F32 = jnp.float32
BF16 = jnp.bfloat16
C = 128
PLANE = 8
PLANES = 8
BLK = 3 * C + 16
B = 16
EPS = 1e-06
NEG = -1e30
VMEM_LIMIT = 24 * 1024 * 1024


def params(limit=VMEM_LIMIT):
    return pltpu.CompilerParams(vmem_limit_bytes=limit)


def cost(flops, nbytes, trans=0):
    return pl.CostEstimate(flops=int(flops), bytes_accessed=int(nbytes), transcendentals=int(trans))


def vmem():
    return pl.BlockSpec(memory_space=pltpu.VMEM)


def split(a):
    hi = a.astype(BF16)
    lo = (a - hi.astype(F32)).astype(BF16)
    return hi, lo


def dot(a, b):
    return lax.dot_general(a, b, (((1,), (0,)), ((), ())), preferred_element_type=F32)


def dot_nt(a, b):
    return lax.dot_general(a, b, (((1,), (1,)), ((), ())), preferred_element_type=F32)


def dot_tn(a, b):
    return lax.dot_general(a, b, (((0,), (0,)), ((), ())), preferred_element_type=F32)


def mm(a, b):
    ah, al = split(a)
    bh, bl = split(b)
    left = jnp.concatenate([ah, al], axis=1)
    n = b.shape[1]
    if n > C:
        return dot(left, jnp.concatenate([bh, bh], axis=0)) + dot(ah, bl)
    pair = jnp.concatenate([bh, bl], axis=1)
    out = dot(left, jnp.concatenate([pair, pair], axis=0))
    return out[:, :n] + out[:, n:]


def mm_exact_right(a, b):
    ah, al = split(a)
    return dot(jnp.concatenate([ah, al], axis=1), jnp.concatenate([b, b], axis=0))


def iotas():
    row = lax.broadcasted_iota(jnp.int32, (C, C), 0)
    col = lax.broadcasted_iota(jnp.int32, (C, C), 1)
    return row, col


def pack_kernel(q_ref, k_ref, v_ref, decay_ref, beta_ref, *rest):
    keep, send, gate, raw, sems = rest
    me = lax.axis_index("seq") % PLANE
    copies = [
        pltpu.make_async_copy(decay_ref, raw.at[0], sems.at[24]),
        pltpu.make_async_copy(beta_ref, raw.at[1], sems.at[25]),
    ]
    for d in range(PLANE):
        cols = pl.ds(pl.multiple_of(jnp.bitwise_xor(me, d) * C, C), C)
        out = send if d % 2 else keep
        at = d // 2
        copies += [
            pltpu.make_async_copy(k_ref.at[:, cols], out.at[at, pl.ds(0, C)], sems.at[3 * d]),
            pltpu.make_async_copy(v_ref.at[:, cols], out.at[at, pl.ds(C, C)], sems.at[3 * d + 1]),
            pltpu.make_async_copy(q_ref.at[:, cols], out.at[at, pl.ds(2 * C, C)], sems.at[3 * d + 2]),
        ]
    for copy in copies:
        copy.start()
    copies[0].wait()
    copies[1].wait()
    for i in range(2):
        x = raw[i]
        for j in range(3):
            part = x.astype(BF16).astype(F32)
            gate[3 * i + j] = part
            x = x - part
    zeros = jnp.zeros((10, C), F32)
    for d in range(PLANE):
        head = jnp.bitwise_xor(me, d)
        rows = [gate[i, pl.ds(head, 1), :] for i in range(6)]
        out = send if d % 2 else keep
        out[d // 2, 3 * C :, :] = jnp.concatenate(rows + [zeros], axis=0).astype(BF16)
    for copy in copies[2:]:
        copy.wait()


def pack(q, k, v, decay, beta):
    any_space = pl.BlockSpec(memory_space=pltpu.HBM)
    wide = jax.ShapeDtypeStruct((4, BLK, C), BF16)
    return pl.pallas_call(
        pack_kernel,
        out_shape=[wide, wide],
        in_specs=[any_space] * 5,
        out_specs=[vmem()] * 2,
        scratch_shapes=[
            pltpu.VMEM((6, PLANE, C), F32),
            pltpu.VMEM((2, PLANE, C), F32),
            pltpu.SemaphoreType.DMA((26,)),
        ],
        compiler_params=params(),
        name="pack",
    )(*[pltpu.with_memory_space_constraint(x, pltpu.HBM) for x in (q, k, v, decay, beta)])


def gather_slots(refs, out_ref):
    keep, came = refs[0], refs[1]
    out_ref[0] = keep[0]
    out_ref[1] = came[0]
    for dx in range(1, 4):
        out_ref[2 * dx] = refs[dx + 1][0]
        out_ref[2 * dx + 1] = refs[dx + 1][1]


def gates(kv_ref):
    row, col = iotas()
    pieces = jnp.concatenate([kv_ref[d, 3 * C :, :] for d in range(PLANE)], axis=0)
    upper = jnp.where(row <= col, 1.0, 0.0).astype(BF16)
    lower = jnp.where(row >= col, 1.0, 0.0).astype(BF16)
    eye = jnp.where(row == col, 1.0, 0.0).astype(BF16)
    along_row = dot(pieces, upper)
    along_col = dot_nt(jnp.concatenate([lower, eye], axis=0), pieces)
    plain = pieces.astype(F32)
    found = []
    for d in range(PLANE):
        o = 16 * d
        g_row = -(along_row[o : o + 1] + along_row[o + 1 : o + 2] + along_row[o + 2 : o + 3])
        b_row = plain[o + 3 : o + 4] + plain[o + 4 : o + 5] + plain[o + 5 : o + 6]
        g_col = -(
            along_col[:C, o : o + 1] + along_col[:C, o + 1 : o + 2] + along_col[:C, o + 2 : o + 3]
        )
        b_col = (
            along_col[C:, o + 3 : o + 4]
            + along_col[C:, o + 4 : o + 5]
            + along_col[C:, o + 5 : o + 6]
        )
        found.append((g_row, b_row, g_col, b_col))
    return found


def base_inverses(packed):
    row, col = iotas()
    high = packed.astype(BF16)
    rest = packed - high.astype(F32)
    mid = rest.astype(BF16)
    low = (rest - mid.astype(F32)).astype(BF16)
    three = jnp.concatenate([high, mid, low], axis=1)
    x = jnp.where(row % B == col % B, 1.0, 0.0)
    for j in range(B - 1):
        pick = jnp.where(row == col - col % B + j, 1.0, 0.0).astype(BF16)
        factor = dot(three, jnp.concatenate([pick, pick, pick], axis=0))
        line = x.reshape(PLANE, B, C)[:, j : j + 1, :]
        x = x - factor * jnp.broadcast_to(line, (PLANE, B, C)).reshape(C, C)
    return x


def after(earlier, later):
    both = mm(later[:, :C], earlier)
    return jnp.concatenate([both[:, :C], both[:, C:] + later[:, C:]], axis=1)


def prep_kernel(*refs):
    kv_ref, mix_ref, wu_ref, ab_ref, level_ref = refs[5:10]
    maps = refs[10]
    me = lax.axis_index("seq") % PLANE
    row, col = iotas()
    gather_slots(refs[:5], kv_ref)
    every = range(PLANE)
    blocks = (row // B) == (col // B)
    apart = jnp.bitwise_xor(row, col)
    found = gates(kv_ref)
    keys = [kv_ref[d, 0:C, :] for d in every]
    grams = [dot_nt(k, k) for k in keys]
    diags = [jnp.where(row == col, g, 0.0) for g in grams]
    r_cols = [lax.rsqrt(jnp.sum(g, axis=1, keepdims=True) + EPS) for g in diags]
    r_rows = [lax.rsqrt(jnp.sum(g, axis=0, keepdims=True) + EPS) for g in diags]
    lows, packs = [], []
    for d in every:
        g_row, b_row, g_col, _ = found[d]
        ratio = jnp.where(row >= col, jnp.exp(jnp.minimum(g_col - g_row, 0.0)), 0.0)
        mix = ratio * (b_row * r_rows[d])
        mix_ref[d] = mix
        low = jnp.where(row > col, mix * grams[d] * r_cols[d], 0.0)
        lows.append(low)
        held = jnp.where(blocks, low, 0.0)
        packed = held[0:B]
        for b in range(1, C // B):
            packed = packed + held[B * b : B * b + B]
        packs.append(packed)
    base = base_inverses(jnp.concatenate(packs, axis=0))
    inverse = [
        jnp.where(blocks, jnp.concatenate([base[B * d : B * d + B]] * (C // B), axis=0), 0.0)
        for d in every
    ]
    size = B
    while size < C:
        level = (row > col) & (apart >= size) & (apart < 2 * size)
        half = [mm(x, jnp.where(level, low, 0.0)) for x, low in zip(inverse, lows)]
        inverse = [x - mm(h, x) for x, h in zip(inverse, half)]
        size *= 2
    folded = [inverse[d] * (jnp.exp(found[d][0]) * r_rows[d]) for d in every]
    values = [kv_ref[d, C : 2 * C, :] for d in every]
    w = [mm_exact_right(folded[d], keys[d]) for d in every]
    u = [mm_exact_right(inverse[d], values[d]) for d in every]
    halves = []
    for d in every:
        wu = jnp.concatenate([w[d], u[d]], axis=1)
        wu_ref[d] = wu
        g_row, _, g_col, b_col = found[d]
        tail = jnp.exp(g_row[:, C - 1 : C] - g_col) * b_col * r_cols[d]
        halves.append(jnp.concatenate(split(wu * tail), axis=0))
    made = [dot_tn(jnp.concatenate([keys[d], keys[d]], axis=0), halves[d]) for d in every]
    for d in every:
        g_end = found[d][0][:, C - 1 : C]
        maps[jnp.bitwise_xor(me, d)] = jnp.concatenate(
            [jnp.where(row == col, jnp.exp(g_end), 0.0) - made[d][:, :C], made[d][:, C:]], axis=1
        )
    one = [maps[i] for i in every]
    two = [after(one[2 * i], one[2 * i + 1]) for i in range(4)]
    four = [after(two[2 * i], two[2 * i + 1]) for i in range(2)]
    ab_ref[...] = after(four[0], four[1]).astype(BF16)
    for i, part in enumerate((one[0], two[0], one[2], four[0], one[4], two[2], one[6])):
        level_ref[i] = part


def prep(slots):
    return pl.pallas_call(
        prep_kernel,
        out_shape=[
            jax.ShapeDtypeStruct((PLANE, BLK, C), BF16),
            jax.ShapeDtypeStruct((PLANE, C, C), F32),
            jax.ShapeDtypeStruct((PLANE, C, 2 * C), F32),
            jax.ShapeDtypeStruct((C, 2 * C), BF16),
            jax.ShapeDtypeStruct((7, C, 2 * C), F32),
        ],
        in_specs=[vmem()] * 5,
        out_specs=[vmem()] * 5,
        scratch_shapes=[
            pltpu.VMEM((PLANE, C, 2 * C), F32),
        ],
        compiler_params=params(),
        cost_estimate=cost(2e9, 4e6),
        name="prep",
    )(*slots)


def query_kernel(*refs):
    kv_ref, mix_ref, wu_ref, level_ref, no_ref, before = refs
    me = lax.axis_index("seq") % PLANE
    row, col = iotas()
    before[0] = jnp.concatenate([jnp.where(row == col, 1.0, 0.0), jnp.zeros((C, C), F32)], axis=1)
    before[1] = level_ref[0]
    before[2] = level_ref[1]
    before[3] = after(level_ref[1], level_ref[2])
    before[4] = level_ref[3]
    before[5] = after(level_ref[3], level_ref[4])
    six = after(level_ref[3], level_ref[5])
    before[6] = six
    before[7] = after(six, level_ref[6])

    every = range(PLANE)
    found = gates(kv_ref)
    queries = [kv_ref[d, 2 * C : 3 * C, :] for d in every]
    scored = [dot_nt(queries[d], kv_ref[d, 0:C, :]) for d in every]
    r_cols = []
    for q in queries:
        wide = q.astype(F32)
        r_cols.append(lax.rsqrt(jnp.sum(wide * wide, axis=1, keepdims=True) + EPS) * (C**-0.5))
    scored = [scored[d] * r_cols[d] * mix_ref[d] for d in every]
    parts = [mm(scored[d], wu_ref[d]) for d in every]
    reach = [
        queries[d].astype(F32) * (r_cols[d] * jnp.exp(found[d][2])) - parts[d][:, :C]
        for d in every
    ]
    chunks = [jnp.bitwise_xor(me, d) for d in every]
    both = [mm(reach[d], before[chunks[d]]) for d in every]
    for d in every:
        rows = pl.ds(pl.multiple_of(chunks[d] * C, C), C)
        no_ref[rows, :] = jnp.concatenate(
            [both[d][:, :C], both[d][:, C:] + parts[d][:, C:]], axis=1
        )


def query(kv, mix, wu, level):
    return pl.pallas_call(
        query_kernel,
        out_shape=jax.ShapeDtypeStruct((PLANE * C, 2 * C), F32),
        in_specs=[vmem()] * 4,
        out_specs=vmem(),
        scratch_shapes=[
            pltpu.VMEM((PLANE, C, 2 * C), F32),
        ],
        compiler_params=params(),
        cost_estimate=cost(1e9, 4e6),
        name="query",
    )(kv, mix, wu, level)


def times(a, x):
    hi, lo = split(x)
    return dot(jnp.concatenate([a, a], axis=1), jnp.concatenate([hi, lo], axis=0))


def combine_kernel(own_ref, one_ref, two_ref, before_ref, upto_ref, only_ref):
    a_one, a_own = one_ref[:, :C], own_ref[:, :C]
    reach = dot(a_one, two_ref[:, :C])
    state = one_ref[:, C:].astype(F32) + dot(a_one, two_ref[:, C:])
    before_ref[:, :C] = reach
    before_ref[:, C:] = state
    upto_ref[:, :C] = times(a_own, reach).astype(BF16)
    total = (own_ref[:, C:].astype(F32) + times(a_own, state)).astype(BF16)
    upto_ref[:, C:] = total
    only_ref[...] = total


def combine(own_map, one, two):
    return pl.pallas_call(
        combine_kernel,
        out_shape=[
            jax.ShapeDtypeStruct((C, 2 * C), F32),
            jax.ShapeDtypeStruct((C, 2 * C), BF16),
            jax.ShapeDtypeStruct((C, C), BF16),
        ],
        in_specs=[vmem()] * 3,
        out_specs=[vmem()] * 3,
        compiler_params=params(),
        name="combine",
    )(own_map, one, two)


def norm_kernel(no_ref, gain_ref, before_ref, three_ref, six_ref, normed_ref):
    state = three_ref[:, C:].astype(F32) + dot(three_ref[:, :C], six_ref[...])
    state = before_ref[:, C:] + mm(before_ref[:, :C], state)
    out = mm(no_ref[:, :C], state) + no_ref[:, C:]
    scale = lax.rsqrt(jnp.mean(out * out, axis=1, keepdims=True) + EPS)
    normed_ref[...] = (out * scale * gain_ref[...]).astype(BF16)


def norm(no, gain, before, three, six):
    return pl.pallas_call(
        norm_kernel,
        out_shape=jax.ShapeDtypeStruct((PLANE * C, C), BF16),
        in_specs=[vmem()] * 5,
        out_specs=vmem(),
        compiler_params=params(),
        cost_estimate=cost(2e8, 2e6),
        name="norm",
    )(no, gain, before, three, six)


QB = 256
SCALE = C**-0.5 * 1.4426950408889634


def squares():
    row = lax.broadcasted_iota(jnp.int32, (QB, QB), 0)
    col = lax.broadcasted_iota(jnp.int32, (QB, QB), 1)
    return row, col


def row_max(parts):
    top = jnp.max(parts[0], axis=1, keepdims=True)
    for part in parts[1:]:
        top = jnp.maximum(top, jnp.max(part, axis=1, keepdims=True))
    return top


def row_sum(parts):
    total = jnp.sum(parts[0], axis=1, keepdims=True)
    for part in parts[1:]:
        total = total + jnp.sum(part, axis=1, keepdims=True)
    return total


def weighted(parts, values):
    out = dot(parts[0].astype(BF16), values[0])
    for part, value in zip(parts[1:], values[1:]):
        out = out + dot(part.astype(BF16), value)
    return out


def tiled(column, like):
    return jnp.concatenate([column] * (like.shape[1] // C), axis=1)


def own_kernel(normed_ref, weight_ref, acc_ref, stat_ref, q2_ref):
    me = lax.axis_index("seq") % PLANE
    proj = dot(normed_ref[...], weight_ref[me]).astype(BF16)
    q2_ref[...] = proj[:, :C]
    row, col = squares()
    starts = range(0, PLANE * C, QB)
    spans = [[(at, at + QB)] + ([(0, at)] if at else []) for at in starts]
    scores = [
        [dot_nt(proj[at : at + QB, :C], proj[a:b, C : 2 * C]) for a, b in span]
        for at, span in zip(starts, spans)
    ]
    scores = [[jnp.where(col <= row, parts[0], NEG)] + parts[1:] for parts in scores]
    tops = [row_max(parts) for parts in scores]
    raised = [[jnp.exp2((s - top) * SCALE) for s in parts] for parts, top in zip(scores, tops)]
    for i, at in enumerate(starts):
        rows = slice(at, at + QB)
        acc_ref[rows, :] = weighted(raised[i], [proj[a:b, 2 * C :] for a, b in spans[i]])
        stat_ref[0, rows, :] = jnp.broadcast_to(tops[i], (QB, C))
        stat_ref[1, rows, :] = jnp.broadcast_to(row_sum(raised[i]), (QB, C))


def own(normed, weight):
    n = PLANE * C
    return pl.pallas_call(
        own_kernel,
        out_shape=[
            jax.ShapeDtypeStruct((n, C), F32),
            jax.ShapeDtypeStruct((2, n, C), F32),
            jax.ShapeDtypeStruct((n, C), BF16),
        ],
        in_specs=[vmem()] * 2,
        out_specs=[vmem()] * 3,
        compiler_params=params(),
        cost_estimate=cost(1e9, 3e6, 6e5),
        name="own",
    )(normed, weight)


def halo_kernel(halo_ref, weight_ref, acc_ref, stat_ref, q2_ref, keep, send, attended):
    place = lax.axis_index("seq")
    me, plane = place % PLANE, place // PLANE
    proj = dot(halo_ref[...], weight_ref[me, :, C:]).astype(BF16)
    n = PLANE * C
    row, col = squares()
    starts = range(0, n, QB)
    spans = [[(at, at + QB)] + ([(at + QB, n)] if at + QB < n else []) for at in starts]
    floor = jnp.where(plane > 0, 0.0, NEG)
    scores = [
        [dot_nt(q2_ref[at : at + QB, :], proj[a:b, :C]) for a, b in span]
        for at, span in zip(starts, spans)
    ]
    scores = [[jnp.where(col > row, parts[0], NEG)] + parts[1:] for parts in scores]
    before = [stat_ref[0, at : at + QB, :] for at in starts]
    tops = [jnp.maximum(row_max(parts) + floor, old) for parts, old in zip(scores, before)]
    raised = [
        [jnp.exp2((s - tiled(top - floor, s)) * SCALE) for s in parts]
        for parts, top in zip(scores, tops)
    ]
    fades = [jnp.exp2((old - top) * SCALE) for old, top in zip(before, tops)]
    for i, at in enumerate(starts):
        rows = slice(at, at + QB)
        total = row_sum(raised[i]) + fades[i] * stat_ref[1, rows, :]
        acc = acc_ref[rows, :] * fades[i] + weighted(
            raised[i], [proj[a:b, C:] for a, b in spans[i]]
        )
        attended[rows, :] = (acc / total).astype(BF16)
    for d in range(PLANE):
        chunk = jnp.bitwise_xor(me, d)
        out = send if d % 2 else keep
        out[d // 2] = attended[pl.ds(pl.multiple_of(chunk * C, C), C), :]


def halo_part(halo, weight, acc, stat, q2):
    n = PLANE * C
    return pl.pallas_call(
        halo_kernel,
        out_shape=[jax.ShapeDtypeStruct((4, C, C), BF16)] * 2,
        in_specs=[vmem()] * 5,
        out_specs=[vmem()] * 2,
        scratch_shapes=[pltpu.VMEM((n, C), BF16)],
        compiler_params=params(),
        cost_estimate=cost(1e9, 3e6, 6e5),
        name="halo",
    )(halo, weight, acc, stat, q2)


COLS = 1024


def pair_part(first, second, dx):
    core, mine = lax.axis_index("seq") % 2, lax.axis_index("heads")
    rows = [pl.ds(pl.multiple_of(jnp.bitwise_xor(mine, e) * 32, 32), 32) for e in range(4)]
    one = jnp.concatenate([first[r, :] for r in rows], axis=0)
    two = jnp.concatenate([second[r, :] for r in rows], axis=0)
    swapped = core > 0
    left = jnp.where(swapped, two.astype(F32), one.astype(F32)).astype(BF16)
    right = jnp.where(swapped, one.astype(F32), two.astype(F32)).astype(BF16)
    chip = lax.axis_index("seq") % PLANE // 2
    at = pl.multiple_of(jnp.bitwise_xor(chip, dx) * 2 * C, 2 * C)
    return jnp.concatenate([left, right], axis=1), pl.ds(at, 2 * C)


def early_kernel(keep, came, one, two, weight_ref, acc_ref):
    parts = [
        pair_part(keep.at[0], came.at[0], 0),
        pair_part(two.at[0], two.at[1], 2),
        pair_part(one.at[0], one.at[1], 1),
    ]
    for at in range(0, weight_ref.shape[1], COLS):
        cols = slice(at, at + COLS)
        got = dot(parts[0][0], weight_ref[parts[0][1], cols])
        for part, rows in parts[1:]:
            got = got + dot(part, weight_ref[rows, cols])
        acc_ref[:, cols] = got


def late_kernel(three, weight_ref, acc_ref, *outs):
    part, rows = pair_part(three.at[0], three.at[1], 3)
    for at in range(0, weight_ref.shape[1], COLS):
        cols = slice(at, at + COLS)
        got = acc_ref[:, cols] + dot(part, weight_ref[rows, cols])
        for e in range(4):
            outs[e][:, cols] = got[e * 32 : e * 32 + 32].astype(outs[e].dtype)


def project(slots, weight):
    width = weight.shape[1]
    keep, came, one, two, three = slots
    acc = pl.pallas_call(
        early_kernel,
        out_shape=jax.ShapeDtypeStruct((C, width), F32),
        in_specs=[vmem()] * 5,
        out_specs=vmem(),
        compiler_params=params(),
        cost_estimate=cost(8e8, 8e6),
        name="early",
    )(keep, came, one, two, weight)
    return pl.pallas_call(
        late_kernel,
        out_shape=[jax.ShapeDtypeStruct((32, width), F32)]
        + [jax.ShapeDtypeStruct((32, width), BF16)] * 3,
        in_specs=[vmem()] * 3,
        out_specs=[vmem()] * 4,
        compiler_params=params(),
        cost_estimate=cost(3e8, 4e6),
        name="late",
    )(three, weight, acc)


def swap(block, d):
    return lax.ppermute(block, "seq", [(s, s ^ d) for s in range(PLANE * PLANES)])


def exchange(keep, send):
    came = swap(send, 1)
    slots = [keep, came]
    for dx in (2, 1, 3):
        slots.append((dx, swap(jnp.stack([keep[dx], came[dx]]), 2 * dx)))
    return slots[:2] + [pair for _, pair in sorted(slots[2:], key=lambda item: item[0])]


def later_plane(block, distance):
    step = PLANE * distance
    route = [(s, s + step) for s in range(PLANE * PLANES - step)]
    return lax.ppermute(block, "seq", route)


def local(q_delta, k_delta, v_delta, decay, beta, gain, attn_weight, out_weight):
    kv, mix, wu, ab, level = prep(exchange(*pack(q_delta, k_delta, v_delta, decay, beta)))
    one = later_plane(ab, 1)
    two = later_plane(ab, 2)
    no = query(kv, mix, wu, level)
    before, upto, only = combine(ab, one, two)
    three = later_plane(upto, 3)
    six = later_plane(only, 6)
    normed = norm(no, gain[None, :], before, three, six)
    halo = later_plane(normed, 1)
    acc, stat, q2 = own(normed, attn_weight)
    attended = exchange(*halo_part(halo, attn_weight, acc, stat, q2))
    sums = project(attended, out_weight)
    moved = {}
    for d in (2, 1, 3):
        moved[d] = lax.ppermute(sums[d], "heads", [(s, s ^ d) for s in range(4)])
    total = sums[0]
    for d in (1, 3, 2):
        total = total + moved[d].astype(F32)
    return total.astype(BF16)


def solution(mesh):
    placed = (
        P("seq", "heads"),
        P("seq", "heads"),
        P("seq", "heads"),
        P("heads", "seq"),
        P("heads", "seq"),
        P(),
        P("heads", None, None),
        P("heads", None),
    )
    return jax.shard_map(
        local, mesh=mesh, in_specs=placed, out_specs=P(("seq", "heads"), None), check_vma=False
    )
```

```python
import jax
import jax.numpy as jnp
from jax import lax
from jax.experimental import pallas as pl
from jax.experimental.pallas import tpu as pltpu
from jax.sharding import PartitionSpec as P

F32 = jnp.float32
BF16 = jnp.bfloat16
C = 128
PLANE = 8
PLANES = 8
KROWS = C + 16
B = 16
EPS = 1e-06
NEG = -1e30
VMEM_LIMIT = 24 * 1024 * 1024


def params(limit=VMEM_LIMIT):
    return pltpu.CompilerParams(vmem_limit_bytes=limit)


def cost(flops, nbytes, trans=0):
    return pl.CostEstimate(flops=int(flops), bytes_accessed=int(nbytes), transcendentals=int(trans))


def vmem():
    return pl.BlockSpec(memory_space=pltpu.VMEM)


def split(a):
    hi = a.astype(BF16)
    lo = (a - hi.astype(F32)).astype(BF16)
    return hi, lo


def dot(a, b):
    return lax.dot_general(a, b, (((1,), (0,)), ((), ())), preferred_element_type=F32)


def dot_nt(a, b):
    return lax.dot_general(a, b, (((1,), (1,)), ((), ())), preferred_element_type=F32)


def dot_tn(a, b):
    return lax.dot_general(a, b, (((0,), (0,)), ((), ())), preferred_element_type=F32)


def mm(a, b):
    ah, al = split(a)
    bh, bl = split(b)
    left = jnp.concatenate([ah, al], axis=1)
    n = b.shape[1]
    if n > C:
        return dot(left, jnp.concatenate([bh, bh], axis=0)) + dot(ah, bl)
    pair = jnp.concatenate([bh, bl], axis=1)
    out = dot(left, jnp.concatenate([pair, pair], axis=0))
    return out[:, :n] + out[:, n:]


def mm_exact_right(a, b):
    ah, al = split(a)
    return dot(jnp.concatenate([ah, al], axis=1), jnp.concatenate([b, b], axis=0))


def iotas():
    row = lax.broadcasted_iota(jnp.int32, (C, C), 0)
    col = lax.broadcasted_iota(jnp.int32, (C, C), 1)
    return row, col


def pack_kernel(q_ref, k_ref, v_ref, decay_ref, beta_ref, *rest):
    keep_k, send_k, keep, send, gate, raw, sems = rest
    me = lax.axis_index("seq") % PLANE
    copies = [
        pltpu.make_async_copy(decay_ref, raw.at[0], sems.at[24]),
        pltpu.make_async_copy(beta_ref, raw.at[1], sems.at[25]),
    ]
    for d in range(PLANE):
        cols = pl.ds(pl.multiple_of(jnp.bitwise_xor(me, d) * C, C), C)
        out_k, out = (send_k, send) if d % 2 else (keep_k, keep)
        at = d // 2
        copies += [
            pltpu.make_async_copy(k_ref.at[:, cols], out_k.at[at, pl.ds(0, C)], sems.at[3 * d]),
            pltpu.make_async_copy(v_ref.at[:, cols], out.at[at, pl.ds(0, C)], sems.at[3 * d + 1]),
            pltpu.make_async_copy(q_ref.at[:, cols], out.at[at, pl.ds(C, C)], sems.at[3 * d + 2]),
        ]
    for copy in copies:
        copy.start()
    copies[0].wait()
    copies[1].wait()
    for i in range(2):
        x = raw[i]
        for j in range(3):
            part = x.astype(BF16).astype(F32)
            gate[3 * i + j] = part
            x = x - part
    zeros = jnp.zeros((10, C), F32)
    for d in range(PLANE):
        head = jnp.bitwise_xor(me, d)
        rows = [gate[i, pl.ds(head, 1), :] for i in range(6)]
        out = send_k if d % 2 else keep_k
        out[d // 2, C:, :] = jnp.concatenate(rows + [zeros], axis=0).astype(BF16)
    for copy in copies[2:]:
        copy.wait()


def pack(q, k, v, decay, beta):
    any_space = pl.BlockSpec(memory_space=pltpu.HBM)
    first = jax.ShapeDtypeStruct((4, KROWS, C), BF16)
    wide = jax.ShapeDtypeStruct((4, 2 * C, C), BF16)
    return pl.pallas_call(
        pack_kernel,
        out_shape=[first, first, wide, wide],
        in_specs=[any_space] * 5,
        out_specs=[vmem()] * 4,
        scratch_shapes=[
            pltpu.VMEM((6, PLANE, C), F32),
            pltpu.VMEM((2, PLANE, C), F32),
            pltpu.SemaphoreType.DMA((26,)),
        ],
        compiler_params=params(),
        name="pack",
    )(*[pltpu.with_memory_space_constraint(x, pltpu.HBM) for x in (q, k, v, decay, beta)])


def gather_slots(refs, out_ref):
    keep, came = refs[0], refs[1]
    out_ref[0] = keep[0]
    out_ref[1] = came[0]
    for dx in range(1, 4):
        out_ref[2 * dx] = refs[dx + 1][0]
        out_ref[2 * dx + 1] = refs[dx + 1][1]


def gates(k_ref):
    row, col = iotas()
    pieces = jnp.concatenate([k_ref[d, C:, :] for d in range(PLANE)], axis=0)
    upper = jnp.where(row <= col, 1.0, 0.0).astype(BF16)
    lower = jnp.where(row >= col, 1.0, 0.0).astype(BF16)
    eye = jnp.where(row == col, 1.0, 0.0).astype(BF16)
    along_row = dot(pieces, upper)
    along_col = dot_nt(jnp.concatenate([lower, eye], axis=0), pieces)
    plain = pieces.astype(F32)
    found = []
    for d in range(PLANE):
        o = 16 * d
        g_row = -(along_row[o : o + 1] + along_row[o + 1 : o + 2] + along_row[o + 2 : o + 3])
        b_row = plain[o + 3 : o + 4] + plain[o + 4 : o + 5] + plain[o + 5 : o + 6]
        g_col = -(
            along_col[:C, o : o + 1] + along_col[:C, o + 1 : o + 2] + along_col[:C, o + 2 : o + 3]
        )
        b_col = (
            along_col[C:, o + 3 : o + 4]
            + along_col[C:, o + 4 : o + 5]
            + along_col[C:, o + 5 : o + 6]
        )
        found.append((g_row, b_row, g_col, b_col))
    return found


def base_inverses(packed):
    row, col = iotas()
    high = packed.astype(BF16)
    rest = packed - high.astype(F32)
    mid = rest.astype(BF16)
    low = (rest - mid.astype(F32)).astype(BF16)
    three = jnp.concatenate([high, mid, low], axis=1)
    x = jnp.where(row % B == col % B, 1.0, 0.0)
    for j in range(B - 1):
        pick = jnp.where(row == col - col % B + j, 1.0, 0.0).astype(BF16)
        factor = dot(three, jnp.concatenate([pick, pick, pick], axis=0))
        line = x.reshape(PLANE, B, C)[:, j : j + 1, :]
        x = x - factor * jnp.broadcast_to(line, (PLANE, B, C)).reshape(C, C)
    return x


def after(earlier, later):
    both = mm(later[:, :C], earlier)
    return jnp.concatenate([both[:, :C], both[:, C:] + later[:, C:]], axis=1)


def key_kernel(*refs):
    k_ref, mix_ref, inverse_ref, w_ref, tail_ref, reach_ref = refs[5:11]
    maps = refs[11]
    me = lax.axis_index("seq") % PLANE
    row, col = iotas()
    gather_slots(refs[:5], k_ref)
    every = range(PLANE)
    blocks = (row // B) == (col // B)
    apart = jnp.bitwise_xor(row, col)
    found = gates(k_ref)
    keys = [k_ref[d, 0:C, :] for d in every]
    grams = [dot_nt(k, k) for k in keys]
    diags = [jnp.where(row == col, g, 0.0) for g in grams]
    r_cols = [lax.rsqrt(jnp.sum(g, axis=1, keepdims=True) + EPS) for g in diags]
    r_rows = [lax.rsqrt(jnp.sum(g, axis=0, keepdims=True) + EPS) for g in diags]
    lows, packs = [], []
    for d in every:
        g_row, b_row, g_col, _ = found[d]
        ratio = jnp.where(row >= col, jnp.exp(jnp.minimum(g_col - g_row, 0.0)), 0.0)
        mix = ratio * (b_row * r_rows[d])
        mix_ref[d] = mix
        low = jnp.where(row > col, mix * grams[d] * r_cols[d], 0.0)
        lows.append(low)
        held = jnp.where(blocks, low, 0.0)
        packed = held[0:B]
        for b in range(1, C // B):
            packed = packed + held[B * b : B * b + B]
        packs.append(packed)
    base = base_inverses(jnp.concatenate(packs, axis=0))
    inverse = [
        jnp.where(blocks, jnp.concatenate([base[B * d : B * d + B]] * (C // B), axis=0), 0.0)
        for d in every
    ]
    size = B
    while size < C:
        level = (row > col) & (apart >= size) & (apart < 2 * size)
        half = [mm(x, jnp.where(level, low, 0.0)) for x, low in zip(inverse, lows)]
        inverse = [x - mm(h, x) for x, h in zip(inverse, half)]
        size *= 2
    folded = [inverse[d] * (jnp.exp(found[d][0]) * r_rows[d]) for d in every]
    w = [mm_exact_right(folded[d], keys[d]) for d in every]
    halves = []
    for d in every:
        g_row, _, g_col, b_col = found[d]
        tail = jnp.broadcast_to(jnp.exp(g_row[:, C - 1 : C] - g_col) * b_col * r_cols[d], (C, C))
        inverse_ref[d] = inverse[d]
        w_ref[d] = w[d]
        tail_ref[d] = tail
        halves.append(jnp.concatenate(split(w[d] * tail), axis=0))
    made = [dot_tn(jnp.concatenate([keys[d], keys[d]], axis=0), halves[d]) for d in every]
    for d in every:
        g_end = found[d][0][:, C - 1 : C]
        maps[jnp.bitwise_xor(me, d)] = jnp.where(row == col, jnp.exp(g_end), 0.0) - made[d]
    one = [maps[i] for i in every]
    two = [mm(one[2 * i + 1], one[2 * i]) for i in range(4)]
    four = [mm(two[2 * i + 1], two[2 * i]) for i in range(2)]
    for i, part in enumerate(one + two + four + [mm(four[1], four[0])]):
        reach_ref[i] = part


def value_kernel(*refs):
    k_ref, inverse_ref, w_ref, tail_ref, reach_ref, vq_ref, wu_ref, ab_ref, level_ref, states = (
        refs[5:]
    )
    me = lax.axis_index("seq") % PLANE
    gather_slots(refs[:5], vq_ref)
    every = range(PLANE)
    u = [mm_exact_right(inverse_ref[d], vq_ref[d, 0:C, :]) for d in every]
    halves = []
    for d in every:
        wu_ref[d, :, :C] = w_ref[d]
        wu_ref[d, :, C:] = u[d]
        halves.append(jnp.concatenate(split(u[d] * tail_ref[d]), axis=0))
    keys = [k_ref[d, 0:C, :] for d in every]
    made = [dot_tn(jnp.concatenate([keys[d], keys[d]], axis=0), halves[d]) for d in every]
    for d in every:
        states[jnp.bitwise_xor(me, d)] = made[d]
    one = [states[i] for i in every]
    two = [mm(reach_ref[2 * i + 1], one[2 * i]) + one[2 * i + 1] for i in range(4)]
    four = [mm(reach_ref[8 + 2 * i + 1], two[2 * i]) + two[2 * i + 1] for i in range(2)]
    last = mm(reach_ref[13], four[0]) + four[1]
    ab_ref[:, :C] = reach_ref[14].astype(BF16)
    ab_ref[:, C:] = last.astype(BF16)
    both = ((0, one[0]), (8, two[0]), (2, one[2]), (12, four[0]), (4, one[4]), (10, two[2]), (6, one[6]))
    for i, (at, state) in enumerate(both):
        level_ref[i, :, :C] = reach_ref[at]
        level_ref[i, :, C:] = state


def key_part(slots):
    square = jax.ShapeDtypeStruct((PLANE, C, C), F32)
    return pl.pallas_call(
        key_kernel,
        out_shape=[jax.ShapeDtypeStruct((PLANE, KROWS, C), BF16)]
        + [square] * 4
        + [jax.ShapeDtypeStruct((15, C, C), F32)],
        in_specs=[vmem()] * 5,
        out_specs=[vmem()] * 6,
        scratch_shapes=[pltpu.VMEM((PLANE, C, C), F32)],
        compiler_params=params(),
        cost_estimate=cost(2e9, 4e6),
        name="keys",
    )(*slots)


def value_part(slots, k, inverse, w, tail, reach):
    return pl.pallas_call(
        value_kernel,
        out_shape=[
            jax.ShapeDtypeStruct((PLANE, 2 * C, C), BF16),
            jax.ShapeDtypeStruct((PLANE, C, 2 * C), F32),
            jax.ShapeDtypeStruct((C, 2 * C), BF16),
            jax.ShapeDtypeStruct((7, C, 2 * C), F32),
        ],
        in_specs=[vmem()] * 10,
        out_specs=[vmem()] * 4,
        scratch_shapes=[pltpu.VMEM((PLANE, C, C), F32)],
        compiler_params=params(),
        cost_estimate=cost(1e9, 4e6),
        name="values",
    )(*slots, k, inverse, w, tail, reach)


def query_kernel(*refs):
    k_ref, vq_ref, mix_ref, wu_ref, level_ref, no_ref, before = refs
    me = lax.axis_index("seq") % PLANE
    row, col = iotas()
    before[0] = jnp.concatenate([jnp.where(row == col, 1.0, 0.0), jnp.zeros((C, C), F32)], axis=1)
    before[1] = level_ref[0]
    before[2] = level_ref[1]
    before[3] = after(level_ref[1], level_ref[2])
    before[4] = level_ref[3]
    before[5] = after(level_ref[3], level_ref[4])
    six = after(level_ref[3], level_ref[5])
    before[6] = six
    before[7] = after(six, level_ref[6])

    every = range(PLANE)
    found = gates(k_ref)
    queries = [vq_ref[d, C : 2 * C, :] for d in every]
    scored = [dot_nt(queries[d], k_ref[d, 0:C, :]) for d in every]
    r_cols = []
    for q in queries:
        wide = q.astype(F32)
        r_cols.append(lax.rsqrt(jnp.sum(wide * wide, axis=1, keepdims=True) + EPS) * (C**-0.5))
    scored = [scored[d] * r_cols[d] * mix_ref[d] for d in every]
    parts = [mm(scored[d], wu_ref[d]) for d in every]
    reach = [
        queries[d].astype(F32) * (r_cols[d] * jnp.exp(found[d][2])) - parts[d][:, :C]
        for d in every
    ]
    chunks = [jnp.bitwise_xor(me, d) for d in every]
    both = [mm(reach[d], before[chunks[d]]) for d in every]
    for d in every:
        rows = pl.ds(pl.multiple_of(chunks[d] * C, C), C)
        no_ref[rows, :] = jnp.concatenate(
            [both[d][:, :C], both[d][:, C:] + parts[d][:, C:]], axis=1
        )


def query(k, vq, mix, wu, level):
    return pl.pallas_call(
        query_kernel,
        out_shape=jax.ShapeDtypeStruct((PLANE * C, 2 * C), F32),
        in_specs=[vmem()] * 5,
        out_specs=vmem(),
        scratch_shapes=[
            pltpu.VMEM((PLANE, C, 2 * C), F32),
        ],
        compiler_params=params(),
        cost_estimate=cost(1e9, 4e6),
        name="query",
    )(k, vq, mix, wu, level)


def times(a, x):
    hi, lo = split(x)
    return dot(jnp.concatenate([a, a], axis=1), jnp.concatenate([hi, lo], axis=0))


def combine_kernel(own_ref, one_ref, two_ref, before_ref, upto_ref, only_ref):
    a_one, a_own = one_ref[:, :C], own_ref[:, :C]
    reach = dot(a_one, two_ref[:, :C])
    state = one_ref[:, C:].astype(F32) + dot(a_one, two_ref[:, C:])
    before_ref[:, :C] = reach
    before_ref[:, C:] = state
    upto_ref[:, :C] = times(a_own, reach).astype(BF16)
    total = (own_ref[:, C:].astype(F32) + times(a_own, state)).astype(BF16)
    upto_ref[:, C:] = total
    only_ref[...] = total


def combine(own_map, one, two):
    return pl.pallas_call(
        combine_kernel,
        out_shape=[
            jax.ShapeDtypeStruct((C, 2 * C), F32),
            jax.ShapeDtypeStruct((C, 2 * C), BF16),
            jax.ShapeDtypeStruct((C, C), BF16),
        ],
        in_specs=[vmem()] * 3,
        out_specs=[vmem()] * 3,
        compiler_params=params(),
        name="combine",
    )(own_map, one, two)


def norm_kernel(no_ref, gain_ref, before_ref, three_ref, six_ref, normed_ref):
    state = three_ref[:, C:].astype(F32) + dot(three_ref[:, :C], six_ref[...])
    state = before_ref[:, C:] + mm(before_ref[:, :C], state)
    out = mm(no_ref[:, :C], state) + no_ref[:, C:]
    scale = lax.rsqrt(jnp.mean(out * out, axis=1, keepdims=True) + EPS)
    normed_ref[...] = (out * scale * gain_ref[...]).astype(BF16)


def norm(no, gain, before, three, six):
    return pl.pallas_call(
        norm_kernel,
        out_shape=jax.ShapeDtypeStruct((PLANE * C, C), BF16),
        in_specs=[vmem()] * 5,
        out_specs=vmem(),
        compiler_params=params(),
        cost_estimate=cost(2e8, 2e6),
        name="norm",
    )(no, gain, before, three, six)


QB = 256
SCALE = C**-0.5 * 1.4426950408889634


def squares():
    row = lax.broadcasted_iota(jnp.int32, (QB, QB), 0)
    col = lax.broadcasted_iota(jnp.int32, (QB, QB), 1)
    return row, col


def row_max(parts):
    top = jnp.max(parts[0], axis=1, keepdims=True)
    for part in parts[1:]:
        top = jnp.maximum(top, jnp.max(part, axis=1, keepdims=True))
    return top


def row_sum(parts):
    total = jnp.sum(parts[0], axis=1, keepdims=True)
    for part in parts[1:]:
        total = total + jnp.sum(part, axis=1, keepdims=True)
    return total


def weighted(parts, values):
    out = dot(parts[0].astype(BF16), values[0])
    for part, value in zip(parts[1:], values[1:]):
        out = out + dot(part.astype(BF16), value)
    return out


def tiled(column, like):
    return jnp.concatenate([column] * (like.shape[1] // C), axis=1)


def own_kernel(normed_ref, weight_ref, acc_ref, stat_ref, q2_ref):
    me = lax.axis_index("seq") % PLANE
    proj = dot(normed_ref[...], weight_ref[me]).astype(BF16)
    q2_ref[...] = proj[:, :C]
    row, col = squares()
    starts = range(0, PLANE * C, QB)
    spans = [[(at, at + QB)] + ([(0, at)] if at else []) for at in starts]
    scores = [
        [dot_nt(proj[at : at + QB, :C], proj[a:b, C : 2 * C]) for a, b in span]
        for at, span in zip(starts, spans)
    ]
    scores = [[jnp.where(col <= row, parts[0], NEG)] + parts[1:] for parts in scores]
    tops = [row_max(parts) for parts in scores]
    raised = [[jnp.exp2((s - top) * SCALE) for s in parts] for parts, top in zip(scores, tops)]
    for i, at in enumerate(starts):
        rows = slice(at, at + QB)
        acc_ref[rows, :] = weighted(raised[i], [proj[a:b, 2 * C :] for a, b in spans[i]])
        stat_ref[0, rows, :] = jnp.broadcast_to(tops[i], (QB, C))
        stat_ref[1, rows, :] = jnp.broadcast_to(row_sum(raised[i]), (QB, C))


def own(normed, weight):
    n = PLANE * C
    return pl.pallas_call(
        own_kernel,
        out_shape=[
            jax.ShapeDtypeStruct((n, C), F32),
            jax.ShapeDtypeStruct((2, n, C), F32),
            jax.ShapeDtypeStruct((n, C), BF16),
        ],
        in_specs=[vmem()] * 2,
        out_specs=[vmem()] * 3,
        compiler_params=params(),
        cost_estimate=cost(1e9, 3e6, 6e5),
        name="own",
    )(normed, weight)


def halo_kernel(halo_ref, weight_ref, acc_ref, stat_ref, q2_ref, *refs):
    outs, attended = refs[:4], refs[4]
    place = lax.axis_index("seq")
    me, plane = place % PLANE, place // PLANE
    proj = dot(halo_ref[...], weight_ref[me, :, C:]).astype(BF16)
    n = PLANE * C
    row, col = squares()
    starts = range(0, n, QB)
    spans = [[(at, at + QB)] + ([(at + QB, n)] if at + QB < n else []) for at in starts]
    floor = jnp.where(plane > 0, 0.0, NEG)
    scores = [
        [dot_nt(q2_ref[at : at + QB, :], proj[a:b, :C]) for a, b in span]
        for at, span in zip(starts, spans)
    ]
    scores = [[jnp.where(col > row, parts[0], NEG)] + parts[1:] for parts in scores]
    before = [stat_ref[0, at : at + QB, :] for at in starts]
    tops = [jnp.maximum(row_max(parts) + floor, old) for parts, old in zip(scores, before)]
    raised = [
        [jnp.exp2((s - tiled(top - floor, s)) * SCALE) for s in parts]
        for parts, top in zip(scores, tops)
    ]
    fades = [jnp.exp2((old - top) * SCALE) for old, top in zip(before, tops)]
    for i, at in enumerate(starts):
        rows = slice(at, at + QB)
        total = row_sum(raised[i]) + fades[i] * stat_ref[1, rows, :]
        acc = acc_ref[rows, :] * fades[i] + weighted(
            raised[i], [proj[a:b, C:] for a, b in spans[i]]
        )
        attended[rows, :] = (acc / total).astype(BF16)
    for d in range(PLANE):
        chunk = jnp.bitwise_xor(me, d)
        outs[d // 2][d % 2] = attended[pl.ds(pl.multiple_of(chunk * C, C), C), :]


def halo_part(halo, weight, acc, stat, q2):
    n = PLANE * C
    return pl.pallas_call(
        halo_kernel,
        out_shape=[jax.ShapeDtypeStruct((2, C, C), BF16)] * 4,
        in_specs=[vmem()] * 5,
        out_specs=[vmem()] * 4,
        scratch_shapes=[pltpu.VMEM((n, C), BF16)],
        compiler_params=params(),
        cost_estimate=cost(1e9, 3e6, 6e5),
        name="halo",
    )(halo, weight, acc, stat, q2)


COLS = 1024


def pair_part(first, second, dx):
    core, mine = lax.axis_index("seq") % 2, lax.axis_index("heads")
    rows = [pl.ds(pl.multiple_of(jnp.bitwise_xor(mine, e) * 32, 32), 32) for e in range(4)]
    one = jnp.concatenate([first[r, :] for r in rows], axis=0)
    two = jnp.concatenate([second[r, :] for r in rows], axis=0)
    swapped = core > 0
    left = jnp.where(swapped, two.astype(F32), one.astype(F32)).astype(BF16)
    right = jnp.where(swapped, one.astype(F32), two.astype(F32)).astype(BF16)
    chip = lax.axis_index("seq") % PLANE // 2
    at = pl.multiple_of(jnp.bitwise_xor(chip, dx) * 2 * C, 2 * C)
    return jnp.concatenate([left, right], axis=1), pl.ds(at, 2 * C)


def early_kernel(own_pair, own_came, two, two_came, one, one_came, weight_ref, acc_ref):
    parts = [
        pair_part(own_pair.at[0], own_came, 0),
        pair_part(two.at[0], two_came, 2),
        pair_part(one.at[0], one_came, 1),
    ]
    for at in range(0, weight_ref.shape[1], COLS):
        cols = slice(at, at + COLS)
        got = dot(parts[0][0], weight_ref[parts[0][1], cols])
        for part, rows in parts[1:]:
            got = got + dot(part, weight_ref[rows, cols])
        acc_ref[:, cols] = got


def late_kernel(three, three_came, weight_ref, acc_ref, *outs):
    part, rows = pair_part(three.at[0], three_came, 3)
    for at in range(0, weight_ref.shape[1], COLS):
        cols = slice(at, at + COLS)
        got = acc_ref[:, cols] + dot(part, weight_ref[rows, cols])
        for e in range(4):
            outs[e][:, cols] = got[e * 32 : e * 32 + 32].astype(outs[e].dtype)


def project(slots, weight):
    width = weight.shape[1]
    (own_pair, one, two, three), (own_came, one_came, two_came, three_came) = slots
    acc = pl.pallas_call(
        early_kernel,
        out_shape=jax.ShapeDtypeStruct((C, width), F32),
        in_specs=[vmem()] * 7,
        out_specs=vmem(),
        compiler_params=params(),
        cost_estimate=cost(8e8, 8e6),
        name="early",
    )(own_pair, own_came, two, two_came, one, one_came, weight)
    return pl.pallas_call(
        late_kernel,
        out_shape=[jax.ShapeDtypeStruct((32, width), F32)]
        + [jax.ShapeDtypeStruct((32, width), BF16)] * 3,
        in_specs=[vmem()] * 4,
        out_specs=[vmem()] * 4,
        compiler_params=params(),
        cost_estimate=cost(3e8, 4e6),
        name="late",
    )(three, three_came, weight, acc)


def swap(block, d):
    return lax.ppermute(block, "seq", [(s, s ^ d) for s in range(PLANE * PLANES)])


def exchange(keep, send):
    came = swap(send, 1)
    slots = [keep, came]
    for dx in (2, 1, 3):
        slots.append((dx, swap(jnp.stack([keep[dx], came[dx]]), 2 * dx)))
    return slots[:2] + [pair for _, pair in sorted(slots[2:], key=lambda item: item[0])]


def exchange_back(pairs):
    found = {dx: swap(pairs[dx], 2 * dx) for dx in (2, 1, 3)}
    found[0] = pairs[0]
    came = {dx: swap(found[dx][1], 1) for dx in (0, 2, 1, 3)}
    return [found[dx] for dx in range(4)], [came[dx] for dx in range(4)]


def later_plane(block, distance):
    step = PLANE * distance
    route = [(s, s + step) for s in range(PLANE * PLANES - step)]
    return lax.ppermute(block, "seq", route)


def local(q_delta, k_delta, v_delta, decay, beta, gain, attn_weight, out_weight):
    keep_k, send_k, keep, send = pack(q_delta, k_delta, v_delta, decay, beta)
    slots_k = exchange(keep_k, send_k)
    slots = exchange(keep, send)
    k, mix, inverse, w, tail, reach = key_part(slots_k)
    vq, wu, ab, level = value_part(slots, k, inverse, w, tail, reach)
    one = later_plane(ab, 1)
    two = later_plane(ab, 2)
    no = query(k, vq, mix, wu, level)
    before, upto, only = combine(ab, one, two)
    three = later_plane(upto, 3)
    six = later_plane(only, 6)
    normed = norm(no, gain[None, :], before, three, six)
    halo = later_plane(normed, 1)
    acc, stat, q2 = own(normed, attn_weight)
    attended = exchange_back(halo_part(halo, attn_weight, acc, stat, q2))
    sums = project(attended, out_weight)
    moved = {}
    for d in (2, 1, 3):
        moved[d] = lax.ppermute(sums[d], "heads", [(s, s ^ d) for s in range(4)])
    total = sums[0]
    for d in (1, 3, 2):
        total = total + moved[d].astype(F32)
    return total.astype(BF16)


def solution(mesh):
    placed = (
        P("seq", "heads"),
        P("seq", "heads"),
        P("seq", "heads"),
        P("heads", "seq"),
        P("heads", "seq"),
        P(),
        P("heads", None, None),
        P("heads", None),
    )
    return jax.shard_map(
        local, mesh=mesh, in_specs=placed, out_specs=P(("seq", "heads"), None), check_vma=False
    )
```

```python
import jax
import jax.numpy as jnp
from jax import lax
from jax.experimental import pallas as pl
from jax.experimental.pallas import tpu as pltpu
from jax.sharding import PartitionSpec as P

F32 = jnp.float32
BF16 = jnp.bfloat16
C = 128
PLANE = 8
PLANES = 8
KROWS = C + 16
B = 16
EPS = 1e-06
NEG = -1e30
VMEM_LIMIT = 24 * 1024 * 1024


def params(limit=VMEM_LIMIT):
    return pltpu.CompilerParams(vmem_limit_bytes=limit)


def cost(flops, nbytes, trans=0):
    return pl.CostEstimate(flops=int(flops), bytes_accessed=int(nbytes), transcendentals=int(trans))


def vmem():
    return pl.BlockSpec(memory_space=pltpu.VMEM)


def split(a):
    hi = a.astype(BF16)
    lo = (a - hi.astype(F32)).astype(BF16)
    return hi, lo


def dot(a, b):
    return lax.dot_general(a, b, (((1,), (0,)), ((), ())), preferred_element_type=F32)


def dot_nt(a, b):
    return lax.dot_general(a, b, (((1,), (1,)), ((), ())), preferred_element_type=F32)


def dot_tn(a, b):
    return lax.dot_general(a, b, (((0,), (0,)), ((), ())), preferred_element_type=F32)


def mm(a, b):
    ah, al = split(a)
    bh, bl = split(b)
    left = jnp.concatenate([ah, al], axis=1)
    n = b.shape[1]
    if n > C:
        return dot(left, jnp.concatenate([bh, bh], axis=0)) + dot(ah, bl)
    pair = jnp.concatenate([bh, bl], axis=1)
    out = dot(left, jnp.concatenate([pair, pair], axis=0))
    return out[:, :n] + out[:, n:]


def mm_exact_right(a, b):
    ah, al = split(a)
    return dot(jnp.concatenate([ah, al], axis=1), jnp.concatenate([b, b], axis=0))


def iotas():
    row = lax.broadcasted_iota(jnp.int32, (C, C), 0)
    col = lax.broadcasted_iota(jnp.int32, (C, C), 1)
    return row, col


def pack_kernel(q_ref, k_ref, v_ref, decay_ref, beta_ref, *rest):
    keep_k, send_k, keep, send, gate, raw, sems = rest
    me = lax.axis_index("seq") % PLANE
    copies = [
        pltpu.make_async_copy(decay_ref, raw.at[0], sems.at[24]),
        pltpu.make_async_copy(beta_ref, raw.at[1], sems.at[25]),
    ]
    for d in range(PLANE):
        cols = pl.ds(pl.multiple_of(jnp.bitwise_xor(me, d) * C, C), C)
        out_k, out = (send_k, send) if d % 2 else (keep_k, keep)
        at = d // 2
        copies += [
            pltpu.make_async_copy(k_ref.at[:, cols], out_k.at[at, pl.ds(0, C)], sems.at[3 * d]),
            pltpu.make_async_copy(v_ref.at[:, cols], out.at[at, pl.ds(0, C)], sems.at[3 * d + 1]),
            pltpu.make_async_copy(q_ref.at[:, cols], out.at[at, pl.ds(C, C)], sems.at[3 * d + 2]),
        ]
    for copy in copies:
        copy.start()
    copies[0].wait()
    copies[1].wait()
    for i in range(2):
        x = raw[i]
        for j in range(3):
            part = x.astype(BF16).astype(F32)
            gate[3 * i + j] = part
            x = x - part
    zeros = jnp.zeros((10, C), F32)
    for d in range(PLANE):
        head = jnp.bitwise_xor(me, d)
        rows = [gate[i, pl.ds(head, 1), :] for i in range(6)]
        out = send_k if d % 2 else keep_k
        out[d // 2, C:, :] = jnp.concatenate(rows + [zeros], axis=0).astype(BF16)
    for copy in copies[2:]:
        copy.wait()


def pack(q, k, v, decay, beta):
    any_space = pl.BlockSpec(memory_space=pltpu.HBM)
    first = jax.ShapeDtypeStruct((4, KROWS, C), BF16)
    wide = jax.ShapeDtypeStruct((4, 2 * C, C), BF16)
    return pl.pallas_call(
        pack_kernel,
        out_shape=[first, first, wide, wide],
        in_specs=[any_space] * 5,
        out_specs=[vmem()] * 4,
        scratch_shapes=[
            pltpu.VMEM((6, PLANE, C), F32),
            pltpu.VMEM((2, PLANE, C), F32),
            pltpu.SemaphoreType.DMA((26,)),
        ],
        compiler_params=params(),
        name="pack",
    )(*[pltpu.with_memory_space_constraint(x, pltpu.HBM) for x in (q, k, v, decay, beta)])


def gather_slots(refs, out_ref):
    keep, came = refs[0], refs[1]
    out_ref[0] = keep[0]
    out_ref[1] = came[0]
    for dx in range(1, 4):
        out_ref[2 * dx] = refs[dx + 1][0]
        out_ref[2 * dx + 1] = refs[dx + 1][1]


def gates(k_ref):
    row, col = iotas()
    pieces = jnp.concatenate([k_ref[d, C:, :] for d in range(PLANE)], axis=0)
    upper = jnp.where(row <= col, 1.0, 0.0).astype(BF16)
    lower = jnp.where(row >= col, 1.0, 0.0).astype(BF16)
    eye = jnp.where(row == col, 1.0, 0.0).astype(BF16)
    along_row = dot(pieces, upper)
    along_col = dot_nt(jnp.concatenate([lower, eye], axis=0), pieces)
    plain = pieces.astype(F32)
    found = []
    for d in range(PLANE):
        o = 16 * d
        g_row = -(along_row[o : o + 1] + along_row[o + 1 : o + 2] + along_row[o + 2 : o + 3])
        b_row = plain[o + 3 : o + 4] + plain[o + 4 : o + 5] + plain[o + 5 : o + 6]
        g_col = -(
            along_col[:C, o : o + 1] + along_col[:C, o + 1 : o + 2] + along_col[:C, o + 2 : o + 3]
        )
        b_col = (
            along_col[C:, o + 3 : o + 4]
            + along_col[C:, o + 4 : o + 5]
            + along_col[C:, o + 5 : o + 6]
        )
        found.append((g_row, b_row, g_col, b_col))
    return found


def base_inverses(packed):
    row, col = iotas()
    high = packed.astype(BF16)
    rest = packed - high.astype(F32)
    mid = rest.astype(BF16)
    low = (rest - mid.astype(F32)).astype(BF16)
    three = jnp.concatenate([high, mid, low], axis=1)
    x = jnp.where(row % B == col % B, 1.0, 0.0)
    for j in range(B - 1):
        pick = jnp.where(row == col - col % B + j, 1.0, 0.0).astype(BF16)
        factor = dot(three, jnp.concatenate([pick, pick, pick], axis=0))
        line = x.reshape(PLANE, B, C)[:, j : j + 1, :]
        x = x - factor * jnp.broadcast_to(line, (PLANE, B, C)).reshape(C, C)
    return x


def after(earlier, later):
    both = mm(later[:, :C], earlier)
    return jnp.concatenate([both[:, :C], both[:, C:] + later[:, C:]], axis=1)


def key_kernel(*refs):
    k_ref, mix_ref, inverse_ref, w_ref, tail_ref, reach_ref = refs[5:11]
    maps = refs[11]
    me = lax.axis_index("seq") % PLANE
    row, col = iotas()
    gather_slots(refs[:5], k_ref)
    every = range(PLANE)
    blocks = (row // B) == (col // B)
    apart = jnp.bitwise_xor(row, col)
    found = gates(k_ref)
    keys = [k_ref[d, 0:C, :] for d in every]
    grams = [dot_nt(k, k) for k in keys]
    diags = [jnp.where(row == col, g, 0.0) for g in grams]
    r_cols = [lax.rsqrt(jnp.sum(g, axis=1, keepdims=True) + EPS) for g in diags]
    r_rows = [lax.rsqrt(jnp.sum(g, axis=0, keepdims=True) + EPS) for g in diags]
    lows, packs = [], []
    for d in every:
        g_row, b_row, g_col, _ = found[d]
        ratio = jnp.where(row >= col, jnp.exp(jnp.minimum(g_col - g_row, 0.0)), 0.0)
        mix = ratio * (b_row * r_rows[d])
        mix_ref[d] = mix
        low = jnp.where(row > col, mix * grams[d] * r_cols[d], 0.0)
        lows.append(low)
        held = jnp.where(blocks, low, 0.0)
        packed = held[0:B]
        for b in range(1, C // B):
            packed = packed + held[B * b : B * b + B]
        packs.append(packed)
    base = base_inverses(jnp.concatenate(packs, axis=0))
    inverse = [
        jnp.where(blocks, jnp.concatenate([base[B * d : B * d + B]] * (C // B), axis=0), 0.0)
        for d in every
    ]
    size = B
    while size < C:
        level = (row > col) & (apart >= size) & (apart < 2 * size)
        half = [mm(x, jnp.where(level, low, 0.0)) for x, low in zip(inverse, lows)]
        inverse = [x - mm(h, x) for x, h in zip(inverse, half)]
        size *= 2
    folded = [inverse[d] * (jnp.exp(found[d][0]) * r_rows[d]) for d in every]
    w = [mm_exact_right(folded[d], keys[d]) for d in every]
    halves = []
    for d in every:
        g_row, _, g_col, b_col = found[d]
        tail = jnp.broadcast_to(jnp.exp(g_row[:, C - 1 : C] - g_col) * b_col * r_cols[d], (C, C))
        inverse_ref[d] = inverse[d]
        w_ref[d] = w[d]
        tail_ref[d] = tail
        halves.append(jnp.concatenate(split(w[d] * tail), axis=0))
    made = [dot_tn(jnp.concatenate([keys[d], keys[d]], axis=0), halves[d]) for d in every]
    for d in every:
        g_end = found[d][0][:, C - 1 : C]
        maps[jnp.bitwise_xor(me, d)] = jnp.where(row == col, jnp.exp(g_end), 0.0) - made[d]
    one = [maps[i] for i in every]
    two = [mm(one[2 * i + 1], one[2 * i]) for i in range(4)]
    four = [mm(two[2 * i + 1], two[2 * i]) for i in range(2)]
    for i, part in enumerate(one + two + four + [mm(four[1], four[0])]):
        reach_ref[i] = part


def value_kernel(*refs):
    k_ref, inverse_ref, w_ref, tail_ref, reach_ref, vq_ref, wu_ref, ab_ref, level_ref, states = (
        refs[5:]
    )
    me = lax.axis_index("seq") % PLANE
    gather_slots(refs[:5], vq_ref)
    every = range(PLANE)
    u = [mm_exact_right(inverse_ref[d], vq_ref[d, 0:C, :]) for d in every]
    halves = []
    for d in every:
        wu_ref[d, :, :C] = w_ref[d]
        wu_ref[d, :, C:] = u[d]
        halves.append(jnp.concatenate(split(u[d] * tail_ref[d]), axis=0))
    keys = [k_ref[d, 0:C, :] for d in every]
    made = [dot_tn(jnp.concatenate([keys[d], keys[d]], axis=0), halves[d]) for d in every]
    for d in every:
        states[jnp.bitwise_xor(me, d)] = made[d]
    one = [states[i] for i in every]
    two = [mm(reach_ref[2 * i + 1], one[2 * i]) + one[2 * i + 1] for i in range(4)]
    four = [mm(reach_ref[8 + 2 * i + 1], two[2 * i]) + two[2 * i + 1] for i in range(2)]
    last = mm(reach_ref[13], four[0]) + four[1]
    ab_ref[:, :C] = reach_ref[14].astype(BF16)
    ab_ref[:, C:] = last.astype(BF16)
    both = ((0, one[0]), (8, two[0]), (2, one[2]), (12, four[0]), (4, one[4]), (10, two[2]), (6, one[6]))
    for i, (at, state) in enumerate(both):
        level_ref[i, :, :C] = reach_ref[at]
        level_ref[i, :, C:] = state


def key_part(slots):
    square = jax.ShapeDtypeStruct((PLANE, C, C), F32)
    return pl.pallas_call(
        key_kernel,
        out_shape=[jax.ShapeDtypeStruct((PLANE, KROWS, C), BF16)]
        + [square] * 4
        + [jax.ShapeDtypeStruct((15, C, C), F32)],
        in_specs=[vmem()] * 5,
        out_specs=[vmem()] * 6,
        scratch_shapes=[pltpu.VMEM((PLANE, C, C), F32)],
        compiler_params=params(),
        cost_estimate=cost(2e9, 4e6),
        name="keys",
    )(*slots)


def value_part(slots, k, inverse, w, tail, reach):
    return pl.pallas_call(
        value_kernel,
        out_shape=[
            jax.ShapeDtypeStruct((PLANE, 2 * C, C), BF16),
            jax.ShapeDtypeStruct((PLANE, C, 2 * C), F32),
            jax.ShapeDtypeStruct((C, 2 * C), BF16),
            jax.ShapeDtypeStruct((7, C, 2 * C), F32),
        ],
        in_specs=[vmem()] * 10,
        out_specs=[vmem()] * 4,
        scratch_shapes=[pltpu.VMEM((PLANE, C, C), F32)],
        compiler_params=params(),
        cost_estimate=cost(1e9, 4e6),
        name="values",
    )(*slots, k, inverse, w, tail, reach)


def query_kernel(*refs):
    k_ref, vq_ref, mix_ref, wu_ref, level_ref, no_ref, before = refs
    me = lax.axis_index("seq") % PLANE
    row, col = iotas()
    before[0] = jnp.concatenate([jnp.where(row == col, 1.0, 0.0), jnp.zeros((C, C), F32)], axis=1)
    before[1] = level_ref[0]
    before[2] = level_ref[1]
    before[3] = after(level_ref[1], level_ref[2])
    before[4] = level_ref[3]
    before[5] = after(level_ref[3], level_ref[4])
    six = after(level_ref[3], level_ref[5])
    before[6] = six
    before[7] = after(six, level_ref[6])

    every = range(PLANE)
    found = gates(k_ref)
    queries = [vq_ref[d, C : 2 * C, :] for d in every]
    scored = [dot_nt(queries[d], k_ref[d, 0:C, :]) for d in every]
    r_cols = []
    for q in queries:
        wide = q.astype(F32)
        r_cols.append(lax.rsqrt(jnp.sum(wide * wide, axis=1, keepdims=True) + EPS) * (C**-0.5))
    scored = [scored[d] * r_cols[d] * mix_ref[d] for d in every]
    parts = [mm(scored[d], wu_ref[d]) for d in every]
    reach = [
        queries[d].astype(F32) * (r_cols[d] * jnp.exp(found[d][2])) - parts[d][:, :C]
        for d in every
    ]
    chunks = [jnp.bitwise_xor(me, d) for d in every]
    both = [mm(reach[d], before[chunks[d]]) for d in every]
    for d in every:
        rows = pl.ds(pl.multiple_of(chunks[d] * C, C), C)
        no_ref[rows, :] = jnp.concatenate(
            [both[d][:, :C], both[d][:, C:] + parts[d][:, C:]], axis=1
        )


def query(k, vq, mix, wu, level):
    return pl.pallas_call(
        query_kernel,
        out_shape=jax.ShapeDtypeStruct((PLANE * C, 2 * C), F32),
        in_specs=[vmem()] * 5,
        out_specs=vmem(),
        scratch_shapes=[
            pltpu.VMEM((PLANE, C, 2 * C), F32),
        ],
        compiler_params=params(),
        cost_estimate=cost(1e9, 4e6),
        name="query",
    )(k, vq, mix, wu, level)


def times(a, x):
    hi, lo = split(x)
    return dot(jnp.concatenate([a, a], axis=1), jnp.concatenate([hi, lo], axis=0))


def combine_kernel(own_ref, one_ref, two_ref, before_ref, upto_ref):
    a_one, a_own = one_ref[:, :C], own_ref[:, :C]
    reach = dot(a_one, two_ref[:, :C])
    state = one_ref[:, C:].astype(F32) + dot(a_one, two_ref[:, C:])
    before_ref[:, :C] = reach
    before_ref[:, C:] = state
    upto_ref[:, :C] = times(a_own, reach).astype(BF16)
    upto_ref[:, C:] = (own_ref[:, C:].astype(F32) + times(a_own, state)).astype(BF16)


def combine(own_map, one, two):
    return pl.pallas_call(
        combine_kernel,
        out_shape=[
            jax.ShapeDtypeStruct((C, 2 * C), F32),
            jax.ShapeDtypeStruct((C, 2 * C), BF16),
        ],
        in_specs=[vmem()] * 3,
        out_specs=[vmem()] * 2,
        compiler_params=params(),
        name="combine",
    )(own_map, one, two)


def norm_kernel(no_ref, gain_ref, before_ref, six_ref, three_ref, normed_ref):
    state = three_ref[:, C:].astype(F32) + dot(three_ref[:, :C], six_ref[:, C:])
    state = before_ref[:, C:] + mm(before_ref[:, :C], state)
    out = mm(no_ref[:, :C], state) + no_ref[:, C:]
    scale = lax.rsqrt(jnp.mean(out * out, axis=1, keepdims=True) + EPS)
    normed_ref[...] = (out * scale * gain_ref[...]).astype(BF16)


def norm(no, gain, before, six, three):
    return pl.pallas_call(
        norm_kernel,
        out_shape=jax.ShapeDtypeStruct((PLANE * C, C), BF16),
        in_specs=[vmem()] * 5,
        out_specs=vmem(),
        compiler_params=params(),
        cost_estimate=cost(2e8, 2e6),
        name="norm",
    )(no, gain, before, six, three)


QB = 256
SCALE = C**-0.5 * 1.4426950408889634


def squares():
    row = lax.broadcasted_iota(jnp.int32, (QB, QB), 0)
    col = lax.broadcasted_iota(jnp.int32, (QB, QB), 1)
    return row, col


def row_max(parts):
    top = jnp.max(parts[0], axis=1, keepdims=True)
    for part in parts[1:]:
        top = jnp.maximum(top, jnp.max(part, axis=1, keepdims=True))
    return top


def row_sum(parts):
    total = jnp.sum(parts[0], axis=1, keepdims=True)
    for part in parts[1:]:
        total = total + jnp.sum(part, axis=1, keepdims=True)
    return total


def weighted(parts, values):
    out = dot(parts[0].astype(BF16), values[0])
    for part, value in zip(parts[1:], values[1:]):
        out = out + dot(part.astype(BF16), value)
    return out


def tiled(column, like):
    return jnp.concatenate([column] * (like.shape[1] // C), axis=1)


def own_kernel(normed_ref, weight_ref, acc_ref, stat_ref, q2_ref):
    me = lax.axis_index("seq") % PLANE
    proj = dot(normed_ref[...], weight_ref[me]).astype(BF16)
    q2_ref[...] = proj[:, :C]
    row, col = squares()
    starts = range(0, PLANE * C, QB)
    spans = [[(at, at + QB)] + ([(0, at)] if at else []) for at in starts]
    scores = [
        [dot_nt(proj[at : at + QB, :C], proj[a:b, C : 2 * C]) for a, b in span]
        for at, span in zip(starts, spans)
    ]
    scores = [[jnp.where(col <= row, parts[0], NEG)] + parts[1:] for parts in scores]
    tops = [row_max(parts) for parts in scores]
    raised = [[jnp.exp2((s - top) * SCALE) for s in parts] for parts, top in zip(scores, tops)]
    for i, at in enumerate(starts):
        rows = slice(at, at + QB)
        acc_ref[rows, :] = weighted(raised[i], [proj[a:b, 2 * C :] for a, b in spans[i]])
        stat_ref[0, rows, :] = jnp.broadcast_to(tops[i], (QB, C))
        stat_ref[1, rows, :] = jnp.broadcast_to(row_sum(raised[i]), (QB, C))


def own(normed, weight):
    n = PLANE * C
    return pl.pallas_call(
        own_kernel,
        out_shape=[
            jax.ShapeDtypeStruct((n, C), F32),
            jax.ShapeDtypeStruct((2, n, C), F32),
            jax.ShapeDtypeStruct((n, C), BF16),
        ],
        in_specs=[vmem()] * 2,
        out_specs=[vmem()] * 3,
        compiler_params=params(),
        cost_estimate=cost(1e9, 3e6, 6e5),
        name="own",
    )(normed, weight)


def halo_kernel(halo_ref, weight_ref, acc_ref, stat_ref, q2_ref, *refs):
    outs, attended = refs[:4], refs[4]
    place = lax.axis_index("seq")
    me, plane = place % PLANE, place // PLANE
    proj = dot(halo_ref[...], weight_ref[me, :, C:]).astype(BF16)
    n = PLANE * C
    row, col = squares()
    starts = range(0, n, QB)
    spans = [[(at, at + QB)] + ([(at + QB, n)] if at + QB < n else []) for at in starts]
    floor = jnp.where(plane > 0, 0.0, NEG)
    scores = [
        [dot_nt(q2_ref[at : at + QB, :], proj[a:b, :C]) for a, b in span]
        for at, span in zip(starts, spans)
    ]
    scores = [[jnp.where(col > row, parts[0], NEG)] + parts[1:] for parts in scores]
    before = [stat_ref[0, at : at + QB, :] for at in starts]
    tops = [jnp.maximum(row_max(parts) + floor, old) for parts, old in zip(scores, before)]
    raised = [
        [jnp.exp2((s - tiled(top - floor, s)) * SCALE) for s in parts]
        for parts, top in zip(scores, tops)
    ]
    fades = [jnp.exp2((old - top) * SCALE) for old, top in zip(before, tops)]
    for i, at in enumerate(starts):
        rows = slice(at, at + QB)
        total = row_sum(raised[i]) + fades[i] * stat_ref[1, rows, :]
        acc = acc_ref[rows, :] * fades[i] + weighted(
            raised[i], [proj[a:b, C:] for a, b in spans[i]]
        )
        attended[rows, :] = (acc / total).astype(BF16)
    for d in range(PLANE):
        chunk = jnp.bitwise_xor(me, d)
        outs[d // 2][d % 2] = attended[pl.ds(pl.multiple_of(chunk * C, C), C), :]


def halo_part(halo, weight, acc, stat, q2):
    n = PLANE * C
    return pl.pallas_call(
        halo_kernel,
        out_shape=[jax.ShapeDtypeStruct((2, C, C), BF16)] * 4,
        in_specs=[vmem()] * 5,
        out_specs=[vmem()] * 4,
        scratch_shapes=[pltpu.VMEM((n, C), BF16)],
        compiler_params=params(),
        cost_estimate=cost(1e9, 3e6, 6e5),
        name="halo",
    )(halo, weight, acc, stat, q2)


COLS = 1024


def pair_part(first, second, dx):
    core, mine = lax.axis_index("seq") % 2, lax.axis_index("heads")
    rows = [pl.ds(pl.multiple_of(jnp.bitwise_xor(mine, e) * 32, 32), 32) for e in range(4)]
    one = jnp.concatenate([first[r, :] for r in rows], axis=0)
    two = jnp.concatenate([second[r, :] for r in rows], axis=0)
    swapped = core > 0
    left = jnp.where(swapped, two.astype(F32), one.astype(F32)).astype(BF16)
    right = jnp.where(swapped, one.astype(F32), two.astype(F32)).astype(BF16)
    chip = lax.axis_index("seq") % PLANE // 2
    at = pl.multiple_of(jnp.bitwise_xor(chip, dx) * 2 * C, 2 * C)
    return jnp.concatenate([left, right], axis=1), pl.ds(at, 2 * C)


def early_kernel(own_pair, own_came, two, two_came, one, one_came, weight_ref, acc_ref):
    parts = [
        pair_part(own_pair.at[0], own_came, 0),
        pair_part(two.at[0], two_came, 2),
        pair_part(one.at[0], one_came, 1),
    ]
    for at in range(0, weight_ref.shape[1], COLS):
        cols = slice(at, at + COLS)
        got = dot(parts[0][0], weight_ref[parts[0][1], cols])
        for part, rows in parts[1:]:
            got = got + dot(part, weight_ref[rows, cols])
        acc_ref[:, cols] = got


def late_kernel(three, three_came, weight_ref, acc_ref, *outs):
    part, rows = pair_part(three.at[0], three_came, 3)
    for at in range(0, weight_ref.shape[1], COLS):
        cols = slice(at, at + COLS)
        got = acc_ref[:, cols] + dot(part, weight_ref[rows, cols])
        for e in range(4):
            outs[e][:, cols] = got[e * 32 : e * 32 + 32].astype(outs[e].dtype)


def project(slots, weight):
    width = weight.shape[1]
    (own_pair, one, two, three), (own_came, one_came, two_came, three_came) = slots
    acc = pl.pallas_call(
        early_kernel,
        out_shape=jax.ShapeDtypeStruct((C, width), F32),
        in_specs=[vmem()] * 7,
        out_specs=vmem(),
        compiler_params=params(),
        cost_estimate=cost(8e8, 8e6),
        name="early",
    )(own_pair, own_came, two, two_came, one, one_came, weight)
    return pl.pallas_call(
        late_kernel,
        out_shape=[jax.ShapeDtypeStruct((32, width), F32)]
        + [jax.ShapeDtypeStruct((32, width), BF16)] * 3,
        in_specs=[vmem()] * 4,
        out_specs=[vmem()] * 4,
        compiler_params=params(),
        cost_estimate=cost(3e8, 4e6),
        name="late",
    )(three, three_came, weight, acc)


def swap(block, d):
    return lax.ppermute(block, "seq", [(s, s ^ d) for s in range(PLANE * PLANES)])


def exchange(keep, send):
    came = swap(send, 1)
    slots = [keep, came]
    for dx in (2, 1, 3):
        slots.append((dx, swap(jnp.stack([keep[dx], came[dx]]), 2 * dx)))
    return slots[:2] + [pair for _, pair in sorted(slots[2:], key=lambda item: item[0])]


def exchange_back(pairs):
    found = {dx: swap(pairs[dx], 2 * dx) for dx in (2, 1, 3)}
    found[0], found[2] = lax.optimization_barrier((pairs[0], found[2]))
    came = {dx: swap(found[dx][1], 1) for dx in (2, 0, 1, 3)}
    return [found[dx] for dx in range(4)], [came[dx] for dx in range(4)]


def later_plane(block, distance):
    step = PLANE * distance
    route = [(s, s + step) for s in range(PLANE * PLANES - step)]
    return lax.ppermute(block, "seq", route)


def local(q_delta, k_delta, v_delta, decay, beta, gain, attn_weight, out_weight):
    keep_k, send_k, keep, send = pack(q_delta, k_delta, v_delta, decay, beta)
    slots_k = exchange(keep_k, send_k)
    slots = exchange(keep, send)
    k, mix, inverse, w, tail, reach = key_part(slots_k)
    vq, wu, ab, level = value_part(slots, k, inverse, w, tail, reach)
    one = later_plane(ab, 1)
    two = later_plane(ab, 2)
    no = query(k, vq, mix, wu, level)
    before, upto = combine(ab, one, two)
    six = later_plane(upto, 6)
    three = later_plane(upto, 3)
    normed = norm(no, gain[None, :], before, six, three)
    halo = later_plane(normed, 1)
    acc, stat, q2 = own(normed, attn_weight)
    attended = exchange_back(halo_part(halo, attn_weight, acc, stat, q2))
    sums = project(attended, out_weight)
    moved = {}
    for d in (2, 1, 3):
        moved[d] = lax.ppermute(sums[d], "heads", [(s, s ^ d) for s in range(4)])
    total = sums[0]
    for d in (1, 3, 2):
        total = total + moved[d].astype(F32)
    return total.astype(BF16)


def solution(mesh):
    placed = (
        P("seq", "heads"),
        P("seq", "heads"),
        P("seq", "heads"),
        P("heads", "seq"),
        P("heads", "seq"),
        P(),
        P("heads", None, None),
        P("heads", None),
    )
    return jax.shard_map(
        local, mesh=mesh, in_specs=placed, out_specs=P(("seq", "heads"), None), check_vma=False
    )
```

```python
import jax
import jax.numpy as jnp
from jax import lax
from jax.experimental import pallas as pl
from jax.experimental.pallas import tpu as pltpu
from jax.sharding import PartitionSpec as P

F32 = jnp.float32
BF16 = jnp.bfloat16
C = 128
PLANE = 8
PLANES = 8
KROWS = C + 16
B = 16
EPS = 1e-06
NEG = -1e30
VMEM_LIMIT = 24 * 1024 * 1024


def params(limit=VMEM_LIMIT):
    return pltpu.CompilerParams(vmem_limit_bytes=limit)


def cost(flops, nbytes, trans=0):
    return pl.CostEstimate(flops=int(flops), bytes_accessed=int(nbytes), transcendentals=int(trans))


def vmem():
    return pl.BlockSpec(memory_space=pltpu.VMEM)


def split(a):
    hi = a.astype(BF16)
    lo = (a - hi.astype(F32)).astype(BF16)
    return hi, lo


def dot(a, b):
    return lax.dot_general(a, b, (((1,), (0,)), ((), ())), preferred_element_type=F32)


def dot_nt(a, b):
    return lax.dot_general(a, b, (((1,), (1,)), ((), ())), preferred_element_type=F32)


def dot_tn(a, b):
    return lax.dot_general(a, b, (((0,), (0,)), ((), ())), preferred_element_type=F32)


def mm(a, b):
    ah, al = split(a)
    bh, bl = split(b)
    left = jnp.concatenate([ah, al], axis=1)
    n = b.shape[1]
    if n > C:
        return dot(left, jnp.concatenate([bh, bh], axis=0)) + dot(ah, bl)
    pair = jnp.concatenate([bh, bl], axis=1)
    out = dot(left, jnp.concatenate([pair, pair], axis=0))
    return out[:, :n] + out[:, n:]


def mm_exact_right(a, b):
    ah, al = split(a)
    return dot(jnp.concatenate([ah, al], axis=1), jnp.concatenate([b, b], axis=0))


def iotas():
    row = lax.broadcasted_iota(jnp.int32, (C, C), 0)
    col = lax.broadcasted_iota(jnp.int32, (C, C), 1)
    return row, col


def pack_kernel(q_ref, k_ref, v_ref, decay_ref, beta_ref, *rest):
    keep_k, send_k, keep, send, gate, raw, sems = rest
    me = lax.axis_index("seq") % PLANE
    copies = [
        pltpu.make_async_copy(decay_ref, raw.at[0], sems.at[24]),
        pltpu.make_async_copy(beta_ref, raw.at[1], sems.at[25]),
    ]
    for d in range(PLANE):
        cols = pl.ds(pl.multiple_of(jnp.bitwise_xor(me, d) * C, C), C)
        out_k, out = (send_k, send) if d % 2 else (keep_k, keep)
        at = d // 2
        copies += [
            pltpu.make_async_copy(k_ref.at[:, cols], out_k.at[at, pl.ds(0, C)], sems.at[3 * d]),
            pltpu.make_async_copy(v_ref.at[:, cols], out.at[at, pl.ds(0, C)], sems.at[3 * d + 1]),
            pltpu.make_async_copy(q_ref.at[:, cols], out.at[at, pl.ds(C, C)], sems.at[3 * d + 2]),
        ]
    for copy in copies:
        copy.start()
    copies[0].wait()
    copies[1].wait()
    for i in range(2):
        x = raw[i]
        for j in range(3):
            part = x.astype(BF16).astype(F32)
            gate[3 * i + j] = part
            x = x - part
    zeros = jnp.zeros((10, C), F32)
    for d in range(PLANE):
        head = jnp.bitwise_xor(me, d)
        rows = [gate[i, pl.ds(head, 1), :] for i in range(6)]
        out = send_k if d % 2 else keep_k
        out[d // 2, C:, :] = jnp.concatenate(rows + [zeros], axis=0).astype(BF16)
    for copy in copies[2:]:
        copy.wait()


def pack(q, k, v, decay, beta):
    any_space = pl.BlockSpec(memory_space=pltpu.HBM)
    first = jax.ShapeDtypeStruct((4, KROWS, C), BF16)
    wide = jax.ShapeDtypeStruct((4, 2 * C, C), BF16)
    return pl.pallas_call(
        pack_kernel,
        out_shape=[first, first, wide, wide],
        in_specs=[any_space] * 5,
        out_specs=[vmem()] * 4,
        scratch_shapes=[
            pltpu.VMEM((6, PLANE, C), F32),
            pltpu.VMEM((2, PLANE, C), F32),
            pltpu.SemaphoreType.DMA((26,)),
        ],
        compiler_params=params(),
        name="pack",
    )(*[pltpu.with_memory_space_constraint(x, pltpu.HBM) for x in (q, k, v, decay, beta)])


def gather_slots(refs, out_ref, part=None):
    keep, came = refs[0], refs[1]
    out_ref[0] = keep[0] if part is None else keep[0, part, :]
    out_ref[1] = came[0] if part is None else came[0, part, :]
    for dx in range(1, 4):
        out_ref[2 * dx] = refs[dx + 1][0]
        out_ref[2 * dx + 1] = refs[dx + 1][1]


def gates(k_ref):
    row, col = iotas()
    pieces = jnp.concatenate([k_ref[d, C:, :] for d in range(PLANE)], axis=0)
    upper = jnp.where(row <= col, 1.0, 0.0).astype(BF16)
    lower = jnp.where(row >= col, 1.0, 0.0).astype(BF16)
    eye = jnp.where(row == col, 1.0, 0.0).astype(BF16)
    along_row = dot(pieces, upper)
    along_col = dot_nt(jnp.concatenate([lower, eye], axis=0), pieces)
    plain = pieces.astype(F32)
    found = []
    for d in range(PLANE):
        o = 16 * d
        g_row = -(along_row[o : o + 1] + along_row[o + 1 : o + 2] + along_row[o + 2 : o + 3])
        b_row = plain[o + 3 : o + 4] + plain[o + 4 : o + 5] + plain[o + 5 : o + 6]
        g_col = -(
            along_col[:C, o : o + 1] + along_col[:C, o + 1 : o + 2] + along_col[:C, o + 2 : o + 3]
        )
        b_col = (
            along_col[C:, o + 3 : o + 4]
            + along_col[C:, o + 4 : o + 5]
            + along_col[C:, o + 5 : o + 6]
        )
        found.append((g_row, b_row, g_col, b_col))
    return found


def base_inverses(packed):
    row, col = iotas()
    high = packed.astype(BF16)
    rest = packed - high.astype(F32)
    mid = rest.astype(BF16)
    low = (rest - mid.astype(F32)).astype(BF16)
    three = jnp.concatenate([high, mid, low], axis=1)
    x = jnp.where(row % B == col % B, 1.0, 0.0)
    for j in range(B - 1):
        pick = jnp.where(row == col - col % B + j, 1.0, 0.0).astype(BF16)
        factor = dot(three, jnp.concatenate([pick, pick, pick], axis=0))
        line = x.reshape(PLANE, B, C)[:, j : j + 1, :]
        x = x - factor * jnp.broadcast_to(line, (PLANE, B, C)).reshape(C, C)
    return x


def after(earlier, later):
    both = mm(later[:, :C], earlier)
    return jnp.concatenate([both[:, :C], both[:, C:] + later[:, C:]], axis=1)


def key_kernel(*refs):
    k_ref, mix_ref, inverse_ref, w_ref, tail_ref, reach_ref = refs[5:11]
    maps = refs[11]
    me = lax.axis_index("seq") % PLANE
    row, col = iotas()
    gather_slots(refs[:5], k_ref)
    every = range(PLANE)
    blocks = (row // B) == (col // B)
    apart = jnp.bitwise_xor(row, col)
    found = gates(k_ref)
    keys = [k_ref[d, 0:C, :] for d in every]
    grams = [dot_nt(k, k) for k in keys]
    diags = [jnp.where(row == col, g, 0.0) for g in grams]
    r_cols = [lax.rsqrt(jnp.sum(g, axis=1, keepdims=True) + EPS) for g in diags]
    r_rows = [lax.rsqrt(jnp.sum(g, axis=0, keepdims=True) + EPS) for g in diags]
    lows, packs = [], []
    for d in every:
        g_row, b_row, g_col, _ = found[d]
        ratio = jnp.where(row >= col, jnp.exp(jnp.minimum(g_col - g_row, 0.0)), 0.0)
        mix = ratio * (b_row * r_rows[d])
        mix_ref[d] = mix
        low = jnp.where(row > col, mix * grams[d] * r_cols[d], 0.0)
        lows.append(low)
        held = jnp.where(blocks, low, 0.0)
        packed = held[0:B]
        for b in range(1, C // B):
            packed = packed + held[B * b : B * b + B]
        packs.append(packed)
    base = base_inverses(jnp.concatenate(packs, axis=0))
    inverse = [
        jnp.where(blocks, jnp.concatenate([base[B * d : B * d + B]] * (C // B), axis=0), 0.0)
        for d in every
    ]
    size = B
    while size < C:
        level = (row > col) & (apart >= size) & (apart < 2 * size)
        half = [mm(x, jnp.where(level, low, 0.0)) for x, low in zip(inverse, lows)]
        inverse = [x - mm(h, x) for x, h in zip(inverse, half)]
        size *= 2
    folded = [inverse[d] * (jnp.exp(found[d][0]) * r_rows[d]) for d in every]
    w = [mm_exact_right(folded[d], keys[d]) for d in every]
    halves = []
    for d in every:
        g_row, _, g_col, b_col = found[d]
        tail = jnp.broadcast_to(jnp.exp(g_row[:, C - 1 : C] - g_col) * b_col * r_cols[d], (C, C))
        inverse_ref[d] = inverse[d]
        w_ref[d] = w[d]
        tail_ref[d] = tail
        halves.append(jnp.concatenate(split(w[d] * tail), axis=0))
    made = [dot_tn(jnp.concatenate([keys[d], keys[d]], axis=0), halves[d]) for d in every]
    for d in every:
        g_end = found[d][0][:, C - 1 : C]
        maps[jnp.bitwise_xor(me, d)] = jnp.where(row == col, jnp.exp(g_end), 0.0) - made[d]
    one = [maps[i] for i in every]
    two = [mm(one[2 * i + 1], one[2 * i]) for i in range(4)]
    four = [mm(two[2 * i + 1], two[2 * i]) for i in range(2)]
    for i, part in enumerate(one + two + four + [mm(four[1], four[0])]):
        reach_ref[i] = part


def value_kernel(*refs):
    k_ref, inverse_ref, w_ref, tail_ref, reach_ref = refs[5:10]
    wu_ref, ab_ref, level_ref, states, v_ref = refs[10:]
    me = lax.axis_index("seq") % PLANE
    gather_slots(refs[:5], v_ref, slice(0, C))
    every = range(PLANE)
    u = [mm_exact_right(inverse_ref[d], v_ref[d]) for d in every]
    halves = []
    for d in every:
        wu_ref[d, :, :C] = w_ref[d]
        wu_ref[d, :, C:] = u[d]
        halves.append(jnp.concatenate(split(u[d] * tail_ref[d]), axis=0))
    keys = [k_ref[d, 0:C, :] for d in every]
    made = [dot_tn(jnp.concatenate([keys[d], keys[d]], axis=0), halves[d]) for d in every]
    for d in every:
        states[jnp.bitwise_xor(me, d)] = made[d]
    one = [states[i] for i in every]
    two = [mm(reach_ref[2 * i + 1], one[2 * i]) + one[2 * i + 1] for i in range(4)]
    four = [mm(reach_ref[8 + 2 * i + 1], two[2 * i]) + two[2 * i + 1] for i in range(2)]
    last = mm(reach_ref[13], four[0]) + four[1]
    ab_ref[:, :C] = reach_ref[14].astype(BF16)
    ab_ref[:, C:] = last.astype(BF16)
    both = ((0, one[0]), (8, two[0]), (2, one[2]), (12, four[0]), (4, one[4]), (10, two[2]), (6, one[6]))
    for i, (at, state) in enumerate(both):
        level_ref[i, :, :C] = reach_ref[at]
        level_ref[i, :, C:] = state


def key_part(slots):
    square = jax.ShapeDtypeStruct((PLANE, C, C), F32)
    return pl.pallas_call(
        key_kernel,
        out_shape=[jax.ShapeDtypeStruct((PLANE, KROWS, C), BF16)]
        + [square] * 4
        + [jax.ShapeDtypeStruct((15, C, C), F32)],
        in_specs=[vmem()] * 5,
        out_specs=[vmem()] * 6,
        scratch_shapes=[pltpu.VMEM((PLANE, C, C), F32)],
        compiler_params=params(),
        cost_estimate=cost(2e9, 4e6),
        name="keys",
    )(*slots)


def value_part(slots, k, inverse, w, tail, reach):
    return pl.pallas_call(
        value_kernel,
        out_shape=[
            jax.ShapeDtypeStruct((PLANE, C, 2 * C), F32),
            jax.ShapeDtypeStruct((C, 2 * C), BF16),
            jax.ShapeDtypeStruct((7, C, 2 * C), F32),
        ],
        in_specs=[vmem()] * 10,
        out_specs=[vmem()] * 3,
        scratch_shapes=[pltpu.VMEM((PLANE, C, C), F32), pltpu.VMEM((PLANE, C, C), BF16)],
        compiler_params=params(),
        cost_estimate=cost(1e9, 4e6),
        name="values",
    )(*slots, k, inverse, w, tail, reach)


def query_kernel(*refs):
    k_ref, mix_ref, wu_ref, level_ref, no_ref, before, q_ref = refs[5:]
    gather_slots(refs[:5], q_ref, slice(C, 2 * C))
    me = lax.axis_index("seq") % PLANE
    row, col = iotas()
    before[0] = jnp.concatenate([jnp.where(row == col, 1.0, 0.0), jnp.zeros((C, C), F32)], axis=1)
    before[1] = level_ref[0]
    before[2] = level_ref[1]
    before[3] = after(level_ref[1], level_ref[2])
    before[4] = level_ref[3]
    before[5] = after(level_ref[3], level_ref[4])
    six = after(level_ref[3], level_ref[5])
    before[6] = six
    before[7] = after(six, level_ref[6])

    every = range(PLANE)
    found = gates(k_ref)
    queries = [q_ref[d] for d in every]
    scored = [dot_nt(queries[d], k_ref[d, 0:C, :]) for d in every]
    r_cols = []
    for q in queries:
        wide = q.astype(F32)
        r_cols.append(lax.rsqrt(jnp.sum(wide * wide, axis=1, keepdims=True) + EPS) * (C**-0.5))
    scored = [scored[d] * r_cols[d] * mix_ref[d] for d in every]
    parts = [mm(scored[d], wu_ref[d]) for d in every]
    reach = [
        queries[d].astype(F32) * (r_cols[d] * jnp.exp(found[d][2])) - parts[d][:, :C]
        for d in every
    ]
    chunks = [jnp.bitwise_xor(me, d) for d in every]
    both = [mm(reach[d], before[chunks[d]]) for d in every]
    for d in every:
        rows = pl.ds(pl.multiple_of(chunks[d] * C, C), C)
        no_ref[rows, :] = jnp.concatenate(
            [both[d][:, :C], both[d][:, C:] + parts[d][:, C:]], axis=1
        )


def query(slots, k, mix, wu, level):
    return pl.pallas_call(
        query_kernel,
        out_shape=jax.ShapeDtypeStruct((PLANE * C, 2 * C), F32),
        in_specs=[vmem()] * 9,
        out_specs=vmem(),
        scratch_shapes=[
            pltpu.VMEM((PLANE, C, 2 * C), F32),
            pltpu.VMEM((PLANE, C, C), BF16),
        ],
        compiler_params=params(),
        cost_estimate=cost(1e9, 4e6),
        name="query",
    )(*slots, k, mix, wu, level)


def times(a, x):
    hi, lo = split(x)
    return dot(jnp.concatenate([a, a], axis=1), jnp.concatenate([hi, lo], axis=0))


def combine_kernel(own_ref, one_ref, two_ref, before_ref, upto_ref):
    a_one, a_own = one_ref[:, :C], own_ref[:, :C]
    reach = dot(a_one, two_ref[:, :C])
    state = one_ref[:, C:].astype(F32) + dot(a_one, two_ref[:, C:])
    before_ref[:, :C] = reach
    before_ref[:, C:] = state
    upto_ref[:, :C] = times(a_own, reach).astype(BF16)
    upto_ref[:, C:] = (own_ref[:, C:].astype(F32) + times(a_own, state)).astype(BF16)


def combine(own_map, one, two):
    return pl.pallas_call(
        combine_kernel,
        out_shape=[
            jax.ShapeDtypeStruct((C, 2 * C), F32),
            jax.ShapeDtypeStruct((C, 2 * C), BF16),
        ],
        in_specs=[vmem()] * 3,
        out_specs=[vmem()] * 2,
        compiler_params=params(),
        name="combine",
    )(own_map, one, two)


def norm_kernel(no_ref, gain_ref, before_ref, six_ref, three_ref, normed_ref):
    state = three_ref[:, C:].astype(F32) + dot(three_ref[:, :C], six_ref[:, C:])
    state = before_ref[:, C:] + mm(before_ref[:, :C], state)
    out = mm(no_ref[:, :C], state) + no_ref[:, C:]
    scale = lax.rsqrt(jnp.mean(out * out, axis=1, keepdims=True) + EPS)
    normed_ref[...] = (out * scale * gain_ref[...]).astype(BF16)


def norm(no, gain, before, six, three):
    return pl.pallas_call(
        norm_kernel,
        out_shape=jax.ShapeDtypeStruct((PLANE * C, C), BF16),
        in_specs=[vmem()] * 5,
        out_specs=vmem(),
        compiler_params=params(),
        cost_estimate=cost(2e8, 2e6),
        name="norm",
    )(no, gain, before, six, three)


QB = 256
SCALE = C**-0.5 * 1.4426950408889634


def squares():
    row = lax.broadcasted_iota(jnp.int32, (QB, QB), 0)
    col = lax.broadcasted_iota(jnp.int32, (QB, QB), 1)
    return row, col


def row_max(parts):
    top = jnp.max(parts[0], axis=1, keepdims=True)
    for part in parts[1:]:
        top = jnp.maximum(top, jnp.max(part, axis=1, keepdims=True))
    return top


def row_sum(parts):
    total = jnp.sum(parts[0], axis=1, keepdims=True)
    for part in parts[1:]:
        total = total + jnp.sum(part, axis=1, keepdims=True)
    return total


def weighted(parts, values):
    out = dot(parts[0].astype(BF16), values[0])
    for part, value in zip(parts[1:], values[1:]):
        out = out + dot(part.astype(BF16), value)
    return out


def tiled(column, like):
    return jnp.concatenate([column] * (like.shape[1] // C), axis=1)


def own_kernel(normed_ref, weight_ref, acc_ref, stat_ref, q2_ref):
    me = lax.axis_index("seq") % PLANE
    proj = dot(normed_ref[...], weight_ref[me]).astype(BF16)
    q2_ref[...] = proj[:, :C]
    row, col = squares()
    starts = range(0, PLANE * C, QB)
    spans = [[(at, at + QB)] + ([(0, at)] if at else []) for at in starts]
    scores = [
        [dot_nt(proj[at : at + QB, :C], proj[a:b, C : 2 * C]) for a, b in span]
        for at, span in zip(starts, spans)
    ]
    scores = [[jnp.where(col <= row, parts[0], NEG)] + parts[1:] for parts in scores]
    tops = [row_max(parts) for parts in scores]
    raised = [[jnp.exp2((s - top) * SCALE) for s in parts] for parts, top in zip(scores, tops)]
    for i, at in enumerate(starts):
        rows = slice(at, at + QB)
        acc_ref[rows, :] = weighted(raised[i], [proj[a:b, 2 * C :] for a, b in spans[i]])
        stat_ref[0, rows, :] = jnp.broadcast_to(tops[i], (QB, C))
        stat_ref[1, rows, :] = jnp.broadcast_to(row_sum(raised[i]), (QB, C))


def own(normed, weight):
    n = PLANE * C
    return pl.pallas_call(
        own_kernel,
        out_shape=[
            jax.ShapeDtypeStruct((n, C), F32),
            jax.ShapeDtypeStruct((2, n, C), F32),
            jax.ShapeDtypeStruct((n, C), BF16),
        ],
        in_specs=[vmem()] * 2,
        out_specs=[vmem()] * 3,
        compiler_params=params(),
        cost_estimate=cost(1e9, 3e6, 6e5),
        name="own",
    )(normed, weight)


def halo_kernel(halo_ref, weight_ref, acc_ref, stat_ref, q2_ref, *refs):
    keep, send, attended = refs
    place = lax.axis_index("seq")
    me, plane = place % PLANE, place // PLANE
    proj = dot(halo_ref[...], weight_ref[me, :, C:]).astype(BF16)
    n = PLANE * C
    row, col = squares()
    starts = range(0, n, QB)
    spans = [[(at, at + QB)] + ([(at + QB, n)] if at + QB < n else []) for at in starts]
    floor = jnp.where(plane > 0, 0.0, NEG)
    scores = [
        [dot_nt(q2_ref[at : at + QB, :], proj[a:b, :C]) for a, b in span]
        for at, span in zip(starts, spans)
    ]
    scores = [[jnp.where(col > row, parts[0], NEG)] + parts[1:] for parts in scores]
    before = [stat_ref[0, at : at + QB, :] for at in starts]
    tops = [jnp.maximum(row_max(parts) + floor, old) for parts, old in zip(scores, before)]
    raised = [
        [jnp.exp2((s - tiled(top - floor, s)) * SCALE) for s in parts]
        for parts, top in zip(scores, tops)
    ]
    fades = [jnp.exp2((old - top) * SCALE) for old, top in zip(before, tops)]
    for i, at in enumerate(starts):
        rows = slice(at, at + QB)
        total = row_sum(raised[i]) + fades[i] * stat_ref[1, rows, :]
        acc = acc_ref[rows, :] * fades[i] + weighted(
            raised[i], [proj[a:b, C:] for a, b in spans[i]]
        )
        attended[rows, :] = (acc / total).astype(BF16)
    for d in range(PLANE):
        chunk = jnp.bitwise_xor(me, d)
        out = send if d % 2 else keep
        out[d // 2] = attended[pl.ds(pl.multiple_of(chunk * C, C), C), :]


def halo_part(halo, weight, acc, stat, q2):
    n = PLANE * C
    return pl.pallas_call(
        halo_kernel,
        out_shape=[jax.ShapeDtypeStruct((4, C, C), BF16)] * 2,
        in_specs=[vmem()] * 5,
        out_specs=[vmem()] * 2,
        scratch_shapes=[pltpu.VMEM((n, C), BF16)],
        compiler_params=params(),
        cost_estimate=cost(1e9, 3e6, 6e5),
        name="halo",
    )(halo, weight, acc, stat, q2)


COLS = 1024


def pair_part(first, second, dx):
    core, mine = lax.axis_index("seq") % 2, lax.axis_index("heads")
    rows = [pl.ds(pl.multiple_of(jnp.bitwise_xor(mine, e) * 32, 32), 32) for e in range(4)]
    one = jnp.concatenate([first[r, :] for r in rows], axis=0)
    two = jnp.concatenate([second[r, :] for r in rows], axis=0)
    swapped = core > 0
    left = jnp.where(swapped, two.astype(F32), one.astype(F32)).astype(BF16)
    right = jnp.where(swapped, one.astype(F32), two.astype(F32)).astype(BF16)
    chip = lax.axis_index("seq") % PLANE // 2
    at = pl.multiple_of(jnp.bitwise_xor(chip, dx) * 2 * C, 2 * C)
    return jnp.concatenate([left, right], axis=1), pl.ds(at, 2 * C)


def early_kernel(keep, came, one, two, weight_ref, acc_ref):
    parts = [
        pair_part(keep.at[0], came.at[0], 0),
        pair_part(two.at[0], two.at[1], 2),
        pair_part(one.at[0], one.at[1], 1),
    ]
    for at in range(0, weight_ref.shape[1], COLS):
        cols = slice(at, at + COLS)
        got = dot(parts[0][0], weight_ref[parts[0][1], cols])
        for part, rows in parts[1:]:
            got = got + dot(part, weight_ref[rows, cols])
        acc_ref[:, cols] = got


def late_kernel(three, weight_ref, acc_ref, *outs):
    part, rows = pair_part(three.at[0], three.at[1], 3)
    for at in range(0, weight_ref.shape[1], COLS):
        cols = slice(at, at + COLS)
        got = acc_ref[:, cols] + dot(part, weight_ref[rows, cols])
        for e in range(4):
            outs[e][:, cols] = got[e * 32 : e * 32 + 32].astype(outs[e].dtype)


def project(slots, weight):
    width = weight.shape[1]
    keep, came, one, two, three = slots
    acc = pl.pallas_call(
        early_kernel,
        out_shape=jax.ShapeDtypeStruct((C, width), F32),
        in_specs=[vmem()] * 5,
        out_specs=vmem(),
        compiler_params=params(),
        cost_estimate=cost(8e8, 8e6),
        name="early",
    )(keep, came, one, two, weight)
    return pl.pallas_call(
        late_kernel,
        out_shape=[jax.ShapeDtypeStruct((32, width), F32)]
        + [jax.ShapeDtypeStruct((32, width), BF16)] * 3,
        in_specs=[vmem()] * 3,
        out_specs=[vmem()] * 4,
        compiler_params=params(),
        cost_estimate=cost(3e8, 4e6),
        name="late",
    )(three, weight, acc)


def swap(block, d):
    return lax.ppermute(block, "seq", [(s, s ^ d) for s in range(PLANE * PLANES)])


def along_x(keep, came, part=slice(None)):
    pairs = {}
    for dx in (2, 1, 3):
        pairs[dx] = swap(jnp.stack([keep[dx, part], came[dx, part]]), 2 * dx)
    return [keep, came] + [pairs[dx] for dx in (1, 2, 3)]


def exchange(keep, send):
    return along_x(keep, swap(send, 1))


def later_plane(block, distance):
    step = PLANE * distance
    route = [(s, s + step) for s in range(PLANE * PLANES - step)]
    return lax.ppermute(block, "seq", route)


def local(q_delta, k_delta, v_delta, decay, beta, gain, attn_weight, out_weight):
    keep_k, send_k, keep, send = pack(q_delta, k_delta, v_delta, decay, beta)
    slots_k = exchange(keep_k, send_k)
    came = swap(send, 1)
    slots_v = along_x(keep, came, slice(0, C))
    k, mix, inverse, w, tail, reach = key_part(slots_k)
    wu, ab, level = value_part(slots_v, k, inverse, w, tail, reach)
    one = later_plane(ab, 1)
    two = later_plane(ab, 2)
    keep_q, came_q, _ = lax.optimization_barrier((keep, came, ab))
    slots_q = along_x(keep_q, came_q, slice(C, 2 * C))
    no = query(slots_q, k, mix, wu, level)
    before, upto = combine(ab, one, two)
    six = later_plane(upto, 6)
    three = later_plane(upto, 3)
    normed = norm(no, gain[None, :], before, six, three)
    halo = later_plane(normed, 1)
    acc, stat, q2 = own(normed, attn_weight)
    attended = exchange(*halo_part(halo, attn_weight, acc, stat, q2))
    sums = project(attended, out_weight)
    moved = {}
    for d in (2, 1, 3):
        moved[d] = lax.ppermute(sums[d], "heads", [(s, s ^ d) for s in range(4)])
    total = sums[0]
    for d in (1, 3, 2):
        total = total + moved[d].astype(F32)
    return total.astype(BF16)


def solution(mesh):
    placed = (
        P("seq", "heads"),
        P("seq", "heads"),
        P("seq", "heads"),
        P("heads", "seq"),
        P("heads", "seq"),
        P(),
        P("heads", None, None),
        P("heads", None),
    )
    return jax.shard_map(
        local, mesh=mesh, in_specs=placed, out_specs=P(("seq", "heads"), None), check_vma=False
    )
```

```python
import jax
import jax.numpy as jnp
from jax import lax
from jax.experimental import pallas as pl
from jax.experimental.pallas import tpu as pltpu
from jax.sharding import PartitionSpec as P

F32 = jnp.float32
BF16 = jnp.bfloat16
C = 128
PLANE = 8
PLANES = 8
KROWS = C + 16
B = 16
EPS = 1e-06
NEG = -1e30
VMEM_LIMIT = 24 * 1024 * 1024


def params(limit=VMEM_LIMIT):
    return pltpu.CompilerParams(vmem_limit_bytes=limit)


def cost(flops, nbytes, trans=0):
    return pl.CostEstimate(flops=int(flops), bytes_accessed=int(nbytes), transcendentals=int(trans))


def vmem():
    return pl.BlockSpec(memory_space=pltpu.VMEM)


def split(a):
    hi = a.astype(BF16)
    lo = (a - hi.astype(F32)).astype(BF16)
    return hi, lo


def dot(a, b):
    return lax.dot_general(a, b, (((1,), (0,)), ((), ())), preferred_element_type=F32)


def dot_nt(a, b):
    return lax.dot_general(a, b, (((1,), (1,)), ((), ())), preferred_element_type=F32)


def dot_tn(a, b):
    return lax.dot_general(a, b, (((0,), (0,)), ((), ())), preferred_element_type=F32)


def mm(a, b):
    ah, al = split(a)
    bh, bl = split(b)
    left = jnp.concatenate([ah, al], axis=1)
    n = b.shape[1]
    if n > C:
        return dot(left, jnp.concatenate([bh, bh], axis=0)) + dot(ah, bl)
    pair = jnp.concatenate([bh, bl], axis=1)
    out = dot(left, jnp.concatenate([pair, pair], axis=0))
    return out[:, :n] + out[:, n:]


def mm_exact_right(a, b):
    ah, al = split(a)
    return dot(jnp.concatenate([ah, al], axis=1), jnp.concatenate([b, b], axis=0))


def iotas():
    row = lax.broadcasted_iota(jnp.int32, (C, C), 0)
    col = lax.broadcasted_iota(jnp.int32, (C, C), 1)
    return row, col


def pack_kernel(q_ref, k_ref, v_ref, decay_ref, beta_ref, *rest):
    keep_k, send_k, keep, send, gate, raw, sems = rest
    me = lax.axis_index("seq") % PLANE
    copies = [
        pltpu.make_async_copy(decay_ref, raw.at[0], sems.at[24]),
        pltpu.make_async_copy(beta_ref, raw.at[1], sems.at[25]),
    ]
    for d in range(PLANE):
        cols = pl.ds(pl.multiple_of(jnp.bitwise_xor(me, d) * C, C), C)
        out_k, out = (send_k, send) if d % 2 else (keep_k, keep)
        at = d // 2
        copies += [
            pltpu.make_async_copy(k_ref.at[:, cols], out_k.at[at, pl.ds(0, C)], sems.at[3 * d]),
            pltpu.make_async_copy(v_ref.at[:, cols], out.at[at, pl.ds(0, C)], sems.at[3 * d + 1]),
            pltpu.make_async_copy(q_ref.at[:, cols], out.at[at, pl.ds(C, C)], sems.at[3 * d + 2]),
        ]
    for copy in copies:
        copy.start()
    copies[0].wait()
    copies[1].wait()
    for i in range(2):
        x = raw[i]
        for j in range(3):
            part = x.astype(BF16).astype(F32)
            gate[3 * i + j] = part
            x = x - part
    zeros = jnp.zeros((10, C), F32)
    for d in range(PLANE):
        head = jnp.bitwise_xor(me, d)
        rows = [gate[i, pl.ds(head, 1), :] for i in range(6)]
        out = send_k if d % 2 else keep_k
        out[d // 2, C:, :] = jnp.concatenate(rows + [zeros], axis=0).astype(BF16)
    for copy in copies[2:]:
        copy.wait()


def pack(q, k, v, decay, beta):
    any_space = pl.BlockSpec(memory_space=pltpu.HBM)
    first = jax.ShapeDtypeStruct((4, KROWS, C), BF16)
    wide = jax.ShapeDtypeStruct((4, 2 * C, C), BF16)
    return pl.pallas_call(
        pack_kernel,
        out_shape=[first, first, wide, wide],
        in_specs=[any_space] * 5,
        out_specs=[vmem()] * 4,
        scratch_shapes=[
            pltpu.VMEM((6, PLANE, C), F32),
            pltpu.VMEM((2, PLANE, C), F32),
            pltpu.SemaphoreType.DMA((26,)),
        ],
        compiler_params=params(),
        name="pack",
    )(*[pltpu.with_memory_space_constraint(x, pltpu.HBM) for x in (q, k, v, decay, beta)])


def gather_slots(refs, out_ref, part=None):
    keep, came = refs[0], refs[1]
    out_ref[0] = keep[0] if part is None else keep[0, part, :]
    out_ref[1] = came[0] if part is None else came[0, part, :]
    for dx in range(1, 4):
        out_ref[2 * dx] = refs[dx + 1][0]
        out_ref[2 * dx + 1] = refs[dx + 1][1]


def gates(k_ref):
    row, col = iotas()
    pieces = jnp.concatenate([k_ref[d, C:, :] for d in range(PLANE)], axis=0)
    upper = jnp.where(row <= col, 1.0, 0.0).astype(BF16)
    lower = jnp.where(row >= col, 1.0, 0.0).astype(BF16)
    eye = jnp.where(row == col, 1.0, 0.0).astype(BF16)
    along_row = dot(pieces, upper)
    along_col = dot_nt(jnp.concatenate([lower, eye], axis=0), pieces)
    plain = pieces.astype(F32)
    found = []
    for d in range(PLANE):
        o = 16 * d
        g_row = -(along_row[o : o + 1] + along_row[o + 1 : o + 2] + along_row[o + 2 : o + 3])
        b_row = plain[o + 3 : o + 4] + plain[o + 4 : o + 5] + plain[o + 5 : o + 6]
        g_col = -(
            along_col[:C, o : o + 1] + along_col[:C, o + 1 : o + 2] + along_col[:C, o + 2 : o + 3]
        )
        b_col = (
            along_col[C:, o + 3 : o + 4]
            + along_col[C:, o + 4 : o + 5]
            + along_col[C:, o + 5 : o + 6]
        )
        found.append((g_row, b_row, g_col, b_col))
    return found


def base_inverses(packed):
    row, col = iotas()
    high = packed.astype(BF16)
    rest = packed - high.astype(F32)
    mid = rest.astype(BF16)
    low = (rest - mid.astype(F32)).astype(BF16)
    three = jnp.concatenate([high, mid, low], axis=1)
    x = jnp.where(row % B == col % B, 1.0, 0.0)
    for j in range(B - 1):
        pick = jnp.where(row == col - col % B + j, 1.0, 0.0).astype(BF16)
        factor = dot(three, jnp.concatenate([pick, pick, pick], axis=0))
        line = x.reshape(PLANE, B, C)[:, j : j + 1, :]
        x = x - factor * jnp.broadcast_to(line, (PLANE, B, C)).reshape(C, C)
    return x


def after(earlier, later):
    both = mm(later[:, :C], earlier)
    return jnp.concatenate([both[:, :C], both[:, C:] + later[:, C:]], axis=1)


def key_kernel(*refs):
    k_ref, mix_ref, inverse_ref, w_ref, tail_ref, reach_ref = refs[5:11]
    maps = refs[11]
    me = lax.axis_index("seq") % PLANE
    row, col = iotas()
    gather_slots(refs[:5], k_ref)
    every = range(PLANE)
    blocks = (row // B) == (col // B)
    apart = jnp.bitwise_xor(row, col)
    found = gates(k_ref)
    keys = [k_ref[d, 0:C, :] for d in every]
    grams = [dot_nt(k, k) for k in keys]
    diags = [jnp.where(row == col, g, 0.0) for g in grams]
    r_cols = [lax.rsqrt(jnp.sum(g, axis=1, keepdims=True) + EPS) for g in diags]
    r_rows = [lax.rsqrt(jnp.sum(g, axis=0, keepdims=True) + EPS) for g in diags]
    lows, packs = [], []
    for d in every:
        g_row, b_row, g_col, _ = found[d]
        ratio = jnp.where(row >= col, jnp.exp(jnp.minimum(g_col - g_row, 0.0)), 0.0)
        mix = ratio * (b_row * r_rows[d])
        mix_ref[d] = mix
        low = jnp.where(row > col, mix * grams[d] * r_cols[d], 0.0)
        lows.append(low)
        held = jnp.where(blocks, low, 0.0)
        packed = held[0:B]
        for b in range(1, C // B):
            packed = packed + held[B * b : B * b + B]
        packs.append(packed)
    base = base_inverses(jnp.concatenate(packs, axis=0))
    inverse = [
        jnp.where(blocks, jnp.concatenate([base[B * d : B * d + B]] * (C // B), axis=0), 0.0)
        for d in every
    ]
    size = B
    while size < C:
        level = (row > col) & (apart >= size) & (apart < 2 * size)
        half = [mm(x, jnp.where(level, low, 0.0)) for x, low in zip(inverse, lows)]
        inverse = [x - mm(h, x) for x, h in zip(inverse, half)]
        size *= 2
    folded = [inverse[d] * (jnp.exp(found[d][0]) * r_rows[d]) for d in every]
    w = [mm_exact_right(folded[d], keys[d]) for d in every]
    halves = []
    for d in every:
        g_row, _, g_col, b_col = found[d]
        tail = jnp.broadcast_to(jnp.exp(g_row[:, C - 1 : C] - g_col) * b_col * r_cols[d], (C, C))
        inverse_ref[d] = inverse[d]
        w_ref[d] = w[d]
        tail_ref[d] = tail
        halves.append(jnp.concatenate(split(w[d] * tail), axis=0))
    made = [dot_tn(jnp.concatenate([keys[d], keys[d]], axis=0), halves[d]) for d in every]
    for d in every:
        g_end = found[d][0][:, C - 1 : C]
        maps[jnp.bitwise_xor(me, d)] = jnp.where(row == col, jnp.exp(g_end), 0.0) - made[d]
    one = [maps[i] for i in every]
    two = [mm(one[2 * i + 1], one[2 * i]) for i in range(4)]
    four = [mm(two[2 * i + 1], two[2 * i]) for i in range(2)]
    for i, part in enumerate(one + two + four + [mm(four[1], four[0])]):
        reach_ref[i] = part


def value_kernel(*refs):
    k_ref, inverse_ref, w_ref, tail_ref, reach_ref = refs[5:10]
    wu_ref, ab_ref, level_ref, states, v_ref = refs[10:]
    me = lax.axis_index("seq") % PLANE
    gather_slots(refs[:5], v_ref, slice(0, C))
    every = range(PLANE)
    u = [mm_exact_right(inverse_ref[d], v_ref[d]) for d in every]
    halves = []
    for d in every:
        wu_ref[d, :, :C] = w_ref[d]
        wu_ref[d, :, C:] = u[d]
        halves.append(jnp.concatenate(split(u[d] * tail_ref[d]), axis=0))
    keys = [k_ref[d, 0:C, :] for d in every]
    made = [dot_tn(jnp.concatenate([keys[d], keys[d]], axis=0), halves[d]) for d in every]
    for d in every:
        states[jnp.bitwise_xor(me, d)] = made[d]
    one = [states[i] for i in every]
    two = [mm(reach_ref[2 * i + 1], one[2 * i]) + one[2 * i + 1] for i in range(4)]
    four = [mm(reach_ref[8 + 2 * i + 1], two[2 * i]) + two[2 * i + 1] for i in range(2)]
    last = mm(reach_ref[13], four[0]) + four[1]
    ab_ref[:, :C] = reach_ref[14].astype(BF16)
    ab_ref[:, C:] = last.astype(BF16)
    both = ((0, one[0]), (8, two[0]), (2, one[2]), (12, four[0]), (4, one[4]), (10, two[2]), (6, one[6]))
    for i, (at, state) in enumerate(both):
        level_ref[i, :, :C] = reach_ref[at]
        level_ref[i, :, C:] = state


def key_part(slots):
    square = jax.ShapeDtypeStruct((PLANE, C, C), F32)
    return pl.pallas_call(
        key_kernel,
        out_shape=[jax.ShapeDtypeStruct((PLANE, KROWS, C), BF16)]
        + [square] * 4
        + [jax.ShapeDtypeStruct((15, C, C), F32)],
        in_specs=[vmem()] * 5,
        out_specs=[vmem()] * 6,
        scratch_shapes=[pltpu.VMEM((PLANE, C, C), F32)],
        compiler_params=params(),
        cost_estimate=cost(2e9, 4e6),
        name="keys",
    )(*slots)


def value_part(slots, k, inverse, w, tail, reach):
    return pl.pallas_call(
        value_kernel,
        out_shape=[
            jax.ShapeDtypeStruct((PLANE, C, 2 * C), F32),
            jax.ShapeDtypeStruct((C, 2 * C), BF16),
            jax.ShapeDtypeStruct((7, C, 2 * C), F32),
        ],
        in_specs=[vmem()] * 10,
        out_specs=[vmem()] * 3,
        scratch_shapes=[pltpu.VMEM((PLANE, C, C), F32), pltpu.VMEM((PLANE, C, C), BF16)],
        compiler_params=params(),
        cost_estimate=cost(1e9, 4e6),
        name="values",
    )(*slots, k, inverse, w, tail, reach)


def query_kernel(*refs):
    k_ref, mix_ref, wu_ref, level_ref, no_ref, before, q_ref = refs[5:]
    gather_slots(refs[:5], q_ref, slice(C, 2 * C))
    me = lax.axis_index("seq") % PLANE
    row, col = iotas()
    before[0] = jnp.concatenate([jnp.where(row == col, 1.0, 0.0), jnp.zeros((C, C), F32)], axis=1)
    before[1] = level_ref[0]
    before[2] = level_ref[1]
    before[3] = after(level_ref[1], level_ref[2])
    before[4] = level_ref[3]
    before[5] = after(level_ref[3], level_ref[4])
    six = after(level_ref[3], level_ref[5])
    before[6] = six
    before[7] = after(six, level_ref[6])

    every = range(PLANE)
    found = gates(k_ref)
    queries = [q_ref[d] for d in every]
    scored = [dot_nt(queries[d], k_ref[d, 0:C, :]) for d in every]
    r_cols = []
    for q in queries:
        wide = q.astype(F32)
        r_cols.append(lax.rsqrt(jnp.sum(wide * wide, axis=1, keepdims=True) + EPS) * (C**-0.5))
    scored = [scored[d] * r_cols[d] * mix_ref[d] for d in every]
    parts = [mm(scored[d], wu_ref[d]) for d in every]
    reach = [
        queries[d].astype(F32) * (r_cols[d] * jnp.exp(found[d][2])) - parts[d][:, :C]
        for d in every
    ]
    chunks = [jnp.bitwise_xor(me, d) for d in every]
    both = [mm(reach[d], before[chunks[d]]) for d in every]
    for d in every:
        rows = pl.ds(pl.multiple_of(chunks[d] * C, C), C)
        no_ref[rows, :] = jnp.concatenate(
            [both[d][:, :C], both[d][:, C:] + parts[d][:, C:]], axis=1
        )


def query(slots, k, mix, wu, level):
    return pl.pallas_call(
        query_kernel,
        out_shape=jax.ShapeDtypeStruct((PLANE * C, 2 * C), F32),
        in_specs=[vmem()] * 9,
        out_specs=vmem(),
        scratch_shapes=[
            pltpu.VMEM((PLANE, C, 2 * C), F32),
            pltpu.VMEM((PLANE, C, C), BF16),
        ],
        compiler_params=params(),
        cost_estimate=cost(1e9, 4e6),
        name="query",
    )(*slots, k, mix, wu, level)


def times(a, x):
    hi, lo = split(x)
    return dot(jnp.concatenate([a, a], axis=1), jnp.concatenate([hi, lo], axis=0))


def combine_kernel(own_ref, one_ref, two_ref, before_ref, upto_ref):
    a_one, a_own = one_ref[:, :C], own_ref[:, :C]
    reach = dot(a_one, two_ref[:, :C])
    state = one_ref[:, C:].astype(F32) + dot(a_one, two_ref[:, C:])
    before_ref[:, :C] = reach
    before_ref[:, C:] = state
    upto_ref[:, :C] = times(a_own, reach).astype(BF16)
    upto_ref[:, C:] = (own_ref[:, C:].astype(F32) + times(a_own, state)).astype(BF16)


def combine(own_map, one, two):
    return pl.pallas_call(
        combine_kernel,
        out_shape=[
            jax.ShapeDtypeStruct((C, 2 * C), F32),
            jax.ShapeDtypeStruct((C, 2 * C), BF16),
        ],
        in_specs=[vmem()] * 3,
        out_specs=[vmem()] * 2,
        compiler_params=params(),
        name="combine",
    )(own_map, one, two)


def norm_kernel(no_ref, gain_ref, before_ref, six_ref, three_ref, normed_ref):
    state = three_ref[:, C:].astype(F32) + dot(three_ref[:, :C], six_ref[:, C:])
    state = before_ref[:, C:] + mm(before_ref[:, :C], state)
    out = mm(no_ref[:, :C], state) + no_ref[:, C:]
    scale = lax.rsqrt(jnp.mean(out * out, axis=1, keepdims=True) + EPS)
    normed_ref[...] = (out * scale * gain_ref[...]).astype(BF16)


def norm(no, gain, before, six, three):
    return pl.pallas_call(
        norm_kernel,
        out_shape=jax.ShapeDtypeStruct((PLANE * C, C), BF16),
        in_specs=[vmem()] * 5,
        out_specs=vmem(),
        compiler_params=params(),
        cost_estimate=cost(2e8, 2e6),
        name="norm",
    )(no, gain, before, six, three)


QB = 256
SCALE = C**-0.5 * 1.4426950408889634


def squares():
    row = lax.broadcasted_iota(jnp.int32, (QB, QB), 0)
    col = lax.broadcasted_iota(jnp.int32, (QB, QB), 1)
    return row, col


def row_max(parts):
    top = jnp.max(parts[0], axis=1, keepdims=True)
    for part in parts[1:]:
        top = jnp.maximum(top, jnp.max(part, axis=1, keepdims=True))
    return top


def row_sum(parts):
    total = jnp.sum(parts[0], axis=1, keepdims=True)
    for part in parts[1:]:
        total = total + jnp.sum(part, axis=1, keepdims=True)
    return total


def weighted(parts, values):
    out = dot(parts[0].astype(BF16), values[0])
    for part, value in zip(parts[1:], values[1:]):
        out = out + dot(part.astype(BF16), value)
    return out


def tiled(column, like):
    return jnp.concatenate([column] * (like.shape[1] // C), axis=1)


def own_kernel(normed_ref, weight_ref, acc_ref, stat_ref, q2_ref):
    me = lax.axis_index("seq") % PLANE
    proj = dot(normed_ref[...], weight_ref[me]).astype(BF16)
    q2_ref[...] = proj[:, :C]
    row, col = squares()
    starts = range(0, PLANE * C, QB)
    spans = [[(at, at + QB)] + ([(0, at)] if at else []) for at in starts]
    scores = [
        [dot_nt(proj[at : at + QB, :C], proj[a:b, C : 2 * C]) for a, b in span]
        for at, span in zip(starts, spans)
    ]
    scores = [[jnp.where(col <= row, parts[0], NEG)] + parts[1:] for parts in scores]
    tops = [row_max(parts) for parts in scores]
    raised = [[jnp.exp2((s - top) * SCALE) for s in parts] for parts, top in zip(scores, tops)]
    for i, at in enumerate(starts):
        rows = slice(at, at + QB)
        acc_ref[rows, :] = weighted(raised[i], [proj[a:b, 2 * C :] for a, b in spans[i]])
        stat_ref[0, rows, :] = jnp.broadcast_to(tops[i], (QB, C))
        stat_ref[1, rows, :] = jnp.broadcast_to(row_sum(raised[i]), (QB, C))


def own(normed, weight):
    n = PLANE * C
    return pl.pallas_call(
        own_kernel,
        out_shape=[
            jax.ShapeDtypeStruct((n, C), F32),
            jax.ShapeDtypeStruct((2, n, C), F32),
            jax.ShapeDtypeStruct((n, C), BF16),
        ],
        in_specs=[vmem()] * 2,
        out_specs=[vmem()] * 3,
        compiler_params=params(),
        cost_estimate=cost(1e9, 3e6, 6e5),
        name="own",
    )(normed, weight)


def halo_kernel(halo_ref, weight_ref, acc_ref, stat_ref, q2_ref, *refs):
    keep, send, attended = refs
    place = lax.axis_index("seq")
    me, plane = place % PLANE, place // PLANE
    proj = dot(halo_ref[...], weight_ref[me, :, C:]).astype(BF16)
    n = PLANE * C
    row, col = squares()
    starts = range(0, n, QB)
    spans = [[(at, at + QB)] + ([(at + QB, n)] if at + QB < n else []) for at in starts]
    floor = jnp.where(plane > 0, 0.0, NEG)
    scores = [
        [dot_nt(q2_ref[at : at + QB, :], proj[a:b, :C]) for a, b in span]
        for at, span in zip(starts, spans)
    ]
    scores = [[jnp.where(col > row, parts[0], NEG)] + parts[1:] for parts in scores]
    before = [stat_ref[0, at : at + QB, :] for at in starts]
    tops = [jnp.maximum(row_max(parts) + floor, old) for parts, old in zip(scores, before)]
    raised = [
        [jnp.exp2((s - tiled(top - floor, s)) * SCALE) for s in parts]
        for parts, top in zip(scores, tops)
    ]
    fades = [jnp.exp2((old - top) * SCALE) for old, top in zip(before, tops)]
    for i, at in enumerate(starts):
        rows = slice(at, at + QB)
        total = row_sum(raised[i]) + fades[i] * stat_ref[1, rows, :]
        acc = acc_ref[rows, :] * fades[i] + weighted(
            raised[i], [proj[a:b, C:] for a, b in spans[i]]
        )
        attended[rows, :] = (acc / total).astype(BF16)
    for d in range(PLANE):
        chunk = jnp.bitwise_xor(me, d)
        out = send if d % 2 else keep
        out[d // 2] = attended[pl.ds(pl.multiple_of(chunk * C, C), C), :]


def halo_part(halo, weight, acc, stat, q2):
    n = PLANE * C
    return pl.pallas_call(
        halo_kernel,
        out_shape=[jax.ShapeDtypeStruct((4, C, C), BF16)] * 2,
        in_specs=[vmem()] * 5,
        out_specs=[vmem()] * 2,
        scratch_shapes=[pltpu.VMEM((n, C), BF16)],
        compiler_params=params(),
        cost_estimate=cost(1e9, 3e6, 6e5),
        name="halo",
    )(halo, weight, acc, stat, q2)


COLS = 1024


def pair_part(first, second, dx):
    core, mine = lax.axis_index("seq") % 2, lax.axis_index("heads")
    rows = [pl.ds(pl.multiple_of(lax.rem(mine + e, 4) * 32, 32), 32) for e in range(4)]
    one = jnp.concatenate([first[r, :] for r in rows], axis=0)
    two = jnp.concatenate([second[r, :] for r in rows], axis=0)
    swapped = core > 0
    left = jnp.where(swapped, two.astype(F32), one.astype(F32)).astype(BF16)
    right = jnp.where(swapped, one.astype(F32), two.astype(F32)).astype(BF16)
    chip = lax.axis_index("seq") % PLANE // 2
    at = pl.multiple_of(jnp.bitwise_xor(chip, dx) * 2 * C, 2 * C)
    return jnp.concatenate([left, right], axis=1), pl.ds(at, 2 * C)


def early_kernel(keep, came, one, two, weight_ref, acc_ref):
    parts = [
        pair_part(keep.at[0], came.at[0], 0),
        pair_part(two.at[0], two.at[1], 2),
        pair_part(one.at[0], one.at[1], 1),
    ]
    for at in range(0, weight_ref.shape[1], COLS):
        cols = slice(at, at + COLS)
        got = dot(parts[0][0], weight_ref[parts[0][1], cols])
        for part, rows in parts[1:]:
            got = got + dot(part, weight_ref[rows, cols])
        acc_ref[:, cols] = got


def late_kernel(three, weight_ref, acc_ref, own_ref, right_ref, left_ref, *outs):
    part, rows = pair_part(three.at[0], three.at[1], 3)
    far_right, far_left, plain_right, plain_left = outs
    half = weight_ref.shape[1] // 2
    for at in range(0, 2 * half, COLS):
        cols = slice(at, at + COLS)
        got = acc_ref[:, cols] + dot(part, weight_ref[rows, cols])
        own_ref[:, cols] = got[0:32]
        if at < half:
            right_ref[:, cols] = got[32:64]
            far_right[:, cols] = got[64:96].astype(BF16)
            plain_left[:, cols] = got[96:128].astype(BF16)
        else:
            cols = slice(at - half, at - half + COLS)
            plain_right[:, cols] = got[32:64].astype(BF16)
            far_left[:, cols] = got[64:96].astype(BF16)
            left_ref[:, cols] = got[96:128]


def project(slots, weight):
    width = weight.shape[1]
    keep, came, one, two, three = slots
    acc = pl.pallas_call(
        early_kernel,
        out_shape=jax.ShapeDtypeStruct((C, width), F32),
        in_specs=[vmem()] * 5,
        out_specs=vmem(),
        compiler_params=params(),
        cost_estimate=cost(8e8, 8e6),
        name="early",
    )(keep, came, one, two, weight)
    return pl.pallas_call(
        late_kernel,
        out_shape=[jax.ShapeDtypeStruct((32, width), F32)]
        + [jax.ShapeDtypeStruct((32, width // 2), F32)] * 2
        + [jax.ShapeDtypeStruct((32, width // 2), BF16)] * 4,
        in_specs=[vmem()] * 3,
        out_specs=[vmem()] * 7,
        compiler_params=params(),
        cost_estimate=cost(3e8, 4e6),
        name="late",
    )(three, weight, acc)


def swap(block, d):
    return lax.ppermute(block, "seq", [(s, s ^ d) for s in range(PLANE * PLANES)])


def along_x(keep, came, part=slice(None)):
    pairs = {}
    for dx in (2, 1, 3):
        pairs[dx] = swap(jnp.stack([keep[dx, part], came[dx, part]]), 2 * dx)
    return [keep, came] + [pairs[dx] for dx in (1, 2, 3)]


def exchange(keep, send):
    return along_x(keep, swap(send, 1))


def later_plane(block, distance):
    step = PLANE * distance
    route = [(s, s + step) for s in range(PLANE * PLANES - step)]
    return lax.ppermute(block, "seq", route)


def local(q_delta, k_delta, v_delta, decay, beta, gain, attn_weight, out_weight):
    keep_k, send_k, keep, send = pack(q_delta, k_delta, v_delta, decay, beta)
    slots_k = exchange(keep_k, send_k)
    came = swap(send, 1)
    slots_v = along_x(keep, came, slice(0, C))
    k, mix, inverse, w, tail, reach = key_part(slots_k)
    wu, ab, level = value_part(slots_v, k, inverse, w, tail, reach)
    one = later_plane(ab, 1)
    two = later_plane(ab, 2)
    keep_q, came_q, _ = lax.optimization_barrier((keep, came, ab))
    slots_q = along_x(keep_q, came_q, slice(C, 2 * C))
    no = query(slots_q, k, mix, wu, level)
    before, upto = combine(ab, one, two)
    six = later_plane(upto, 6)
    three = later_plane(upto, 3)
    normed = norm(no, gain[None, :], before, six, three)
    halo = later_plane(normed, 1)
    acc, stat, q2 = own(normed, attn_weight)
    attended = exchange(*halo_part(halo, attn_weight, acc, stat, q2))
    return sum_over_heads(*project(attended, out_weight))


def sum_over_heads(own_sum, right, left, far_right, far_left, plain_right, plain_left):
    def turn(block, step):
        return lax.ppermute(block, "heads", [(s, (s + step) % 4) for s in range(4)])

    passed_right = turn(far_right, 1)
    passed_left = turn(far_left, 3)
    plain_right = turn(plain_right, 1)
    plain_left = turn(plain_left, 3)
    right = turn((right + passed_right.astype(F32)).astype(BF16), 1)
    left = turn((left + passed_left.astype(F32)).astype(BF16), 3)
    others = jnp.concatenate(
        [right.astype(F32) + plain_left.astype(F32), left.astype(F32) + plain_right.astype(F32)],
        axis=1,
    )
    return (own_sum + others).astype(BF16)


def solution(mesh):
    placed = (
        P("seq", "heads"),
        P("seq", "heads"),
        P("seq", "heads"),
        P("heads", "seq"),
        P("heads", "seq"),
        P(),
        P("heads", None, None),
        P("heads", None),
    )
    return jax.shard_map(
        local, mesh=mesh, in_specs=placed, out_specs=P(("seq", "heads"), None), check_vma=False
    )
```

```python
import jax
import jax.numpy as jnp
from jax import lax
from jax.experimental import pallas as pl
from jax.experimental.pallas import tpu as pltpu
from jax.sharding import PartitionSpec as P

F32 = jnp.float32
BF16 = jnp.bfloat16
C = 128
PLANE = 8
PLANES = 8
KROWS = C + 16
B = 16
EPS = 1e-06
NEG = -1e30
VMEM_LIMIT = 24 * 1024 * 1024


def params(limit=VMEM_LIMIT):
    return pltpu.CompilerParams(vmem_limit_bytes=limit)


def cost(flops, nbytes, trans=0):
    return pl.CostEstimate(flops=int(flops), bytes_accessed=int(nbytes), transcendentals=int(trans))


def vmem():
    return pl.BlockSpec(memory_space=pltpu.VMEM)


def split(a):
    hi = a.astype(BF16)
    lo = (a - hi.astype(F32)).astype(BF16)
    return hi, lo


def dot(a, b):
    return lax.dot_general(a, b, (((1,), (0,)), ((), ())), preferred_element_type=F32)


def dot_nt(a, b):
    return lax.dot_general(a, b, (((1,), (1,)), ((), ())), preferred_element_type=F32)


def dot_tn(a, b):
    return lax.dot_general(a, b, (((0,), (0,)), ((), ())), preferred_element_type=F32)


def mm(a, b):
    ah, al = split(a)
    bh, bl = split(b)
    left = jnp.concatenate([ah, al], axis=1)
    n = b.shape[1]
    if n > C:
        return dot(left, jnp.concatenate([bh, bh], axis=0)) + dot(ah, bl)
    pair = jnp.concatenate([bh, bl], axis=1)
    out = dot(left, jnp.concatenate([pair, pair], axis=0))
    return out[:, :n] + out[:, n:]


def mm_exact_right(a, b):
    ah, al = split(a)
    return dot(jnp.concatenate([ah, al], axis=1), jnp.concatenate([b, b], axis=0))


def iotas():
    row = lax.broadcasted_iota(jnp.int32, (C, C), 0)
    col = lax.broadcasted_iota(jnp.int32, (C, C), 1)
    return row, col


def head_columns(me, d):
    return pl.ds(pl.multiple_of(jnp.bitwise_xor(me, d) * C, C), C)


def pack_keys_kernel(k_ref, decay_ref, beta_ref, keep, send, gate, raw, sems):
    me = lax.axis_index("seq") % PLANE
    copies = [
        pltpu.make_async_copy(decay_ref, raw.at[0], sems.at[8]),
        pltpu.make_async_copy(beta_ref, raw.at[1], sems.at[9]),
    ]
    for d in range(PLANE):
        out = send if d % 2 else keep
        into = out.at[d // 2, pl.ds(0, C)]
        copies.append(pltpu.make_async_copy(k_ref.at[:, head_columns(me, d)], into, sems.at[d]))
    for copy in copies:
        copy.start()
    copies[0].wait()
    copies[1].wait()
    for i in range(2):
        x = raw[i]
        for j in range(3):
            part = x.astype(BF16).astype(F32)
            gate[3 * i + j] = part
            x = x - part
    zeros = jnp.zeros((10, C), F32)
    for d in range(PLANE):
        head = jnp.bitwise_xor(me, d)
        rows = [gate[i, pl.ds(head, 1), :] for i in range(6)]
        out = send if d % 2 else keep
        out[d // 2, C:, :] = jnp.concatenate(rows + [zeros], axis=0).astype(BF16)
    for copy in copies[2:]:
        copy.wait()


def pack_rest_kernel(q_ref, v_ref, keep, send, sems):
    me = lax.axis_index("seq") % PLANE
    copies = []
    for d in range(PLANE):
        out = send if d % 2 else keep
        for part, ref in enumerate((v_ref, q_ref)):
            into = out.at[d // 2, pl.ds(part * C, C)]
            source = ref.at[:, head_columns(me, d)]
            copies.append(pltpu.make_async_copy(source, into, sems.at[2 * d + part]))
    for copy in copies:
        copy.start()
    for copy in copies:
        copy.wait()


def in_hbm(*arrays):
    return [pltpu.with_memory_space_constraint(x, pltpu.HBM) for x in arrays]


def pack_keys(k, decay, beta):
    return pl.pallas_call(
        pack_keys_kernel,
        out_shape=[jax.ShapeDtypeStruct((4, KROWS, C), BF16)] * 2,
        in_specs=[pl.BlockSpec(memory_space=pltpu.HBM)] * 3,
        out_specs=[vmem()] * 2,
        scratch_shapes=[
            pltpu.VMEM((6, PLANE, C), F32),
            pltpu.VMEM((2, PLANE, C), F32),
            pltpu.SemaphoreType.DMA((10,)),
        ],
        compiler_params=params(),
        name="pack_keys",
    )(*in_hbm(k, decay, beta))


def pack_rest(q, v):
    return pl.pallas_call(
        pack_rest_kernel,
        out_shape=[jax.ShapeDtypeStruct((4, 2 * C, C), BF16)] * 2,
        in_specs=[pl.BlockSpec(memory_space=pltpu.HBM)] * 2,
        out_specs=[vmem()] * 2,
        scratch_shapes=[pltpu.SemaphoreType.DMA((16,))],
        compiler_params=params(),
        name="pack_rest",
    )(*in_hbm(q, v))


def gather_slots(refs, out_ref, part=None):
    keep, came = refs[0], refs[1]
    out_ref[0] = keep[0] if part is None else keep[0, part, :]
    out_ref[1] = came[0] if part is None else came[0, part, :]
    for dx in range(1, 4):
        out_ref[2 * dx] = refs[dx + 1][0]
        out_ref[2 * dx + 1] = refs[dx + 1][1]


def gates(k_ref):
    row, col = iotas()
    pieces = jnp.concatenate([k_ref[d, C:, :] for d in range(PLANE)], axis=0)
    upper = jnp.where(row <= col, 1.0, 0.0).astype(BF16)
    lower = jnp.where(row >= col, 1.0, 0.0).astype(BF16)
    eye = jnp.where(row == col, 1.0, 0.0).astype(BF16)
    along_row = dot(pieces, upper)
    along_col = dot_nt(jnp.concatenate([lower, eye], axis=0), pieces)
    plain = pieces.astype(F32)
    found = []
    for d in range(PLANE):
        o = 16 * d
        g_row = -(along_row[o : o + 1] + along_row[o + 1 : o + 2] + along_row[o + 2 : o + 3])
        b_row = plain[o + 3 : o + 4] + plain[o + 4 : o + 5] + plain[o + 5 : o + 6]
        g_col = -(
            along_col[:C, o : o + 1] + along_col[:C, o + 1 : o + 2] + along_col[:C, o + 2 : o + 3]
        )
        b_col = (
            along_col[C:, o + 3 : o + 4]
            + along_col[C:, o + 4 : o + 5]
            + along_col[C:, o + 5 : o + 6]
        )
        found.append((g_row, b_row, g_col, b_col))
    return found


def base_inverses(packed):
    row, col = iotas()
    high = packed.astype(BF16)
    rest = packed - high.astype(F32)
    mid = rest.astype(BF16)
    low = (rest - mid.astype(F32)).astype(BF16)
    three = jnp.concatenate([high, mid, low], axis=1)
    x = jnp.where(row % B == col % B, 1.0, 0.0)
    for j in range(B - 1):
        pick = jnp.where(row == col - col % B + j, 1.0, 0.0).astype(BF16)
        factor = dot(three, jnp.concatenate([pick, pick, pick], axis=0))
        line = x.reshape(PLANE, B, C)[:, j : j + 1, :]
        x = x - factor * jnp.broadcast_to(line, (PLANE, B, C)).reshape(C, C)
    return x


def after(earlier, later):
    both = mm(later[:, :C], earlier)
    return jnp.concatenate([both[:, :C], both[:, C:] + later[:, C:]], axis=1)


def key_kernel(*refs):
    k_ref, mix_ref, inverse_ref, w_ref, tail_ref, reach_ref = refs[5:]
    me = lax.axis_index("seq") % PLANE
    row, col = iotas()
    gather_slots(refs[:5], k_ref)
    every = range(PLANE)
    blocks = (row // B) == (col // B)
    apart = jnp.bitwise_xor(row, col)
    found = gates(k_ref)
    keys = [k_ref[d, 0:C, :] for d in every]
    grams = [dot_nt(k, k) for k in keys]
    diags = [jnp.where(row == col, g, 0.0) for g in grams]
    r_cols = [lax.rsqrt(jnp.sum(g, axis=1, keepdims=True) + EPS) for g in diags]
    r_rows = [lax.rsqrt(jnp.sum(g, axis=0, keepdims=True) + EPS) for g in diags]
    lows, packs = [], []
    for d in every:
        g_row, b_row, g_col, _ = found[d]
        ratio = jnp.where(row >= col, jnp.exp(jnp.minimum(g_col - g_row, 0.0)), 0.0)
        mix = ratio * (b_row * r_rows[d])
        mix_ref[d] = mix
        low = jnp.where(row > col, mix * grams[d] * r_cols[d], 0.0)
        lows.append(low)
        held = jnp.where(blocks, low, 0.0)
        packed = held[0:B]
        for b in range(1, C // B):
            packed = packed + held[B * b : B * b + B]
        packs.append(packed)
    base = base_inverses(jnp.concatenate(packs, axis=0))
    inverse = [
        jnp.where(blocks, jnp.concatenate([base[B * d : B * d + B]] * (C // B), axis=0), 0.0)
        for d in every
    ]
    size = B
    while size < C:
        level = (row > col) & (apart >= size) & (apart < 2 * size)
        half = [mm(x, jnp.where(level, low, 0.0)) for x, low in zip(inverse, lows)]
        inverse = [x - mm(h, x) for x, h in zip(inverse, half)]
        size *= 2
    folded = [inverse[d] * (jnp.exp(found[d][0]) * r_rows[d]) for d in every]
    w = [mm_exact_right(folded[d], keys[d]) for d in every]
    halves = []
    for d in every:
        g_row, _, g_col, b_col = found[d]
        tail = jnp.broadcast_to(jnp.exp(g_row[:, C - 1 : C] - g_col) * b_col * r_cols[d], (C, C))
        inverse_ref[d] = inverse[d]
        w_ref[d] = w[d]
        tail_ref[d] = tail
        halves.append(jnp.concatenate(split(w[d] * tail), axis=0))
    made = [dot_tn(jnp.concatenate([keys[d], keys[d]], axis=0), halves[d]) for d in every]
    for d in every:
        g_end = found[d][0][:, C - 1 : C]
        reach_ref[jnp.bitwise_xor(me, d)] = jnp.where(row == col, jnp.exp(g_end), 0.0) - made[d]


def value_kernel(*refs):
    k_ref, inverse_ref, w_ref, tail_ref, reach_ref = refs[5:10]
    wu_ref, ab_ref, level_ref, states, v_ref = refs[10:]
    me = lax.axis_index("seq") % PLANE
    gather_slots(refs[:5], v_ref, slice(0, C))
    every = range(PLANE)
    reach = [reach_ref[i] for i in every]
    u = [mm_exact_right(inverse_ref[d], v_ref[d]) for d in every]
    reach_two = [mm(reach[2 * i + 1], reach[2 * i]) for i in range(4)]
    halves = []
    for d in every:
        wu_ref[d, :, :C] = w_ref[d]
        wu_ref[d, :, C:] = u[d]
        halves.append(jnp.concatenate(split(u[d] * tail_ref[d]), axis=0))
    keys = [k_ref[d, 0:C, :] for d in every]
    made = [dot_tn(jnp.concatenate([keys[d], keys[d]], axis=0), halves[d]) for d in every]
    reach_four = [mm(reach_two[2 * i + 1], reach_two[2 * i]) for i in range(2)]
    for d in every:
        states[jnp.bitwise_xor(me, d)] = made[d]
    one = [states[i] for i in every]
    two = [mm(reach[2 * i + 1], one[2 * i]) + one[2 * i + 1] for i in range(4)]
    ab_ref[:, :C] = mm(reach_four[1], reach_four[0]).astype(BF16)
    four = [mm(reach_two[2 * i + 1], two[2 * i]) + two[2 * i + 1] for i in range(2)]
    ab_ref[:, C:] = (mm(reach_four[1], four[0]) + four[1]).astype(BF16)
    levels = [(reach[0], one[0]), (reach_two[0], two[0]), (reach[2], one[2])]
    levels += [(reach_four[0], four[0]), (reach[4], one[4]), (reach_two[2], two[2])]
    for i, (across, state) in enumerate(levels + [(reach[6], one[6])]):
        level_ref[i, :, :C] = across
        level_ref[i, :, C:] = state


def key_part(slots):
    square = jax.ShapeDtypeStruct((PLANE, C, C), F32)
    return pl.pallas_call(
        key_kernel,
        out_shape=[jax.ShapeDtypeStruct((PLANE, KROWS, C), BF16)]
        + [square] * 5,
        in_specs=[vmem()] * 5,
        out_specs=[vmem()] * 6,
        compiler_params=params(),
        cost_estimate=cost(2e9, 4e6),
        name="keys",
    )(*slots)


def value_part(slots, k, inverse, w, tail, reach):
    return pl.pallas_call(
        value_kernel,
        out_shape=[
            jax.ShapeDtypeStruct((PLANE, C, 2 * C), F32),
            jax.ShapeDtypeStruct((C, 2 * C), BF16),
            jax.ShapeDtypeStruct((7, C, 2 * C), F32),
        ],
        in_specs=[vmem()] * 10,
        out_specs=[vmem()] * 3,
        scratch_shapes=[pltpu.VMEM((PLANE, C, C), F32), pltpu.VMEM((PLANE, C, C), BF16)],
        compiler_params=params(),
        cost_estimate=cost(1e9, 4e6),
        name="values",
    )(*slots, k, inverse, w, tail, reach)


def query_kernel(*refs):
    k_ref, mix_ref, wu_ref, level_ref, no_ref, before, q_ref = refs[5:]
    gather_slots(refs[:5], q_ref, slice(C, 2 * C))
    me = lax.axis_index("seq") % PLANE
    row, col = iotas()
    before[0] = jnp.concatenate([jnp.where(row == col, 1.0, 0.0), jnp.zeros((C, C), F32)], axis=1)
    before[1] = level_ref[0]
    before[2] = level_ref[1]
    before[3] = after(level_ref[1], level_ref[2])
    before[4] = level_ref[3]
    before[5] = after(level_ref[3], level_ref[4])
    six = after(level_ref[3], level_ref[5])
    before[6] = six
    before[7] = after(six, level_ref[6])

    every = range(PLANE)
    found = gates(k_ref)
    queries = [q_ref[d] for d in every]
    scored = [dot_nt(queries[d], k_ref[d, 0:C, :]) for d in every]
    r_cols = []
    for q in queries:
        wide = q.astype(F32)
        r_cols.append(lax.rsqrt(jnp.sum(wide * wide, axis=1, keepdims=True) + EPS) * (C**-0.5))
    scored = [scored[d] * r_cols[d] * mix_ref[d] for d in every]
    parts = [mm(scored[d], wu_ref[d]) for d in every]
    reach = [
        queries[d].astype(F32) * (r_cols[d] * jnp.exp(found[d][2])) - parts[d][:, :C]
        for d in every
    ]
    chunks = [jnp.bitwise_xor(me, d) for d in every]
    both = [mm(reach[d], before[chunks[d]]) for d in every]
    for d in every:
        rows = pl.ds(pl.multiple_of(chunks[d] * C, C), C)
        no_ref[rows, :] = jnp.concatenate(
            [both[d][:, :C], both[d][:, C:] + parts[d][:, C:]], axis=1
        )


def query(slots, k, mix, wu, level):
    return pl.pallas_call(
        query_kernel,
        out_shape=jax.ShapeDtypeStruct((PLANE * C, 2 * C), F32),
        in_specs=[vmem()] * 9,
        out_specs=vmem(),
        scratch_shapes=[
            pltpu.VMEM((PLANE, C, 2 * C), F32),
            pltpu.VMEM((PLANE, C, C), BF16),
        ],
        compiler_params=params(),
        cost_estimate=cost(1e9, 4e6),
        name="query",
    )(*slots, k, mix, wu, level)


def times(a, x):
    hi, lo = split(x)
    return dot(jnp.concatenate([a, a], axis=1), jnp.concatenate([hi, lo], axis=0))


def combine_kernel(own_ref, one_ref, two_ref, before_ref, upto_ref):
    a_one, a_own = one_ref[:, :C], own_ref[:, :C]
    reach = dot(a_one, two_ref[:, :C])
    state = one_ref[:, C:].astype(F32) + dot(a_one, two_ref[:, C:])
    before_ref[:, :C] = reach
    before_ref[:, C:] = state
    upto_ref[:, :C] = times(a_own, reach).astype(BF16)
    upto_ref[:, C:] = (own_ref[:, C:].astype(F32) + times(a_own, state)).astype(BF16)


def combine(own_map, one, two):
    return pl.pallas_call(
        combine_kernel,
        out_shape=[
            jax.ShapeDtypeStruct((C, 2 * C), F32),
            jax.ShapeDtypeStruct((C, 2 * C), BF16),
        ],
        in_specs=[vmem()] * 3,
        out_specs=[vmem()] * 2,
        compiler_params=params(),
        name="combine",
    )(own_map, one, two)


def norm_kernel(no_ref, gain_ref, before_ref, six_ref, three_ref, normed_ref):
    state = three_ref[:, C:].astype(F32) + dot(three_ref[:, :C], six_ref[:, C:])
    state = before_ref[:, C:] + mm(before_ref[:, :C], state)
    out = mm(no_ref[:, :C], state) + no_ref[:, C:]
    scale = lax.rsqrt(jnp.mean(out * out, axis=1, keepdims=True) + EPS)
    normed_ref[...] = (out * scale * gain_ref[...]).astype(BF16)


def norm(no, gain, before, six, three):
    return pl.pallas_call(
        norm_kernel,
        out_shape=jax.ShapeDtypeStruct((PLANE * C, C), BF16),
        in_specs=[vmem()] * 5,
        out_specs=vmem(),
        compiler_params=params(),
        cost_estimate=cost(2e8, 2e6),
        name="norm",
    )(no, gain, before, six, three)


QB = 256
SCALE = C**-0.5 * 1.4426950408889634


def squares():
    row = lax.broadcasted_iota(jnp.int32, (QB, QB), 0)
    col = lax.broadcasted_iota(jnp.int32, (QB, QB), 1)
    return row, col


def row_max(parts):
    top = jnp.max(parts[0], axis=1, keepdims=True)
    for part in parts[1:]:
        top = jnp.maximum(top, jnp.max(part, axis=1, keepdims=True))
    return top


def row_sum(parts):
    total = jnp.sum(parts[0], axis=1, keepdims=True)
    for part in parts[1:]:
        total = total + jnp.sum(part, axis=1, keepdims=True)
    return total


def weighted(parts, values):
    out = dot(parts[0].astype(BF16), values[0])
    for part, value in zip(parts[1:], values[1:]):
        out = out + dot(part.astype(BF16), value)
    return out


def tiled(column, like):
    return jnp.concatenate([column] * (like.shape[1] // C), axis=1)


def own_kernel(normed_ref, weight_ref, acc_ref, stat_ref, q2_ref):
    me = lax.axis_index("seq") % PLANE
    proj = dot(normed_ref[...], weight_ref[me]).astype(BF16)
    q2_ref[...] = proj[:, :C]
    row, col = squares()
    starts = range(0, PLANE * C, QB)
    spans = [[(at, at + QB)] + ([(0, at)] if at else []) for at in starts]
    scores = [
        [dot_nt(proj[at : at + QB, :C], proj[a:b, C : 2 * C]) for a, b in span]
        for at, span in zip(starts, spans)
    ]
    scores = [[jnp.where(col <= row, parts[0], NEG)] + parts[1:] for parts in scores]
    tops = [row_max(parts) for parts in scores]
    raised = [[jnp.exp2((s - top) * SCALE) for s in parts] for parts, top in zip(scores, tops)]
    for i, at in enumerate(starts):
        rows = slice(at, at + QB)
        acc_ref[rows, :] = weighted(raised[i], [proj[a:b, 2 * C :] for a, b in spans[i]])
        stat_ref[0, rows, :] = jnp.broadcast_to(tops[i], (QB, C))
        stat_ref[1, rows, :] = jnp.broadcast_to(row_sum(raised[i]), (QB, C))


def own(normed, weight):
    n = PLANE * C
    return pl.pallas_call(
        own_kernel,
        out_shape=[
            jax.ShapeDtypeStruct((n, C), F32),
            jax.ShapeDtypeStruct((2, n, C), F32),
            jax.ShapeDtypeStruct((n, C), BF16),
        ],
        in_specs=[vmem()] * 2,
        out_specs=[vmem()] * 3,
        compiler_params=params(),
        cost_estimate=cost(1e9, 3e6, 6e5),
        name="own",
    )(normed, weight)


def halo_kernel(halo_ref, weight_ref, acc_ref, stat_ref, q2_ref, *refs):
    outs, attended = refs[:4], refs[4]
    place = lax.axis_index("seq")
    me, plane = place % PLANE, place // PLANE
    proj = dot(halo_ref[...], weight_ref[me, :, C:]).astype(BF16)
    n = PLANE * C
    row, col = squares()
    starts = range(0, n, QB)
    spans = [[(at, at + QB)] + ([(at + QB, n)] if at + QB < n else []) for at in starts]
    floor = jnp.where(plane > 0, 0.0, NEG)
    scores = [
        [dot_nt(q2_ref[at : at + QB, :], proj[a:b, :C]) for a, b in span]
        for at, span in zip(starts, spans)
    ]
    scores = [[jnp.where(col > row, parts[0], NEG)] + parts[1:] for parts in scores]
    before = [stat_ref[0, at : at + QB, :] for at in starts]
    tops = [jnp.maximum(row_max(parts) + floor, old) for parts, old in zip(scores, before)]
    raised = [
        [jnp.exp2((s - tiled(top - floor, s)) * SCALE) for s in parts]
        for parts, top in zip(scores, tops)
    ]
    fades = [jnp.exp2((old - top) * SCALE) for old, top in zip(before, tops)]
    for i, at in enumerate(starts):
        rows = slice(at, at + QB)
        total = row_sum(raised[i]) + fades[i] * stat_ref[1, rows, :]
        acc = acc_ref[rows, :] * fades[i] + weighted(
            raised[i], [proj[a:b, C:] for a, b in spans[i]]
        )
        attended[rows, :] = (acc / total).astype(BF16)
    for d in range(PLANE):
        chunk = jnp.bitwise_xor(me, d)
        outs[d // 2][d % 2] = attended[pl.ds(pl.multiple_of(chunk * C, C), C), :]


def halo_part(halo, weight, acc, stat, q2):
    n = PLANE * C
    return pl.pallas_call(
        halo_kernel,
        out_shape=[jax.ShapeDtypeStruct((2, C, C), BF16)] * 4,
        in_specs=[vmem()] * 5,
        out_specs=[vmem()] * 4,
        scratch_shapes=[pltpu.VMEM((n, C), BF16)],
        compiler_params=params(),
        cost_estimate=cost(1e9, 3e6, 6e5),
        name="halo",
    )(halo, weight, acc, stat, q2)


COLS = 1024


def pair_part(first, second, dx):
    core, mine = lax.axis_index("seq") % 2, lax.axis_index("heads")
    rows = [pl.ds(pl.multiple_of(lax.rem(mine + e, 4) * 32, 32), 32) for e in range(4)]
    one = jnp.concatenate([first[r, :] for r in rows], axis=0)
    two = jnp.concatenate([second[r, :] for r in rows], axis=0)
    swapped = core > 0
    left = jnp.where(swapped, two.astype(F32), one.astype(F32)).astype(BF16)
    right = jnp.where(swapped, one.astype(F32), two.astype(F32)).astype(BF16)
    chip = lax.axis_index("seq") % PLANE // 2
    at = pl.multiple_of(jnp.bitwise_xor(chip, dx) * 2 * C, 2 * C)
    return jnp.concatenate([left, right], axis=1), pl.ds(at, 2 * C)


def early_kernel(own_pair, own_came, two, two_came, weight_ref, acc_ref):
    parts = [pair_part(own_pair.at[0], own_came, 0), pair_part(two.at[0], two_came, 2)]
    for at in range(0, weight_ref.shape[1], COLS):
        cols = slice(at, at + COLS)
        got = dot(parts[0][0], weight_ref[parts[0][1], cols])
        for part, rows in parts[1:]:
            got = got + dot(part, weight_ref[rows, cols])
        acc_ref[:, cols] = got


def late_kernel(one, one_came, three, three_came, weight_ref, acc_ref, own_ref, right_ref, left_ref, *outs):
    parts = [pair_part(one.at[0], one_came, 1), pair_part(three.at[0], three_came, 3)]
    far_right, far_left, plain_right, plain_left = outs
    half = weight_ref.shape[1] // 2
    for at in range(0, 2 * half, COLS):
        cols = slice(at, at + COLS)
        got = acc_ref[:, cols]
        for part, rows in parts:
            got = got + dot(part, weight_ref[rows, cols])
        own_ref[:, cols] = got[0:32]
        if at < half:
            right_ref[:, cols] = got[32:64]
            far_right[:, cols] = got[64:96].astype(BF16)
            plain_left[:, cols] = got[96:128].astype(BF16)
        else:
            cols = slice(at - half, at - half + COLS)
            plain_right[:, cols] = got[32:64].astype(BF16)
            far_left[:, cols] = got[64:96].astype(BF16)
            left_ref[:, cols] = got[96:128]


def project(slots, weight):
    width = weight.shape[1]
    (own_pair, one, two, three), (own_came, one_came, two_came, three_came) = slots
    acc = pl.pallas_call(
        early_kernel,
        out_shape=jax.ShapeDtypeStruct((C, width), F32),
        in_specs=[vmem()] * 5,
        out_specs=vmem(),
        compiler_params=params(),
        cost_estimate=cost(8e8, 8e6),
        name="early",
    )(own_pair, own_came, two, two_came, weight)
    return pl.pallas_call(
        late_kernel,
        out_shape=[jax.ShapeDtypeStruct((32, width), F32)]
        + [jax.ShapeDtypeStruct((32, width // 2), F32)] * 2
        + [jax.ShapeDtypeStruct((32, width // 2), BF16)] * 4,
        in_specs=[vmem()] * 6,
        out_specs=[vmem()] * 7,
        compiler_params=params(),
        cost_estimate=cost(3e8, 4e6),
        name="late",
    )(one, one_came, three, three_came, weight, acc)


def swap(block, d):
    return lax.ppermute(block, "seq", [(s, s ^ d) for s in range(PLANE * PLANES)])


def along_x(keep, came, part=slice(None)):
    pairs = {}
    for dx in (2, 1, 3):
        pairs[dx] = swap(jnp.stack([keep[dx, part], came[dx, part]]), 2 * dx)
    return [keep, came] + [pairs[dx] for dx in (1, 2, 3)]


def exchange(keep, send):
    return along_x(keep, swap(send, 1))


def exchange_back(pairs):
    found = {dx: swap(pairs[dx], 2 * dx) for dx in (2, 1, 3)}
    found[0], found[2] = lax.optimization_barrier((pairs[0], found[2]))
    came = {dx: swap(found[dx][1], 1) for dx in (2, 0, 1, 3)}
    return [found[dx] for dx in range(4)], [came[dx] for dx in range(4)]


def later_plane(block, distance):
    step = PLANE * distance
    route = [(s, s + step) for s in range(PLANE * PLANES - step)]
    return lax.ppermute(block, "seq", route)


def local(q_delta, k_delta, v_delta, decay, beta, gain, attn_weight, out_weight):
    slots_k = exchange(*pack_keys(k_delta, decay, beta))
    keep, send = pack_rest(q_delta, v_delta)
    came = swap(send, 1)
    slots_v = along_x(keep, came, slice(0, C))
    k, mix, inverse, w, tail, reach = key_part(slots_k)
    wu, ab, level = value_part(slots_v, k, inverse, w, tail, reach)
    one = later_plane(ab, 1)
    two = later_plane(ab, 2)
    keep_q, came_q, _ = lax.optimization_barrier((keep, came, ab))
    slots_q = along_x(keep_q, came_q, slice(C, 2 * C))
    no = query(slots_q, k, mix, wu, level)
    before, upto = combine(ab, one, two)
    six = later_plane(upto, 6)
    three = later_plane(upto, 3)
    normed = norm(no, gain[None, :], before, six, three)
    halo = later_plane(normed, 1)
    acc, stat, q2 = own(normed, attn_weight)
    attended = exchange_back(halo_part(halo, attn_weight, acc, stat, q2))
    return sum_over_heads(*project(attended, out_weight))


def sum_over_heads(own_sum, right, left, far_right, far_left, plain_right, plain_left):
    def turn(block, step):
        return lax.ppermute(block, "heads", [(s, (s + step) % 4) for s in range(4)])

    passed_right = turn(far_right, 1)
    passed_left = turn(far_left, 3)
    plain_right = turn(plain_right, 1)
    plain_left = turn(plain_left, 3)
    right = turn((right + passed_right.astype(F32)).astype(BF16), 1)
    left = turn((left + passed_left.astype(F32)).astype(BF16), 3)
    others = jnp.concatenate(
        [right.astype(F32) + plain_left.astype(F32), left.astype(F32) + plain_right.astype(F32)],
        axis=1,
    )
    return (own_sum + others).astype(BF16)


def solution(mesh):
    placed = (
        P("seq", "heads"),
        P("seq", "heads"),
        P("seq", "heads"),
        P("heads", "seq"),
        P("heads", "seq"),
        P(),
        P("heads", None, None),
        P("heads", None),
    )
    return jax.shard_map(
        local, mesh=mesh, in_specs=placed, out_specs=P(("seq", "heads"), None), check_vma=False
    )
```

```python
import jax
import jax.numpy as jnp
from jax import lax
from jax.experimental import pallas as pl
from jax.experimental.pallas import tpu as pltpu
from jax.sharding import PartitionSpec as P

F32 = jnp.float32
BF16 = jnp.bfloat16
C = 128
PLANE = 8
PLANES = 8
KROWS = C + 16
B = 16
EPS = 1e-06
NEG = -1e30
VMEM_LIMIT = 24 * 1024 * 1024


def params(limit=VMEM_LIMIT):
    return pltpu.CompilerParams(vmem_limit_bytes=limit)


def cost(flops, nbytes, trans=0):
    return pl.CostEstimate(flops=int(flops), bytes_accessed=int(nbytes), transcendentals=int(trans))


def vmem():
    return pl.BlockSpec(memory_space=pltpu.VMEM)


def split(a):
    hi = a.astype(BF16)
    lo = (a - hi.astype(F32)).astype(BF16)
    return hi, lo


def dot(a, b):
    return lax.dot_general(a, b, (((1,), (0,)), ((), ())), preferred_element_type=F32)


def dot_nt(a, b):
    return lax.dot_general(a, b, (((1,), (1,)), ((), ())), preferred_element_type=F32)


def dot_tn(a, b):
    return lax.dot_general(a, b, (((0,), (0,)), ((), ())), preferred_element_type=F32)


def mm(a, b):
    ah, al = split(a)
    bh, bl = split(b)
    left = jnp.concatenate([ah, al], axis=1)
    n = b.shape[1]
    if n > C:
        return dot(left, jnp.concatenate([bh, bh], axis=0)) + dot(ah, bl)
    pair = jnp.concatenate([bh, bl], axis=1)
    out = dot(left, jnp.concatenate([pair, pair], axis=0))
    return out[:, :n] + out[:, n:]


def mm_exact_right(a, b):
    ah, al = split(a)
    return dot(jnp.concatenate([ah, al], axis=1), jnp.concatenate([b, b], axis=0))


def iotas():
    row = lax.broadcasted_iota(jnp.int32, (C, C), 0)
    col = lax.broadcasted_iota(jnp.int32, (C, C), 1)
    return row, col


def pack_kernel(q_ref, k_ref, v_ref, decay_ref, beta_ref, *rest):
    keep_k, send_k, keep, send, gate, raw, sems = rest
    me = lax.axis_index("seq") % PLANE
    copies = [
        pltpu.make_async_copy(decay_ref, raw.at[0], sems.at[24]),
        pltpu.make_async_copy(beta_ref, raw.at[1], sems.at[25]),
    ]
    for d in range(PLANE):
        cols = pl.ds(pl.multiple_of(jnp.bitwise_xor(me, d) * C, C), C)
        out_k, out = (send_k, send) if d % 2 else (keep_k, keep)
        at = d // 2
        copies += [
            pltpu.make_async_copy(k_ref.at[:, cols], out_k.at[at, pl.ds(0, C)], sems.at[3 * d]),
            pltpu.make_async_copy(v_ref.at[:, cols], out.at[at, pl.ds(0, C)], sems.at[3 * d + 1]),
            pltpu.make_async_copy(q_ref.at[:, cols], out.at[at, pl.ds(C, C)], sems.at[3 * d + 2]),
        ]
    for copy in copies:
        copy.start()
    copies[0].wait()
    copies[1].wait()
    for i in range(2):
        x = raw[i]
        for j in range(3):
            part = x.astype(BF16).astype(F32)
            gate[3 * i + j] = part
            x = x - part
    zeros = jnp.zeros((10, C), F32)
    for d in range(PLANE):
        head = jnp.bitwise_xor(me, d)
        rows = [gate[i, pl.ds(head, 1), :] for i in range(6)]
        out = send_k if d % 2 else keep_k
        out[d // 2, C:, :] = jnp.concatenate(rows + [zeros], axis=0).astype(BF16)
    for copy in copies[2:]:
        copy.wait()


def pack(q, k, v, decay, beta):
    any_space = pl.BlockSpec(memory_space=pltpu.HBM)
    first = jax.ShapeDtypeStruct((4, KROWS, C), BF16)
    wide = jax.ShapeDtypeStruct((4, 2 * C, C), BF16)
    return pl.pallas_call(
        pack_kernel,
        out_shape=[first, first, wide, wide],
        in_specs=[any_space] * 5,
        out_specs=[vmem()] * 4,
        scratch_shapes=[
            pltpu.VMEM((6, PLANE, C), F32),
            pltpu.VMEM((2, PLANE, C), F32),
            pltpu.SemaphoreType.DMA((26,)),
        ],
        compiler_params=params(),
        name="pack",
    )(*[pltpu.with_memory_space_constraint(x, pltpu.HBM) for x in (q, k, v, decay, beta)])


def gather_slots(refs, out_ref, part=None):
    keep, came = refs[0], refs[1]
    out_ref[0] = keep[0] if part is None else keep[0, part, :]
    out_ref[1] = came[0] if part is None else came[0, part, :]
    for dx in range(1, 4):
        out_ref[2 * dx] = refs[dx + 1][0]
        out_ref[2 * dx + 1] = refs[dx + 1][1]


def gates(k_ref):
    row, col = iotas()
    pieces = jnp.concatenate([k_ref[d, C:, :] for d in range(PLANE)], axis=0)
    upper = jnp.where(row <= col, 1.0, 0.0).astype(BF16)
    lower = jnp.where(row >= col, 1.0, 0.0).astype(BF16)
    eye = jnp.where(row == col, 1.0, 0.0).astype(BF16)
    along_row = dot(pieces, upper)
    along_col = dot_nt(jnp.concatenate([lower, eye], axis=0), pieces)
    plain = pieces.astype(F32)
    found = []
    for d in range(PLANE):
        o = 16 * d
        g_row = -(along_row[o : o + 1] + along_row[o + 1 : o + 2] + along_row[o + 2 : o + 3])
        b_row = plain[o + 3 : o + 4] + plain[o + 4 : o + 5] + plain[o + 5 : o + 6]
        g_col = -(
            along_col[:C, o : o + 1] + along_col[:C, o + 1 : o + 2] + along_col[:C, o + 2 : o + 3]
        )
        b_col = (
            along_col[C:, o + 3 : o + 4]
            + along_col[C:, o + 4 : o + 5]
            + along_col[C:, o + 5 : o + 6]
        )
        found.append((g_row, b_row, g_col, b_col))
    return found


def base_inverses(packed):
    row, col = iotas()
    high = packed.astype(BF16)
    rest = packed - high.astype(F32)
    mid = rest.astype(BF16)
    low = (rest - mid.astype(F32)).astype(BF16)
    three = jnp.concatenate([high, mid, low], axis=1)
    x = jnp.where(row % B == col % B, 1.0, 0.0)
    for j in range(B - 1):
        pick = jnp.where(row == col - col % B + j, 1.0, 0.0).astype(BF16)
        factor = dot(three, jnp.concatenate([pick, pick, pick], axis=0))
        line = x.reshape(PLANE, B, C)[:, j : j + 1, :]
        x = x - factor * jnp.broadcast_to(line, (PLANE, B, C)).reshape(C, C)
    return x


def after(earlier, later):
    both = mm(later[:, :C], earlier)
    return jnp.concatenate([both[:, :C], both[:, C:] + later[:, C:]], axis=1)


def key_kernel(*refs):
    k_ref, mix_ref, inverse_ref, w_ref, tail_ref, reach_ref = refs[5:]
    me = lax.axis_index("seq") % PLANE
    row, col = iotas()
    gather_slots(refs[:5], k_ref)
    every = range(PLANE)
    blocks = (row // B) == (col // B)
    apart = jnp.bitwise_xor(row, col)
    found = gates(k_ref)
    keys = [k_ref[d, 0:C, :] for d in every]
    grams = [dot_nt(k, k) for k in keys]
    diags = [jnp.where(row == col, g, 0.0) for g in grams]
    r_cols = [lax.rsqrt(jnp.sum(g, axis=1, keepdims=True) + EPS) for g in diags]
    r_rows = [lax.rsqrt(jnp.sum(g, axis=0, keepdims=True) + EPS) for g in diags]
    lows, packs = [], []
    for d in every:
        g_row, b_row, g_col, _ = found[d]
        ratio = jnp.where(row >= col, jnp.exp(jnp.minimum(g_col - g_row, 0.0)), 0.0)
        mix = ratio * (b_row * r_rows[d])
        mix_ref[d] = mix
        low = jnp.where(row > col, mix * grams[d] * r_cols[d], 0.0)
        lows.append(low)
        held = jnp.where(blocks, low, 0.0)
        packed = held[0:B]
        for b in range(1, C // B):
            packed = packed + held[B * b : B * b + B]
        packs.append(packed)
    base = base_inverses(jnp.concatenate(packs, axis=0))
    inverse = [
        jnp.where(blocks, jnp.concatenate([base[B * d : B * d + B]] * (C // B), axis=0), 0.0)
        for d in every
    ]
    size = B
    while size < C:
        level = (row > col) & (apart >= size) & (apart < 2 * size)
        half = [mm(x, jnp.where(level, low, 0.0)) for x, low in zip(inverse, lows)]
        inverse = [x - mm(h, x) for x, h in zip(inverse, half)]
        size *= 2
    folded = [inverse[d] * (jnp.exp(found[d][0]) * r_rows[d]) for d in every]
    w = [mm_exact_right(folded[d], keys[d]) for d in every]
    halves = []
    for d in every:
        g_row, _, g_col, b_col = found[d]
        tail = jnp.broadcast_to(jnp.exp(g_row[:, C - 1 : C] - g_col) * b_col * r_cols[d], (C, C))
        inverse_ref[d] = inverse[d]
        w_ref[d] = w[d]
        tail_ref[d] = tail
        halves.append(jnp.concatenate(split(w[d] * tail), axis=0))
    made = [dot_tn(jnp.concatenate([keys[d], keys[d]], axis=0), halves[d]) for d in every]
    for d in every:
        g_end = found[d][0][:, C - 1 : C]
        reach_ref[jnp.bitwise_xor(me, d)] = jnp.where(row == col, jnp.exp(g_end), 0.0) - made[d]


def value_kernel(*refs):
    k_ref, inverse_ref, w_ref, tail_ref, reach_ref = refs[5:10]
    wu_ref, ab_ref, level_ref, states, v_ref = refs[10:]
    me = lax.axis_index("seq") % PLANE
    gather_slots(refs[:5], v_ref, slice(0, C))
    every = range(PLANE)
    reach = [reach_ref[i] for i in every]
    u = [mm_exact_right(inverse_ref[d], v_ref[d]) for d in every]
    reach_two = [mm(reach[2 * i + 1], reach[2 * i]) for i in range(4)]
    halves = []
    for d in every:
        wu_ref[d, :, :C] = w_ref[d]
        wu_ref[d, :, C:] = u[d]
        halves.append(jnp.concatenate(split(u[d] * tail_ref[d]), axis=0))
    keys = [k_ref[d, 0:C, :] for d in every]
    made = [dot_tn(jnp.concatenate([keys[d], keys[d]], axis=0), halves[d]) for d in every]
    reach_four = [mm(reach_two[2 * i + 1], reach_two[2 * i]) for i in range(2)]
    for d in every:
        states[jnp.bitwise_xor(me, d)] = made[d]
    one = [states[i] for i in every]
    two = [mm(reach[2 * i + 1], one[2 * i]) + one[2 * i + 1] for i in range(4)]
    ab_ref[:, :C] = mm(reach_four[1], reach_four[0]).astype(BF16)
    four = [mm(reach_two[2 * i + 1], two[2 * i]) + two[2 * i + 1] for i in range(2)]
    ab_ref[:, C:] = (mm(reach_four[1], four[0]) + four[1]).astype(BF16)
    levels = [(reach[0], one[0]), (reach_two[0], two[0]), (reach[2], one[2])]
    levels += [(reach_four[0], four[0]), (reach[4], one[4]), (reach_two[2], two[2])]
    for i, (across, state) in enumerate(levels + [(reach[6], one[6])]):
        level_ref[i, :, :C] = across
        level_ref[i, :, C:] = state


def key_part(slots):
    square = jax.ShapeDtypeStruct((PLANE, C, C), F32)
    return pl.pallas_call(
        key_kernel,
        out_shape=[jax.ShapeDtypeStruct((PLANE, KROWS, C), BF16)]
        + [square] * 5,
        in_specs=[vmem()] * 5,
        out_specs=[vmem()] * 6,
        compiler_params=params(),
        cost_estimate=cost(2e9, 4e6),
        name="keys",
    )(*slots)


def value_part(slots, k, inverse, w, tail, reach):
    return pl.pallas_call(
        value_kernel,
        out_shape=[
            jax.ShapeDtypeStruct((PLANE, C, 2 * C), F32),
            jax.ShapeDtypeStruct((C, 2 * C), BF16),
            jax.ShapeDtypeStruct((7, C, 2 * C), F32),
        ],
        in_specs=[vmem()] * 10,
        out_specs=[vmem()] * 3,
        scratch_shapes=[pltpu.VMEM((PLANE, C, C), F32), pltpu.VMEM((PLANE, C, C), BF16)],
        compiler_params=params(),
        cost_estimate=cost(1e9, 4e6),
        name="values",
    )(*slots, k, inverse, w, tail, reach)


def query_kernel(*refs):
    k_ref, mix_ref, wu_ref, level_ref, no_ref, before, q_ref = refs[5:]
    gather_slots(refs[:5], q_ref, slice(C, 2 * C))
    me = lax.axis_index("seq") % PLANE
    row, col = iotas()
    before[0] = jnp.concatenate([jnp.where(row == col, 1.0, 0.0), jnp.zeros((C, C), F32)], axis=1)
    before[1] = level_ref[0]
    before[2] = level_ref[1]
    before[3] = after(level_ref[1], level_ref[2])
    before[4] = level_ref[3]
    before[5] = after(level_ref[3], level_ref[4])
    six = after(level_ref[3], level_ref[5])
    before[6] = six
    before[7] = after(six, level_ref[6])

    every = range(PLANE)
    found = gates(k_ref)
    queries = [q_ref[d] for d in every]
    scored = [dot_nt(queries[d], k_ref[d, 0:C, :]) for d in every]
    r_cols = []
    for q in queries:
        wide = q.astype(F32)
        r_cols.append(lax.rsqrt(jnp.sum(wide * wide, axis=1, keepdims=True) + EPS) * (C**-0.5))
    scored = [scored[d] * r_cols[d] * mix_ref[d] for d in every]
    parts = [mm(scored[d], wu_ref[d]) for d in every]
    reach = [
        queries[d].astype(F32) * (r_cols[d] * jnp.exp(found[d][2])) - parts[d][:, :C]
        for d in every
    ]
    chunks = [jnp.bitwise_xor(me, d) for d in every]
    both = [mm(reach[d], before[chunks[d]]) for d in every]
    for d in every:
        rows = pl.ds(pl.multiple_of(chunks[d] * C, C), C)
        no_ref[rows, :] = jnp.concatenate(
            [both[d][:, :C], both[d][:, C:] + parts[d][:, C:]], axis=1
        )


def query(slots, k, mix, wu, level):
    return pl.pallas_call(
        query_kernel,
        out_shape=jax.ShapeDtypeStruct((PLANE * C, 2 * C), F32),
        in_specs=[vmem()] * 9,
        out_specs=vmem(),
        scratch_shapes=[
            pltpu.VMEM((PLANE, C, 2 * C), F32),
            pltpu.VMEM((PLANE, C, C), BF16),
        ],
        compiler_params=params(),
        cost_estimate=cost(1e9, 4e6),
        name="query",
    )(*slots, k, mix, wu, level)


def times(a, x):
    hi, lo = split(x)
    return dot(jnp.concatenate([a, a], axis=1), jnp.concatenate([hi, lo], axis=0))


def combine_kernel(own_ref, one_ref, two_ref, before_ref, upto_ref):
    a_one, a_own = one_ref[:, :C], own_ref[:, :C]
    reach = dot(a_one, two_ref[:, :C])
    state = one_ref[:, C:].astype(F32) + dot(a_one, two_ref[:, C:])
    before_ref[:, :C] = reach
    before_ref[:, C:] = state
    upto_ref[:, :C] = times(a_own, reach).astype(BF16)
    upto_ref[:, C:] = (own_ref[:, C:].astype(F32) + times(a_own, state)).astype(BF16)


def combine(own_map, one, two):
    return pl.pallas_call(
        combine_kernel,
        out_shape=[
            jax.ShapeDtypeStruct((C, 2 * C), F32),
            jax.ShapeDtypeStruct((C, 2 * C), BF16),
        ],
        in_specs=[vmem()] * 3,
        out_specs=[vmem()] * 2,
        compiler_params=params(),
        name="combine",
    )(own_map, one, two)


def norm_kernel(no_ref, gain_ref, before_ref, six_ref, three_ref, normed_ref):
    state = three_ref[:, C:].astype(F32) + dot(three_ref[:, :C], six_ref[:, C:])
    state = before_ref[:, C:] + mm(before_ref[:, :C], state)
    out = mm(no_ref[:, :C], state) + no_ref[:, C:]
    scale = lax.rsqrt(jnp.mean(out * out, axis=1, keepdims=True) + EPS)
    normed_ref[...] = (out * scale * gain_ref[...]).astype(BF16)


def norm(no, gain, before, six, three):
    return pl.pallas_call(
        norm_kernel,
        out_shape=jax.ShapeDtypeStruct((PLANE * C, C), BF16),
        in_specs=[vmem()] * 5,
        out_specs=vmem(),
        compiler_params=params(),
        cost_estimate=cost(2e8, 2e6),
        name="norm",
    )(no, gain, before, six, three)


QB = 256
SCALE = C**-0.5 * 1.4426950408889634


def squares():
    row = lax.broadcasted_iota(jnp.int32, (QB, QB), 0)
    col = lax.broadcasted_iota(jnp.int32, (QB, QB), 1)
    return row, col


def row_max(parts):
    top = jnp.max(parts[0], axis=1, keepdims=True)
    for part in parts[1:]:
        top = jnp.maximum(top, jnp.max(part, axis=1, keepdims=True))
    return top


def row_sum(parts):
    total = jnp.sum(parts[0], axis=1, keepdims=True)
    for part in parts[1:]:
        total = total + jnp.sum(part, axis=1, keepdims=True)
    return total


def weighted(parts, values):
    out = dot(parts[0].astype(BF16), values[0])
    for part, value in zip(parts[1:], values[1:]):
        out = out + dot(part.astype(BF16), value)
    return out


def tiled(column, like):
    return jnp.concatenate([column] * (like.shape[1] // C), axis=1)


def own_kernel(normed_ref, weight_ref, acc_ref, stat_ref, q2_ref):
    me = lax.axis_index("seq") % PLANE
    proj = dot(normed_ref[...], weight_ref[me]).astype(BF16)
    q2_ref[...] = proj[:, :C]
    row, col = squares()
    starts = range(0, PLANE * C, QB)
    spans = [[(at, at + QB)] + ([(0, at)] if at else []) for at in starts]
    scores = [
        [dot_nt(proj[at : at + QB, :C], proj[a:b, C : 2 * C]) for a, b in span]
        for at, span in zip(starts, spans)
    ]
    scores = [[jnp.where(col <= row, parts[0], NEG)] + parts[1:] for parts in scores]
    tops = [row_max(parts) for parts in scores]
    raised = [[jnp.exp2((s - top) * SCALE) for s in parts] for parts, top in zip(scores, tops)]
    for i, at in enumerate(starts):
        rows = slice(at, at + QB)
        acc_ref[rows, :] = weighted(raised[i], [proj[a:b, 2 * C :] for a, b in spans[i]])
        stat_ref[0, rows, :] = jnp.broadcast_to(tops[i], (QB, C))
        stat_ref[1, rows, :] = jnp.broadcast_to(row_sum(raised[i]), (QB, C))


def own(normed, weight):
    n = PLANE * C
    return pl.pallas_call(
        own_kernel,
        out_shape=[
            jax.ShapeDtypeStruct((n, C), F32),
            jax.ShapeDtypeStruct((2, n, C), F32),
            jax.ShapeDtypeStruct((n, C), BF16),
        ],
        in_specs=[vmem()] * 2,
        out_specs=[vmem()] * 3,
        compiler_params=params(),
        cost_estimate=cost(1e9, 3e6, 6e5),
        name="own",
    )(normed, weight)


def halo_kernel(halo_ref, weight_ref, acc_ref, stat_ref, q2_ref, *refs):
    keep, send, attended = refs
    place = lax.axis_index("seq")
    me, plane = place % PLANE, place // PLANE
    proj = dot(halo_ref[...], weight_ref[me, :, C:]).astype(BF16)
    n = PLANE * C
    row, col = squares()
    starts = range(0, n, QB)
    spans = [[(at, at + QB)] + ([(at + QB, n)] if at + QB < n else []) for at in starts]
    floor = jnp.where(plane > 0, 0.0, NEG)
    scores = [
        [dot_nt(q2_ref[at : at + QB, :], proj[a:b, :C]) for a, b in span]
        for at, span in zip(starts, spans)
    ]
    scores = [[jnp.where(col > row, parts[0], NEG)] + parts[1:] for parts in scores]
    before = [stat_ref[0, at : at + QB, :] for at in starts]
    tops = [jnp.maximum(row_max(parts) + floor, old) for parts, old in zip(scores, before)]
    raised = [
        [jnp.exp2((s - tiled(top - floor, s)) * SCALE) for s in parts]
        for parts, top in zip(scores, tops)
    ]
    fades = [jnp.exp2((old - top) * SCALE) for old, top in zip(before, tops)]
    for i, at in enumerate(starts):
        rows = slice(at, at + QB)
        total = row_sum(raised[i]) + fades[i] * stat_ref[1, rows, :]
        acc = acc_ref[rows, :] * fades[i] + weighted(
            raised[i], [proj[a:b, C:] for a, b in spans[i]]
        )
        attended[rows, :] = (acc / total).astype(BF16)
    for d in range(PLANE):
        chunk = jnp.bitwise_xor(me, d)
        out = send if d % 2 else keep
        out[d // 2] = attended[pl.ds(pl.multiple_of(chunk * C, C), C), :]


def halo_part(halo, weight, acc, stat, q2):
    n = PLANE * C
    return pl.pallas_call(
        halo_kernel,
        out_shape=[jax.ShapeDtypeStruct((4, C, C), BF16)] * 2,
        in_specs=[vmem()] * 5,
        out_specs=[vmem()] * 2,
        scratch_shapes=[pltpu.VMEM((n, C), BF16)],
        compiler_params=params(),
        cost_estimate=cost(1e9, 3e6, 6e5),
        name="halo",
    )(halo, weight, acc, stat, q2)


COLS = 1024


def pair_part(first, second, dx):
    core, mine = lax.axis_index("seq") % 2, lax.axis_index("heads")
    rows = [pl.ds(pl.multiple_of(lax.rem(mine + e, 4) * 32, 32), 32) for e in range(4)]
    one = jnp.concatenate([first[r, :] for r in rows], axis=0)
    two = jnp.concatenate([second[r, :] for r in rows], axis=0)
    swapped = core > 0
    left = jnp.where(swapped, two.astype(F32), one.astype(F32)).astype(BF16)
    right = jnp.where(swapped, one.astype(F32), two.astype(F32)).astype(BF16)
    chip = lax.axis_index("seq") % PLANE // 2
    at = pl.multiple_of(jnp.bitwise_xor(chip, dx) * 2 * C, 2 * C)
    return jnp.concatenate([left, right], axis=1), pl.ds(at, 2 * C)


def early_kernel(keep, came, one, two, weight_ref, acc_ref):
    parts = [
        pair_part(keep.at[0], came.at[0], 0),
        pair_part(two.at[0], two.at[1], 2),
        pair_part(one.at[0], one.at[1], 1),
    ]
    for at in range(0, weight_ref.shape[1], COLS):
        cols = slice(at, at + COLS)
        got = dot(parts[0][0], weight_ref[parts[0][1], cols])
        for part, rows in parts[1:]:
            got = got + dot(part, weight_ref[rows, cols])
        acc_ref[:, cols] = got


def late_kernel(three, weight_ref, acc_ref, own_ref, right_ref, left_ref, *outs):
    part, rows = pair_part(three.at[0], three.at[1], 3)
    far_right, far_left, plain_right, plain_left = outs
    half = weight_ref.shape[1] // 2
    for at in range(0, 2 * half, COLS):
        cols = slice(at, at + COLS)
        got = acc_ref[:, cols] + dot(part, weight_ref[rows, cols])
        own_ref[:, cols] = got[0:32]
        if at < half:
            right_ref[:, cols] = got[32:64]
            far_right[:, cols] = got[64:96].astype(BF16)
            plain_left[:, cols] = got[96:128].astype(BF16)
        else:
            cols = slice(at - half, at - half + COLS)
            plain_right[:, cols] = got[32:64].astype(BF16)
            far_left[:, cols] = got[64:96].astype(BF16)
            left_ref[:, cols] = got[96:128]


def project(slots, weight):
    width = weight.shape[1]
    keep, came, one, two, three = slots
    acc = pl.pallas_call(
        early_kernel,
        out_shape=jax.ShapeDtypeStruct((C, width), F32),
        in_specs=[vmem()] * 5,
        out_specs=vmem(),
        compiler_params=params(),
        cost_estimate=cost(8e8, 8e6),
        name="early",
    )(keep, came, one, two, weight)
    return pl.pallas_call(
        late_kernel,
        out_shape=[jax.ShapeDtypeStruct((32, width), F32)]
        + [jax.ShapeDtypeStruct((32, width // 2), F32)] * 2
        + [jax.ShapeDtypeStruct((32, width // 2), BF16)] * 4,
        in_specs=[vmem()] * 3,
        out_specs=[vmem()] * 7,
        compiler_params=params(),
        cost_estimate=cost(3e8, 4e6),
        name="late",
    )(three, weight, acc)


def swap(block, d):
    return lax.ppermute(block, "seq", [(s, s ^ d) for s in range(PLANE * PLANES)])


def along_x(keep, came, part=slice(None)):
    pairs = {}
    for dx in (2, 1, 3):
        pairs[dx] = swap(jnp.stack([keep[dx, part], came[dx, part]]), 2 * dx)
    return [keep, came] + [pairs[dx] for dx in (1, 2, 3)]


def exchange(keep, send):
    return along_x(keep, swap(send, 1))


def later_plane(block, distance):
    step = PLANE * distance
    route = [(s, s + step) for s in range(PLANE * PLANES - step)]
    return lax.ppermute(block, "seq", route)


def local(q_delta, k_delta, v_delta, decay, beta, gain, attn_weight, out_weight):
    keep_k, send_k, keep, send = pack(q_delta, k_delta, v_delta, decay, beta)
    slots_k = exchange(keep_k, send_k)
    came = swap(send, 1)
    slots_v = along_x(keep, came, slice(0, C))
    k, mix, inverse, w, tail, reach = key_part(slots_k)
    wu, ab, level = value_part(slots_v, k, inverse, w, tail, reach)
    one = later_plane(ab, 1)
    two = later_plane(ab, 2)
    keep_q, came_q, _ = lax.optimization_barrier((keep, came, ab))
    slots_q = along_x(keep_q, came_q, slice(C, 2 * C))
    no = query(slots_q, k, mix, wu, level)
    before, upto = combine(ab, one, two)
    six = later_plane(upto, 6)
    three = later_plane(upto, 3)
    normed = norm(no, gain[None, :], before, six, three)
    halo = later_plane(normed, 1)
    acc, stat, q2 = own(normed, attn_weight)
    attended = exchange(*halo_part(halo, attn_weight, acc, stat, q2))
    return sum_over_heads(*project(attended, out_weight))


def sum_over_heads(own_sum, right, left, far_right, far_left, plain_right, plain_left):
    def turn(block, step):
        return lax.ppermute(block, "heads", [(s, (s + step) % 4) for s in range(4)])

    passed_right = turn(far_right, 1)
    passed_left = turn(far_left, 3)
    passed_right, passed_left = lax.optimization_barrier((passed_right, passed_left))
    plain_right = turn(plain_right, 1)
    plain_left = turn(plain_left, 3)
    right = turn((right + passed_right.astype(F32)).astype(BF16), 1)
    left = turn((left + passed_left.astype(F32)).astype(BF16), 3)
    others = jnp.concatenate(
        [right.astype(F32) + plain_left.astype(F32), left.astype(F32) + plain_right.astype(F32)],
        axis=1,
    )
    return (own_sum + others).astype(BF16)


def solution(mesh):
    placed = (
        P("seq", "heads"),
        P("seq", "heads"),
        P("seq", "heads"),
        P("heads", "seq"),
        P("heads", "seq"),
        P(),
        P("heads", None, None),
        P("heads", None),
    )
    return jax.shard_map(
        local, mesh=mesh, in_specs=placed, out_specs=P(("seq", "heads"), None), check_vma=False
    )
```

```python
import jax
import jax.numpy as jnp
from jax import lax
from jax.experimental import pallas as pl
from jax.experimental.pallas import tpu as pltpu
from jax.sharding import PartitionSpec as P

F32 = jnp.float32
BF16 = jnp.bfloat16
C = 128
PLANE = 8
PLANES = 8
KROWS = C + 16
B = 16
EPS = 1e-06
NEG = -1e30
VMEM_LIMIT = 24 * 1024 * 1024


def params(limit=VMEM_LIMIT):
    return pltpu.CompilerParams(vmem_limit_bytes=limit)


def cost(flops, nbytes, trans=0):
    return pl.CostEstimate(flops=int(flops), bytes_accessed=int(nbytes), transcendentals=int(trans))


def vmem():
    return pl.BlockSpec(memory_space=pltpu.VMEM)


def split(a):
    hi = a.astype(BF16)
    lo = (a - hi.astype(F32)).astype(BF16)
    return hi, lo


def dot(a, b):
    return lax.dot_general(a, b, (((1,), (0,)), ((), ())), preferred_element_type=F32)


def dot_nt(a, b):
    return lax.dot_general(a, b, (((1,), (1,)), ((), ())), preferred_element_type=F32)


def dot_tn(a, b):
    return lax.dot_general(a, b, (((0,), (0,)), ((), ())), preferred_element_type=F32)


def mm(a, b):
    ah, al = split(a)
    bh, bl = split(b)
    left = jnp.concatenate([ah, al], axis=1)
    n = b.shape[1]
    if n > C:
        return dot(left, jnp.concatenate([bh, bh], axis=0)) + dot(ah, bl)
    pair = jnp.concatenate([bh, bl], axis=1)
    out = dot(left, jnp.concatenate([pair, pair], axis=0))
    return out[:, :n] + out[:, n:]


def mm_exact_right(a, b):
    ah, al = split(a)
    return dot(jnp.concatenate([ah, al], axis=1), jnp.concatenate([b, b], axis=0))


def iotas():
    row = lax.broadcasted_iota(jnp.int32, (C, C), 0)
    col = lax.broadcasted_iota(jnp.int32, (C, C), 1)
    return row, col


def pack_kernel(q_ref, k_ref, v_ref, decay_ref, beta_ref, *rest):
    keep_k, send_k, keep, send, gate, raw, sems = rest
    me = lax.axis_index("seq") % PLANE
    copies = [
        pltpu.make_async_copy(decay_ref, raw.at[0], sems.at[24]),
        pltpu.make_async_copy(beta_ref, raw.at[1], sems.at[25]),
    ]
    for d in range(PLANE):
        cols = pl.ds(pl.multiple_of(jnp.bitwise_xor(me, d) * C, C), C)
        out_k, out = (send_k, send) if d % 2 else (keep_k, keep)
        at = d // 2
        copies += [
            pltpu.make_async_copy(k_ref.at[:, cols], out_k.at[at, pl.ds(0, C)], sems.at[3 * d]),
            pltpu.make_async_copy(v_ref.at[:, cols], out.at[at, pl.ds(0, C)], sems.at[3 * d + 1]),
            pltpu.make_async_copy(q_ref.at[:, cols], out.at[at, pl.ds(C, C)], sems.at[3 * d + 2]),
        ]
    for copy in copies:
        copy.start()
    copies[0].wait()
    copies[1].wait()
    for i in range(2):
        x = raw[i]
        for j in range(3):
            part = x.astype(BF16).astype(F32)
            gate[3 * i + j] = part
            x = x - part
    zeros = jnp.zeros((10, C), F32)
    for d in range(PLANE):
        head = jnp.bitwise_xor(me, d)
        rows = [gate[i, pl.ds(head, 1), :] for i in range(6)]
        out = send_k if d % 2 else keep_k
        out[d // 2, C:, :] = jnp.concatenate(rows + [zeros], axis=0).astype(BF16)
    for copy in copies[2:]:
        copy.wait()


def pack(q, k, v, decay, beta):
    any_space = pl.BlockSpec(memory_space=pltpu.HBM)
    first = jax.ShapeDtypeStruct((4, KROWS, C), BF16)
    wide = jax.ShapeDtypeStruct((4, 2 * C, C), BF16)
    return pl.pallas_call(
        pack_kernel,
        out_shape=[first, first, wide, wide],
        in_specs=[any_space] * 5,
        out_specs=[vmem()] * 4,
        scratch_shapes=[
            pltpu.VMEM((6, PLANE, C), F32),
            pltpu.VMEM((2, PLANE, C), F32),
            pltpu.SemaphoreType.DMA((26,)),
        ],
        compiler_params=params(),
        name="pack",
    )(*[pltpu.with_memory_space_constraint(x, pltpu.HBM) for x in (q, k, v, decay, beta)])


def gather_slots(refs, out_ref, part=None):
    keep, came = refs[0], refs[1]
    out_ref[0] = keep[0] if part is None else keep[0, part, :]
    out_ref[1] = came[0] if part is None else came[0, part, :]
    for dx in range(1, 4):
        out_ref[2 * dx] = refs[dx + 1][0]
        out_ref[2 * dx + 1] = refs[dx + 1][1]


def gates(k_ref):
    row, col = iotas()
    pieces = jnp.concatenate([k_ref[d, C:, :] for d in range(PLANE)], axis=0)
    upper = jnp.where(row <= col, 1.0, 0.0).astype(BF16)
    lower = jnp.where(row >= col, 1.0, 0.0).astype(BF16)
    eye = jnp.where(row == col, 1.0, 0.0).astype(BF16)
    along_row = dot(pieces, upper)
    along_col = dot_nt(jnp.concatenate([lower, eye], axis=0), pieces)
    plain = pieces.astype(F32)
    found = []
    for d in range(PLANE):
        o = 16 * d
        g_row = -(along_row[o : o + 1] + along_row[o + 1 : o + 2] + along_row[o + 2 : o + 3])
        b_row = plain[o + 3 : o + 4] + plain[o + 4 : o + 5] + plain[o + 5 : o + 6]
        g_col = -(
            along_col[:C, o : o + 1] + along_col[:C, o + 1 : o + 2] + along_col[:C, o + 2 : o + 3]
        )
        b_col = (
            along_col[C:, o + 3 : o + 4]
            + along_col[C:, o + 4 : o + 5]
            + along_col[C:, o + 5 : o + 6]
        )
        found.append((g_row, b_row, g_col, b_col))
    return found


def base_inverses(packed):
    row, col = iotas()
    high = packed.astype(BF16)
    rest = packed - high.astype(F32)
    mid = rest.astype(BF16)
    low = (rest - mid.astype(F32)).astype(BF16)
    three = jnp.concatenate([high, mid, low], axis=1)
    x = jnp.where(row % B == col % B, 1.0, 0.0)
    for j in range(B - 1):
        pick = jnp.where(row == col - col % B + j, 1.0, 0.0).astype(BF16)
        factor = dot(three, jnp.concatenate([pick, pick, pick], axis=0))
        line = x.reshape(PLANE, B, C)[:, j : j + 1, :]
        x = x - factor * jnp.broadcast_to(line, (PLANE, B, C)).reshape(C, C)
    return x


def after(earlier, later):
    both = mm(later[:, :C], earlier)
    return jnp.concatenate([both[:, :C], both[:, C:] + later[:, C:]], axis=1)


def key_kernel(*refs):
    k_ref, mix_ref, inverse_ref, w_ref, tail_ref, reach_ref = refs[5:]
    me = lax.axis_index("seq") % PLANE
    row, col = iotas()
    gather_slots(refs[:5], k_ref)
    every = range(PLANE)
    blocks = (row // B) == (col // B)
    apart = jnp.bitwise_xor(row, col)
    found = gates(k_ref)
    keys = [k_ref[d, 0:C, :] for d in every]
    grams = [dot_nt(k, k) for k in keys]
    diags = [jnp.where(row == col, g, 0.0) for g in grams]
    r_cols = [lax.rsqrt(jnp.sum(g, axis=1, keepdims=True) + EPS) for g in diags]
    r_rows = [lax.rsqrt(jnp.sum(g, axis=0, keepdims=True) + EPS) for g in diags]
    lows, packs = [], []
    for d in every:
        g_row, b_row, g_col, _ = found[d]
        ratio = jnp.where(row >= col, jnp.exp(jnp.minimum(g_col - g_row, 0.0)), 0.0)
        mix = ratio * (b_row * r_rows[d])
        mix_ref[d] = mix
        low = jnp.where(row > col, mix * grams[d] * r_cols[d], 0.0)
        lows.append(low)
        held = jnp.where(blocks, low, 0.0)
        packed = held[0:B]
        for b in range(1, C // B):
            packed = packed + held[B * b : B * b + B]
        packs.append(packed)
    base = base_inverses(jnp.concatenate(packs, axis=0))
    inverse = [
        jnp.where(blocks, jnp.concatenate([base[B * d : B * d + B]] * (C // B), axis=0), 0.0)
        for d in every
    ]
    size = B
    while size < C:
        level = (row > col) & (apart >= size) & (apart < 2 * size)
        half = [mm(x, jnp.where(level, low, 0.0)) for x, low in zip(inverse, lows)]
        inverse = [x - mm(h, x) for x, h in zip(inverse, half)]
        size *= 2
    folded = [inverse[d] * (jnp.exp(found[d][0]) * r_rows[d]) for d in every]
    w = [mm_exact_right(folded[d], keys[d]) for d in every]
    halves = []
    for d in every:
        g_row, _, g_col, b_col = found[d]
        tail = jnp.broadcast_to(jnp.exp(g_row[:, C - 1 : C] - g_col) * b_col * r_cols[d], (C, C))
        inverse_ref[d] = inverse[d]
        w_ref[d] = w[d]
        tail_ref[d] = tail
        halves.append(jnp.concatenate(split(w[d] * tail), axis=0))
    made = [dot_tn(jnp.concatenate([keys[d], keys[d]], axis=0), halves[d]) for d in every]
    for d in every:
        g_end = found[d][0][:, C - 1 : C]
        reach_ref[jnp.bitwise_xor(me, d)] = jnp.where(row == col, jnp.exp(g_end), 0.0) - made[d]


def value_kernel(*refs):
    k_ref, inverse_ref, w_ref, tail_ref, reach_ref = refs[5:10]
    wu_ref, ab_ref, level_ref, states, v_ref = refs[10:]
    me = lax.axis_index("seq") % PLANE
    gather_slots(refs[:5], v_ref, slice(0, C))
    every = range(PLANE)
    reach = [reach_ref[i] for i in every]
    u = [mm_exact_right(inverse_ref[d], v_ref[d]) for d in every]
    reach_two = [mm(reach[2 * i + 1], reach[2 * i]) for i in range(4)]
    halves = []
    for d in every:
        wu_ref[d, :, :C] = w_ref[d]
        wu_ref[d, :, C:] = u[d]
        halves.append(jnp.concatenate(split(u[d] * tail_ref[d]), axis=0))
    keys = [k_ref[d, 0:C, :] for d in every]
    made = [dot_tn(jnp.concatenate([keys[d], keys[d]], axis=0), halves[d]) for d in every]
    reach_four = [mm(reach_two[2 * i + 1], reach_two[2 * i]) for i in range(2)]
    for d in every:
        states[jnp.bitwise_xor(me, d)] = made[d]
    one = [states[i] for i in every]
    two = [mm(reach[2 * i + 1], one[2 * i]) + one[2 * i + 1] for i in range(4)]
    ab_ref[:, :C] = mm(reach_four[1], reach_four[0]).astype(BF16)
    four = [mm(reach_two[2 * i + 1], two[2 * i]) + two[2 * i + 1] for i in range(2)]
    ab_ref[:, C:] = (mm(reach_four[1], four[0]) + four[1]).astype(BF16)
    levels = [(reach[0], one[0]), (reach_two[0], two[0]), (reach[2], one[2])]
    levels += [(reach_four[0], four[0]), (reach[4], one[4]), (reach_two[2], two[2])]
    for i, (across, state) in enumerate(levels + [(reach[6], one[6])]):
        level_ref[i, :, :C] = across
        level_ref[i, :, C:] = state


def key_part(slots):
    square = jax.ShapeDtypeStruct((PLANE, C, C), F32)
    return pl.pallas_call(
        key_kernel,
        out_shape=[jax.ShapeDtypeStruct((PLANE, KROWS, C), BF16)]
        + [square] * 5,
        in_specs=[vmem()] * 5,
        out_specs=[vmem()] * 6,
        compiler_params=params(),
        cost_estimate=cost(2e9, 4e6),
        name="keys",
    )(*slots)


def value_part(slots, k, inverse, w, tail, reach):
    return pl.pallas_call(
        value_kernel,
        out_shape=[
            jax.ShapeDtypeStruct((PLANE, C, 2 * C), F32),
            jax.ShapeDtypeStruct((C, 2 * C), BF16),
            jax.ShapeDtypeStruct((7, C, 2 * C), F32),
        ],
        in_specs=[vmem()] * 10,
        out_specs=[vmem()] * 3,
        scratch_shapes=[pltpu.VMEM((PLANE, C, C), F32), pltpu.VMEM((PLANE, C, C), BF16)],
        compiler_params=params(),
        cost_estimate=cost(1e9, 4e6),
        name="values",
    )(*slots, k, inverse, w, tail, reach)


def query_kernel(*refs):
    k_ref, mix_ref, wu_ref, level_ref, no_ref, before, q_ref = refs[5:]
    gather_slots(refs[:5], q_ref, slice(C, 2 * C))
    me = lax.axis_index("seq") % PLANE
    row, col = iotas()
    before[0] = jnp.concatenate([jnp.where(row == col, 1.0, 0.0), jnp.zeros((C, C), F32)], axis=1)
    before[1] = level_ref[0]
    before[2] = level_ref[1]
    before[3] = after(level_ref[1], level_ref[2])
    before[4] = level_ref[3]
    before[5] = after(level_ref[3], level_ref[4])
    six = after(level_ref[3], level_ref[5])
    before[6] = six
    before[7] = after(six, level_ref[6])

    every = range(PLANE)
    found = gates(k_ref)
    queries = [q_ref[d] for d in every]
    scored = [dot_nt(queries[d], k_ref[d, 0:C, :]) for d in every]
    r_cols = []
    for q in queries:
        wide = q.astype(F32)
        r_cols.append(lax.rsqrt(jnp.sum(wide * wide, axis=1, keepdims=True) + EPS) * (C**-0.5))
    scored = [scored[d] * r_cols[d] * mix_ref[d] for d in every]
    parts = [mm(scored[d], wu_ref[d]) for d in every]
    reach = [
        queries[d].astype(F32) * (r_cols[d] * jnp.exp(found[d][2])) - parts[d][:, :C]
        for d in every
    ]
    chunks = [jnp.bitwise_xor(me, d) for d in every]
    both = [mm(reach[d], before[chunks[d]]) for d in every]
    for d in every:
        rows = pl.ds(pl.multiple_of(chunks[d] * C, C), C)
        no_ref[rows, :] = jnp.concatenate(
            [both[d][:, :C], both[d][:, C:] + parts[d][:, C:]], axis=1
        )


def query(slots, k, mix, wu, level):
    return pl.pallas_call(
        query_kernel,
        out_shape=jax.ShapeDtypeStruct((PLANE * C, 2 * C), F32),
        in_specs=[vmem()] * 9,
        out_specs=vmem(),
        scratch_shapes=[
            pltpu.VMEM((PLANE, C, 2 * C), F32),
            pltpu.VMEM((PLANE, C, C), BF16),
        ],
        compiler_params=params(),
        cost_estimate=cost(1e9, 4e6),
        name="query",
    )(*slots, k, mix, wu, level)


def times(a, x):
    hi, lo = split(x)
    return dot(jnp.concatenate([a, a], axis=1), jnp.concatenate([hi, lo], axis=0))


def combine_kernel(own_ref, one_ref, two_ref, before_ref, upto_ref):
    a_one, a_own = one_ref[:, :C], own_ref[:, :C]
    reach = dot(a_one, two_ref[:, :C])
    state = one_ref[:, C:].astype(F32) + dot(a_one, two_ref[:, C:])
    before_ref[:, :C] = reach
    before_ref[:, C:] = state
    upto_ref[:, :C] = times(a_own, reach).astype(BF16)
    upto_ref[:, C:] = (own_ref[:, C:].astype(F32) + times(a_own, state)).astype(BF16)


def combine(own_map, one, two):
    return pl.pallas_call(
        combine_kernel,
        out_shape=[
            jax.ShapeDtypeStruct((C, 2 * C), F32),
            jax.ShapeDtypeStruct((C, 2 * C), BF16),
        ],
        in_specs=[vmem()] * 3,
        out_specs=[vmem()] * 2,
        compiler_params=params(),
        name="combine",
    )(own_map, one, two)


def norm_kernel(no_ref, gain_ref, before_ref, six_ref, three_ref, normed_ref):
    state = three_ref[:, C:].astype(F32) + dot(three_ref[:, :C], six_ref[:, C:])
    state = before_ref[:, C:] + mm(before_ref[:, :C], state)
    out = mm(no_ref[:, :C], state) + no_ref[:, C:]
    scale = lax.rsqrt(jnp.mean(out * out, axis=1, keepdims=True) + EPS)
    normed_ref[...] = (out * scale * gain_ref[...]).astype(BF16)


def norm(no, gain, before, six, three):
    return pl.pallas_call(
        norm_kernel,
        out_shape=jax.ShapeDtypeStruct((PLANE * C, C), BF16),
        in_specs=[vmem()] * 5,
        out_specs=vmem(),
        compiler_params=params(),
        cost_estimate=cost(2e8, 2e6),
        name="norm",
    )(no, gain, before, six, three)


QB = 256
SCALE = C**-0.5 * 1.4426950408889634


def squares():
    row = lax.broadcasted_iota(jnp.int32, (QB, QB), 0)
    col = lax.broadcasted_iota(jnp.int32, (QB, QB), 1)
    return row, col


def row_max(parts):
    top = jnp.max(parts[0], axis=1, keepdims=True)
    for part in parts[1:]:
        top = jnp.maximum(top, jnp.max(part, axis=1, keepdims=True))
    return top


def row_sum(parts):
    total = jnp.sum(parts[0], axis=1, keepdims=True)
    for part in parts[1:]:
        total = total + jnp.sum(part, axis=1, keepdims=True)
    return total


def weighted(parts, values):
    out = dot(parts[0].astype(BF16), values[0])
    for part, value in zip(parts[1:], values[1:]):
        out = out + dot(part.astype(BF16), value)
    return out


def tiled(column, like):
    return jnp.concatenate([column] * (like.shape[1] // C), axis=1)


def own_kernel(normed_ref, weight_ref, acc_ref, stat_ref, q2_ref):
    me = lax.axis_index("seq") % PLANE
    proj = dot(normed_ref[...], weight_ref[me]).astype(BF16)
    q2_ref[...] = proj[:, :C]
    row, col = squares()
    starts = range(0, PLANE * C, QB)
    spans = [[(at, at + QB)] + ([(0, at)] if at else []) for at in starts]
    scores = [
        [dot_nt(proj[at : at + QB, :C], proj[a:b, C : 2 * C]) for a, b in span]
        for at, span in zip(starts, spans)
    ]
    scores = [[jnp.where(col <= row, parts[0], NEG)] + parts[1:] for parts in scores]
    tops = [row_max(parts) for parts in scores]
    raised = [[jnp.exp2((s - top) * SCALE) for s in parts] for parts, top in zip(scores, tops)]
    for i, at in enumerate(starts):
        rows = slice(at, at + QB)
        acc_ref[rows, :] = weighted(raised[i], [proj[a:b, 2 * C :] for a, b in spans[i]])
        stat_ref[0, rows, :] = jnp.broadcast_to(tops[i], (QB, C))
        stat_ref[1, rows, :] = jnp.broadcast_to(row_sum(raised[i]), (QB, C))


def own(normed, weight):
    n = PLANE * C
    return pl.pallas_call(
        own_kernel,
        out_shape=[
            jax.ShapeDtypeStruct((n, C), F32),
            jax.ShapeDtypeStruct((2, n, C), F32),
            jax.ShapeDtypeStruct((n, C), BF16),
        ],
        in_specs=[vmem()] * 2,
        out_specs=[vmem()] * 3,
        compiler_params=params(),
        cost_estimate=cost(1e9, 3e6, 6e5),
        name="own",
    )(normed, weight)


def halo_kernel(halo_ref, weight_ref, acc_ref, stat_ref, q2_ref, *refs):
    keep, send, attended = refs
    place = lax.axis_index("seq")
    me, plane = place % PLANE, place // PLANE
    proj = dot(halo_ref[...], weight_ref[me, :, C:]).astype(BF16)
    n = PLANE * C
    row, col = squares()
    starts = range(0, n, QB)
    spans = [[(at, at + QB)] + ([(at + QB, n)] if at + QB < n else []) for at in starts]
    floor = jnp.where(plane > 0, 0.0, NEG)
    scores = [
        [dot_nt(q2_ref[at : at + QB, :], proj[a:b, :C]) for a, b in span]
        for at, span in zip(starts, spans)
    ]
    scores = [[jnp.where(col > row, parts[0], NEG)] + parts[1:] for parts in scores]
    before = [stat_ref[0, at : at + QB, :] for at in starts]
    tops = [jnp.maximum(row_max(parts) + floor, old) for parts, old in zip(scores, before)]
    raised = [
        [jnp.exp2((s - tiled(top - floor, s)) * SCALE) for s in parts]
        for parts, top in zip(scores, tops)
    ]
    fades = [jnp.exp2((old - top) * SCALE) for old, top in zip(before, tops)]
    for i, at in enumerate(starts):
        rows = slice(at, at + QB)
        total = row_sum(raised[i]) + fades[i] * stat_ref[1, rows, :]
        acc = acc_ref[rows, :] * fades[i] + weighted(
            raised[i], [proj[a:b, C:] for a, b in spans[i]]
        )
        attended[rows, :] = (acc / total).astype(BF16)
    for d in range(PLANE):
        chunk = jnp.bitwise_xor(me, d)
        out = send if d % 2 else keep
        out[d // 2] = attended[pl.ds(pl.multiple_of(chunk * C, C), C), :]


def halo_part(halo, weight, acc, stat, q2):
    n = PLANE * C
    return pl.pallas_call(
        halo_kernel,
        out_shape=[jax.ShapeDtypeStruct((4, C, C), BF16)] * 2,
        in_specs=[vmem()] * 5,
        out_specs=[vmem()] * 2,
        scratch_shapes=[pltpu.VMEM((n, C), BF16)],
        compiler_params=params(),
        cost_estimate=cost(1e9, 3e6, 6e5),
        name="halo",
    )(halo, weight, acc, stat, q2)


COLS = 1024


def pair_part(first, second, dx):
    core, mine = lax.axis_index("seq") % 2, lax.axis_index("heads")
    rows = [pl.ds(pl.multiple_of(lax.rem(mine + e, 4) * 32, 32), 32) for e in range(4)]
    one = jnp.concatenate([first[r, :] for r in rows], axis=0)
    two = jnp.concatenate([second[r, :] for r in rows], axis=0)
    swapped = core > 0
    left = jnp.where(swapped, two.astype(F32), one.astype(F32)).astype(BF16)
    right = jnp.where(swapped, one.astype(F32), two.astype(F32)).astype(BF16)
    chip = lax.axis_index("seq") % PLANE // 2
    at = pl.multiple_of(jnp.bitwise_xor(chip, dx) * 2 * C, 2 * C)
    return jnp.concatenate([left, right], axis=1), pl.ds(at, 2 * C)


def early_kernel(keep, came, one, weight_ref, acc_ref):
    parts = [pair_part(keep.at[0], came.at[0], 0), pair_part(one.at[0], one.at[1], 1)]
    for at in range(0, weight_ref.shape[1], COLS):
        cols = slice(at, at + COLS)
        got = dot(parts[0][0], weight_ref[parts[0][1], cols])
        for part, rows in parts[1:]:
            got = got + dot(part, weight_ref[rows, cols])
        acc_ref[:, cols] = got


def late_kernel(two, three, weight_ref, acc_ref, own_ref, right_ref, left_ref, *outs):
    parts = [pair_part(two.at[0], two.at[1], 2), pair_part(three.at[0], three.at[1], 3)]
    far_right, far_left, plain_right, plain_left = outs
    half = weight_ref.shape[1] // 2
    for at in range(0, 2 * half, COLS):
        cols = slice(at, at + COLS)
        got = acc_ref[:, cols]
        for part, rows in parts:
            got = got + dot(part, weight_ref[rows, cols])
        own_ref[:, cols] = got[0:32]
        if at < half:
            right_ref[:, cols] = got[32:64]
            far_right[:, cols] = got[64:96].astype(BF16)
            plain_left[:, cols] = got[96:128].astype(BF16)
        else:
            cols = slice(at - half, at - half + COLS)
            plain_right[:, cols] = got[32:64].astype(BF16)
            far_left[:, cols] = got[64:96].astype(BF16)
            left_ref[:, cols] = got[96:128]


def project(slots, weight):
    width = weight.shape[1]
    keep, came, one, two, three = slots
    acc = pl.pallas_call(
        early_kernel,
        out_shape=jax.ShapeDtypeStruct((C, width), F32),
        in_specs=[vmem()] * 4,
        out_specs=vmem(),
        compiler_params=params(),
        cost_estimate=cost(5e8, 4e6),
        name="early",
    )(keep, came, one, weight)
    return pl.pallas_call(
        late_kernel,
        out_shape=[jax.ShapeDtypeStruct((32, width), F32)]
        + [jax.ShapeDtypeStruct((32, width // 2), F32)] * 2
        + [jax.ShapeDtypeStruct((32, width // 2), BF16)] * 4,
        in_specs=[vmem()] * 4,
        out_specs=[vmem()] * 7,
        compiler_params=params(),
        cost_estimate=cost(3e8, 4e6),
        name="late",
    )(two, three, weight, acc)


def swap(block, d):
    return lax.ppermute(block, "seq", [(s, s ^ d) for s in range(PLANE * PLANES)])


def along_x_one(keep, came, dx, part):
    return swap(jnp.stack([keep[dx, part], came[dx, part]]), 2 * dx)


def along_x(keep, came, part=slice(None)):
    pairs = {dx: along_x_one(keep, came, dx, part) for dx in (2, 1, 3)}
    return [keep, came] + [pairs[dx] for dx in (1, 2, 3)]


def exchange(keep, send):
    return along_x(keep, swap(send, 1))


def later_plane(block, distance):
    step = PLANE * distance
    route = [(s, s + step) for s in range(PLANE * PLANES - step)]
    return lax.ppermute(block, "seq", route)


def local(q_delta, k_delta, v_delta, decay, beta, gain, attn_weight, out_weight):
    keep_k, send_k, keep, send = pack(q_delta, k_delta, v_delta, decay, beta)
    slots_k = exchange(keep_k, send_k)
    came = swap(send, 1)
    slots_v = along_x(keep, came, slice(0, C))
    k, mix, inverse, w, tail, reach = key_part(slots_k)
    wu, ab, level = value_part(slots_v, k, inverse, w, tail, reach)
    one = later_plane(ab, 1)
    two = later_plane(ab, 2)
    q_part = slice(C, 2 * C)
    keep_q, came_q, _ = lax.optimization_barrier((keep, came, ab))
    slots_q = along_x(keep_q, came_q, q_part)
    no = query(slots_q, k, mix, wu, level)
    before, upto = combine(ab, one, two)
    six = later_plane(upto, 6)
    three = later_plane(upto, 3)
    normed = norm(no, gain[None, :], before, six, three)
    halo = later_plane(normed, 1)
    acc, stat, q2 = own(normed, attn_weight)
    attended = exchange(*halo_part(halo, attn_weight, acc, stat, q2))
    return sum_over_heads(*project(attended, out_weight))


def sum_over_heads(own_sum, right, left, far_right, far_left, plain_right, plain_left):
    def turn(block, step):
        return lax.ppermute(block, "heads", [(s, (s + step) % 4) for s in range(4)])

    passed_right = turn(far_right, 1)
    passed_left = turn(far_left, 3)
    passed_right, passed_left = lax.optimization_barrier((passed_right, passed_left))
    plain_right = turn(plain_right, 1)
    plain_left = turn(plain_left, 3)
    right = turn((right + passed_right.astype(F32)).astype(BF16), 1)
    left = turn((left + passed_left.astype(F32)).astype(BF16), 3)
    others = jnp.concatenate(
        [right.astype(F32) + plain_left.astype(F32), left.astype(F32) + plain_right.astype(F32)],
        axis=1,
    )
    return (own_sum + others).astype(BF16)


def solution(mesh):
    placed = (
        P("seq", "heads"),
        P("seq", "heads"),
        P("seq", "heads"),
        P("heads", "seq"),
        P("heads", "seq"),
        P(),
        P("heads", None, None),
        P("heads", None),
    )
    return jax.shard_map(
        local, mesh=mesh, in_specs=placed, out_specs=P(("seq", "heads"), None), check_vma=False
    )
```

```python
import jax
import jax.numpy as jnp
from jax import lax
from jax.experimental import pallas as pl
from jax.experimental.pallas import tpu as pltpu
from jax.sharding import PartitionSpec as P

F32 = jnp.float32
BF16 = jnp.bfloat16
C = 128
PLANE = 8
PLANES = 8
KROWS = C + 16
B = 16
EPS = 1e-06
NEG = -1e30
VMEM_LIMIT = 24 * 1024 * 1024


def params(limit=VMEM_LIMIT):
    return pltpu.CompilerParams(vmem_limit_bytes=limit)


def cost(flops, nbytes, trans=0):
    return pl.CostEstimate(flops=int(flops), bytes_accessed=int(nbytes), transcendentals=int(trans))


def vmem():
    return pl.BlockSpec(memory_space=pltpu.VMEM)


def split(a):
    hi = a.astype(BF16)
    lo = (a - hi.astype(F32)).astype(BF16)
    return hi, lo


def dot(a, b):
    return lax.dot_general(a, b, (((1,), (0,)), ((), ())), preferred_element_type=F32)


def dot_nt(a, b):
    return lax.dot_general(a, b, (((1,), (1,)), ((), ())), preferred_element_type=F32)


def dot_tn(a, b):
    return lax.dot_general(a, b, (((0,), (0,)), ((), ())), preferred_element_type=F32)


def mm(a, b):
    ah, al = split(a)
    bh, bl = split(b)
    left = jnp.concatenate([ah, al], axis=1)
    n = b.shape[1]
    if n > C:
        return dot(left, jnp.concatenate([bh, bh], axis=0)) + dot(ah, bl)
    pair = jnp.concatenate([bh, bl], axis=1)
    out = dot(left, jnp.concatenate([pair, pair], axis=0))
    return out[:, :n] + out[:, n:]


def mm_exact_right(a, b):
    ah, al = split(a)
    return dot(jnp.concatenate([ah, al], axis=1), jnp.concatenate([b, b], axis=0))


def iotas():
    row = lax.broadcasted_iota(jnp.int32, (C, C), 0)
    col = lax.broadcasted_iota(jnp.int32, (C, C), 1)
    return row, col


def pack_kernel(q_ref, k_ref, v_ref, decay_ref, beta_ref, *rest):
    keep_k, send_k, keep, send, gate, raw, sems = rest
    me = lax.axis_index("seq") % PLANE
    copies = [
        pltpu.make_async_copy(decay_ref, raw.at[0], sems.at[24]),
        pltpu.make_async_copy(beta_ref, raw.at[1], sems.at[25]),
    ]
    for d in range(PLANE):
        cols = pl.ds(pl.multiple_of(jnp.bitwise_xor(me, d) * C, C), C)
        out_k, out = (send_k, send) if d % 2 else (keep_k, keep)
        at = d // 2
        copies += [
            pltpu.make_async_copy(k_ref.at[:, cols], out_k.at[at, pl.ds(0, C)], sems.at[3 * d]),
            pltpu.make_async_copy(v_ref.at[:, cols], out.at[at, pl.ds(0, C)], sems.at[3 * d + 1]),
            pltpu.make_async_copy(q_ref.at[:, cols], out.at[at, pl.ds(C, C)], sems.at[3 * d + 2]),
        ]
    for copy in copies:
        copy.start()
    copies[0].wait()
    copies[1].wait()
    for i in range(2):
        x = raw[i]
        for j in range(3):
            part = x.astype(BF16).astype(F32)
            gate[3 * i + j] = part
            x = x - part
    zeros = jnp.zeros((10, C), F32)
    for d in range(PLANE):
        head = jnp.bitwise_xor(me, d)
        rows = [gate[i, pl.ds(head, 1), :] for i in range(6)]
        out = send_k if d % 2 else keep_k
        out[d // 2, C:, :] = jnp.concatenate(rows + [zeros], axis=0).astype(BF16)
    for copy in copies[2:]:
        copy.wait()


def pack(q, k, v, decay, beta):
    any_space = pl.BlockSpec(memory_space=pltpu.HBM)
    first = jax.ShapeDtypeStruct((4, KROWS, C), BF16)
    wide = jax.ShapeDtypeStruct((4, 2 * C, C), BF16)
    return pl.pallas_call(
        pack_kernel,
        out_shape=[first, first, wide, wide],
        in_specs=[any_space] * 5,
        out_specs=[vmem()] * 4,
        scratch_shapes=[
            pltpu.VMEM((6, PLANE, C), F32),
            pltpu.VMEM((2, PLANE, C), F32),
            pltpu.SemaphoreType.DMA((26,)),
        ],
        compiler_params=params(),
        name="pack",
    )(*[pltpu.with_memory_space_constraint(x, pltpu.HBM) for x in (q, k, v, decay, beta)])


def gather_slots(refs, out_ref, part=None):
    keep, came = refs[0], refs[1]
    out_ref[0] = keep[0] if part is None else keep[0, part, :]
    out_ref[1] = came[0] if part is None else came[0, part, :]
    for dx in range(1, 4):
        out_ref[2 * dx] = refs[dx + 1][0]
        out_ref[2 * dx + 1] = refs[dx + 1][1]


def gates(k_ref):
    row, col = iotas()
    pieces = jnp.concatenate([k_ref[d, C:, :] for d in range(PLANE)], axis=0)
    upper = jnp.where(row <= col, 1.0, 0.0).astype(BF16)
    lower = jnp.where(row >= col, 1.0, 0.0).astype(BF16)
    eye = jnp.where(row == col, 1.0, 0.0).astype(BF16)
    along_row = dot(pieces, upper)
    along_col = dot_nt(jnp.concatenate([lower, eye], axis=0), pieces)
    plain = pieces.astype(F32)
    found = []
    for d in range(PLANE):
        o = 16 * d
        g_row = -(along_row[o : o + 1] + along_row[o + 1 : o + 2] + along_row[o + 2 : o + 3])
        b_row = plain[o + 3 : o + 4] + plain[o + 4 : o + 5] + plain[o + 5 : o + 6]
        g_col = -(
            along_col[:C, o : o + 1] + along_col[:C, o + 1 : o + 2] + along_col[:C, o + 2 : o + 3]
        )
        b_col = (
            along_col[C:, o + 3 : o + 4]
            + along_col[C:, o + 4 : o + 5]
            + along_col[C:, o + 5 : o + 6]
        )
        found.append((g_row, b_row, g_col, b_col))
    return found


def base_inverses(packed):
    row, col = iotas()
    high = packed.astype(BF16)
    rest = packed - high.astype(F32)
    mid = rest.astype(BF16)
    low = (rest - mid.astype(F32)).astype(BF16)
    three = jnp.concatenate([high, mid, low], axis=1)
    x = jnp.where(row % B == col % B, 1.0, 0.0)
    for j in range(B - 1):
        pick = jnp.where(row == col - col % B + j, 1.0, 0.0).astype(BF16)
        factor = dot(three, jnp.concatenate([pick, pick, pick], axis=0))
        line = x.reshape(PLANE, B, C)[:, j : j + 1, :]
        x = x - factor * jnp.broadcast_to(line, (PLANE, B, C)).reshape(C, C)
    return x


def after(earlier, later):
    both = mm(later[:, :C], earlier)
    return jnp.concatenate([both[:, :C], both[:, C:] + later[:, C:]], axis=1)


def key_kernel(*refs):
    k_ref, mix_ref, inverse_ref, w_ref, tail_ref, reach_ref = refs[5:]
    me = lax.axis_index("seq") % PLANE
    row, col = iotas()
    gather_slots(refs[:5], k_ref)
    every = range(PLANE)
    blocks = (row // B) == (col // B)
    apart = jnp.bitwise_xor(row, col)
    found = gates(k_ref)
    keys = [k_ref[d, 0:C, :] for d in every]
    grams = [dot_nt(k, k) for k in keys]
    diags = [jnp.where(row == col, g, 0.0) for g in grams]
    r_cols = [lax.rsqrt(jnp.sum(g, axis=1, keepdims=True) + EPS) for g in diags]
    r_rows = [lax.rsqrt(jnp.sum(g, axis=0, keepdims=True) + EPS) for g in diags]
    lows, packs = [], []
    for d in every:
        g_row, b_row, g_col, _ = found[d]
        ratio = jnp.where(row >= col, jnp.exp(jnp.minimum(g_col - g_row, 0.0)), 0.0)
        mix = ratio * (b_row * r_rows[d])
        mix_ref[d] = mix
        low = jnp.where(row > col, mix * grams[d] * r_cols[d], 0.0)
        lows.append(low)
        held = jnp.where(blocks, low, 0.0)
        packed = held[0:B]
        for b in range(1, C // B):
            packed = packed + held[B * b : B * b + B]
        packs.append(packed)
    base = base_inverses(jnp.concatenate(packs, axis=0))
    inverse = [
        jnp.where(blocks, jnp.concatenate([base[B * d : B * d + B]] * (C // B), axis=0), 0.0)
        for d in every
    ]
    size = B
    while size < C:
        level = (row > col) & (apart >= size) & (apart < 2 * size)
        half = [mm(x, jnp.where(level, low, 0.0)) for x, low in zip(inverse, lows)]
        inverse = [x - mm(h, x) for x, h in zip(inverse, half)]
        size *= 2
    folded = [inverse[d] * (jnp.exp(found[d][0]) * r_rows[d]) for d in every]
    w = [mm_exact_right(folded[d], keys[d]) for d in every]
    halves = []
    for d in every:
        g_row, _, g_col, b_col = found[d]
        tail = jnp.broadcast_to(jnp.exp(g_row[:, C - 1 : C] - g_col) * b_col * r_cols[d], (C, C))
        inverse_ref[d] = inverse[d]
        w_ref[d] = w[d]
        tail_ref[d] = tail
        halves.append(jnp.concatenate(split(w[d] * tail), axis=0))
    made = [dot_tn(jnp.concatenate([keys[d], keys[d]], axis=0), halves[d]) for d in every]
    for d in every:
        g_end = found[d][0][:, C - 1 : C]
        reach_ref[jnp.bitwise_xor(me, d)] = jnp.where(row == col, jnp.exp(g_end), 0.0) - made[d]


def value_kernel(*refs):
    k_ref, inverse_ref, w_ref, tail_ref, reach_ref = refs[5:10]
    wu_ref, ab_ref, level_ref, states, v_ref = refs[10:]
    me = lax.axis_index("seq") % PLANE
    gather_slots(refs[:5], v_ref, slice(0, C))
    every = range(PLANE)
    reach = [reach_ref[i] for i in every]
    u = [mm_exact_right(inverse_ref[d], v_ref[d]) for d in every]
    reach_two = [mm(reach[2 * i + 1], reach[2 * i]) for i in range(4)]
    halves = []
    for d in every:
        wu_ref[d, :, :C] = w_ref[d]
        wu_ref[d, :, C:] = u[d]
        halves.append(jnp.concatenate(split(u[d] * tail_ref[d]), axis=0))
    keys = [k_ref[d, 0:C, :] for d in every]
    made = [dot_tn(jnp.concatenate([keys[d], keys[d]], axis=0), halves[d]) for d in every]
    reach_four = [mm(reach_two[2 * i + 1], reach_two[2 * i]) for i in range(2)]
    for d in every:
        states[jnp.bitwise_xor(me, d)] = made[d]
    one = [states[i] for i in every]
    two = [mm(reach[2 * i + 1], one[2 * i]) + one[2 * i + 1] for i in range(4)]
    ab_ref[:, :C] = mm(reach_four[1], reach_four[0]).astype(BF16)
    four = [mm(reach_two[2 * i + 1], two[2 * i]) + two[2 * i + 1] for i in range(2)]
    ab_ref[:, C:] = (mm(reach_four[1], four[0]) + four[1]).astype(BF16)
    levels = [(reach[0], one[0]), (reach_two[0], two[0]), (reach[2], one[2])]
    levels += [(reach_four[0], four[0]), (reach[4], one[4]), (reach_two[2], two[2])]
    for i, (across, state) in enumerate(levels + [(reach[6], one[6])]):
        level_ref[i, :, :C] = across
        level_ref[i, :, C:] = state


def key_part(slots):
    square = jax.ShapeDtypeStruct((PLANE, C, C), F32)
    return pl.pallas_call(
        key_kernel,
        out_shape=[jax.ShapeDtypeStruct((PLANE, KROWS, C), BF16)]
        + [square] * 5,
        in_specs=[vmem()] * 5,
        out_specs=[vmem()] * 6,
        compiler_params=params(),
        cost_estimate=cost(2e9, 4e6),
        name="keys",
    )(*slots)


def value_part(slots, k, inverse, w, tail, reach):
    return pl.pallas_call(
        value_kernel,
        out_shape=[
            jax.ShapeDtypeStruct((PLANE, C, 2 * C), F32),
            jax.ShapeDtypeStruct((C, 2 * C), BF16),
            jax.ShapeDtypeStruct((7, C, 2 * C), F32),
        ],
        in_specs=[vmem()] * 10,
        out_specs=[vmem()] * 3,
        scratch_shapes=[pltpu.VMEM((PLANE, C, C), F32), pltpu.VMEM((PLANE, C, C), BF16)],
        compiler_params=params(),
        cost_estimate=cost(1e9, 4e6),
        name="values",
    )(*slots, k, inverse, w, tail, reach)


def query_kernel(*refs):
    k_ref, mix_ref, wu_ref, level_ref, no_ref, before, q_ref = refs[5:]
    gather_slots(refs[:5], q_ref, slice(C, 2 * C))
    me = lax.axis_index("seq") % PLANE
    row, col = iotas()
    before[0] = jnp.concatenate([jnp.where(row == col, 1.0, 0.0), jnp.zeros((C, C), F32)], axis=1)
    before[1] = level_ref[0]
    before[2] = level_ref[1]
    before[3] = after(level_ref[1], level_ref[2])
    before[4] = level_ref[3]
    before[5] = after(level_ref[3], level_ref[4])
    six = after(level_ref[3], level_ref[5])
    before[6] = six
    before[7] = after(six, level_ref[6])

    every = range(PLANE)
    found = gates(k_ref)
    queries = [q_ref[d] for d in every]
    scored = [dot_nt(queries[d], k_ref[d, 0:C, :]) for d in every]
    r_cols = []
    for q in queries:
        wide = q.astype(F32)
        r_cols.append(lax.rsqrt(jnp.sum(wide * wide, axis=1, keepdims=True) + EPS) * (C**-0.5))
    scored = [scored[d] * r_cols[d] * mix_ref[d] for d in every]
    parts = [mm(scored[d], wu_ref[d]) for d in every]
    reach = [
        queries[d].astype(F32) * (r_cols[d] * jnp.exp(found[d][2])) - parts[d][:, :C]
        for d in every
    ]
    chunks = [jnp.bitwise_xor(me, d) for d in every]
    both = [mm(reach[d], before[chunks[d]]) for d in every]
    for d in every:
        rows = pl.ds(pl.multiple_of(chunks[d] * C, C), C)
        no_ref[rows, :] = jnp.concatenate(
            [both[d][:, :C], both[d][:, C:] + parts[d][:, C:]], axis=1
        )


def query(slots, k, mix, wu, level):
    return pl.pallas_call(
        query_kernel,
        out_shape=jax.ShapeDtypeStruct((PLANE * C, 2 * C), F32),
        in_specs=[vmem()] * 9,
        out_specs=vmem(),
        scratch_shapes=[
            pltpu.VMEM((PLANE, C, 2 * C), F32),
            pltpu.VMEM((PLANE, C, C), BF16),
        ],
        compiler_params=params(),
        cost_estimate=cost(1e9, 4e6),
        name="query",
    )(*slots, k, mix, wu, level)


def times(a, x):
    hi, lo = split(x)
    return dot(jnp.concatenate([a, a], axis=1), jnp.concatenate([hi, lo], axis=0))


def combine_kernel(own_ref, two_ref, one_ref, before_ref, upto_ref):
    a_one, a_own = one_ref[:, :C], own_ref[:, :C]
    reach = dot(a_one, two_ref[:, :C])
    state = one_ref[:, C:].astype(F32) + dot(a_one, two_ref[:, C:])
    before_ref[:, :C] = reach
    before_ref[:, C:] = state
    upto_ref[:, :C] = times(a_own, reach).astype(BF16)
    upto_ref[:, C:] = (own_ref[:, C:].astype(F32) + times(a_own, state)).astype(BF16)


def combine(own_map, two, one):
    return pl.pallas_call(
        combine_kernel,
        out_shape=[
            jax.ShapeDtypeStruct((C, 2 * C), F32),
            jax.ShapeDtypeStruct((C, 2 * C), BF16),
        ],
        in_specs=[vmem()] * 3,
        out_specs=[vmem()] * 2,
        compiler_params=params(),
        name="combine",
    )(own_map, two, one)


def norm_kernel(no_ref, gain_ref, before_ref, six_ref, three_ref, normed_ref):
    state = three_ref[:, C:].astype(F32) + dot(three_ref[:, :C], six_ref[:, C:])
    state = before_ref[:, C:] + mm(before_ref[:, :C], state)
    out = mm(no_ref[:, :C], state) + no_ref[:, C:]
    scale = lax.rsqrt(jnp.mean(out * out, axis=1, keepdims=True) + EPS)
    normed_ref[...] = (out * scale * gain_ref[...]).astype(BF16)


def norm(no, gain, before, six, three):
    return pl.pallas_call(
        norm_kernel,
        out_shape=jax.ShapeDtypeStruct((PLANE * C, C), BF16),
        in_specs=[vmem()] * 5,
        out_specs=vmem(),
        compiler_params=params(),
        cost_estimate=cost(2e8, 2e6),
        name="norm",
    )(no, gain, before, six, three)


QB = 256
SCALE = C**-0.5 * 1.4426950408889634


def squares():
    row = lax.broadcasted_iota(jnp.int32, (QB, QB), 0)
    col = lax.broadcasted_iota(jnp.int32, (QB, QB), 1)
    return row, col


def row_max(parts):
    top = jnp.max(parts[0], axis=1, keepdims=True)
    for part in parts[1:]:
        top = jnp.maximum(top, jnp.max(part, axis=1, keepdims=True))
    return top


def row_sum(parts):
    total = jnp.sum(parts[0], axis=1, keepdims=True)
    for part in parts[1:]:
        total = total + jnp.sum(part, axis=1, keepdims=True)
    return total


def weighted(parts, values):
    out = dot(parts[0].astype(BF16), values[0])
    for part, value in zip(parts[1:], values[1:]):
        out = out + dot(part.astype(BF16), value)
    return out


def tiled(column, like):
    return jnp.concatenate([column] * (like.shape[1] // C), axis=1)


def own_kernel(normed_ref, weight_ref, acc_ref, stat_ref, q2_ref):
    me = lax.axis_index("seq") % PLANE
    proj = dot(normed_ref[...], weight_ref[me]).astype(BF16)
    q2_ref[...] = proj[:, :C]
    row, col = squares()
    starts = range(0, PLANE * C, QB)
    spans = [[(at, at + QB)] + ([(0, at)] if at else []) for at in starts]
    scores = [
        [dot_nt(proj[at : at + QB, :C], proj[a:b, C : 2 * C]) for a, b in span]
        for at, span in zip(starts, spans)
    ]
    scores = [[jnp.where(col <= row, parts[0], NEG)] + parts[1:] for parts in scores]
    tops = [row_max(parts) for parts in scores]
    raised = [[jnp.exp2((s - top) * SCALE) for s in parts] for parts, top in zip(scores, tops)]
    for i, at in enumerate(starts):
        rows = slice(at, at + QB)
        acc_ref[rows, :] = weighted(raised[i], [proj[a:b, 2 * C :] for a, b in spans[i]])
        stat_ref[0, rows, :] = jnp.broadcast_to(tops[i], (QB, C))
        stat_ref[1, rows, :] = jnp.broadcast_to(row_sum(raised[i]), (QB, C))


def own(normed, weight):
    n = PLANE * C
    return pl.pallas_call(
        own_kernel,
        out_shape=[
            jax.ShapeDtypeStruct((n, C), F32),
            jax.ShapeDtypeStruct((2, n, C), F32),
            jax.ShapeDtypeStruct((n, C), BF16),
        ],
        in_specs=[vmem()] * 2,
        out_specs=[vmem()] * 3,
        compiler_params=params(),
        cost_estimate=cost(1e9, 3e6, 6e5),
        name="own",
    )(normed, weight)


def halo_kernel(halo_ref, weight_ref, acc_ref, stat_ref, q2_ref, *refs):
    keep, send, attended = refs
    place = lax.axis_index("seq")
    me, plane = place % PLANE, place // PLANE
    proj = dot(halo_ref[...], weight_ref[me, :, C:]).astype(BF16)
    n = PLANE * C
    row, col = squares()
    starts = range(0, n, QB)
    spans = [[(at, at + QB)] + ([(at + QB, n)] if at + QB < n else []) for at in starts]
    floor = jnp.where(plane > 0, 0.0, NEG)
    scores = [
        [dot_nt(q2_ref[at : at + QB, :], proj[a:b, :C]) for a, b in span]
        for at, span in zip(starts, spans)
    ]
    scores = [[jnp.where(col > row, parts[0], NEG)] + parts[1:] for parts in scores]
    before = [stat_ref[0, at : at + QB, :] for at in starts]
    tops = [jnp.maximum(row_max(parts) + floor, old) for parts, old in zip(scores, before)]
    raised = [
        [jnp.exp2((s - tiled(top - floor, s)) * SCALE) for s in parts]
        for parts, top in zip(scores, tops)
    ]
    fades = [jnp.exp2((old - top) * SCALE) for old, top in zip(before, tops)]
    for i, at in enumerate(starts):
        rows = slice(at, at + QB)
        total = row_sum(raised[i]) + fades[i] * stat_ref[1, rows, :]
        acc = acc_ref[rows, :] * fades[i] + weighted(
            raised[i], [proj[a:b, C:] for a, b in spans[i]]
        )
        attended[rows, :] = (acc / total).astype(BF16)
    for d in range(PLANE):
        chunk = jnp.bitwise_xor(me, d)
        out = send if d % 2 else keep
        out[d // 2] = attended[pl.ds(pl.multiple_of(chunk * C, C), C), :]


def halo_part(halo, weight, acc, stat, q2):
    n = PLANE * C
    return pl.pallas_call(
        halo_kernel,
        out_shape=[jax.ShapeDtypeStruct((4, C, C), BF16)] * 2,
        in_specs=[vmem()] * 5,
        out_specs=[vmem()] * 2,
        scratch_shapes=[pltpu.VMEM((n, C), BF16)],
        compiler_params=params(),
        cost_estimate=cost(1e9, 3e6, 6e5),
        name="halo",
    )(halo, weight, acc, stat, q2)


COLS = 1024


def pair_part(first, second, dx):
    core, mine = lax.axis_index("seq") % 2, lax.axis_index("heads")
    rows = [pl.ds(pl.multiple_of(lax.rem(mine + e, 4) * 32, 32), 32) for e in range(4)]
    one = jnp.concatenate([first[r, :] for r in rows], axis=0)
    two = jnp.concatenate([second[r, :] for r in rows], axis=0)
    swapped = core > 0
    left = jnp.where(swapped, two.astype(F32), one.astype(F32)).astype(BF16)
    right = jnp.where(swapped, one.astype(F32), two.astype(F32)).astype(BF16)
    chip = lax.axis_index("seq") % PLANE // 2
    at = pl.multiple_of(jnp.bitwise_xor(chip, dx) * 2 * C, 2 * C)
    return jnp.concatenate([left, right], axis=1), pl.ds(at, 2 * C)


def early_kernel(keep, came, one, two, weight_ref, acc_ref):
    parts = [
        pair_part(keep.at[0], came.at[0], 0),
        pair_part(two.at[0], two.at[1], 2),
        pair_part(one.at[0], one.at[1], 1),
    ]
    for at in range(0, weight_ref.shape[1], COLS):
        cols = slice(at, at + COLS)
        got = dot(parts[0][0], weight_ref[parts[0][1], cols])
        for part, rows in parts[1:]:
            got = got + dot(part, weight_ref[rows, cols])
        acc_ref[:, cols] = got


def late_kernel(three, weight_ref, acc_ref, own_ref, right_ref, left_ref, *outs):
    part, rows = pair_part(three.at[0], three.at[1], 3)
    far_right, far_left, plain_right, plain_left = outs
    half = weight_ref.shape[1] // 2
    for at in range(0, 2 * half, COLS):
        cols = slice(at, at + COLS)
        got = acc_ref[:, cols] + dot(part, weight_ref[rows, cols])
        own_ref[:, cols] = got[0:32]
        if at < half:
            right_ref[:, cols] = got[32:64]
            far_right[:, cols] = got[64:96].astype(BF16)
            plain_left[:, cols] = got[96:128].astype(BF16)
        else:
            cols = slice(at - half, at - half + COLS)
            plain_right[:, cols] = got[32:64].astype(BF16)
            far_left[:, cols] = got[64:96].astype(BF16)
            left_ref[:, cols] = got[96:128]


def project(slots, weight):
    width = weight.shape[1]
    keep, came, one, two, three = slots
    acc = pl.pallas_call(
        early_kernel,
        out_shape=jax.ShapeDtypeStruct((C, width), F32),
        in_specs=[vmem()] * 5,
        out_specs=vmem(),
        compiler_params=params(),
        cost_estimate=cost(8e8, 8e6),
        name="early",
    )(keep, came, one, two, weight)
    return pl.pallas_call(
        late_kernel,
        out_shape=[jax.ShapeDtypeStruct((32, width), F32)]
        + [jax.ShapeDtypeStruct((32, width // 2), F32)] * 2
        + [jax.ShapeDtypeStruct((32, width // 2), BF16)] * 4,
        in_specs=[vmem()] * 3,
        out_specs=[vmem()] * 7,
        compiler_params=params(),
        cost_estimate=cost(3e8, 4e6),
        name="late",
    )(three, weight, acc)


def swap(block, d):
    return lax.ppermute(block, "seq", [(s, s ^ d) for s in range(PLANE * PLANES)])


def along_x(keep, came, part=slice(None)):
    pairs = {}
    for dx in (2, 1, 3):
        pairs[dx] = swap(jnp.stack([keep[dx, part], came[dx, part]]), 2 * dx)
    return [keep, came] + [pairs[dx] for dx in (1, 2, 3)]


def exchange(keep, send):
    return along_x(keep, swap(send, 1))


def later_plane(block, distance):
    step = PLANE * distance
    route = [(s, s + step) for s in range(PLANE * PLANES - step)]
    return lax.ppermute(block, "seq", route)


def local(q_delta, k_delta, v_delta, decay, beta, gain, attn_weight, out_weight):
    keep_k, send_k, keep, send = pack(q_delta, k_delta, v_delta, decay, beta)
    slots_k = exchange(keep_k, send_k)
    came = swap(send, 1)
    slots_v = along_x(keep, came, slice(0, C))
    k, mix, inverse, w, tail, reach = key_part(slots_k)
    wu, ab, level = value_part(slots_v, k, inverse, w, tail, reach)
    one = later_plane(ab, 1)
    two = later_plane(ab, 2)
    keep_q, came_q, _ = lax.optimization_barrier((keep, came, ab))
    slots_q = along_x(keep_q, came_q, slice(C, 2 * C))
    no = query(slots_q, k, mix, wu, level)
    before, upto = combine(ab, two, one)
    six = later_plane(upto, 6)
    three = later_plane(upto, 3)
    normed = norm(no, gain[None, :], before, six, three)
    halo = later_plane(normed, 1)
    acc, stat, q2 = own(normed, attn_weight)
    attended = exchange(*halo_part(halo, attn_weight, acc, stat, q2))
    return sum_over_heads(*project(attended, out_weight))


def sum_over_heads(own_sum, right, left, far_right, far_left, plain_right, plain_left):
    def turn(block, step):
        return lax.ppermute(block, "heads", [(s, (s + step) % 4) for s in range(4)])

    passed_right = turn(far_right, 1)
    passed_left = turn(far_left, 3)
    passed_right, passed_left = lax.optimization_barrier((passed_right, passed_left))
    plain_right = turn(plain_right, 1)
    plain_left = turn(plain_left, 3)
    right = turn((right + passed_right.astype(F32)).astype(BF16), 1)
    left = turn((left + passed_left.astype(F32)).astype(BF16), 3)
    others = jnp.concatenate(
        [right.astype(F32) + plain_left.astype(F32), left.astype(F32) + plain_right.astype(F32)],
        axis=1,
    )
    return (own_sum + others).astype(BF16)


def solution(mesh):
    placed = (
        P("seq", "heads"),
        P("seq", "heads"),
        P("seq", "heads"),
        P("heads", "seq"),
        P("heads", "seq"),
        P(),
        P("heads", None, None),
        P("heads", None),
    )
    return jax.shard_map(
        local, mesh=mesh, in_specs=placed, out_specs=P(("seq", "heads"), None), check_vma=False
    )
```

```python
import jax
import jax.numpy as jnp
from jax import lax
from jax.experimental import pallas as pl
from jax.experimental.pallas import tpu as pltpu
from jax.sharding import PartitionSpec as P

F32 = jnp.float32
BF16 = jnp.bfloat16
C = 128
PLANE = 8
PLANES = 8
KROWS = C + 16
B = 16
HALF = 512
EPS = 1e-06
NEG = -1e30
VMEM_LIMIT = 24 * 1024 * 1024


def params(limit=VMEM_LIMIT):
    return pltpu.CompilerParams(vmem_limit_bytes=limit)


def cost(flops, nbytes, trans=0):
    return pl.CostEstimate(flops=int(flops), bytes_accessed=int(nbytes), transcendentals=int(trans))


def vmem():
    return pl.BlockSpec(memory_space=pltpu.VMEM)


def split(a):
    hi = a.astype(BF16)
    lo = (a - hi.astype(F32)).astype(BF16)
    return hi, lo


def dot(a, b):
    return lax.dot_general(a, b, (((1,), (0,)), ((), ())), preferred_element_type=F32)


def dot_nt(a, b):
    return lax.dot_general(a, b, (((1,), (1,)), ((), ())), preferred_element_type=F32)


def dot_tn(a, b):
    return lax.dot_general(a, b, (((0,), (0,)), ((), ())), preferred_element_type=F32)


def mm(a, b):
    ah, al = split(a)
    bh, bl = split(b)
    left = jnp.concatenate([ah, al], axis=1)
    n = b.shape[1]
    if n > C:
        return dot(left, jnp.concatenate([bh, bh], axis=0)) + dot(ah, bl)
    pair = jnp.concatenate([bh, bl], axis=1)
    out = dot(left, jnp.concatenate([pair, pair], axis=0))
    return out[:, :n] + out[:, n:]


def mm_exact_right(a, b):
    ah, al = split(a)
    return dot(jnp.concatenate([ah, al], axis=1), jnp.concatenate([b, b], axis=0))


def iotas():
    row = lax.broadcasted_iota(jnp.int32, (C, C), 0)
    col = lax.broadcasted_iota(jnp.int32, (C, C), 1)
    return row, col


def pack_kernel(q_ref, k_ref, v_ref, decay_ref, beta_ref, *rest):
    keep_k, send_k, keep, send, gate, raw, sems = rest
    me = lax.axis_index("seq") % PLANE
    copies = [
        pltpu.make_async_copy(decay_ref, raw.at[0], sems.at[24]),
        pltpu.make_async_copy(beta_ref, raw.at[1], sems.at[25]),
    ]
    for d in range(PLANE):
        cols = pl.ds(pl.multiple_of(jnp.bitwise_xor(me, d) * C, C), C)
        out_k, out = (send_k, send) if d % 2 else (keep_k, keep)
        at = d // 2
        copies += [
            pltpu.make_async_copy(k_ref.at[:, cols], out_k.at[at, pl.ds(0, C)], sems.at[3 * d]),
            pltpu.make_async_copy(v_ref.at[:, cols], out.at[at, pl.ds(0, C)], sems.at[3 * d + 1]),
            pltpu.make_async_copy(q_ref.at[:, cols], out.at[at, pl.ds(C, C)], sems.at[3 * d + 2]),
        ]
    for copy in copies:
        copy.start()
    copies[0].wait()
    copies[1].wait()
    for i in range(2):
        x = raw[i]
        for j in range(3):
            part = x.astype(BF16).astype(F32)
            gate[3 * i + j] = part
            x = x - part
    zeros = jnp.zeros((10, C), F32)
    for d in range(PLANE):
        head = jnp.bitwise_xor(me, d)
        rows = [gate[i, pl.ds(head, 1), :] for i in range(6)]
        out = send_k if d % 2 else keep_k
        out[d // 2, C:, :] = jnp.concatenate(rows + [zeros], axis=0).astype(BF16)
    for copy in copies[2:]:
        copy.wait()


def pack(q, k, v, decay, beta):
    any_space = pl.BlockSpec(memory_space=pltpu.HBM)
    first = jax.ShapeDtypeStruct((4, KROWS, C), BF16)
    wide = jax.ShapeDtypeStruct((4, 2 * C, C), BF16)
    return pl.pallas_call(
        pack_kernel,
        out_shape=[first, first, wide, wide],
        in_specs=[any_space] * 5,
        out_specs=[vmem()] * 4,
        scratch_shapes=[
            pltpu.VMEM((6, PLANE, C), F32),
            pltpu.VMEM((2, PLANE, C), F32),
            pltpu.SemaphoreType.DMA((26,)),
        ],
        compiler_params=params(),
        name="pack",
    )(*[pltpu.with_memory_space_constraint(x, pltpu.HBM) for x in (q, k, v, decay, beta)])


def gather_slots(refs, out_ref, part=None):
    keep, came = refs[0], refs[1]
    out_ref[0] = keep[0] if part is None else keep[0, part, :]
    out_ref[1] = came[0] if part is None else came[0, part, :]
    for dx in range(1, 4):
        out_ref[2 * dx] = refs[dx + 1][0]
        out_ref[2 * dx + 1] = refs[dx + 1][1]


def gates(k_ref):
    row, col = iotas()
    pieces = jnp.concatenate([k_ref[d, C:, :] for d in range(PLANE)], axis=0)
    upper = jnp.where(row <= col, 1.0, 0.0).astype(BF16)
    lower = jnp.where(row >= col, 1.0, 0.0).astype(BF16)
    eye = jnp.where(row == col, 1.0, 0.0).astype(BF16)
    along_row = dot(pieces, upper)
    along_col = dot_nt(jnp.concatenate([lower, eye], axis=0), pieces)
    plain = pieces.astype(F32)
    found = []
    for d in range(PLANE):
        o = 16 * d
        g_row = -(along_row[o : o + 1] + along_row[o + 1 : o + 2] + along_row[o + 2 : o + 3])
        b_row = plain[o + 3 : o + 4] + plain[o + 4 : o + 5] + plain[o + 5 : o + 6]
        g_col = -(
            along_col[:C, o : o + 1] + along_col[:C, o + 1 : o + 2] + along_col[:C, o + 2 : o + 3]
        )
        b_col = (
            along_col[C:, o + 3 : o + 4]
            + along_col[C:, o + 4 : o + 5]
            + along_col[C:, o + 5 : o + 6]
        )
        found.append((g_row, b_row, g_col, b_col))
    return found


def base_inverses(packed):
    row, col = iotas()
    high = packed.astype(BF16)
    rest = packed - high.astype(F32)
    mid = rest.astype(BF16)
    low = (rest - mid.astype(F32)).astype(BF16)
    three = jnp.concatenate([high, mid, low], axis=1)
    x = jnp.where(row % B == col % B, 1.0, 0.0)
    for j in range(B - 1):
        pick = jnp.where(row == col - col % B + j, 1.0, 0.0).astype(BF16)
        factor = dot(three, jnp.concatenate([pick, pick, pick], axis=0))
        line = x.reshape(PLANE, B, C)[:, j : j + 1, :]
        x = x - factor * jnp.broadcast_to(line, (PLANE, B, C)).reshape(C, C)
    return x


def after(earlier, later):
    both = mm(later[:, :C], earlier)
    return jnp.concatenate([both[:, :C], both[:, C:] + later[:, C:]], axis=1)


def key_kernel(*refs):
    k_ref, mix_ref, inverse_ref, w_ref, tail_ref, reach_ref = refs[5:]
    me = lax.axis_index("seq") % PLANE
    row, col = iotas()
    gather_slots(refs[:5], k_ref)
    every = range(PLANE)
    blocks = (row // B) == (col // B)
    apart = jnp.bitwise_xor(row, col)
    found = gates(k_ref)
    keys = [k_ref[d, 0:C, :] for d in every]
    grams = [dot_nt(k, k) for k in keys]
    diags = [jnp.where(row == col, g, 0.0) for g in grams]
    r_cols = [lax.rsqrt(jnp.sum(g, axis=1, keepdims=True) + EPS) for g in diags]
    r_rows = [lax.rsqrt(jnp.sum(g, axis=0, keepdims=True) + EPS) for g in diags]
    lows, packs = [], []
    for d in every:
        g_row, b_row, g_col, _ = found[d]
        ratio = jnp.where(row >= col, jnp.exp(jnp.minimum(g_col - g_row, 0.0)), 0.0)
        mix = ratio * (b_row * r_rows[d])
        mix_ref[d] = mix
        low = jnp.where(row > col, mix * grams[d] * r_cols[d], 0.0)
        lows.append(low)
        held = jnp.where(blocks, low, 0.0)
        packed = held[0:B]
        for b in range(1, C // B):
            packed = packed + held[B * b : B * b + B]
        packs.append(packed)
    base = base_inverses(jnp.concatenate(packs, axis=0))
    inverse = [
        jnp.where(blocks, jnp.concatenate([base[B * d : B * d + B]] * (C // B), axis=0), 0.0)
        for d in every
    ]
    size = B
    while size < C:
        level = (row > col) & (apart >= size) & (apart < 2 * size)
        half = [mm(x, jnp.where(level, low, 0.0)) for x, low in zip(inverse, lows)]
        inverse = [x - mm(h, x) for x, h in zip(inverse, half)]
        size *= 2
    folded = [inverse[d] * (jnp.exp(found[d][0]) * r_rows[d]) for d in every]
    w = [mm_exact_right(folded[d], keys[d]) for d in every]
    halves = []
    for d in every:
        g_row, _, g_col, b_col = found[d]
        tail = jnp.broadcast_to(jnp.exp(g_row[:, C - 1 : C] - g_col) * b_col * r_cols[d], (C, C))
        inverse_ref[d] = inverse[d]
        w_ref[d] = w[d]
        tail_ref[d] = tail
        halves.append(jnp.concatenate(split(w[d] * tail), axis=0))
    made = [dot_tn(jnp.concatenate([keys[d], keys[d]], axis=0), halves[d]) for d in every]
    for d in every:
        g_end = found[d][0][:, C - 1 : C]
        reach_ref[jnp.bitwise_xor(me, d)] = jnp.where(row == col, jnp.exp(g_end), 0.0) - made[d]


def value_kernel(*refs):
    k_ref, inverse_ref, w_ref, tail_ref, reach_ref = refs[5:10]
    wu_ref, ab_ref, level_ref, states, v_ref = refs[10:]
    me = lax.axis_index("seq") % PLANE
    gather_slots(refs[:5], v_ref, slice(0, C))
    every = range(PLANE)
    reach = [reach_ref[i] for i in every]
    u = [mm_exact_right(inverse_ref[d], v_ref[d]) for d in every]
    reach_two = [mm(reach[2 * i + 1], reach[2 * i]) for i in range(4)]
    halves = []
    for d in every:
        wu_ref[d, :, :C] = w_ref[d]
        wu_ref[d, :, C:] = u[d]
        halves.append(jnp.concatenate(split(u[d] * tail_ref[d]), axis=0))
    keys = [k_ref[d, 0:C, :] for d in every]
    made = [dot_tn(jnp.concatenate([keys[d], keys[d]], axis=0), halves[d]) for d in every]
    reach_four = [mm(reach_two[2 * i + 1], reach_two[2 * i]) for i in range(2)]
    for d in every:
        states[jnp.bitwise_xor(me, d)] = made[d]
    one = [states[i] for i in every]
    two = [mm(reach[2 * i + 1], one[2 * i]) + one[2 * i + 1] for i in range(4)]
    ab_ref[:, :C] = mm(reach_four[1], reach_four[0]).astype(BF16)
    four = [mm(reach_two[2 * i + 1], two[2 * i]) + two[2 * i + 1] for i in range(2)]
    ab_ref[:, C:] = (mm(reach_four[1], four[0]) + four[1]).astype(BF16)
    levels = [(reach[0], one[0]), (reach_two[0], two[0]), (reach[2], one[2])]
    levels += [(reach_four[0], four[0]), (reach[4], one[4]), (reach_two[2], two[2])]
    for i, (across, state) in enumerate(levels + [(reach[6], one[6])]):
        level_ref[i, :, :C] = across
        level_ref[i, :, C:] = state


def key_part(slots):
    square = jax.ShapeDtypeStruct((PLANE, C, C), F32)
    return pl.pallas_call(
        key_kernel,
        out_shape=[jax.ShapeDtypeStruct((PLANE, KROWS, C), BF16)]
        + [square] * 5,
        in_specs=[vmem()] * 5,
        out_specs=[vmem()] * 6,
        compiler_params=params(),
        cost_estimate=cost(2e9, 4e6),
        name="keys",
    )(*slots)


def value_part(slots, k, inverse, w, tail, reach):
    return pl.pallas_call(
        value_kernel,
        out_shape=[
            jax.ShapeDtypeStruct((PLANE, C, 2 * C), F32),
            jax.ShapeDtypeStruct((C, 2 * C), BF16),
            jax.ShapeDtypeStruct((7, C, 2 * C), F32),
        ],
        in_specs=[vmem()] * 10,
        out_specs=[vmem()] * 3,
        scratch_shapes=[pltpu.VMEM((PLANE, C, C), F32), pltpu.VMEM((PLANE, C, C), BF16)],
        compiler_params=params(),
        cost_estimate=cost(1e9, 4e6),
        name="values",
    )(*slots, k, inverse, w, tail, reach)


def query_kernel(*refs):
    k_ref, mix_ref, wu_ref, level_ref, no_ref, before, q_ref = refs[5:]
    gather_slots(refs[:5], q_ref, slice(C, 2 * C))
    me = lax.axis_index("seq") % PLANE
    row, col = iotas()
    before[0] = jnp.concatenate([jnp.where(row == col, 1.0, 0.0), jnp.zeros((C, C), F32)], axis=1)
    before[1] = level_ref[0]
    before[2] = level_ref[1]
    before[3] = after(level_ref[1], level_ref[2])
    before[4] = level_ref[3]
    before[5] = after(level_ref[3], level_ref[4])
    six = after(level_ref[3], level_ref[5])
    before[6] = six
    before[7] = after(six, level_ref[6])

    every = range(PLANE)
    found = gates(k_ref)
    queries = [q_ref[d] for d in every]
    scored = [dot_nt(queries[d], k_ref[d, 0:C, :]) for d in every]
    r_cols = []
    for q in queries:
        wide = q.astype(F32)
        r_cols.append(lax.rsqrt(jnp.sum(wide * wide, axis=1, keepdims=True) + EPS) * (C**-0.5))
    scored = [scored[d] * r_cols[d] * mix_ref[d] for d in every]
    parts = [mm(scored[d], wu_ref[d]) for d in every]
    reach = [
        queries[d].astype(F32) * (r_cols[d] * jnp.exp(found[d][2])) - parts[d][:, :C]
        for d in every
    ]
    chunks = [jnp.bitwise_xor(me, d) for d in every]
    both = [mm(reach[d], before[chunks[d]]) for d in every]
    for d in every:
        rows = pl.ds(pl.multiple_of(chunks[d] * C, C), C)
        no_ref[rows, :] = jnp.concatenate(
            [both[d][:, :C], both[d][:, C:] + parts[d][:, C:]], axis=1
        )


def query(slots, k, mix, wu, level):
    return pl.pallas_call(
        query_kernel,
        out_shape=jax.ShapeDtypeStruct((PLANE * C, 2 * C), F32),
        in_specs=[vmem()] * 9,
        out_specs=vmem(),
        scratch_shapes=[
            pltpu.VMEM((PLANE, C, 2 * C), F32),
            pltpu.VMEM((PLANE, C, C), BF16),
        ],
        compiler_params=params(),
        cost_estimate=cost(1e9, 4e6),
        name="query",
    )(*slots, k, mix, wu, level)


def times(a, x):
    hi, lo = split(x)
    return dot(jnp.concatenate([a, a], axis=1), jnp.concatenate([hi, lo], axis=0))


def combine_kernel(own_ref, one_ref, two_ref, before_ref, upto_ref):
    a_one, a_own = one_ref[:, :C], own_ref[:, :C]
    reach = dot(a_one, two_ref[:, :C])
    state = one_ref[:, C:].astype(F32) + dot(a_one, two_ref[:, C:])
    before_ref[:, :C] = reach
    before_ref[:, C:] = state
    upto_ref[:, :C] = times(a_own, reach).astype(BF16)
    upto_ref[:, C:] = (own_ref[:, C:].astype(F32) + times(a_own, state)).astype(BF16)


def combine(own_map, one, two):
    return pl.pallas_call(
        combine_kernel,
        out_shape=[
            jax.ShapeDtypeStruct((C, 2 * C), F32),
            jax.ShapeDtypeStruct((C, 2 * C), BF16),
        ],
        in_specs=[vmem()] * 3,
        out_specs=[vmem()] * 2,
        compiler_params=params(),
        name="combine",
    )(own_map, one, two)


def norm_kernel(no_ref, gain_ref, before_ref, six_ref, three_ref, far_ref, near_ref):
    state = three_ref[:, C:].astype(F32) + dot(three_ref[:, :C], six_ref[:, C:])
    state = before_ref[:, C:] + mm(before_ref[:, :C], state)
    out = mm(no_ref[:, :C], state) + no_ref[:, C:]
    scale = lax.rsqrt(jnp.mean(out * out, axis=1, keepdims=True) + EPS)
    normed = (out * scale * gain_ref[...]).astype(BF16)
    far_ref[...] = normed[:HALF]
    near_ref[...] = normed[HALF:]


def norm(no, gain, before, six, three):
    return pl.pallas_call(
        norm_kernel,
        out_shape=[jax.ShapeDtypeStruct((HALF, C), BF16)] * 2,
        in_specs=[vmem()] * 5,
        out_specs=[vmem()] * 2,
        compiler_params=params(),
        cost_estimate=cost(2e8, 2e6),
        name="norm",
    )(no, gain, before, six, three)


QB = 256
SCALE = C**-0.5 * 1.4426950408889634


def squares():
    row = lax.broadcasted_iota(jnp.int32, (QB, QB), 0)
    col = lax.broadcasted_iota(jnp.int32, (QB, QB), 1)
    return row, col


def row_max(parts):
    top = jnp.max(parts[0], axis=1, keepdims=True)
    for part in parts[1:]:
        top = jnp.maximum(top, jnp.max(part, axis=1, keepdims=True))
    return top


def row_sum(parts):
    total = jnp.sum(parts[0], axis=1, keepdims=True)
    for part in parts[1:]:
        total = total + jnp.sum(part, axis=1, keepdims=True)
    return total


def weighted(parts, values):
    out = dot(parts[0].astype(BF16), values[0])
    for part, value in zip(parts[1:], values[1:]):
        out = out + dot(part.astype(BF16), value)
    return out


def tiled(column, like):
    return jnp.concatenate([column] * (like.shape[1] // C), axis=1)


def own_kernel(far_ref, near_ref, weight_ref, acc_ref, stat_ref, q2_ref):
    me = lax.axis_index("seq") % PLANE
    normed = jnp.concatenate([far_ref[...], near_ref[...]], axis=0)
    proj = dot(normed, weight_ref[me]).astype(BF16)
    q2_ref[...] = proj[:, :C]
    row, col = squares()
    starts = range(0, PLANE * C, QB)
    spans = [[(at, at + QB)] + ([(0, at)] if at else []) for at in starts]
    scores = [
        [dot_nt(proj[at : at + QB, :C], proj[a:b, C : 2 * C]) for a, b in span]
        for at, span in zip(starts, spans)
    ]
    scores = [[jnp.where(col <= row, parts[0], NEG)] + parts[1:] for parts in scores]
    tops = [row_max(parts) for parts in scores]
    raised = [[jnp.exp2((s - top) * SCALE) for s in parts] for parts, top in zip(scores, tops)]
    for i, at in enumerate(starts):
        rows = slice(at, at + QB)
        acc_ref[rows, :] = weighted(raised[i], [proj[a:b, 2 * C :] for a, b in spans[i]])
        stat_ref[0, rows, :] = jnp.broadcast_to(tops[i], (QB, C))
        stat_ref[1, rows, :] = jnp.broadcast_to(row_sum(raised[i]), (QB, C))


def own(far, near, weight):
    n = PLANE * C
    return pl.pallas_call(
        own_kernel,
        out_shape=[
            jax.ShapeDtypeStruct((n, C), F32),
            jax.ShapeDtypeStruct((2, n, C), F32),
            jax.ShapeDtypeStruct((n, C), BF16),
        ],
        in_specs=[vmem()] * 3,
        out_specs=[vmem()] * 3,
        compiler_params=params(),
        cost_estimate=cost(1e9, 3e6, 6e5),
        name="own",
    )(far, near, weight)


def add_halo(halo_ref, weight_ref, acc_ref, stat_ref, q2_ref, spans):
    place = lax.axis_index("seq")
    me, plane = place % PLANE, place // PLANE
    proj = dot(halo_ref[...], weight_ref[me, :, C:]).astype(BF16)
    row, col = squares()
    floor = jnp.where(plane > 0, 0.0, NEG)
    scores = []
    for at, masked, span in spans:
        parts = [dot_nt(q2_ref[at : at + QB, :], proj[a:b, :C]) for a, b in span]
        scores.append([jnp.where(col > row, parts[0], NEG)] + parts[1:] if masked else parts)
    before = [stat_ref[0, at : at + QB, :] for at, _, _ in spans]
    tops = [jnp.maximum(row_max(parts) + floor, old) for parts, old in zip(scores, before)]
    raised = [
        [jnp.exp2((s - tiled(top - floor, s)) * SCALE) for s in parts]
        for parts, top in zip(scores, tops)
    ]
    fades = [jnp.exp2((old - top) * SCALE) for old, top in zip(before, tops)]
    found = []
    for i, (at, _, span) in enumerate(spans):
        rows = slice(at, at + QB)
        total = row_sum(raised[i]) + fades[i] * stat_ref[1, rows, :]
        acc = acc_ref[rows, :] * fades[i] + weighted(
            raised[i], [proj[a:b, C:] for a, b in span]
        )
        found.append((tops[i], total, acc))
    return found


def near_kernel(halo_ref, weight_ref, acc_ref, stat_ref, q2_ref, new_acc, new_stat, done_ref):
    whole = [(0, HALF)]
    spans = [(0, False, whole), (QB, False, whole)]
    spans += [(2 * QB, True, [(0, QB), (QB, HALF)]), (3 * QB, True, [(QB, HALF)])]
    found = add_halo(halo_ref, weight_ref, acc_ref, stat_ref, q2_ref, spans)
    for i, (top, total, acc) in enumerate(found):
        if i < 2:
            rows = slice(i * QB, i * QB + QB)
            new_acc[rows, :] = acc
            new_stat[0, rows, :] = top
            new_stat[1, rows, :] = total
        else:
            done_ref[i * QB - HALF : i * QB - HALF + QB, :] = (acc / total).astype(BF16)


def far_kernel(halo_ref, weight_ref, acc_ref, stat_ref, q2_ref, done_ref, keep, send, attended):
    me = lax.axis_index("seq") % PLANE
    spans = [(0, True, [(0, QB), (QB, HALF)]), (QB, True, [(QB, HALF)])]
    found = add_halo(halo_ref, weight_ref, acc_ref, stat_ref, q2_ref, spans)
    for i, (_, total, acc) in enumerate(found):
        attended[i * QB : i * QB + QB, :] = (acc / total).astype(BF16)
    attended[HALF:, :] = done_ref[...]
    for d in range(PLANE):
        chunk = jnp.bitwise_xor(me, d)
        out = send if d % 2 else keep
        out[d // 2] = attended[pl.ds(pl.multiple_of(chunk * C, C), C), :]


def near_part(halo, weight, acc, stat, q2):
    return pl.pallas_call(
        near_kernel,
        out_shape=[
            jax.ShapeDtypeStruct((HALF, C), F32),
            jax.ShapeDtypeStruct((2, HALF, C), F32),
            jax.ShapeDtypeStruct((HALF, C), BF16),
        ],
        in_specs=[vmem()] * 5,
        out_specs=[vmem()] * 3,
        compiler_params=params(),
        cost_estimate=cost(8e8, 2e6, 4e5),
        name="near",
    )(halo, weight, acc, stat, q2)


def far_part(halo, weight, acc, stat, q2, done):
    return pl.pallas_call(
        far_kernel,
        out_shape=[jax.ShapeDtypeStruct((4, C, C), BF16)] * 2,
        in_specs=[vmem()] * 6,
        out_specs=[vmem()] * 2,
        scratch_shapes=[pltpu.VMEM((PLANE * C, C), BF16)],
        compiler_params=params(),
        cost_estimate=cost(3e8, 2e6, 2e5),
        name="far",
    )(halo, weight, acc, stat, q2, done)


COLS = 1024


def pair_part(first, second, dx):
    core, mine = lax.axis_index("seq") % 2, lax.axis_index("heads")
    rows = [pl.ds(pl.multiple_of(lax.rem(mine + e, 4) * 32, 32), 32) for e in range(4)]
    one = jnp.concatenate([first[r, :] for r in rows], axis=0)
    two = jnp.concatenate([second[r, :] for r in rows], axis=0)
    swapped = core > 0
    left = jnp.where(swapped, two.astype(F32), one.astype(F32)).astype(BF16)
    right = jnp.where(swapped, one.astype(F32), two.astype(F32)).astype(BF16)
    chip = lax.axis_index("seq") % PLANE // 2
    at = pl.multiple_of(jnp.bitwise_xor(chip, dx) * 2 * C, 2 * C)
    return jnp.concatenate([left, right], axis=1), pl.ds(at, 2 * C)


def early_kernel(keep, came, one, two, weight_ref, acc_ref):
    parts = [
        pair_part(keep.at[0], came.at[0], 0),
        pair_part(two.at[0], two.at[1], 2),
        pair_part(one.at[0], one.at[1], 1),
    ]
    for at in range(0, weight_ref.shape[1], COLS):
        cols = slice(at, at + COLS)
        got = dot(parts[0][0], weight_ref[parts[0][1], cols])
        for part, rows in parts[1:]:
            got = got + dot(part, weight_ref[rows, cols])
        acc_ref[:, cols] = got


def late_kernel(three, weight_ref, acc_ref, own_ref, right_ref, left_ref, *outs):
    part, rows = pair_part(three.at[0], three.at[1], 3)
    far_right, far_left, plain_right, plain_left = outs
    half = weight_ref.shape[1] // 2
    for at in range(0, 2 * half, COLS):
        cols = slice(at, at + COLS)
        got = acc_ref[:, cols] + dot(part, weight_ref[rows, cols])
        own_ref[:, cols] = got[0:32]
        if at < half:
            right_ref[:, cols] = got[32:64]
            far_right[:, cols] = got[64:96].astype(BF16)
            plain_left[:, cols] = got[96:128].astype(BF16)
        else:
            cols = slice(at - half, at - half + COLS)
            plain_right[:, cols] = got[32:64].astype(BF16)
            far_left[:, cols] = got[64:96].astype(BF16)
            left_ref[:, cols] = got[96:128]


def project(slots, weight):
    width = weight.shape[1]
    keep, came, one, two, three = slots
    acc = pl.pallas_call(
        early_kernel,
        out_shape=jax.ShapeDtypeStruct((C, width), F32),
        in_specs=[vmem()] * 5,
        out_specs=vmem(),
        compiler_params=params(),
        cost_estimate=cost(8e8, 8e6),
        name="early",
    )(keep, came, one, two, weight)
    return pl.pallas_call(
        late_kernel,
        out_shape=[jax.ShapeDtypeStruct((32, width), F32)]
        + [jax.ShapeDtypeStruct((32, width // 2), F32)] * 2
        + [jax.ShapeDtypeStruct((32, width // 2), BF16)] * 4,
        in_specs=[vmem()] * 3,
        out_specs=[vmem()] * 7,
        compiler_params=params(),
        cost_estimate=cost(3e8, 4e6),
        name="late",
    )(three, weight, acc)


def swap(block, d):
    return lax.ppermute(block, "seq", [(s, s ^ d) for s in range(PLANE * PLANES)])


def along_x(keep, came, part=slice(None)):
    pairs = {}
    for dx in (2, 1, 3):
        pairs[dx] = swap(jnp.stack([keep[dx, part], came[dx, part]]), 2 * dx)
    return [keep, came] + [pairs[dx] for dx in (1, 2, 3)]


def exchange(keep, send):
    return along_x(keep, swap(send, 1))


def later_plane(block, distance):
    step = PLANE * distance
    route = [(s, s + step) for s in range(PLANE * PLANES - step)]
    return lax.ppermute(block, "seq", route)


def local(q_delta, k_delta, v_delta, decay, beta, gain, attn_weight, out_weight):
    keep_k, send_k, keep, send = pack(q_delta, k_delta, v_delta, decay, beta)
    slots_k = exchange(keep_k, send_k)
    came = swap(send, 1)
    slots_v = along_x(keep, came, slice(0, C))
    k, mix, inverse, w, tail, reach = key_part(slots_k)
    wu, ab, level = value_part(slots_v, k, inverse, w, tail, reach)
    one = later_plane(ab, 1)
    two = later_plane(ab, 2)
    keep_q, came_q, _ = lax.optimization_barrier((keep, came, ab))
    slots_q = along_x(keep_q, came_q, slice(C, 2 * C))
    no = query(slots_q, k, mix, wu, level)
    before, upto = combine(ab, one, two)
    six = later_plane(upto, 6)
    three = later_plane(upto, 3)
    far, near = norm(no, gain[None, :], before, six, three)
    near_halo = later_plane(near, 1)
    far_halo = later_plane(far, 1)
    acc, stat, q2 = own(far, near, attn_weight)
    acc, stat, done = near_part(near_halo, attn_weight, acc, stat, q2)
    attended = exchange(*far_part(far_halo, attn_weight, acc, stat, q2, done))
    return sum_over_heads(*project(attended, out_weight))


def sum_over_heads(own_sum, right, left, far_right, far_left, plain_right, plain_left):
    def turn(block, step):
        return lax.ppermute(block, "heads", [(s, (s + step) % 4) for s in range(4)])

    passed_right = turn(far_right, 1)
    passed_left = turn(far_left, 3)
    passed_right, passed_left = lax.optimization_barrier((passed_right, passed_left))
    plain_right = turn(plain_right, 1)
    plain_left = turn(plain_left, 3)
    right = turn((right + passed_right.astype(F32)).astype(BF16), 1)
    left = turn((left + passed_left.astype(F32)).astype(BF16), 3)
    others = jnp.concatenate(
        [right.astype(F32) + plain_left.astype(F32), left.astype(F32) + plain_right.astype(F32)],
        axis=1,
    )
    return (own_sum + others).astype(BF16)


def solution(mesh):
    placed = (
        P("seq", "heads"),
        P("seq", "heads"),
        P("seq", "heads"),
        P("heads", "seq"),
        P("heads", "seq"),
        P(),
        P("heads", None, None),
        P("heads", None),
    )
    return jax.shard_map(
        local, mesh=mesh, in_specs=placed, out_specs=P(("seq", "heads"), None), check_vma=False
    )
```

```python
import jax
import jax.numpy as jnp
from jax import lax
from jax.experimental import pallas as pl
from jax.experimental.pallas import tpu as pltpu
from jax.sharding import PartitionSpec as P

F32 = jnp.float32
BF16 = jnp.bfloat16
C = 128
PLANE = 8
PLANES = 8
KROWS = C + 16
B = 16
EPS = 1e-06
NEG = -1e30
VMEM_LIMIT = 24 * 1024 * 1024


def params(limit=VMEM_LIMIT):
    return pltpu.CompilerParams(vmem_limit_bytes=limit)


def cost(flops, nbytes, trans=0):
    return pl.CostEstimate(flops=int(flops), bytes_accessed=int(nbytes), transcendentals=int(trans))


def vmem():
    return pl.BlockSpec(memory_space=pltpu.VMEM)


def split(a):
    hi = a.astype(BF16)
    lo = (a - hi.astype(F32)).astype(BF16)
    return hi, lo


def dot(a, b):
    return lax.dot_general(a, b, (((1,), (0,)), ((), ())), preferred_element_type=F32)


def dot_nt(a, b):
    return lax.dot_general(a, b, (((1,), (1,)), ((), ())), preferred_element_type=F32)


def dot_tn(a, b):
    return lax.dot_general(a, b, (((0,), (0,)), ((), ())), preferred_element_type=F32)


def mm(a, b):
    ah, al = split(a)
    bh, bl = split(b)
    left = jnp.concatenate([ah, al], axis=1)
    n = b.shape[1]
    if n > C:
        return dot(left, jnp.concatenate([bh, bh], axis=0)) + dot(ah, bl)
    pair = jnp.concatenate([bh, bl], axis=1)
    out = dot(left, jnp.concatenate([pair, pair], axis=0))
    return out[:, :n] + out[:, n:]


def mm_exact_right(a, b):
    ah, al = split(a)
    return dot(jnp.concatenate([ah, al], axis=1), jnp.concatenate([b, b], axis=0))


def iotas():
    row = lax.broadcasted_iota(jnp.int32, (C, C), 0)
    col = lax.broadcasted_iota(jnp.int32, (C, C), 1)
    return row, col


def pack_kernel(q_ref, k_ref, v_ref, decay_ref, beta_ref, *rest):
    keep_k, send_k, keep, send, gate, raw, sems = rest
    me = lax.axis_index("seq") % PLANE
    copies = [
        pltpu.make_async_copy(decay_ref, raw.at[0], sems.at[24]),
        pltpu.make_async_copy(beta_ref, raw.at[1], sems.at[25]),
    ]
    for d in range(PLANE):
        cols = pl.ds(pl.multiple_of(jnp.bitwise_xor(me, d) * C, C), C)
        out_k, out = (send_k, send) if d % 2 else (keep_k, keep)
        at = d // 2
        copies += [
            pltpu.make_async_copy(k_ref.at[:, cols], out_k.at[at, pl.ds(0, C)], sems.at[3 * d]),
            pltpu.make_async_copy(v_ref.at[:, cols], out.at[at, pl.ds(0, C)], sems.at[3 * d + 1]),
            pltpu.make_async_copy(q_ref.at[:, cols], out.at[at, pl.ds(C, C)], sems.at[3 * d + 2]),
        ]
    for copy in copies:
        copy.start()
    copies[0].wait()
    copies[1].wait()
    for i in range(2):
        x = raw[i]
        for j in range(3):
            part = x.astype(BF16).astype(F32)
            gate[3 * i + j] = part
            x = x - part
    zeros = jnp.zeros((10, C), F32)
    for d in range(PLANE):
        head = jnp.bitwise_xor(me, d)
        rows = [gate[i, pl.ds(head, 1), :] for i in range(6)]
        out = send_k if d % 2 else keep_k
        out[d // 2, C:, :] = jnp.concatenate(rows + [zeros], axis=0).astype(BF16)
    for copy in copies[2:]:
        copy.wait()


def pack(q, k, v, decay, beta):
    any_space = pl.BlockSpec(memory_space=pltpu.HBM)
    first = jax.ShapeDtypeStruct((4, KROWS, C), BF16)
    wide = jax.ShapeDtypeStruct((4, 2 * C, C), BF16)
    return pl.pallas_call(
        pack_kernel,
        out_shape=[first, first, wide, wide],
        in_specs=[any_space] * 5,
        out_specs=[vmem()] * 4,
        scratch_shapes=[
            pltpu.VMEM((6, PLANE, C), F32),
            pltpu.VMEM((2, PLANE, C), F32),
            pltpu.SemaphoreType.DMA((26,)),
        ],
        compiler_params=params(),
        name="pack",
    )(*[pltpu.with_memory_space_constraint(x, pltpu.HBM) for x in (q, k, v, decay, beta)])


def gather_slots(refs, out_ref, part=None):
    keep, came = refs[0], refs[1]
    out_ref[0] = keep[0] if part is None else keep[0, part, :]
    out_ref[1] = came[0] if part is None else came[0, part, :]
    for dx in range(1, 4):
        out_ref[2 * dx] = refs[dx + 1][0]
        out_ref[2 * dx + 1] = refs[dx + 1][1]


def gates(k_ref):
    row, col = iotas()
    pieces = jnp.concatenate([k_ref[d, C:, :] for d in range(PLANE)], axis=0)
    upper = jnp.where(row <= col, 1.0, 0.0).astype(BF16)
    lower = jnp.where(row >= col, 1.0, 0.0).astype(BF16)
    eye = jnp.where(row == col, 1.0, 0.0).astype(BF16)
    along_row = dot(pieces, upper)
    along_col = dot_nt(jnp.concatenate([lower, eye], axis=0), pieces)
    plain = pieces.astype(F32)
    found = []
    for d in range(PLANE):
        o = 16 * d
        g_row = -(along_row[o : o + 1] + along_row[o + 1 : o + 2] + along_row[o + 2 : o + 3])
        b_row = plain[o + 3 : o + 4] + plain[o + 4 : o + 5] + plain[o + 5 : o + 6]
        g_col = -(
            along_col[:C, o : o + 1] + along_col[:C, o + 1 : o + 2] + along_col[:C, o + 2 : o + 3]
        )
        b_col = (
            along_col[C:, o + 3 : o + 4]
            + along_col[C:, o + 4 : o + 5]
            + along_col[C:, o + 5 : o + 6]
        )
        found.append((g_row, b_row, g_col, b_col))
    return found


def base_inverses(packed):
    row, col = iotas()
    high = packed.astype(BF16)
    rest = packed - high.astype(F32)
    mid = rest.astype(BF16)
    low = (rest - mid.astype(F32)).astype(BF16)
    three = jnp.concatenate([high, mid, low], axis=1)
    x = jnp.where(row % B == col % B, 1.0, 0.0)
    for j in range(B - 1):
        pick = jnp.where(row == col - col % B + j, 1.0, 0.0).astype(BF16)
        factor = dot(three, jnp.concatenate([pick, pick, pick], axis=0))
        line = x.reshape(PLANE, B, C)[:, j : j + 1, :]
        x = x - factor * jnp.broadcast_to(line, (PLANE, B, C)).reshape(C, C)
    return x


def after(earlier, later):
    both = mm(later[:, :C], earlier)
    return jnp.concatenate([both[:, :C], both[:, C:] + later[:, C:]], axis=1)


def key_kernel(*refs):
    k_ref, mix_ref, inverse_ref, w_ref, tail_ref, reach_ref = refs[5:]
    me = lax.axis_index("seq") % PLANE
    row, col = iotas()
    gather_slots(refs[:5], k_ref)
    every = range(PLANE)
    blocks = (row // B) == (col // B)
    apart = jnp.bitwise_xor(row, col)
    found = gates(k_ref)
    keys = [k_ref[d, 0:C, :] for d in every]
    grams = [dot_nt(k, k) for k in keys]
    diags = [jnp.where(row == col, g, 0.0) for g in grams]
    r_cols = [lax.rsqrt(jnp.sum(g, axis=1, keepdims=True) + EPS) for g in diags]
    r_rows = [lax.rsqrt(jnp.sum(g, axis=0, keepdims=True) + EPS) for g in diags]
    lows, packs = [], []
    for d in every:
        g_row, b_row, g_col, _ = found[d]
        ratio = jnp.where(row >= col, jnp.exp(jnp.minimum(g_col - g_row, 0.0)), 0.0)
        mix = ratio * (b_row * r_rows[d])
        mix_ref[d] = mix
        low = jnp.where(row > col, mix * grams[d] * r_cols[d], 0.0)
        lows.append(low)
        held = jnp.where(blocks, low, 0.0)
        packed = held[0:B]
        for b in range(1, C // B):
            packed = packed + held[B * b : B * b + B]
        packs.append(packed)
    base = base_inverses(jnp.concatenate(packs, axis=0))
    inverse = [
        jnp.where(blocks, jnp.concatenate([base[B * d : B * d + B]] * (C // B), axis=0), 0.0)
        for d in every
    ]
    size = B
    while size < C:
        level = (row > col) & (apart >= size) & (apart < 2 * size)
        half = [mm(x, jnp.where(level, low, 0.0)) for x, low in zip(inverse, lows)]
        inverse = [x - mm(h, x) for x, h in zip(inverse, half)]
        size *= 2
    folded = [inverse[d] * (jnp.exp(found[d][0]) * r_rows[d]) for d in every]
    w = [mm_exact_right(folded[d], keys[d]) for d in every]
    halves = []
    for d in every:
        g_row, _, g_col, b_col = found[d]
        tail = jnp.broadcast_to(jnp.exp(g_row[:, C - 1 : C] - g_col) * b_col * r_cols[d], (C, C))
        inverse_ref[d] = inverse[d]
        w_ref[d] = w[d]
        tail_ref[d] = tail
        halves.append(jnp.concatenate(split(w[d] * tail), axis=0))
    made = [dot_tn(jnp.concatenate([keys[d], keys[d]], axis=0), halves[d]) for d in every]
    for d in every:
        g_end = found[d][0][:, C - 1 : C]
        reach_ref[jnp.bitwise_xor(me, d)] = jnp.where(row == col, jnp.exp(g_end), 0.0) - made[d]


def value_kernel(*refs):
    k_ref, inverse_ref, w_ref, tail_ref, reach_ref = refs[5:10]
    wu_ref, ab_ref, level_ref, states, v_ref = refs[10:]
    me = lax.axis_index("seq") % PLANE
    gather_slots(refs[:5], v_ref, slice(0, C))
    every = range(PLANE)
    reach = [reach_ref[i] for i in every]
    u = [mm_exact_right(inverse_ref[d], v_ref[d]) for d in every]
    reach_two = [mm(reach[2 * i + 1], reach[2 * i]) for i in range(4)]
    halves = []
    for d in every:
        wu_ref[d, :, :C] = w_ref[d]
        wu_ref[d, :, C:] = u[d]
        halves.append(jnp.concatenate(split(u[d] * tail_ref[d]), axis=0))
    keys = [k_ref[d, 0:C, :] for d in every]
    made = [dot_tn(jnp.concatenate([keys[d], keys[d]], axis=0), halves[d]) for d in every]
    reach_four = [mm(reach_two[2 * i + 1], reach_two[2 * i]) for i in range(2)]
    for d in every:
        states[jnp.bitwise_xor(me, d)] = made[d]
    one = [states[i] for i in every]
    two = [mm(reach[2 * i + 1], one[2 * i]) + one[2 * i + 1] for i in range(4)]
    ab_ref[:, :C] = mm(reach_four[1], reach_four[0]).astype(BF16)
    four = [mm(reach_two[2 * i + 1], two[2 * i]) + two[2 * i + 1] for i in range(2)]
    ab_ref[:, C:] = (mm(reach_four[1], four[0]) + four[1]).astype(BF16)
    levels = [(reach[0], one[0]), (reach_two[0], two[0]), (reach[2], one[2])]
    levels += [(reach_four[0], four[0]), (reach[4], one[4]), (reach_two[2], two[2])]
    for i, (across, state) in enumerate(levels + [(reach[6], one[6])]):
        level_ref[i, :, :C] = across
        level_ref[i, :, C:] = state


def key_part(slots):
    square = jax.ShapeDtypeStruct((PLANE, C, C), F32)
    return pl.pallas_call(
        key_kernel,
        out_shape=[jax.ShapeDtypeStruct((PLANE, KROWS, C), BF16)]
        + [square] * 5,
        in_specs=[vmem()] * 5,
        out_specs=[vmem()] * 6,
        compiler_params=params(),
        cost_estimate=cost(2e9, 4e6),
        name="keys",
    )(*slots)


def value_part(slots, k, inverse, w, tail, reach):
    return pl.pallas_call(
        value_kernel,
        out_shape=[
            jax.ShapeDtypeStruct((PLANE, C, 2 * C), F32),
            jax.ShapeDtypeStruct((C, 2 * C), BF16),
            jax.ShapeDtypeStruct((7, C, 2 * C), F32),
        ],
        in_specs=[vmem()] * 10,
        out_specs=[vmem()] * 3,
        scratch_shapes=[pltpu.VMEM((PLANE, C, C), F32), pltpu.VMEM((PLANE, C, C), BF16)],
        compiler_params=params(),
        cost_estimate=cost(1e9, 4e6),
        name="values",
    )(*slots, k, inverse, w, tail, reach)


def query_kernel(*refs):
    k_ref, mix_ref, wu_ref, level_ref, n_ref, o_ref, before, q_ref = refs[5:]
    gather_slots(refs[:5], q_ref, slice(C, 2 * C))
    me = lax.axis_index("seq") % PLANE
    row, col = iotas()
    before[0] = jnp.concatenate([jnp.where(row == col, 1.0, 0.0), jnp.zeros((C, C), F32)], axis=1)
    before[1] = level_ref[0]
    before[2] = level_ref[1]
    before[3] = after(level_ref[1], level_ref[2])
    before[4] = level_ref[3]
    before[5] = after(level_ref[3], level_ref[4])
    six = after(level_ref[3], level_ref[5])
    before[6] = six
    before[7] = after(six, level_ref[6])

    every = range(PLANE)
    found = gates(k_ref)
    queries = [q_ref[d] for d in every]
    scored = [dot_nt(queries[d], k_ref[d, 0:C, :]) for d in every]
    r_cols = []
    for q in queries:
        wide = q.astype(F32)
        r_cols.append(lax.rsqrt(jnp.sum(wide * wide, axis=1, keepdims=True) + EPS) * (C**-0.5))
    scored = [scored[d] * r_cols[d] * mix_ref[d] for d in every]
    parts = [mm(scored[d], wu_ref[d]) for d in every]
    reach = [
        queries[d].astype(F32) * (r_cols[d] * jnp.exp(found[d][2])) - parts[d][:, :C]
        for d in every
    ]
    chunks = [jnp.bitwise_xor(me, d) for d in every]
    both = [mm(reach[d], before[chunks[d]]) for d in every]
    for d in every:
        rows = pl.ds(pl.multiple_of(chunks[d] * C, C), C)
        n_ref[rows, :] = jnp.concatenate(split(both[d][:, :C]), axis=1)
        o_ref[rows, :] = both[d][:, C:] + parts[d][:, C:]


def query(slots, k, mix, wu, level):
    return pl.pallas_call(
        query_kernel,
        out_shape=[
            jax.ShapeDtypeStruct((PLANE * C, 2 * C), BF16),
            jax.ShapeDtypeStruct((PLANE * C, C), F32),
        ],
        in_specs=[vmem()] * 9,
        out_specs=[vmem()] * 2,
        scratch_shapes=[
            pltpu.VMEM((PLANE, C, 2 * C), F32),
            pltpu.VMEM((PLANE, C, C), BF16),
        ],
        compiler_params=params(),
        cost_estimate=cost(1e9, 4e6),
        name="query",
    )(*slots, k, mix, wu, level)


def times(a, x):
    hi, lo = split(x)
    return dot(jnp.concatenate([a, a], axis=1), jnp.concatenate([hi, lo], axis=0))


def combine_kernel(own_ref, one_ref, two_ref, before_ref, upto_ref):
    a_one, a_own = one_ref[:, :C], own_ref[:, :C]
    reach = dot(a_one, two_ref[:, :C])
    state = one_ref[:, C:].astype(F32) + dot(a_one, two_ref[:, C:])
    before_ref[:, :C] = reach
    before_ref[:, C:] = state
    upto_ref[:, :C] = times(a_own, reach).astype(BF16)
    upto_ref[:, C:] = (own_ref[:, C:].astype(F32) + times(a_own, state)).astype(BF16)


def combine(own_map, one, two):
    return pl.pallas_call(
        combine_kernel,
        out_shape=[
            jax.ShapeDtypeStruct((C, 2 * C), F32),
            jax.ShapeDtypeStruct((C, 2 * C), BF16),
        ],
        in_specs=[vmem()] * 3,
        out_specs=[vmem()] * 2,
        compiler_params=params(),
        name="combine",
    )(own_map, one, two)


def norm_kernel(n_ref, o_ref, gain_ref, before_ref, six_ref, three_ref, normed_ref):
    state = three_ref[:, C:].astype(F32) + dot(three_ref[:, :C], six_ref[:, C:])
    state = before_ref[:, C:] + mm(before_ref[:, :C], state)
    pair = jnp.concatenate(split(state), axis=1)
    out = dot(n_ref[...], jnp.concatenate([pair, pair], axis=0))
    out = out[:, :C] + out[:, C:] + o_ref[...]
    scale = lax.rsqrt(jnp.mean(out * out, axis=1, keepdims=True) + EPS)
    normed_ref[...] = (out * scale * gain_ref[...]).astype(BF16)


def norm(n, o, gain, before, six, three):
    return pl.pallas_call(
        norm_kernel,
        out_shape=jax.ShapeDtypeStruct((PLANE * C, C), BF16),
        in_specs=[vmem()] * 6,
        out_specs=vmem(),
        compiler_params=params(),
        cost_estimate=cost(2e8, 2e6),
        name="norm",
    )(n, o, gain, before, six, three)


QB = 256
SCALE = C**-0.5 * 1.4426950408889634


def squares():
    row = lax.broadcasted_iota(jnp.int32, (QB, QB), 0)
    col = lax.broadcasted_iota(jnp.int32, (QB, QB), 1)
    return row, col


def row_max(parts):
    top = jnp.max(parts[0], axis=1, keepdims=True)
    for part in parts[1:]:
        top = jnp.maximum(top, jnp.max(part, axis=1, keepdims=True))
    return top


def row_sum(parts):
    total = jnp.sum(parts[0], axis=1, keepdims=True)
    for part in parts[1:]:
        total = total + jnp.sum(part, axis=1, keepdims=True)
    return total


def weighted(parts, values):
    out = dot(parts[0].astype(BF16), values[0])
    for part, value in zip(parts[1:], values[1:]):
        out = out + dot(part.astype(BF16), value)
    return out


def tiled(column, like):
    return jnp.concatenate([column] * (like.shape[1] // C), axis=1)


def own_kernel(normed_ref, weight_ref, acc_ref, stat_ref, q2_ref):
    me = lax.axis_index("seq") % PLANE
    proj = dot(normed_ref[...], weight_ref[me]).astype(BF16)
    q2_ref[...] = proj[:, :C]
    row, col = squares()
    starts = range(0, PLANE * C, QB)
    spans = [[(at, at + QB)] + ([(0, at)] if at else []) for at in starts]
    scores = [
        [dot_nt(proj[at : at + QB, :C], proj[a:b, C : 2 * C]) for a, b in span]
        for at, span in zip(starts, spans)
    ]
    scores = [[jnp.where(col <= row, parts[0], NEG)] + parts[1:] for parts in scores]
    tops = [row_max(parts) for parts in scores]
    raised = [[jnp.exp2((s - top) * SCALE) for s in parts] for parts, top in zip(scores, tops)]
    for i, at in enumerate(starts):
        rows = slice(at, at + QB)
        acc_ref[rows, :] = weighted(raised[i], [proj[a:b, 2 * C :] for a, b in spans[i]])
        stat_ref[0, rows, :] = jnp.broadcast_to(tops[i], (QB, C))
        stat_ref[1, rows, :] = jnp.broadcast_to(row_sum(raised[i]), (QB, C))


def own(normed, weight):
    n = PLANE * C
    return pl.pallas_call(
        own_kernel,
        out_shape=[
            jax.ShapeDtypeStruct((n, C), F32),
            jax.ShapeDtypeStruct((2, n, C), F32),
            jax.ShapeDtypeStruct((n, C), BF16),
        ],
        in_specs=[vmem()] * 2,
        out_specs=[vmem()] * 3,
        compiler_params=params(),
        cost_estimate=cost(1e9, 3e6, 6e5),
        name="own",
    )(normed, weight)


def halo_kernel(halo_ref, weight_ref, acc_ref, stat_ref, q2_ref, *refs):
    keep, send, attended = refs
    place = lax.axis_index("seq")
    me, plane = place % PLANE, place // PLANE
    proj = dot(halo_ref[...], weight_ref[me, :, C:]).astype(BF16)
    n = PLANE * C
    row, col = squares()
    starts = range(0, n, QB)
    spans = [[(at, at + QB)] + ([(at + QB, n)] if at + QB < n else []) for at in starts]
    floor = jnp.where(plane > 0, 0.0, NEG)
    scores = [
        [dot_nt(q2_ref[at : at + QB, :], proj[a:b, :C]) for a, b in span]
        for at, span in zip(starts, spans)
    ]
    scores = [[jnp.where(col > row, parts[0], NEG)] + parts[1:] for parts in scores]
    before = [stat_ref[0, at : at + QB, :] for at in starts]
    tops = [jnp.maximum(row_max(parts) + floor, old) for parts, old in zip(scores, before)]
    raised = [
        [jnp.exp2((s - tiled(top - floor, s)) * SCALE) for s in parts]
        for parts, top in zip(scores, tops)
    ]
    fades = [jnp.exp2((old - top) * SCALE) for old, top in zip(before, tops)]
    for i, at in enumerate(starts):
        rows = slice(at, at + QB)
        total = row_sum(raised[i]) + fades[i] * stat_ref[1, rows, :]
        acc = acc_ref[rows, :] * fades[i] + weighted(
            raised[i], [proj[a:b, C:] for a, b in spans[i]]
        )
        attended[rows, :] = (acc / total).astype(BF16)
    for d in range(PLANE):
        chunk = jnp.bitwise_xor(me, d)
        out = send if d % 2 else keep
        out[d // 2] = attended[pl.ds(pl.multiple_of(chunk * C, C), C), :]


def halo_part(halo, weight, acc, stat, q2):
    n = PLANE * C
    return pl.pallas_call(
        halo_kernel,
        out_shape=[jax.ShapeDtypeStruct((4, C, C), BF16)] * 2,
        in_specs=[vmem()] * 5,
        out_specs=[vmem()] * 2,
        scratch_shapes=[pltpu.VMEM((n, C), BF16)],
        compiler_params=params(),
        cost_estimate=cost(1e9, 3e6, 6e5),
        name="halo",
    )(halo, weight, acc, stat, q2)


COLS = 1024


def pair_part(first, second, dx):
    core, mine = lax.axis_index("seq") % 2, lax.axis_index("heads")
    rows = [pl.ds(pl.multiple_of(lax.rem(mine + e, 4) * 32, 32), 32) for e in range(4)]
    one = jnp.concatenate([first[r, :] for r in rows], axis=0)
    two = jnp.concatenate([second[r, :] for r in rows], axis=0)
    swapped = core > 0
    left = jnp.where(swapped, two.astype(F32), one.astype(F32)).astype(BF16)
    right = jnp.where(swapped, one.astype(F32), two.astype(F32)).astype(BF16)
    chip = lax.axis_index("seq") % PLANE // 2
    at = pl.multiple_of(jnp.bitwise_xor(chip, dx) * 2 * C, 2 * C)
    return jnp.concatenate([left, right], axis=1), pl.ds(at, 2 * C)


def early_kernel(keep, came, one, two, weight_ref, acc_ref):
    parts = [
        pair_part(keep.at[0], came.at[0], 0),
        pair_part(two.at[0], two.at[1], 2),
        pair_part(one.at[0], one.at[1], 1),
    ]
    for at in range(0, weight_ref.shape[1], COLS):
        cols = slice(at, at + COLS)
        got = dot(parts[0][0], weight_ref[parts[0][1], cols])
        for part, rows in parts[1:]:
            got = got + dot(part, weight_ref[rows, cols])
        acc_ref[:, cols] = got


def late_kernel(three, weight_ref, acc_ref, own_ref, right_ref, left_ref, *outs):
    part, rows = pair_part(three.at[0], three.at[1], 3)
    far_right, far_left, plain_right, plain_left = outs
    half = weight_ref.shape[1] // 2
    for at in range(0, 2 * half, COLS):
        cols = slice(at, at + COLS)
        got = acc_ref[:, cols] + dot(part, weight_ref[rows, cols])
        own_ref[:, cols] = got[0:32]
        if at < half:
            right_ref[:, cols] = got[32:64]
            far_right[:, cols] = got[64:96].astype(BF16)
            plain_left[:, cols] = got[96:128].astype(BF16)
        else:
            cols = slice(at - half, at - half + COLS)
            plain_right[:, cols] = got[32:64].astype(BF16)
            far_left[:, cols] = got[64:96].astype(BF16)
            left_ref[:, cols] = got[96:128]


def project(slots, weight):
    width = weight.shape[1]
    keep, came, one, two, three = slots
    acc = pl.pallas_call(
        early_kernel,
        out_shape=jax.ShapeDtypeStruct((C, width), F32),
        in_specs=[vmem()] * 5,
        out_specs=vmem(),
        compiler_params=params(),
        cost_estimate=cost(8e8, 8e6),
        name="early",
    )(keep, came, one, two, weight)
    return pl.pallas_call(
        late_kernel,
        out_shape=[jax.ShapeDtypeStruct((32, width), F32)]
        + [jax.ShapeDtypeStruct((32, width // 2), F32)] * 2
        + [jax.ShapeDtypeStruct((32, width // 2), BF16)] * 4,
        in_specs=[vmem()] * 3,
        out_specs=[vmem()] * 7,
        compiler_params=params(),
        cost_estimate=cost(3e8, 4e6),
        name="late",
    )(three, weight, acc)


def swap(block, d):
    return lax.ppermute(block, "seq", [(s, s ^ d) for s in range(PLANE * PLANES)])


def along_x(keep, came, part=slice(None)):
    pairs = {}
    for dx in (2, 1, 3):
        pairs[dx] = swap(jnp.stack([keep[dx, part], came[dx, part]]), 2 * dx)
    return [keep, came] + [pairs[dx] for dx in (1, 2, 3)]


def exchange(keep, send):
    return along_x(keep, swap(send, 1))


def later_plane(block, distance):
    step = PLANE * distance
    route = [(s, s + step) for s in range(PLANE * PLANES - step)]
    return lax.ppermute(block, "seq", route)


def local(q_delta, k_delta, v_delta, decay, beta, gain, attn_weight, out_weight):
    keep_k, send_k, keep, send = pack(q_delta, k_delta, v_delta, decay, beta)
    slots_k = exchange(keep_k, send_k)
    came = swap(send, 1)
    slots_v = along_x(keep, came, slice(0, C))
    k, mix, inverse, w, tail, reach = key_part(slots_k)
    wu, ab, level = value_part(slots_v, k, inverse, w, tail, reach)
    one = later_plane(ab, 1)
    two = later_plane(ab, 2)
    keep_q, came_q, _ = lax.optimization_barrier((keep, came, ab))
    slots_q = along_x(keep_q, came_q, slice(C, 2 * C))
    n, o = query(slots_q, k, mix, wu, level)
    before, upto = combine(ab, one, two)
    six = later_plane(upto, 6)
    three = later_plane(upto, 3)
    normed = norm(n, o, gain[None, :], before, six, three)
    halo = later_plane(normed, 1)
    acc, stat, q2 = own(normed, attn_weight)
    attended = exchange(*halo_part(halo, attn_weight, acc, stat, q2))
    return sum_over_heads(*project(attended, out_weight))


def sum_over_heads(own_sum, right, left, far_right, far_left, plain_right, plain_left):
    def turn(block, step):
        return lax.ppermute(block, "heads", [(s, (s + step) % 4) for s in range(4)])

    passed_right = turn(far_right, 1)
    passed_left = turn(far_left, 3)
    passed_right, passed_left = lax.optimization_barrier((passed_right, passed_left))
    plain_right = turn(plain_right, 1)
    plain_left = turn(plain_left, 3)
    right = turn((right + passed_right.astype(F32)).astype(BF16), 1)
    left = turn((left + passed_left.astype(F32)).astype(BF16), 3)
    others = jnp.concatenate(
        [right.astype(F32) + plain_left.astype(F32), left.astype(F32) + plain_right.astype(F32)],
        axis=1,
    )
    return (own_sum + others).astype(BF16)


def solution(mesh):
    placed = (
        P("seq", "heads"),
        P("seq", "heads"),
        P("seq", "heads"),
        P("heads", "seq"),
        P("heads", "seq"),
        P(),
        P("heads", None, None),
        P("heads", None),
    )
    return jax.shard_map(
        local, mesh=mesh, in_specs=placed, out_specs=P(("seq", "heads"), None), check_vma=False
    )
```
